32 devices in a mesh: row: 16 (over z, x, core), head: 2 (over y).
Axes of the slice: x: 2, y: 2, z: 4, core: 2. Of those that a mesh axis runs over, the one named last changes fastest.
Arguments:
- single: bfloat16 [2, 384, 384], replicated, may hold values from -6 to 6
- residue_index: int32 [2, 384], replicated, may hold values from 1 to 768, as said below
- chain_index: int32 [2, 384], replicated, may hold values from 0 to 1, as said below
- token_mask: int32 [2, 384], replicated, may hold values from 0 to 1, as said below
- pair_valid: int32 [2, 384, 384], P(None, 'row', 'head'), may hold values from 0 to 1
- target_bins: int32 [2, 384, 384], P(None, 'row', 'head'), may hold values from 0 to 63
- relative_table: float32 [66, 128], replicated, may hold values from -6 to 6
- single_weight: float32 [384, 256], replicated, may hold values from -0.3125 to 0.3125
- triangle_input: float32 [2, 2, 128, 640], replicated, may hold values from -0.5 to 0.5
- triangle_output: float32 [2, 2, 128, 128], replicated, may hold values from -0.5 to 0.5
- expand_weight: float32 [2, 128, 1024], replicated, may hold values from -0.5 to 0.5
- reduce_weight: float32 [2, 512, 128], replicated, may hold values from -0.25 to 0.25
- distogram_weight: float32 [128, 64], replicated, may hold values from -1 to 1
- norm_gains: float32 [11, 128], replicated, may hold values from 0.5 to 1.5
- first_table: float32 [66, 128], replicated, may hold values from -1.4305115e-06 to 1.4305115e-06
- second_table: float32 [66, 128], replicated, may hold values from 4.4307387e-15 to 1.7722955e-14
- first_single: float32 [384, 256], replicated, may hold values from -1.4305115e-06 to 1.4305115e-06
- second_single: float32 [384, 256], replicated, may hold values from 4.4307387e-15 to 1.7722955e-14
- first_input: float32 [2, 2, 128, 640], replicated, may hold values from -1.4305115e-06 to 1.4305115e-06
- second_input: float32 [2, 2, 128, 640], replicated, may hold values from 4.4307387e-15 to 1.7722955e-14
- first_output: float32 [2, 2, 128, 128], replicated, may hold values from -1.4305115e-06 to 1.4305115e-06
- second_output: float32 [2, 2, 128, 128], replicated, may hold values from 4.4307387e-15 to 1.7722955e-14
- first_expand: float32 [2, 128, 1024], replicated, may hold values from -1.4305115e-06 to 1.4305115e-06
- second_expand: float32 [2, 128, 1024], replicated, may hold values from 4.4307387e-15 to 1.7722955e-14
- first_reduce: float32 [2, 512, 128], replicated, may hold values from -1.4305115e-06 to 1.4305115e-06
- second_reduce: float32 [2, 512, 128], replicated, may hold values from 4.4307387e-15 to 1.7722955e-14
- first_logits: float32 [128, 64], replicated, may hold values from -1.4305115e-06 to 1.4305115e-06
- second_logits: float32 [128, 64], replicated, may hold values from 4.4307387e-15 to 1.7722955e-14
- first_gains: float32 [11, 128], replicated, may hold values from -6.67572e-06 to 6.67572e-06
- second_gains: float32 [11, 128], replicated, may hold values from 1.1076847e-13 to 4.4307388e-13
Outputs:
- loss_sum: float32 [], replicated
- valid_count: float32 [], replicated
- gradient_norm: float32 [], replicated
- table_moment: float32 [66, 128], replicated
- table_square: float32 [66, 128], replicated
- table_master: float32 [66, 128], replicated
- single_moment: float32 [384, 256], replicated
- single_square: float32 [384, 256], replicated
- single_master: float32 [384, 256], replicated
- input_moment: float32 [2, 2, 128, 640], replicated
- input_square: float32 [2, 2, 128, 640], replicated
- input_master: float32 [2, 2, 128, 640], replicated
- output_moment: float32 [2, 2, 128, 128], replicated
- output_square: float32 [2, 2, 128, 128], replicated
- output_master: float32 [2, 2, 128, 128], replicated
- expand_moment: float32 [2, 128, 1024], replicated
- expand_square: float32 [2, 128, 1024], replicated
- expand_master: float32 [2, 128, 1024], replicated
- reduce_moment: float32 [2, 512, 128], replicated
- reduce_square: float32 [2, 512, 128], replicated
- reduce_master: float32 [2, 512, 128], replicated
- logits_moment: float32 [128, 64], replicated
- logits_square: float32 [128, 64], replicated
- logits_master: float32 [128, 64], replicated
- gains_moment: float32 [11, 128], replicated
- gains_square: float32 [11, 128], replicated
- gains_master: float32 [11, 128], replicated
The draws below stay inside these ranges and needn't reach their ends.
Inputs may be any that keep to these rules, and one draw needn't show every extreme that they name: token_mask is 1 on a prefix of each crop of 192 tokens or more; one crop, drawn from the seed, is whole. chain_index is 0 on a prefix of each crop and 1 on the rest, both present. residue_index rises along each crop, from 1 at its first token to 768 at its last.
All inputs are finite; a program needn't handle non-finite values.
Results may differ from the reference program's by a relative error of at most 0.0069.
Values may be sent and summed in bfloat16 or wider, within the bound.
A program may use at most 832 MiB of HBM per device.

```python
import math
import jax
import jax.numpy as jnp
from jax import lax

C = 128
H = 128
CS = 384
BINS = 64
FF = 512
REACH = 32
NREL = 66
N = 384
CROPS = 2
LAYERS = 2
STEP = 10
PARAMS = 902784


def draw_token_mask(key, part):
    key = jax.random.fold_in(key, 11)
    first_key, second_key = jax.random.split(key)
    lengths = jax.random.randint(first_key, (CROPS,), N // 2, N)
    whole = jax.random.randint(second_key, (), 0, CROPS)
    lengths = jnp.where(jnp.arange(CROPS) == whole, N, lengths)
    return (jnp.arange(N)[None, :] < lengths[:, None]).astype(jnp.int32)


def draw_chain_index(key, part):
    key = jax.random.fold_in(key, 12)
    cuts = jax.random.randint(key, (CROPS, 1), N // 4, 3 * N // 4)
    return (jnp.arange(N)[None, :] >= cuts).astype(jnp.int32)


def draw_residue_index(key, part):
    key = jax.random.fold_in(key, 13)
    paces = jax.random.randint(key, (CROPS, N), 1, 3)
    place = jnp.arange(N)[None, :]
    paces = jnp.where(place == 0, 1, paces)
    walked = jnp.cumsum(paces, axis=1)
    return jnp.where(place == N - 1, 2 * N, walked).astype(jnp.int32)


def draw_pair_valid(key, part):
    key = jax.random.fold_in(key, 14)
    rolls = jax.random.randint(key, (CROPS, N, N), 0, 1000)
    place = jnp.arange(N)
    level = 20 + 480 * (place[:, None] + place[None, :]) // N
    return (rolls < level[None]).astype(jnp.int32)


def touch_ends(array, stream_key, smallest, top_value):
    spot = [jax.random.randint(jax.random.fold_in(stream_key, axis), (), 0, length) for axis, length in enumerate(array.shape)]
    main_axis = array.shape.index(max(array.shape))
    neighbour = spot[:main_axis] + [(spot[main_axis] + 1) % array.shape[main_axis]] + spot[main_axis + 1:]
    return array.at[tuple(spot)].set(smallest).at[tuple(neighbour)].set(top_value)


def scatter_about(stream_key, extent, scale, limit, kind=jnp.bfloat16):
    array = scale * jax.random.normal(stream_key, extent, jnp.float32)
    return jnp.clip(array, min=-limit, max=limit).astype(kind)


def setup_inputs(seed: int = 0) -> dict:
    splits = jax.random.split(jax.random.key(seed), 31)
    return {
        "single": scatter_about(splits[0], (CROPS, N, CS), 1.0, 6.0),
        "residue_index": draw_residue_index(jax.random.fold_in(splits[30], 71), 0),
        "chain_index": draw_chain_index(jax.random.fold_in(splits[30], 71), 0),
        "token_mask": draw_token_mask(jax.random.fold_in(splits[30], 71), 0),
        "pair_valid": draw_pair_valid(jax.random.fold_in(splits[30], 71), 0),
        "target_bins": touch_ends(jax.random.randint(splits[5], (CROPS, N, N), 0, BINS), jax.random.fold_in(splits[5], 1), 0, BINS - 1).astype(jnp.int32),
        "relative_table": scatter_about(splits[6], (NREL, C), 1.0, 6.0, jnp.float32),
        "single_weight": scatter_about(splits[7], (CS, 2 * C), CS ** -0.5, 0.3125, jnp.float32),
        "triangle_input": scatter_about(splits[8], (LAYERS, 2, C, 4 * H + C), C ** -0.5, 0.5, jnp.float32),
        "triangle_output": scatter_about(splits[9], (LAYERS, 2, H, C), H ** -0.5, 0.5, jnp.float32),
        "expand_weight": scatter_about(splits[10], (LAYERS, C, 2 * FF), C ** -0.5, 0.5, jnp.float32),
        "reduce_weight": scatter_about(splits[11], (LAYERS, FF, C), FF ** -0.5, 0.25, jnp.float32),
        "distogram_weight": scatter_about(splits[12], (C, BINS), (C // 4) ** -0.5, 1.0, jnp.float32),
        "norm_gains": jnp.clip(1.0 + 0.1 * jax.random.normal(splits[13], (5 * LAYERS + 1, C), jnp.float32), 0.5, 1.5),
        "first_table": scatter_about(splits[14], (NREL, C), (0.00022 * PARAMS ** -0.5), 1.430511474609375e-06, jnp.float32),
        "second_table": jnp.clip(jnp.exp(jax.random.uniform(splits[15], (NREL, C), jnp.float32, math.log(4.430738714561889e-15), math.log(1.7722954858247555e-14))), 4.430738714561889e-15, 1.7722954858247555e-14),
        "first_single": scatter_about(splits[16], (CS, 2 * C), (0.00022 * PARAMS ** -0.5), 1.430511474609375e-06, jnp.float32),
        "second_single": jnp.clip(jnp.exp(jax.random.uniform(splits[17], (CS, 2 * C), jnp.float32, math.log(4.430738714561889e-15), math.log(1.7722954858247555e-14))), 4.430738714561889e-15, 1.7722954858247555e-14),
        "first_input": scatter_about(splits[18], (LAYERS, 2, C, 4 * H + C), (0.00022 * PARAMS ** -0.5), 1.430511474609375e-06, jnp.float32),
        "second_input": jnp.clip(jnp.exp(jax.random.uniform(splits[19], (LAYERS, 2, C, 4 * H + C), jnp.float32, math.log(4.430738714561889e-15), math.log(1.7722954858247555e-14))), 4.430738714561889e-15, 1.7722954858247555e-14),
        "first_output": scatter_about(splits[20], (LAYERS, 2, H, C), (0.00022 * PARAMS ** -0.5), 1.430511474609375e-06, jnp.float32),
        "second_output": jnp.clip(jnp.exp(jax.random.uniform(splits[21], (LAYERS, 2, H, C), jnp.float32, math.log(4.430738714561889e-15), math.log(1.7722954858247555e-14))), 4.430738714561889e-15, 1.7722954858247555e-14),
        "first_expand": scatter_about(splits[22], (LAYERS, C, 2 * FF), (0.00022 * PARAMS ** -0.5), 1.430511474609375e-06, jnp.float32),
        "second_expand": jnp.clip(jnp.exp(jax.random.uniform(splits[23], (LAYERS, C, 2 * FF), jnp.float32, math.log(4.430738714561889e-15), math.log(1.7722954858247555e-14))), 4.430738714561889e-15, 1.7722954858247555e-14),
        "first_reduce": scatter_about(splits[24], (LAYERS, FF, C), (0.00022 * PARAMS ** -0.5), 1.430511474609375e-06, jnp.float32),
        "second_reduce": jnp.clip(jnp.exp(jax.random.uniform(splits[25], (LAYERS, FF, C), jnp.float32, math.log(4.430738714561889e-15), math.log(1.7722954858247555e-14))), 4.430738714561889e-15, 1.7722954858247555e-14),
        "first_logits": scatter_about(splits[26], (C, BINS), (0.00022 * PARAMS ** -0.5), 1.430511474609375e-06, jnp.float32),
        "second_logits": jnp.clip(jnp.exp(jax.random.uniform(splits[27], (C, BINS), jnp.float32, math.log(4.430738714561889e-15), math.log(1.7722954858247555e-14))), 4.430738714561889e-15, 1.7722954858247555e-14),
        "first_gains": scatter_about(splits[28], (5 * LAYERS + 1, C), (0.0011 * PARAMS ** -0.5), 6.67572021484375e-06, jnp.float32),
        "second_gains": jnp.clip(jnp.exp(jax.random.uniform(splits[29], (5 * LAYERS + 1, C), jnp.float32, math.log(1.1076847040514606e-13), math.log(4.4307388162058425e-13))), 1.1076847040514606e-13, 4.4307388162058425e-13),
    }


@jax.custom_vjp
def low(v):
    return lax.optimization_barrier(v.astype(jnp.bfloat16)).astype(jnp.float32)

@jax.custom_vjp
def low_back(v):
    return v

def low_keep(v):
    return (low(v), None)

def low_pass(kept, grad):
    return (grad,)

def back_keep(v):
    return (v, None)

def back_low(kept, grad):
    return (low(grad),)
low.defvjp(low_keep, low_pass)
low_back.defvjp(back_keep, back_low)
EPS = 1e-05
BETA_ONE = 0.9
BETA_TWO = 0.999
ADAM_EPS = 1e-08
WEIGHT_RATE = 0.1
GAIN_RATE = 0.5
WEIGHT_DECAY = 0.01
CLIP_NORM = 0.002

def normalize(value, gain):
    mean = lax.optimization_barrier(jnp.mean(value, axis=-1, keepdims=True))
    centred = value - mean
    spread = lax.optimization_barrier(jnp.mean(centred * centred, axis=-1, keepdims=True))
    return centred * lax.rsqrt(spread + EPS) * gain

def project(value, weight):
    return jnp.einsum('...c,cd->...d', value, weight, precision=lax.Precision.HIGHEST)

def triangle_update(state, weight_in, weight_out, gains, pair_mask, form):
    normed = low(normalize(state, gains[0]))
    mixed = low_back(project(normed, low(weight_in)))
    mask = pair_mask[..., None]
    left = low_back(low(mask * jax.nn.sigmoid(mixed[..., :H]) * mixed[..., H:2 * H]))
    right = low_back(low(mask * jax.nn.sigmoid(mixed[..., 2 * H:3 * H]) * mixed[..., 3 * H:4 * H]))
    triangle = jnp.einsum(form, left, right, precision=lax.Precision.HIGHEST)
    triangle = low_back(low(triangle))
    shaped = low(normalize(triangle, gains[1]))
    branch = low_back(project(shaped, low(weight_out)))
    return state + jax.nn.sigmoid(mixed[..., 4 * H:]) * branch

def pair_block(state, weight_in, weight_out, weight_up, weight_down, gains, pair_mask):
    state = triangle_update(state, weight_in[0], weight_out[0], gains[0:2], pair_mask, 'bikc,bjkc->bijc')
    middle = triangle_update(state, weight_in[1], weight_out[1], gains[2:4], pair_mask, 'bkic,bkjc->bijc')
    lifted = low(normalize(middle, gains[4]))
    inner = low_back(project(lifted, low(weight_up)))
    product = low(jax.nn.silu(inner[..., :FF]) * inner[..., FF:])
    return middle + low_back(project(product, low(weight_down)))

def full_loss(weights, single, relative_hot, pair_mask, loss_weight, target_hot):
    table, single_weight, weight_in, weight_out, weight_up, weight_down, weight_logits, gains = weights
    proj = project(low(single), low(single_weight))
    state = project(relative_hot, low(table)) + proj[:, :, None, :C] + proj[:, None, :, C:]
    block = jax.checkpoint(pair_block)
    for layer in range(LAYERS):
        state = block(state, weight_in[layer], weight_out[layer], weight_up[layer], weight_down[layer], gains[5 * layer:5 * layer + 5], pair_mask)
    shown = low(normalize(state, gains[5 * LAYERS]))
    logits = low_back(project(shown, low(weight_logits)))
    largest = lax.optimization_barrier(jnp.max(logits, axis=-1, keepdims=True))
    log_total = largest[..., 0] + jnp.log(lax.optimization_barrier(jnp.sum(jnp.exp(logits - largest), axis=-1)))
    picked = lax.optimization_barrier(jnp.sum(logits * target_hot, axis=-1))
    return jnp.sum(loss_weight * (log_total - picked))

def adamw(weight, grad, first, second, rate, decay):
    first_new = BETA_ONE * first + (1.0 - BETA_ONE) * grad
    second_new = BETA_TWO * second + (1.0 - BETA_TWO) * grad * grad
    moved = first_new / (1.0 - BETA_ONE ** STEP) / (jnp.sqrt(second_new / (1.0 - BETA_TWO ** STEP)) + ADAM_EPS)
    return (first_new, second_new, weight - rate * (moved + decay * weight))

def reference(single, residue_index, chain_index, token_mask, pair_valid, target_bins, relative_table, single_weight, triangle_input, triangle_output, expand_weight, reduce_weight, distogram_weight, norm_gains, first_table, second_table, first_single, second_single, first_input, second_input, first_output, second_output, first_expand, second_expand, first_reduce, second_reduce, first_logits, second_logits, first_gains, second_gains):
    offset = residue_index[:, :, None] - residue_index[:, None, :]
    same = chain_index[:, :, None] == chain_index[:, None, :]
    bins = jnp.where(same, jnp.clip(offset, -REACH, REACH) + REACH, 2 * REACH + 1).astype(jnp.int32)
    relative_hot = (bins[..., None] == jnp.arange(NREL, dtype=jnp.int32)).astype(jnp.float32)
    token = token_mask.astype(jnp.float32)
    pair_mask = token[:, :, None] * token[:, None, :]
    loss_weight = pair_mask * pair_valid.astype(jnp.float32)
    target_hot = (target_bins[..., None] == jnp.arange(BINS, dtype=jnp.int32)).astype(jnp.float32)
    weights = (relative_table, single_weight, triangle_input, triangle_output, expand_weight, reduce_weight, distogram_weight, norm_gains)
    single_wide = single.astype(jnp.float32)

    def scalar_loss(*params):
        return full_loss(params, single_wide, relative_hot, pair_mask, loss_weight, target_hot)
    loss_sum, pullback = jax.vjp(scalar_loss, *weights)
    raw = pullback(jnp.ones((), jnp.float32))
    valid_count = jnp.sum(loss_weight)
    grads = [g / valid_count for g in raw]
    squares = jnp.zeros((), jnp.float32)
    for g in grads:
        squares = squares + jnp.sum(g * g)
    gradient_norm = jnp.sqrt(squares)
    factor = jnp.minimum(1.0, CLIP_NORM / (gradient_norm + 1e-06))
    firsts = (first_table, first_single, first_input, first_output, first_expand, first_reduce, first_logits, first_gains)
    seconds = (second_table, second_single, second_input, second_output, second_expand, second_reduce, second_logits, second_gains)
    result = []
    for index in range(8):
        rate = GAIN_RATE if index == 7 else WEIGHT_RATE
        decay = 0.0 if index == 7 else WEIGHT_DECAY
        result.extend(adamw(weights[index], grads[index] * factor, firsts[index], seconds[index], rate, decay))
    return (loss_sum, valid_count, gradient_norm, result[0], result[1], result[2], result[3], result[4], result[5], result[6], result[7], result[8], result[9], result[10], result[11], result[12], result[13], result[14], result[15], result[16], result[17], result[18], result[19], result[20], result[21], result[22], result[23])
```

```python
import functools

import jax
import jax.numpy as jnp
from jax import lax
from jax.experimental import pallas as pl
from jax.experimental.pallas import tpu as pltpu
from jax.sharding import PartitionSpec as P

STEP = 10


EPS = 1e-05
BETA_ONE = 0.9
BETA_TWO = 0.999
ADAM_EPS = 1e-08
WEIGHT_RATE = 0.1
GAIN_RATE = 0.5
WEIGHT_DECAY = 0.01
CLIP_NORM = 0.002


def normalize(value):
    mean = jnp.mean(value, axis=-1, keepdims=True)
    centred = value - mean
    scale = lax.rsqrt(jnp.mean(centred * centred, axis=-1, keepdims=True) + EPS)
    return (centred * scale, scale)


def norm_back(grad_out, unit, scale, gain):
    scaled = grad_out * gain
    first_mean = jnp.mean(scaled, axis=-1, keepdims=True)
    second_mean = jnp.mean(scaled * unit, axis=-1, keepdims=True)
    grad_in = scale * (scaled - first_mean - unit * second_mean)
    grad_gain = jnp.sum(grad_out * unit, axis=tuple(range(grad_out.ndim - 1)))
    return (grad_in, grad_gain)


def project(value, weight):
    return jnp.einsum("...c,cd->...d", value, weight, preferred_element_type=jnp.float32)


def project_back(grad, weight):
    return jnp.einsum("...d,cd->...c", grad, weight, preferred_element_type=jnp.float32)


def weight_grad(value, grad):
    return jnp.einsum("bijc,bijd->cd", value, grad, preferred_element_type=jnp.float32)


def triangle_forward(state, weight_in, weight_out, gains, pair_mask, incoming):
    hidden = weight_out.shape[0]
    pair_unit, pair_scale = normalize(state)
    normed = (pair_unit * gains[0]).astype(jnp.bfloat16)
    mixed = project(normed, weight_in)
    mask = pair_mask[..., None]
    left = (mask * jax.nn.sigmoid(mixed[..., :hidden]) * mixed[..., hidden : 2 * hidden]).astype(
        jnp.bfloat16
    )
    right = (
        mask
        * jax.nn.sigmoid(mixed[..., 2 * hidden : 3 * hidden])
        * mixed[..., 3 * hidden : 4 * hidden]
    ).astype(jnp.bfloat16)
    left_cols, right_cols = (
        lax.all_to_all(left, "head", split_axis=3, concat_axis=2, tiled=True),
        lax.all_to_all(right, "head", split_axis=3, concat_axis=2, tiled=True),
    )
    if incoming:
        left_cols, right_cols = (
            lax.all_to_all(left_cols, "row", split_axis=2, concat_axis=1, tiled=True),
            lax.all_to_all(right_cols, "row", split_axis=2, concat_axis=1, tiled=True),
        )
        left_cols = jnp.swapaxes(left_cols, 1, 2)
        right_cols = jnp.swapaxes(right_cols, 1, 2)
    right_all = lax.all_gather(right_cols, "row", axis=1, tiled=True)
    triangle = jnp.einsum(
        "bikc,bjkc->bijc", left_cols, right_all, preferred_element_type=jnp.float32
    )
    triangle = lax.all_to_all(
        triangle.astype(jnp.bfloat16), "head", split_axis=2, concat_axis=3, tiled=True
    )
    tri_unit, tri_scale = normalize(triangle.astype(jnp.float32))
    shaped = (tri_unit * gains[1]).astype(jnp.bfloat16)
    branch = project(shaped, weight_out)
    gate = jax.nn.sigmoid(mixed[..., 4 * hidden :])
    kept = (
        pair_unit,
        pair_scale,
        normed,
        mixed,
        left_cols,
        right_all,
        tri_unit,
        tri_scale,
        shaped,
        branch,
        gate,
    )
    return (state + gate * branch, kept)


def triangle_backward(grad_state, kept, weight_in, weight_out, gains, pair_mask, incoming):
    hidden = weight_out.shape[0]
    (
        pair_unit,
        pair_scale,
        normed,
        mixed,
        left_cols,
        right_all,
        tri_unit,
        tri_scale,
        shaped,
        branch,
        gate,
    ) = kept
    grad_branch = (grad_state * gate).astype(jnp.bfloat16)
    grad_gate = grad_state * branch * gate * (1.0 - gate)
    grad_out = weight_grad(shaped, grad_branch)
    grad_shaped = project_back(grad_branch, weight_out)
    grad_tri, gain_two = norm_back(grad_shaped, tri_unit, tri_scale, gains[1])
    tri_cols = lax.all_to_all(
        grad_tri.astype(jnp.bfloat16), "head", split_axis=3, concat_axis=2, tiled=True
    )
    grad_left = jnp.einsum(
        "bijc,bjkc->bikc", tri_cols, right_all, preferred_element_type=jnp.float32
    )
    grad_left = grad_left.astype(jnp.bfloat16)
    summed = lax.psum_scatter(
        jnp.einsum(
            "bijc,bikc->jbkc", tri_cols, left_cols, preferred_element_type=jnp.float32
        ).astype(jnp.bfloat16),
        "row",
        scatter_dimension=0,
        tiled=True,
    ).astype(jnp.float32)
    grad_right = jnp.transpose(summed, (1, 0, 2, 3)).astype(jnp.bfloat16)
    if incoming:
        grad_left, grad_right = (
            lax.all_to_all(
                jnp.swapaxes(grad_left, 1, 2), "row", split_axis=1, concat_axis=2, tiled=True
            ),
            lax.all_to_all(
                jnp.swapaxes(grad_right, 1, 2), "row", split_axis=1, concat_axis=2, tiled=True
            ),
        )
    back_left, back_right = (
        lax.all_to_all(grad_left, "head", split_axis=2, concat_axis=3, tiled=True),
        lax.all_to_all(grad_right, "head", split_axis=2, concat_axis=3, tiled=True),
    )
    mask = pair_mask[..., None]
    back_left = back_left.astype(jnp.float32) * mask
    back_right = back_right.astype(jnp.float32) * mask
    left_sig = jax.nn.sigmoid(mixed[..., :hidden])
    left_value = mixed[..., hidden : 2 * hidden]
    right_sig = jax.nn.sigmoid(mixed[..., 2 * hidden : 3 * hidden])
    right_value = mixed[..., 3 * hidden : 4 * hidden]
    grad_mixed = jnp.concatenate(
        [
            back_left * left_value * left_sig * (1.0 - left_sig),
            back_left * left_sig,
            back_right * right_value * right_sig * (1.0 - right_sig),
            back_right * right_sig,
            grad_gate,
        ],
        axis=-1,
    ).astype(jnp.bfloat16)
    grad_in = weight_grad(normed, grad_mixed)
    grad_normed = project_back(grad_mixed, weight_in)
    grad_first, gain_one = norm_back(grad_normed, pair_unit, pair_scale, gains[0])
    return (grad_state + grad_first, (grad_in, grad_out, gain_one, gain_two))


def transition_forward(state, weight_up, weight_down, gain):
    expand = weight_down.shape[0]
    unit, scale = normalize(state)
    lifted = (unit * gain).astype(jnp.bfloat16)
    inner = project(lifted, weight_up)
    product = (jax.nn.silu(inner[..., :expand]) * inner[..., expand:]).astype(jnp.bfloat16)
    return (state + project(product, weight_down), (unit, scale, lifted, inner, product))


def transition_backward(grad_state, kept, weight_up, weight_down, gain):
    expand = weight_down.shape[0]
    unit, scale, lifted, inner, product = kept
    grad_low = grad_state.astype(jnp.bfloat16)
    grad_down = weight_grad(product, grad_low)
    grad_product = project_back(grad_low, weight_down)
    gate_part = inner[..., :expand]
    up_part = inner[..., expand:]
    gate_sig = jax.nn.sigmoid(gate_part)
    silu_value = gate_part * gate_sig
    silu_slope = gate_sig * (1.0 + gate_part * (1.0 - gate_sig))
    grad_inner = jnp.concatenate(
        [grad_product * up_part * silu_slope, grad_product * silu_value], axis=-1
    )
    grad_inner = grad_inner.astype(jnp.bfloat16)
    grad_up = weight_grad(lifted, grad_inner)
    grad_lifted = project_back(grad_inner, weight_up)
    grad_middle, gain_grad = norm_back(grad_lifted, unit, scale, gain)
    return (grad_middle + grad_state, (grad_up, grad_down, gain_grad))


def block_forward(state, weight_in, weight_out, weight_up, weight_down, gains, pair_mask):
    first, kept_one = triangle_forward(
        state, weight_in[0], weight_out[0], gains[0:2], pair_mask, False
    )
    second, kept_two = triangle_forward(
        first, weight_in[1], weight_out[1], gains[2:4], pair_mask, True
    )
    output, kept_three = transition_forward(second, weight_up, weight_down, gains[4])
    return (output, (kept_one, kept_two, kept_three))


def block_backward(
    grad_state, state, weight_in, weight_out, weight_up, weight_down, gains, pair_mask
):
    skipped, kept = block_forward(
        state, weight_in, weight_out, weight_up, weight_down, gains, pair_mask
    )
    kept_one, kept_two, kept_three = kept
    grad_state, (grad_up, grad_down, gain_five) = transition_backward(
        grad_state, kept_three, weight_up, weight_down, gains[4]
    )
    grad_state, (in_two, out_two, gain_three, gain_four) = triangle_backward(
        grad_state, kept_two, weight_in[1], weight_out[1], gains[2:4], pair_mask, True
    )
    grad_state, (in_one, out_one, gain_one, gain_two) = triangle_backward(
        grad_state, kept_one, weight_in[0], weight_out[0], gains[0:2], pair_mask, False
    )
    return (
        grad_state,
        (
            jnp.stack([in_one, in_two]),
            jnp.stack([out_one, out_two]),
            grad_up,
            grad_down,
            jnp.stack([gain_one, gain_two, gain_three, gain_four, gain_five]),
        ),
    )


def adamw(weight, grad, first, second, rate, decay):
    first_new = BETA_ONE * first + (1.0 - BETA_ONE) * grad
    second_new = BETA_TWO * second + (1.0 - BETA_TWO) * grad * grad
    moved = (
        first_new
        / (1.0 - BETA_ONE**STEP)
        / (jnp.sqrt(second_new / (1.0 - BETA_TWO**STEP)) + ADAM_EPS)
    )
    return (first_new, second_new, weight - rate * (moved + decay * weight))


def gradients_by_block(
    single,
    residue_index,
    chain_index,
    token_mask,
    pair_valid,
    target_bins,
    relative_table,
    single_weight,
    triangle_input,
    triangle_output,
    expand_weight,
    reduce_weight,
    distogram_weight,
    norm_gains,
):
    crops, rows, cols = pair_valid.shape
    width = relative_table.shape[1]
    layers = triangle_input.shape[0]
    row_start = lax.axis_index("row") * rows
    col_start = lax.axis_index("head") * cols

    def take(array, start, count):
        return lax.dynamic_slice_in_dim(array, start, count, 1)

    offset = (
        take(residue_index, row_start, rows)[:, :, None]
        - take(residue_index, col_start, cols)[:, None, :]
    )
    same = (
        take(chain_index, row_start, rows)[:, :, None]
        == take(chain_index, col_start, cols)[:, None, :]
    )
    reach = (relative_table.shape[0] - 2) // 2
    bins = jnp.where(same, jnp.clip(offset, -reach, reach) + reach, 2 * reach + 1)
    relative_hot = (
        bins[..., None] == jnp.arange(relative_table.shape[0])[None, None, None, :]
    ).astype(jnp.float32)
    token_rows = take(token_mask, row_start, rows).astype(jnp.float32)
    token_cols = take(token_mask, col_start, cols).astype(jnp.float32)
    pair_mask = token_rows[:, :, None] * token_cols[:, None, :]
    loss_weight = pair_mask * pair_valid.astype(jnp.float32)
    low_input = triangle_input.astype(jnp.bfloat16)
    low_output = triangle_output.astype(jnp.bfloat16)
    low_expand = expand_weight.astype(jnp.bfloat16)
    low_reduce = reduce_weight.astype(jnp.bfloat16)
    low_logits = distogram_weight.astype(jnp.bfloat16)
    proj = project(single, single_weight.astype(jnp.bfloat16))
    state = project(relative_hot.astype(jnp.bfloat16), relative_table.astype(jnp.bfloat16))
    state = (
        state
        + take(proj, row_start, rows)[:, :, None, :width]
        + take(proj, col_start, cols)[:, None, :, width:]
    )
    inputs = []
    for layer in range(layers):
        inputs.append(state)
        state, unused = block_forward(
            state,
            low_input[layer],
            low_output[layer],
            low_expand[layer],
            low_reduce[layer],
            norm_gains[5 * layer : 5 * layer + 5],
            pair_mask,
        )
    head_unit, head_scale = normalize(state)
    shown = (head_unit * norm_gains[5 * layers]).astype(jnp.bfloat16)
    logits = project(shown, low_logits)
    largest = jnp.max(logits, axis=-1, keepdims=True)
    log_total = largest + jnp.log(jnp.sum(jnp.exp(logits - largest), axis=-1, keepdims=True))
    target_hot = (
        target_bins[..., None] == jnp.arange(logits.shape[-1])[None, None, None, :]
    ).astype(jnp.float32)
    picked = jnp.sum(logits * target_hot, axis=-1)
    loss_local = jnp.sum(loss_weight * (log_total[..., 0] - picked))
    grad_scores = (loss_weight[..., None] * (jnp.exp(logits - log_total) - target_hot)).astype(
        jnp.bfloat16
    )
    grad_logits = weight_grad(shown, grad_scores)
    grad_shown = project_back(grad_scores, low_logits)
    grad_state, gain_last = norm_back(grad_shown, head_unit, head_scale, norm_gains[5 * layers])
    collected = []
    for layer in reversed(range(layers)):
        grad_state, layer_grads = block_backward(
            grad_state,
            inputs[layer],
            low_input[layer],
            low_output[layer],
            low_expand[layer],
            low_reduce[layer],
            norm_gains[5 * layer : 5 * layer + 5],
            pair_mask,
        )
        collected.insert(0, layer_grads)
    grad_input = jnp.stack([entry[0] for entry in collected])
    grad_output = jnp.stack([entry[1] for entry in collected])
    grad_expand = jnp.stack([entry[2] for entry in collected])
    grad_reduce = jnp.stack([entry[3] for entry in collected])
    grad_gains = jnp.concatenate(
        [jnp.concatenate([entry[4] for entry in collected], axis=0), gain_last[None]], axis=0
    )
    grad_table = jnp.einsum(
        "bijr,bijc->rc", relative_hot, grad_state, precision=lax.Precision.HIGHEST
    )
    single_wide = single.astype(jnp.float32)
    row_part = jnp.einsum(
        "bis,bic->sc",
        take(single_wide, row_start, rows),
        jnp.sum(grad_state, axis=2),
        precision=lax.Precision.HIGHEST,
    )
    col_part = jnp.einsum(
        "bjs,bjc->sc",
        take(single_wide, col_start, cols),
        jnp.sum(grad_state, axis=1),
        precision=lax.Precision.HIGHEST,
    )
    grad_single = jnp.concatenate([row_part, col_part], axis=1)
    return (
        loss_local,
        jnp.sum(loss_weight),
        grad_table,
        grad_single,
        grad_input,
        grad_output,
        grad_expand,
        grad_reduce,
        grad_logits,
        grad_gains,
    )


F32 = jnp.float32
BF16 = jnp.bfloat16
LANES = 128
SUBLANES = 8
VMEM_BYTES = 58 * 2**20
ROW_BLOCK = 2
MESH = pl.DeviceIdType.MESH


def dot(left, right):
    return lax.dot_general(left, right, (((1,), (0,)), ((), ())), preferred_element_type=F32)


def dot_pairs(left, right):
    return lax.dot_general(left, right, (((1,), (1,)), ((), ())), preferred_element_type=F32)


def sigmoid(value):
    return 0.5 * jnp.tanh(0.5 * value) + 0.5


def unit_of(value):
    centred = value - jnp.mean(value, axis=0, keepdims=True)
    scale = lax.rsqrt(jnp.mean(centred * centred, axis=0, keepdims=True) + EPS)
    return (centred * scale, scale)


def unit_back(grad, unit, scale, gain):
    scaled = grad * gain
    first = jnp.mean(scaled, axis=0, keepdims=True)
    second = jnp.mean(scaled * unit, axis=0, keepdims=True)
    return scale * (scaled - first - unit * second)


def fold(value):
    total = value[:, :LANES]
    for start in range(LANES, value.shape[1], LANES):
        total = total + value[:, start : start + LANES]
    return total


def read_rows(ref):
    return jnp.concatenate([ref[row] for row in range(ref.shape[0])], axis=1)


def write_rows(ref, value):
    cols = ref.shape[2]
    for row in range(ref.shape[0]):
        ref[row] = value[:, row * cols : (row + 1) * cols].astype(ref.dtype)


def read_wire(ref):
    peers, rows, _ = ref.shape
    pieces = []
    for peer in range(peers):
        piece = ref[peer].astype(F32)
        pieces.append(
            jnp.concatenate(
                [piece[start : start + SUBLANES] for start in range(0, rows, SUBLANES)], axis=1
            )
        )
    return jnp.concatenate(pieces, axis=0)


def write_wire_piece(ref, peer, value):
    cols = ref.shape[2]
    ref[peer] = jnp.concatenate(
        [value[:, start : start + cols] for start in range(0, value.shape[1], cols)], axis=0
    ).astype(ref.dtype)


def write_wire(ref, value):
    for peer in range(ref.shape[0]):
        write_wire_piece(ref, peer, value[peer * SUBLANES : (peer + 1) * SUBLANES])


def triangle_start(r, name, state):
    width = state.shape[0]
    unit, _ = unit_of(state)
    normed = (unit * r[name + "gain0"][...]).astype(BF16)
    mixed = dot(r[name + "mix_t"][...], normed)
    mask = read_rows(r["mask"])
    for out, base in ((r[name + "a"], 0), (r[name + "b"], 2 * width)):
        for peer in range(out.shape[0]):
            start = base + peer * SUBLANES
            gate = mixed[start : start + SUBLANES]
            value = mixed[start + width : start + width + SUBLANES]
            write_wire_piece(out, peer, mask * sigmoid(gate) * value)


def triangle_finish(r, name, state):
    unit, _ = unit_of(state)
    normed = (unit * r[name + "gain0"][...]).astype(BF16)
    gate = sigmoid(dot(r[name + "gate_t"][...], normed))
    tri_unit, tri_scale = unit_of(read_wire(r[name + "tri"]))
    shaped = (tri_unit * r[name + "gain1"][...]).astype(BF16)
    branch = dot(r[name + "out_t"][...], shaped)
    return (state + gate * branch, (gate, tri_unit, tri_scale, shaped, branch))


def triangle_back_start(r, name, grad, kept):
    gate, tri_unit, tri_scale, shaped, branch = kept
    grad_branch = (grad * gate).astype(BF16)
    write_rows(r[name + "dgate"], grad * branch * gate * (1.0 - gate))
    r[name + "d_out"][...] += dot_pairs(shaped, grad_branch)
    grad_shaped = dot(r[name + "out"][...], grad_branch)
    r[name + "d_gain1"][...] += fold(grad_shaped * tri_unit)
    write_wire(r[name + "dtri"], unit_back(grad_shaped, tri_unit, tri_scale, r[name + "gain1"][...]))


def triangle_back_finish(r, name, grad, state):
    width = state.shape[0]
    unit, scale = unit_of(state)
    gain = r[name + "gain0"][...]
    normed = (unit * gain).astype(BF16)
    mixed = dot(r[name + "mix_t"][...], normed)
    mask = read_rows(r["mask"])
    parts = []
    for source, base in ((r[name + "da"], 0), (r[name + "db"], 2 * width)):
        back = read_wire(source) * mask
        gate = sigmoid(mixed[base : base + width])
        back_gate = back * gate
        parts.append((back_gate * mixed[base + width : base + 2 * width] * (1.0 - gate)).astype(BF16))
        parts.append(back_gate.astype(BF16))
    parts.append(read_rows(r[name + "dgate_in"]))
    grad_mixed = jnp.concatenate(parts, axis=0)
    r[name + "d_in"][...] += dot_pairs(normed, grad_mixed)
    grad_normed = dot(r[name + "in"][...], grad_mixed)
    r[name + "d_gain0"][...] += fold(grad_normed * unit)
    return grad + unit_back(grad_normed, unit, scale, gain)


def transition(r, name, state):
    unit, scale = unit_of(state)
    lifted = (unit * r[name + "gain"][...]).astype(BF16)
    inner = dot(r[name + "up_t"][...], lifted)
    half = inner.shape[0] // 2
    gate = inner[:half]
    slope = sigmoid(gate)
    product = (gate * slope * inner[half:]).astype(BF16)
    return (unit, scale, lifted, inner, slope, product)


def transition_finish(r, name, state, kept):
    return state + dot(r[name + "down_t"][...], kept[5])


def transition_back(r, name, grad, kept):
    unit, scale, lifted, inner, slope, product = kept
    half = inner.shape[0] // 2
    gate, up = inner[:half], inner[half:]
    grad_low = grad.astype(BF16)
    r[name + "d_down"][...] += dot_pairs(product, grad_low)
    grad_product = dot(r[name + "down"][...], grad_low)
    scaled = grad_product * slope
    grad_inner = jnp.concatenate(
        [
            (scaled * up * (1.0 + gate * (1.0 - slope))).astype(BF16),
            (scaled * gate).astype(BF16),
        ],
        axis=0,
    )
    r[name + "d_up"][...] += dot_pairs(lifted, grad_inner)
    grad_lifted = dot(r[name + "up"][...], grad_inner)
    r[name + "d_gain"][...] += fold(grad_lifted * unit)
    return grad + unit_back(grad_lifted, unit, scale, r[name + "gain"][...])


def head_back(r, state):
    unit, scale = unit_of(state)
    gain = r["head_gain"][...]
    shown = (unit * gain).astype(BF16)
    logits = dot(r["logits_t"][...], shown)
    largest = jnp.max(logits, axis=0, keepdims=True)
    raised = jnp.exp(logits - largest)
    total = jnp.sum(raised, axis=0, keepdims=True)
    log_total = largest + jnp.log(total)
    target = read_rows(r["target"])
    weight = read_rows(r["weight"])
    hot = lax.broadcasted_iota(jnp.int32, logits.shape, 0) == target
    picked = jnp.sum(jnp.where(hot, logits, 0.0), axis=0, keepdims=True)
    r["loss"][...] += fold(weight * (log_total - picked))
    share = raised * (1.0 / total)
    grad_scores = (weight * (share - jnp.where(hot, 1.0, 0.0))).astype(BF16)
    r["d_logits"][...] += dot_pairs(shown, grad_scores)
    grad_shown = dot(r["logits"][...], grad_scores)
    r["d_head_gain"][...] += fold(grad_shown * unit)
    return unit_back(grad_shown, unit, scale, gain)


def bins_hot(r):
    bins = read_rows(r["bins"])
    shape = (r["table_rows"], bins.shape[1])
    return jnp.where(lax.broadcasted_iota(jnp.int32, shape, 0) == bins, 1.0, 0.0).astype(BF16)


def block_spec(shape, kind):
    if kind == "rows":
        return pl.BlockSpec((ROW_BLOCK,) + shape[1:], lambda step: (step,) + (0,) * (len(shape) - 1))
    if kind == "wire":
        return pl.BlockSpec((shape[0], SUBLANES * ROW_BLOCK, shape[2]), lambda step: (0, step, 0))
    return pl.BlockSpec(shape, lambda step: (0,) * len(shape))


def run_stage(body, name, rows, inputs, outputs, extra=None):
    in_names, out_names = list(inputs), list(outputs)

    def kernel(*refs):
        named = dict(zip(in_names + out_names, refs))
        named.update(extra or {})

        @pl.when(pl.program_id(0) == 0)
        def _():
            for out in out_names:
                if outputs[out][2] == "sum":
                    named[out][...] = jnp.zeros(outputs[out][0], outputs[out][1])

        body(named)

    results = pl.pallas_call(
        kernel,
        grid=(rows // ROW_BLOCK,),
        in_specs=[block_spec(inputs[key][0].shape, inputs[key][1]) for key in in_names],
        out_specs=[block_spec(outputs[key][0], outputs[key][2]) for key in out_names],
        out_shape=[jax.ShapeDtypeStruct(outputs[key][0], outputs[key][1]) for key in out_names],
        compiler_params=pltpu.CompilerParams(
            dimension_semantics=("arbitrary",), vmem_limit_bytes=VMEM_BYTES
        ),
        name=name,
    )(*[inputs[key][0] for key in in_names])
    return dict(zip(out_names, results))


def flip(value, step, count):
    result, bit = 0, 1
    while bit < count:
        result = result + lax.rem(lax.div(value, bit) + (step // bit) % 2, 2) * bit
        bit *= 2
    return result


class Exchange:
    def __init__(self, count, half):
        row, head = lax.axis_index("row"), lax.axis_index("head")
        place = lax.rem(row, half)
        self.count = count
        self.base = row - place
        self.me = place * 2 + head

    def peer(self, step):
        return flip(self.me, step, self.count)

    def device(self, peer):
        return (self.base + lax.div(peer, 2), lax.rem(peer, 2))

    def greet(self):
        barrier = pltpu.get_barrier_semaphore()
        for step in range(1, self.count):
            pl.semaphore_signal(
                barrier, inc=1, device_id=self.device(self.peer(step)), device_id_type=MESH
            )
        pl.semaphore_wait(barrier, self.count - 1)

    def send(self, moves):
        copies = []
        for step in range(1, self.count):
            peer = self.peer(step)
            for source, target, send_sems, recv_sems in moves:
                copy = pltpu.make_async_remote_copy(
                    src_ref=source.at[peer],
                    dst_ref=target.at[self.me],
                    send_sem=send_sems.at[step],
                    recv_sem=recv_sems.at[step],
                    device_id=self.device(peer),
                    device_id_type=MESH,
                )
                copy.start()
                copies.append(copy)
        for source, target, send_sems, _ in moves:
            copy = pltpu.make_async_copy(source.at[self.me], target.at[self.me], send_sems.at[0])
            copy.start()
            copies.append(copy)
        return copies


def wait_all(copies):
    for copy in copies:
        copy.wait()


def widen(wide, low):
    peers, rows, cols = low.shape

    def step(peer, carry):
        value = low[peer].astype(F32)
        start = pl.multiple_of(peer * rows, SUBLANES)
        for lane in range(cols // LANES):
            wide[lane, pl.ds(start, rows), :] = value[:, lane * LANES : (lane + 1) * LANES]
        return carry

    lax.fori_loop(0, peers, step, 0)


def narrow(low, wide):
    peers, rows, cols = low.shape

    def step(peer, carry):
        start = pl.multiple_of(peer * rows, SUBLANES)
        low[peer] = jnp.concatenate(
            [wide[lane, pl.ds(start, rows), :] for lane in range(cols // LANES)], axis=1
        ).astype(low.dtype)
        return carry

    lax.fori_loop(0, peers, step, 0)


def take_channel(wide, channel):
    lanes, rows, _ = wide.shape
    count = rows // SUBLANES
    return jnp.concatenate(
        [wide[lane, pl.ds(channel, count, stride=SUBLANES), :] for lane in range(lanes)], axis=1
    )


def put_channel(wide, channel, value):
    lanes, rows, _ = wide.shape
    count = rows // SUBLANES
    for lane in range(lanes):
        wide[lane, pl.ds(channel, count, stride=SUBLANES), :] = value[
            :, lane * LANES : (lane + 1) * LANES
        ]


def product_of(left, right, left_axis, right_axis):
    return lax.dot_general(
        left, right, (((left_axis,), (right_axis,)), ((), ())), preferred_element_type=F32
    )


def forward_exchange(half, incoming, a, b):
    peers, rows, cols = a.shape
    tokens = peers * rows // SUBLANES

    def kernel(a_ref, b_ref, a_out, b_out, tri_out, a_got, b_got, wide_a, wide_b, low, *sems):
        ring = Exchange(peers, half)
        ring.greet()
        copies = ring.send(
            [(a_ref, a_got, sems[0], sems[1]), (b_ref, b_got, sems[2], sems[3])]
        )
        wait_all(copies)
        widen(wide_a, a_got)
        widen(wide_b, b_got)

        def step(channel, carry):
            left = take_channel(wide_a, channel).astype(BF16)
            right = take_channel(wide_b, channel).astype(BF16)
            a_out[channel] = left
            b_out[channel] = right
            axis = 0 if incoming else 1
            put_channel(wide_a, channel, product_of(left, right, axis, axis))
            return carry

        lax.fori_loop(0, SUBLANES, step, 0)
        narrow(low, wide_a)
        wait_all(ring.send([(low, tri_out, sems[4], sems[5])]))

    wire = jax.ShapeDtypeStruct(a.shape, BF16)
    block = jax.ShapeDtypeStruct((SUBLANES, tokens, cols), BF16)
    wide = pltpu.VMEM((cols // LANES, peers * rows, LANES), F32)
    anywhere = pl.BlockSpec(memory_space=pl.ANY)
    inside = pl.BlockSpec(memory_space=pltpu.VMEM)
    return pl.pallas_call(
        kernel,
        in_specs=[anywhere, anywhere],
        out_specs=[inside, inside, anywhere],
        out_shape=[block, block, wire],
        scratch_shapes=[pltpu.VMEM(a.shape, BF16)] * 2
        + [wide] * 2
        + [pltpu.VMEM(a.shape, BF16)]
        + [pltpu.SemaphoreType.DMA((peers,))] * 6,
        compiler_params=pltpu.CompilerParams(
            collective_id=1 if incoming else 0, has_side_effects=True, vmem_limit_bytes=VMEM_BYTES
        ),
        name="incoming_forward" if incoming else "outgoing_forward",
    )(a, b)


def backward_exchange(half, incoming, dtri, a, b):
    peers, rows, cols = dtri.shape

    def kernel(dtri_ref, a_ref, b_ref, da_out, db_out, got, wide_a, wide_b, low_a, low_b, *sems):
        ring = Exchange(peers, half)
        ring.greet()
        wait_all(ring.send([(dtri_ref, got, sems[0], sems[1])]))
        widen(wide_a, got)

        def step(channel, carry):
            grad = take_channel(wide_a, channel).astype(BF16)
            left, right = a_ref[channel], b_ref[channel]
            if incoming:
                grad_left = product_of(right, grad, 1, 1)
                grad_right = product_of(left, grad, 1, 0)
            else:
                grad_left = product_of(grad, right, 1, 0)
                grad_right = product_of(grad, left, 0, 0)
            put_channel(wide_a, channel, grad_left)
            put_channel(wide_b, channel, grad_right)
            return carry

        lax.fori_loop(0, SUBLANES, step, 0)
        narrow(low_a, wide_a)
        narrow(low_b, wide_b)
        wait_all(
            ring.send([(low_a, da_out, sems[2], sems[3]), (low_b, db_out, sems[4], sems[5])])
        )

    wire = jax.ShapeDtypeStruct(dtri.shape, BF16)
    wide = pltpu.VMEM((cols // LANES, peers * rows, LANES), F32)
    anywhere = pl.BlockSpec(memory_space=pl.ANY)
    inside = pl.BlockSpec(memory_space=pltpu.VMEM)
    return pl.pallas_call(
        kernel,
        in_specs=[anywhere, inside, inside],
        out_specs=[anywhere, anywhere],
        out_shape=[wire, wire],
        scratch_shapes=[pltpu.VMEM(dtri.shape, BF16)]
        + [wide] * 2
        + [pltpu.VMEM(dtri.shape, BF16)] * 2
        + [pltpu.SemaphoreType.DMA((peers,))] * 6,
        compiler_params=pltpu.CompilerParams(
            collective_id=3 if incoming else 2, has_side_effects=True, vmem_limit_bytes=VMEM_BYTES
        ),
        name="incoming_backward" if incoming else "outgoing_backward",
    )(dtri, a, b)


def by_crop(value, rows_axis, head_axis):
    count, heads = rows_axis, head_axis
    half = count // 2
    same, other = [], []
    for row in range(count):
        for head in range(heads):
            source = row * heads + head
            for crop, pairs in ((head, same), (1 - head, other)):
                pairs.append((source, (crop * half + row // 2) * heads + row % 2))
    head = lax.axis_index("head")
    crop = lax.axis_index("row") // half
    mine = lax.dynamic_index_in_dim(value, head, 0, keepdims=False)
    rest = lax.dynamic_index_in_dim(value, 1 - head, 0, keepdims=False)
    mine = lax.ppermute(mine, ("row", "head"), same)
    rest = lax.ppermute(rest, ("row", "head"), other)
    low = jnp.where(crop == 0, mine, rest)
    high = jnp.where(crop == 0, rest, mine)
    return jnp.concatenate([low, high], axis=-1)


def gradients_by_crop(
    row_count,
    head_count,
    single,
    residue_index,
    chain_index,
    token_mask,
    pair_valid,
    target_bins,
    relative_table,
    single_weight,
    triangle_input,
    triangle_output,
    expand_weight,
    reduce_weight,
    distogram_weight,
    norm_gains,
):
    crops, tokens = token_mask.shape
    width = relative_table.shape[1]
    layers = triangle_input.shape[0]
    half = row_count // crops
    peers = half * head_count
    rows = tokens // peers
    row_index = lax.axis_index("row")
    crop = row_index // half
    start = ((row_index % half) * head_count + lax.axis_index("head")) * rows

    placed = by_crop(jnp.stack([pair_valid, target_bins], axis=1), row_count, head_count)
    valid, target = placed[0], placed[1]

    def of_crop(array):
        return lax.dynamic_index_in_dim(array, crop, 0, keepdims=False)

    def of_rows(array):
        return lax.dynamic_slice_in_dim(array, start, rows, 0)

    residues, chains = of_crop(residue_index), of_crop(chain_index)
    reach = (relative_table.shape[0] - 2) // 2
    bins = jnp.where(
        of_rows(chains)[:, None] == chains[None, :],
        jnp.clip(of_rows(residues)[:, None] - residues[None, :], -reach, reach) + reach,
        2 * reach + 1,
    )
    present = of_crop(token_mask).astype(F32)
    pair_mask = of_rows(present)[:, None] * present[None, :]
    loss_weight = pair_mask * valid.astype(F32)
    table_rows = -(-relative_table.shape[0] // 16) * 16
    table_t = jnp.pad(relative_table, ((0, table_rows - relative_table.shape[0]), (0, 0))).T
    tokens_single = of_crop(single)
    proj = project(tokens_single, single_weight.astype(BF16))
    proj_rows = of_rows(proj[:, :width])[:, :, None]
    proj_cols = proj[:, width:].T
    bins, pair_mask = bins[:, None, :], pair_mask[:, None, :]

    low_input = triangle_input.astype(BF16)
    low_output = triangle_output.astype(BF16)
    low_expand = expand_weight.astype(BF16)
    low_reduce = reduce_weight.astype(BF16)
    low_logits = distogram_weight.astype(BF16)

    def gain(index):
        return (norm_gains[index][:, None], "whole")

    def triangle_weights(layer, kind, names):
        weight_in, weight_out = low_input[layer, kind], low_output[layer, kind]
        found = {
            "gain0": gain(5 * layer + 2 * kind),
            "gain1": gain(5 * layer + 2 * kind + 1),
            "mix_t": (weight_in[:, : 4 * width].T, "whole"),
            "gate_t": (weight_in[:, 4 * width :].T, "whole"),
            "in": (weight_in, "whole"),
            "out": (weight_out, "whole"),
            "out_t": (weight_out.T, "whole"),
        }
        return {f"t{layer}{kind}{name}": found[name] for name in names.split()}

    def transition_weights(layer, names):
        found = {
            "gain": gain(5 * layer + 4),
            "up": (low_expand[layer], "whole"),
            "up_t": (low_expand[layer].T, "whole"),
            "down": (low_reduce[layer], "whole"),
            "down_t": (low_reduce[layer].T, "whole"),
        }
        return {f"f{layer}{name}": found[name] for name in names.split()}

    state_shape = (rows, width, tokens)
    wire_shape = (peers, rows * SUBLANES, tokens)
    hidden = low_expand.shape[2]
    state_out = (state_shape, F32, "rows")
    wire_out = (wire_shape, BF16, "wire")
    gate_out = (state_shape, BF16, "rows")
    gain_out = ((width, LANES), F32, "sum")
    mask_in = {"mask": (pair_mask, "rows")}

    def start_outs(name):
        return {name + "a": wire_out, name + "b": wire_out}

    def back_start_outs(name):
        return {
            name + "dgate": gate_out,
            name + "dtri": wire_out,
            name + "d_out": ((width, width), F32, "sum"),
            name + "d_gain1": gain_out,
        }

    def back_finish_outs(name):
        return {name + "d_in": ((width, 5 * width), F32, "sum"), name + "d_gain0": gain_out}

    def transition_outs(name):
        return {
            name + "d_up": ((width, hidden), F32, "sum"),
            name + "d_down": ((hidden // 2, width), F32, "sum"),
            name + "d_gain": gain_out,
        }

    states, tris, lefts, rights, middles = {}, {}, {}, {}, {}
    sums = {}

    def body(r):
        hot = bins_hot(r)
        state = dot(r["table_t"][...], hot)
        cols = r["proj_cols"][...]
        state = state + jnp.concatenate(
            [cols + r["proj_rows"][row] for row in range(ROW_BLOCK)], axis=1
        )
        write_rows(r["state"], state)
        triangle_start(r, "t00", state)

    got = run_stage(
        body,
        "first_state",
        rows,
        {
            "bins": (bins, "rows"),
            "proj_rows": (proj_rows, "rows"),
            "proj_cols": (proj_cols, "whole"),
            "table_t": (table_t.astype(BF16), "whole"),
            **mask_in,
            **triangle_weights(0, 0, "gain0 mix_t"),
        },
        {"state": state_out, **start_outs("t00")},
        {"table_rows": table_rows},
    )
    states["t00"] = got["state"]

    for layer in range(layers):
        for kind in range(2):
            name = f"t{layer}{kind}"
            lefts[name], rights[name], tris[name] = forward_exchange(
                half, kind == 1, got[name + "a"], got[name + "b"]
            )
            inputs = {
                "state": (states[name], "rows"),
                name + "tri": (tris[name], "wire"),
                **triangle_weights(layer, kind, "gain0 gain1 gate_t out_t"),
            }
            if kind == 0:
                following = f"t{layer}1"

                def body(r, name=name, following=following):
                    state, _ = triangle_finish(r, name, read_rows(r["state"]))
                    write_rows(r["next"], state)
                    triangle_start(r, following, state)

                got = run_stage(
                    body,
                    "between_updates",
                    rows,
                    {**inputs, **mask_in, **triangle_weights(layer, 1, "gain0 mix_t")},
                    {"next": state_out, **start_outs(following)},
                )
                states[following] = got["next"]
            elif layer + 1 < layers:
                following = f"t{layer + 1}0"
                lift = f"f{layer}"

                def body(r, name=name, following=following, lift=lift):
                    state, _ = triangle_finish(r, name, read_rows(r["state"]))
                    write_rows(r["middle"], state)
                    state = transition_finish(r, lift, state, transition(r, lift, state))
                    write_rows(r["next"], state)
                    triangle_start(r, following, state)

                got = run_stage(
                    body,
                    "layer_end",
                    rows,
                    {
                        **inputs,
                        **mask_in,
                        **transition_weights(layer, "gain up_t down_t"),
                        **triangle_weights(layer + 1, 0, "gain0 mix_t"),
                    },
                    {"middle": state_out, "next": state_out, **start_outs(following)},
                )
                middles[layer] = got["middle"]
                states[following] = got["next"]

    lift = f"f{layers - 1}"

    def body(r, name=name):
        state, kept = triangle_finish(r, name, read_rows(r["state"]))
        lifted = transition(r, lift, state)
        grad = head_back(r, transition_finish(r, lift, state, lifted))
        grad = transition_back(r, lift, grad, lifted)
        write_rows(r["grad"], grad)
        triangle_back_start(r, name, grad, kept)

    got = run_stage(
        body,
        "loss",
        rows,
        {
            **inputs,
            **triangle_weights(layers - 1, 1, "out"),
            **transition_weights(layers - 1, "gain up_t down_t up down"),
            "head_gain": gain(5 * layers),
            "logits": (low_logits, "whole"),
            "logits_t": (low_logits.T, "whole"),
            "target": (target[:, None, :], "rows"),
            "weight": (loss_weight[:, None, :], "rows"),
        },
        {
            "grad": state_out,
            "loss": ((1, LANES), F32, "sum"),
            "d_logits": (distogram_weight.shape, F32, "sum"),
            "d_head_gain": gain_out,
            **transition_outs(lift),
            **back_start_outs(name),
        },
    )
    sums.update(got)

    for layer in reversed(range(layers)):
        for kind in (1, 0):
            name = f"t{layer}{kind}"
            grad_left, grad_right = backward_exchange(
                half, kind == 1, got[name + "dtri"], lefts[name], rights[name]
            )
            inputs = {
                "grad_in": (got["grad"], "rows"),
                "state": (states[name], "rows"),
                name + "da": (grad_left, "wire"),
                name + "db": (grad_right, "wire"),
                name + "dgate_in": (got[name + "dgate"], "rows"),
                **mask_in,
                **triangle_weights(layer, kind, "gain0 mix_t in"),
            }
            if kind == 1:
                before = f"t{layer}0"

                def body(r, name=name, before=before):
                    grad = triangle_back_finish(
                        r, name, read_rows(r["grad_in"]), read_rows(r["state"])
                    )
                    write_rows(r["grad"], grad)
                    _, kept = triangle_finish(r, before, read_rows(r["before"]))
                    triangle_back_start(r, before, grad, kept)

                got = run_stage(
                    body,
                    "between_updates_back",
                    rows,
                    {
                        **inputs,
                        "before": (states[before], "rows"),
                        before + "tri": (tris[before], "wire"),
                        **triangle_weights(layer, 0, "gain0 gain1 gate_t out out_t"),
                    },
                    {"grad": state_out, **back_finish_outs(name), **back_start_outs(before)},
                )
            elif layer > 0:
                before = f"t{layer - 1}1"
                lift = f"f{layer - 1}"

                def body(r, name=name, before=before, lift=lift):
                    grad = triangle_back_finish(
                        r, name, read_rows(r["grad_in"]), read_rows(r["state"])
                    )
                    grad = transition_back(r, lift, grad, transition(r, lift, read_rows(r["middle"])))
                    write_rows(r["grad"], grad)
                    _, kept = triangle_finish(r, before, read_rows(r["before"]))
                    triangle_back_start(r, before, grad, kept)

                got = run_stage(
                    body,
                    "layer_end_back",
                    rows,
                    {
                        **inputs,
                        "middle": (middles[layer - 1], "rows"),
                        "before": (states[before], "rows"),
                        before + "tri": (tris[before], "wire"),
                        **transition_weights(layer - 1, "gain up_t up down"),
                        **triangle_weights(layer - 1, 1, "gain0 gain1 gate_t out out_t"),
                    },
                    {
                        "grad": state_out,
                        **back_finish_outs(name),
                        **transition_outs(lift),
                        **back_start_outs(before),
                    },
                )
            else:

                def body(r, name=name):
                    grad = triangle_back_finish(
                        r, name, read_rows(r["grad_in"]), read_rows(r["state"])
                    )
                    hot = bins_hot(r)
                    high = grad.astype(BF16)
                    low = (grad - high.astype(F32)).astype(BF16)
                    r["d_table"][...] += dot_pairs(high, hot) + dot_pairs(low, hot)
                    cols = r["d_cols"].shape[1]
                    for row in range(ROW_BLOCK):
                        part = grad[:, row * cols : (row + 1) * cols]
                        r["d_rows"][row] = fold(part)
                        r["d_cols"][...] += part

                got = run_stage(
                    body,
                    "first_state_back",
                    rows,
                    {**inputs, "bins": (bins, "rows")},
                    {
                        **back_finish_outs(name),
                        "d_table": ((width, table_rows), F32, "sum"),
                        "d_rows": ((rows, width, LANES), F32, "rows"),
                        "d_cols": ((width, tokens), F32, "sum"),
                    },
                    {"table_rows": table_rows},
                )
            sums.update(got)

    wide_single = tokens_single.astype(F32)
    row_part = jnp.einsum(
        "is,ic->sc",
        of_rows(wide_single),
        jnp.sum(sums["d_rows"], axis=2),
        precision=lax.Precision.HIGHEST,
    )
    col_part = jnp.einsum(
        "js,cj->sc", wide_single, sums["d_cols"], precision=lax.Precision.HIGHEST
    )
    gains = []
    for layer in range(layers):
        for part in (f"t{layer}0d_gain0", f"t{layer}0d_gain1", f"t{layer}1d_gain0", f"t{layer}1d_gain1", f"f{layer}d_gain"):
            gains.append(jnp.sum(sums[part], axis=1))
    gains.append(jnp.sum(sums["d_head_gain"], axis=1))

    def stacked(part):
        return jnp.stack(
            [jnp.stack([sums[f"t{layer}{kind}{part}"] for kind in range(2)]) for layer in range(layers)]
        )

    return (
        jnp.sum(sums["loss"]),
        jnp.sum(loss_weight),
        sums["d_table"][:, : relative_table.shape[0]].T,
        jnp.concatenate([row_part, col_part], axis=1),
        stacked("d_in"),
        stacked("d_out"),
        jnp.stack([sums[f"f{layer}d_up"] for layer in range(layers)]),
        jnp.stack([sums[f"f{layer}d_down"] for layer in range(layers)]),
        sums["d_logits"],
        jnp.stack(gains),
    )


def per_device(
    row_count,
    head_count,
    single,
    residue_index,
    chain_index,
    token_mask,
    pair_valid,
    target_bins,
    relative_table,
    single_weight,
    triangle_input,
    triangle_output,
    expand_weight,
    reduce_weight,
    distogram_weight,
    norm_gains,
    first_table,
    second_table,
    first_single,
    second_single,
    first_input,
    second_input,
    first_output,
    second_output,
    first_expand,
    second_expand,
    first_reduce,
    second_reduce,
    first_logits,
    second_logits,
    first_gains,
    second_gains,
):
    crops, tokens = token_mask.shape
    width = relative_table.shape[1]
    peers = row_count * head_count // crops
    given = (
        single,
        residue_index,
        chain_index,
        token_mask,
        pair_valid,
        target_bins,
        relative_table,
        single_weight,
        triangle_input,
        triangle_output,
        expand_weight,
        reduce_weight,
        distogram_weight,
        norm_gains,
    )
    if (
        crops == 2
        and head_count == 2
        and width == SUBLANES * peers
        and tokens % (peers * ROW_BLOCK) == 0
        and tokens % LANES == 0
    ):
        local = gradients_by_crop(row_count, head_count, *given)
    else:
        local = gradients_by_block(*given)
    summed = lax.psum(local, ("row", "head"))
    loss_sum, valid_count = summed[0], summed[1]
    grads = [grad / valid_count for grad in summed[2:]]
    squares = jnp.zeros((), jnp.float32)
    for g in grads:
        squares = squares + jnp.sum(g * g)
    gradient_norm = jnp.sqrt(squares)
    factor = jnp.minimum(1.0, CLIP_NORM / (gradient_norm + 1e-06))
    weights = (
        relative_table,
        single_weight,
        triangle_input,
        triangle_output,
        expand_weight,
        reduce_weight,
        distogram_weight,
        norm_gains,
    )
    firsts = (
        first_table,
        first_single,
        first_input,
        first_output,
        first_expand,
        first_reduce,
        first_logits,
        first_gains,
    )
    seconds = (
        second_table,
        second_single,
        second_input,
        second_output,
        second_expand,
        second_reduce,
        second_logits,
        second_gains,
    )
    result = []
    for index in range(8):
        rate = GAIN_RATE if index == 7 else WEIGHT_RATE
        decay = 0.0 if index == 7 else WEIGHT_DECAY
        result.extend(
            adamw(weights[index], grads[index] * factor, firsts[index], seconds[index], rate, decay)
        )
    return (
        loss_sum,
        valid_count,
        gradient_norm,
        result[0],
        result[1],
        result[2],
        result[3],
        result[4],
        result[5],
        result[6],
        result[7],
        result[8],
        result[9],
        result[10],
        result[11],
        result[12],
        result[13],
        result[14],
        result[15],
        result[16],
        result[17],
        result[18],
        result[19],
        result[20],
        result[21],
        result[22],
        result[23],
    )


def solution(mesh):
    placed = (
        P(),
        P(),
        P(),
        P(),
        P(None, "row", "head"),
        P(None, "row", "head"),
        P(),
        P(),
        P(),
        P(),
        P(),
        P(),
        P(),
        P(),
        P(),
        P(),
        P(),
        P(),
        P(),
        P(),
        P(),
        P(),
        P(),
        P(),
        P(),
        P(),
        P(),
        P(),
        P(),
        P(),
    )
    return jax.shard_map(
        functools.partial(per_device, mesh.shape["row"], mesh.shape["head"]),
        mesh=mesh,
        in_specs=placed,
        out_specs=(
            P(),
            P(),
            P(),
            P(),
            P(),
            P(),
            P(),
            P(),
            P(),
            P(),
            P(),
            P(),
            P(),
            P(),
            P(),
            P(),
            P(),
            P(),
            P(),
            P(),
            P(),
            P(),
            P(),
            P(),
            P(),
            P(),
            P(),
        ),
        check_vma=False,
    )
```

```python
import functools

import jax
import jax.numpy as jnp
from jax import lax
from jax.experimental import pallas as pl
from jax.experimental.pallas import tpu as pltpu
from jax.sharding import PartitionSpec as P

STEP = 10


EPS = 1e-05
BETA_ONE = 0.9
BETA_TWO = 0.999
ADAM_EPS = 1e-08
WEIGHT_RATE = 0.1
GAIN_RATE = 0.5
WEIGHT_DECAY = 0.01
CLIP_NORM = 0.002


def normalize(value):
    mean = jnp.mean(value, axis=-1, keepdims=True)
    centred = value - mean
    scale = lax.rsqrt(jnp.mean(centred * centred, axis=-1, keepdims=True) + EPS)
    return (centred * scale, scale)


def norm_back(grad_out, unit, scale, gain):
    scaled = grad_out * gain
    first_mean = jnp.mean(scaled, axis=-1, keepdims=True)
    second_mean = jnp.mean(scaled * unit, axis=-1, keepdims=True)
    grad_in = scale * (scaled - first_mean - unit * second_mean)
    grad_gain = jnp.sum(grad_out * unit, axis=tuple(range(grad_out.ndim - 1)))
    return (grad_in, grad_gain)


def project(value, weight):
    return jnp.einsum("...c,cd->...d", value, weight, preferred_element_type=jnp.float32)


def project_back(grad, weight):
    return jnp.einsum("...d,cd->...c", grad, weight, preferred_element_type=jnp.float32)


def weight_grad(value, grad):
    return jnp.einsum("bijc,bijd->cd", value, grad, preferred_element_type=jnp.float32)


def triangle_forward(state, weight_in, weight_out, gains, pair_mask, incoming):
    hidden = weight_out.shape[0]
    pair_unit, pair_scale = normalize(state)
    normed = (pair_unit * gains[0]).astype(jnp.bfloat16)
    mixed = project(normed, weight_in)
    mask = pair_mask[..., None]
    left = (mask * jax.nn.sigmoid(mixed[..., :hidden]) * mixed[..., hidden : 2 * hidden]).astype(
        jnp.bfloat16
    )
    right = (
        mask
        * jax.nn.sigmoid(mixed[..., 2 * hidden : 3 * hidden])
        * mixed[..., 3 * hidden : 4 * hidden]
    ).astype(jnp.bfloat16)
    left_cols, right_cols = (
        lax.all_to_all(left, "head", split_axis=3, concat_axis=2, tiled=True),
        lax.all_to_all(right, "head", split_axis=3, concat_axis=2, tiled=True),
    )
    if incoming:
        left_cols, right_cols = (
            lax.all_to_all(left_cols, "row", split_axis=2, concat_axis=1, tiled=True),
            lax.all_to_all(right_cols, "row", split_axis=2, concat_axis=1, tiled=True),
        )
        left_cols = jnp.swapaxes(left_cols, 1, 2)
        right_cols = jnp.swapaxes(right_cols, 1, 2)
    right_all = lax.all_gather(right_cols, "row", axis=1, tiled=True)
    triangle = jnp.einsum(
        "bikc,bjkc->bijc", left_cols, right_all, preferred_element_type=jnp.float32
    )
    triangle = lax.all_to_all(
        triangle.astype(jnp.bfloat16), "head", split_axis=2, concat_axis=3, tiled=True
    )
    tri_unit, tri_scale = normalize(triangle.astype(jnp.float32))
    shaped = (tri_unit * gains[1]).astype(jnp.bfloat16)
    branch = project(shaped, weight_out)
    gate = jax.nn.sigmoid(mixed[..., 4 * hidden :])
    kept = (
        pair_unit,
        pair_scale,
        normed,
        mixed,
        left_cols,
        right_all,
        tri_unit,
        tri_scale,
        shaped,
        branch,
        gate,
    )
    return (state + gate * branch, kept)


def triangle_backward(grad_state, kept, weight_in, weight_out, gains, pair_mask, incoming):
    hidden = weight_out.shape[0]
    (
        pair_unit,
        pair_scale,
        normed,
        mixed,
        left_cols,
        right_all,
        tri_unit,
        tri_scale,
        shaped,
        branch,
        gate,
    ) = kept
    grad_branch = (grad_state * gate).astype(jnp.bfloat16)
    grad_gate = grad_state * branch * gate * (1.0 - gate)
    grad_out = weight_grad(shaped, grad_branch)
    grad_shaped = project_back(grad_branch, weight_out)
    grad_tri, gain_two = norm_back(grad_shaped, tri_unit, tri_scale, gains[1])
    tri_cols = lax.all_to_all(
        grad_tri.astype(jnp.bfloat16), "head", split_axis=3, concat_axis=2, tiled=True
    )
    grad_left = jnp.einsum(
        "bijc,bjkc->bikc", tri_cols, right_all, preferred_element_type=jnp.float32
    )
    grad_left = grad_left.astype(jnp.bfloat16)
    summed = lax.psum_scatter(
        jnp.einsum(
            "bijc,bikc->jbkc", tri_cols, left_cols, preferred_element_type=jnp.float32
        ).astype(jnp.bfloat16),
        "row",
        scatter_dimension=0,
        tiled=True,
    ).astype(jnp.float32)
    grad_right = jnp.transpose(summed, (1, 0, 2, 3)).astype(jnp.bfloat16)
    if incoming:
        grad_left, grad_right = (
            lax.all_to_all(
                jnp.swapaxes(grad_left, 1, 2), "row", split_axis=1, concat_axis=2, tiled=True
            ),
            lax.all_to_all(
                jnp.swapaxes(grad_right, 1, 2), "row", split_axis=1, concat_axis=2, tiled=True
            ),
        )
    back_left, back_right = (
        lax.all_to_all(grad_left, "head", split_axis=2, concat_axis=3, tiled=True),
        lax.all_to_all(grad_right, "head", split_axis=2, concat_axis=3, tiled=True),
    )
    mask = pair_mask[..., None]
    back_left = back_left.astype(jnp.float32) * mask
    back_right = back_right.astype(jnp.float32) * mask
    left_sig = jax.nn.sigmoid(mixed[..., :hidden])
    left_value = mixed[..., hidden : 2 * hidden]
    right_sig = jax.nn.sigmoid(mixed[..., 2 * hidden : 3 * hidden])
    right_value = mixed[..., 3 * hidden : 4 * hidden]
    grad_mixed = jnp.concatenate(
        [
            back_left * left_value * left_sig * (1.0 - left_sig),
            back_left * left_sig,
            back_right * right_value * right_sig * (1.0 - right_sig),
            back_right * right_sig,
            grad_gate,
        ],
        axis=-1,
    ).astype(jnp.bfloat16)
    grad_in = weight_grad(normed, grad_mixed)
    grad_normed = project_back(grad_mixed, weight_in)
    grad_first, gain_one = norm_back(grad_normed, pair_unit, pair_scale, gains[0])
    return (grad_state + grad_first, (grad_in, grad_out, gain_one, gain_two))


def transition_forward(state, weight_up, weight_down, gain):
    expand = weight_down.shape[0]
    unit, scale = normalize(state)
    lifted = (unit * gain).astype(jnp.bfloat16)
    inner = project(lifted, weight_up)
    product = (jax.nn.silu(inner[..., :expand]) * inner[..., expand:]).astype(jnp.bfloat16)
    return (state + project(product, weight_down), (unit, scale, lifted, inner, product))


def transition_backward(grad_state, kept, weight_up, weight_down, gain):
    expand = weight_down.shape[0]
    unit, scale, lifted, inner, product = kept
    grad_low = grad_state.astype(jnp.bfloat16)
    grad_down = weight_grad(product, grad_low)
    grad_product = project_back(grad_low, weight_down)
    gate_part = inner[..., :expand]
    up_part = inner[..., expand:]
    gate_sig = jax.nn.sigmoid(gate_part)
    silu_value = gate_part * gate_sig
    silu_slope = gate_sig * (1.0 + gate_part * (1.0 - gate_sig))
    grad_inner = jnp.concatenate(
        [grad_product * up_part * silu_slope, grad_product * silu_value], axis=-1
    )
    grad_inner = grad_inner.astype(jnp.bfloat16)
    grad_up = weight_grad(lifted, grad_inner)
    grad_lifted = project_back(grad_inner, weight_up)
    grad_middle, gain_grad = norm_back(grad_lifted, unit, scale, gain)
    return (grad_middle + grad_state, (grad_up, grad_down, gain_grad))


def block_forward(state, weight_in, weight_out, weight_up, weight_down, gains, pair_mask):
    first, kept_one = triangle_forward(
        state, weight_in[0], weight_out[0], gains[0:2], pair_mask, False
    )
    second, kept_two = triangle_forward(
        first, weight_in[1], weight_out[1], gains[2:4], pair_mask, True
    )
    output, kept_three = transition_forward(second, weight_up, weight_down, gains[4])
    return (output, (kept_one, kept_two, kept_three))


def block_backward(
    grad_state, state, weight_in, weight_out, weight_up, weight_down, gains, pair_mask
):
    skipped, kept = block_forward(
        state, weight_in, weight_out, weight_up, weight_down, gains, pair_mask
    )
    kept_one, kept_two, kept_three = kept
    grad_state, (grad_up, grad_down, gain_five) = transition_backward(
        grad_state, kept_three, weight_up, weight_down, gains[4]
    )
    grad_state, (in_two, out_two, gain_three, gain_four) = triangle_backward(
        grad_state, kept_two, weight_in[1], weight_out[1], gains[2:4], pair_mask, True
    )
    grad_state, (in_one, out_one, gain_one, gain_two) = triangle_backward(
        grad_state, kept_one, weight_in[0], weight_out[0], gains[0:2], pair_mask, False
    )
    return (
        grad_state,
        (
            jnp.stack([in_one, in_two]),
            jnp.stack([out_one, out_two]),
            grad_up,
            grad_down,
            jnp.stack([gain_one, gain_two, gain_three, gain_four, gain_five]),
        ),
    )


def adamw(weight, grad, first, second, rate, decay):
    first_new = BETA_ONE * first + (1.0 - BETA_ONE) * grad
    second_new = BETA_TWO * second + (1.0 - BETA_TWO) * grad * grad
    moved = (
        first_new
        / (1.0 - BETA_ONE**STEP)
        / (jnp.sqrt(second_new / (1.0 - BETA_TWO**STEP)) + ADAM_EPS)
    )
    return (first_new, second_new, weight - rate * (moved + decay * weight))


def gradients_by_block(
    single,
    residue_index,
    chain_index,
    token_mask,
    pair_valid,
    target_bins,
    relative_table,
    single_weight,
    triangle_input,
    triangle_output,
    expand_weight,
    reduce_weight,
    distogram_weight,
    norm_gains,
):
    crops, rows, cols = pair_valid.shape
    width = relative_table.shape[1]
    layers = triangle_input.shape[0]
    row_start = lax.axis_index("row") * rows
    col_start = lax.axis_index("head") * cols

    def take(array, start, count):
        return lax.dynamic_slice_in_dim(array, start, count, 1)

    offset = (
        take(residue_index, row_start, rows)[:, :, None]
        - take(residue_index, col_start, cols)[:, None, :]
    )
    same = (
        take(chain_index, row_start, rows)[:, :, None]
        == take(chain_index, col_start, cols)[:, None, :]
    )
    reach = (relative_table.shape[0] - 2) // 2
    bins = jnp.where(same, jnp.clip(offset, -reach, reach) + reach, 2 * reach + 1)
    relative_hot = (
        bins[..., None] == jnp.arange(relative_table.shape[0])[None, None, None, :]
    ).astype(jnp.float32)
    token_rows = take(token_mask, row_start, rows).astype(jnp.float32)
    token_cols = take(token_mask, col_start, cols).astype(jnp.float32)
    pair_mask = token_rows[:, :, None] * token_cols[:, None, :]
    loss_weight = pair_mask * pair_valid.astype(jnp.float32)
    low_input = triangle_input.astype(jnp.bfloat16)
    low_output = triangle_output.astype(jnp.bfloat16)
    low_expand = expand_weight.astype(jnp.bfloat16)
    low_reduce = reduce_weight.astype(jnp.bfloat16)
    low_logits = distogram_weight.astype(jnp.bfloat16)
    proj = project(single, single_weight.astype(jnp.bfloat16))
    state = project(relative_hot.astype(jnp.bfloat16), relative_table.astype(jnp.bfloat16))
    state = (
        state
        + take(proj, row_start, rows)[:, :, None, :width]
        + take(proj, col_start, cols)[:, None, :, width:]
    )
    inputs = []
    for layer in range(layers):
        inputs.append(state)
        state, unused = block_forward(
            state,
            low_input[layer],
            low_output[layer],
            low_expand[layer],
            low_reduce[layer],
            norm_gains[5 * layer : 5 * layer + 5],
            pair_mask,
        )
    head_unit, head_scale = normalize(state)
    shown = (head_unit * norm_gains[5 * layers]).astype(jnp.bfloat16)
    logits = project(shown, low_logits)
    largest = jnp.max(logits, axis=-1, keepdims=True)
    log_total = largest + jnp.log(jnp.sum(jnp.exp(logits - largest), axis=-1, keepdims=True))
    target_hot = (
        target_bins[..., None] == jnp.arange(logits.shape[-1])[None, None, None, :]
    ).astype(jnp.float32)
    picked = jnp.sum(logits * target_hot, axis=-1)
    loss_local = jnp.sum(loss_weight * (log_total[..., 0] - picked))
    grad_scores = (loss_weight[..., None] * (jnp.exp(logits - log_total) - target_hot)).astype(
        jnp.bfloat16
    )
    grad_logits = weight_grad(shown, grad_scores)
    grad_shown = project_back(grad_scores, low_logits)
    grad_state, gain_last = norm_back(grad_shown, head_unit, head_scale, norm_gains[5 * layers])
    collected = []
    for layer in reversed(range(layers)):
        grad_state, layer_grads = block_backward(
            grad_state,
            inputs[layer],
            low_input[layer],
            low_output[layer],
            low_expand[layer],
            low_reduce[layer],
            norm_gains[5 * layer : 5 * layer + 5],
            pair_mask,
        )
        collected.insert(0, layer_grads)
    grad_input = jnp.stack([entry[0] for entry in collected])
    grad_output = jnp.stack([entry[1] for entry in collected])
    grad_expand = jnp.stack([entry[2] for entry in collected])
    grad_reduce = jnp.stack([entry[3] for entry in collected])
    grad_gains = jnp.concatenate(
        [jnp.concatenate([entry[4] for entry in collected], axis=0), gain_last[None]], axis=0
    )
    grad_table = jnp.einsum(
        "bijr,bijc->rc", relative_hot, grad_state, precision=lax.Precision.HIGHEST
    )
    single_wide = single.astype(jnp.float32)
    row_part = jnp.einsum(
        "bis,bic->sc",
        take(single_wide, row_start, rows),
        jnp.sum(grad_state, axis=2),
        precision=lax.Precision.HIGHEST,
    )
    col_part = jnp.einsum(
        "bjs,bjc->sc",
        take(single_wide, col_start, cols),
        jnp.sum(grad_state, axis=1),
        precision=lax.Precision.HIGHEST,
    )
    grad_single = jnp.concatenate([row_part, col_part], axis=1)
    return (
        loss_local,
        jnp.sum(loss_weight),
        grad_table,
        grad_single,
        grad_input,
        grad_output,
        grad_expand,
        grad_reduce,
        grad_logits,
        grad_gains,
    )


F32 = jnp.float32
BF16 = jnp.bfloat16
LANES = 128
SUBLANES = 8
VMEM_BYTES = 58 * 2**20
ROW_BLOCK = 2
CHUNK_STEPS = 3
MESH = pl.DeviceIdType.MESH


def dot(left, right):
    return lax.dot_general(left, right, (((1,), (0,)), ((), ())), preferred_element_type=F32)


def dot_pairs(left, right):
    return lax.dot_general(left, right, (((1,), (1,)), ((), ())), preferred_element_type=F32)


def sigmoid(value):
    return 0.5 * jnp.tanh(0.5 * value) + 0.5


def unit_of(value):
    centred = value - jnp.mean(value, axis=0, keepdims=True)
    scale = lax.rsqrt(jnp.mean(centred * centred, axis=0, keepdims=True) + EPS)
    return (centred * scale, scale)


def unit_back(grad, unit, scale, gain):
    scaled = grad * gain
    first = jnp.mean(scaled, axis=0, keepdims=True)
    second = jnp.mean(scaled * unit, axis=0, keepdims=True)
    return scale * (scaled - first - unit * second)


def fold(value):
    total = value[:, :LANES]
    for start in range(LANES, value.shape[1], LANES):
        total = total + value[:, start : start + LANES]
    return total


def read_rows(ref):
    return jnp.concatenate([ref[row] for row in range(ref.shape[0])], axis=1)


def write_rows(ref, value):
    cols = ref.shape[2]
    for row in range(ref.shape[0]):
        ref[row] = value[:, row * cols : (row + 1) * cols].astype(ref.dtype)


def read_wire(ref):
    peers, rows, _ = ref.shape
    pieces = []
    for peer in range(peers):
        piece = ref[peer].astype(F32)
        pieces.append(
            jnp.concatenate(
                [piece[start : start + SUBLANES] for start in range(0, rows, SUBLANES)], axis=1
            )
        )
    return jnp.concatenate(pieces, axis=0)


def write_wire_piece(ref, peer, value):
    cols = ref.shape[2]
    ref[peer] = jnp.concatenate(
        [value[:, start : start + cols] for start in range(0, value.shape[1], cols)], axis=0
    ).astype(ref.dtype)


def write_wire(ref, value):
    for peer in range(ref.shape[0]):
        write_wire_piece(ref, peer, value[peer * SUBLANES : (peer + 1) * SUBLANES])


def triangle_start(r, name, state):
    width = state.shape[0]
    unit, _ = unit_of(state)
    normed = (unit * r[name + "gain0"][...]).astype(BF16)
    mixed = dot(r[name + "mix_t"][...], normed)
    mask = read_rows(r["mask"])
    for out, base in ((r[name + "a"], 0), (r[name + "b"], 2 * width)):
        for peer in range(out.shape[0]):
            start = base + peer * SUBLANES
            gate = mixed[start : start + SUBLANES]
            value = mixed[start + width : start + width + SUBLANES]
            write_wire_piece(out, peer, mask * sigmoid(gate) * value)


def triangle_finish(r, name, state):
    unit, _ = unit_of(state)
    normed = (unit * r[name + "gain0"][...]).astype(BF16)
    gate = sigmoid(dot(r[name + "gate_t"][...], normed))
    tri_unit, tri_scale = unit_of(read_wire(r[name + "tri"]))
    shaped = (tri_unit * r[name + "gain1"][...]).astype(BF16)
    branch = dot(r[name + "out_t"][...], shaped)
    return (state + gate * branch, (gate, tri_unit, tri_scale, shaped, branch))


def triangle_back_start(r, name, grad, kept):
    gate, tri_unit, tri_scale, shaped, branch = kept
    grad_branch = (grad * gate).astype(BF16)
    write_rows(r[name + "dgate"], grad * branch * gate * (1.0 - gate))
    r[name + "d_out"][...] += dot_pairs(shaped, grad_branch)
    grad_shaped = dot(r[name + "out"][...], grad_branch)
    r[name + "d_gain1"][...] += fold(grad_shaped * tri_unit)
    write_wire(r[name + "dtri"], unit_back(grad_shaped, tri_unit, tri_scale, r[name + "gain1"][...]))


def triangle_back_finish(r, name, grad, state):
    width = state.shape[0]
    unit, scale = unit_of(state)
    gain = r[name + "gain0"][...]
    normed = (unit * gain).astype(BF16)
    mixed = dot(r[name + "mix_t"][...], normed)
    mask = read_rows(r["mask"])
    parts = []
    for source, base in ((r[name + "da"], 0), (r[name + "db"], 2 * width)):
        back = read_wire(source) * mask
        gate = sigmoid(mixed[base : base + width])
        back_gate = back * gate
        parts.append((back_gate * mixed[base + width : base + 2 * width] * (1.0 - gate)).astype(BF16))
        parts.append(back_gate.astype(BF16))
    parts.append(read_rows(r[name + "dgate_in"]))
    grad_mixed = jnp.concatenate(parts, axis=0)
    r[name + "d_in"][...] += dot_pairs(normed, grad_mixed)
    grad_normed = dot(r[name + "in"][...], grad_mixed)
    r[name + "d_gain0"][...] += fold(grad_normed * unit)
    return grad + unit_back(grad_normed, unit, scale, gain)


def transition(r, name, state):
    unit, scale = unit_of(state)
    lifted = (unit * r[name + "gain"][...]).astype(BF16)
    inner = dot(r[name + "up_t"][...], lifted)
    half = inner.shape[0] // 2
    gate = inner[:half]
    slope = sigmoid(gate)
    product = (gate * slope * inner[half:]).astype(BF16)
    return (unit, scale, lifted, inner, slope, product)


def transition_finish(r, name, state, kept):
    return state + dot(r[name + "down_t"][...], kept[5])


def transition_back(r, name, grad, kept):
    unit, scale, lifted, inner, slope, product = kept
    half = inner.shape[0] // 2
    gate, up = inner[:half], inner[half:]
    grad_low = grad.astype(BF16)
    r[name + "d_down"][...] += dot_pairs(product, grad_low)
    grad_product = dot(r[name + "down"][...], grad_low)
    scaled = grad_product * slope
    grad_inner = jnp.concatenate(
        [
            (scaled * up * (1.0 + gate * (1.0 - slope))).astype(BF16),
            (scaled * gate).astype(BF16),
        ],
        axis=0,
    )
    r[name + "d_up"][...] += dot_pairs(lifted, grad_inner)
    grad_lifted = dot(r[name + "up"][...], grad_inner)
    r[name + "d_gain"][...] += fold(grad_lifted * unit)
    return grad + unit_back(grad_lifted, unit, scale, r[name + "gain"][...])


def head_back(r, state):
    unit, scale = unit_of(state)
    gain = r["head_gain"][...]
    shown = (unit * gain).astype(BF16)
    logits = dot(r["logits_t"][...], shown)
    largest = jnp.max(logits, axis=0, keepdims=True)
    raised = jnp.exp(logits - largest)
    total = jnp.sum(raised, axis=0, keepdims=True)
    log_total = largest + jnp.log(total)
    target = read_rows(r["target"])
    weight = read_rows(r["weight"])
    hot = lax.broadcasted_iota(jnp.int32, logits.shape, 0) == target
    picked = jnp.sum(jnp.where(hot, logits, 0.0), axis=0, keepdims=True)
    r["loss"][...] += fold(weight * (log_total - picked))
    share = raised * (1.0 / total)
    grad_scores = (weight * (share - jnp.where(hot, 1.0, 0.0))).astype(BF16)
    r["d_logits"][...] += dot_pairs(shown, grad_scores)
    grad_shown = dot(r["logits"][...], grad_scores)
    r["d_head_gain"][...] += fold(grad_shown * unit)
    return unit_back(grad_shown, unit, scale, gain)


def bins_hot(r):
    bins = read_rows(r["bins"])
    shape = (r["table_rows"], bins.shape[1])
    return jnp.where(lax.broadcasted_iota(jnp.int32, shape, 0) == bins, 1.0, 0.0).astype(BF16)


def block_spec(shape, kind):
    if kind == "rows":
        return pl.BlockSpec((ROW_BLOCK,) + shape[1:], lambda step: (step,) + (0,) * (len(shape) - 1))
    if kind == "anywhere":
        return pl.BlockSpec(memory_space=pl.ANY)
    if kind == "wire":
        return pl.BlockSpec((shape[0], SUBLANES * ROW_BLOCK, shape[2]), lambda step: (0, step, 0))
    return pl.BlockSpec(shape, lambda step: (0,) * len(shape))


def run_stage(body, name, rows, inputs, outputs, extra=None, exchange=None):
    in_names, out_names = list(inputs), list(outputs)
    steps = rows // ROW_BLOCK
    scratch = exchange.scratch() if exchange else []

    def kernel(*refs):
        step = pl.program_id(0)
        named = dict(zip(in_names + out_names, refs))
        named.update(extra or {})
        held = refs[len(in_names) + len(out_names) :]
        ring = Exchange(exchange.peers, exchange.half) if exchange else None

        @pl.when(step == 0)
        def _():
            if exchange:
                ring.greet()
            for out in out_names:
                if outputs[out][2] == "sum":
                    named[out][...] = jnp.zeros(outputs[out][0], outputs[out][1])

        if exchange:
            here = pl.ds(pl.multiple_of(step * SUBLANES * ROW_BLOCK, 16), SUBLANES * ROW_BLOCK)
            for index, wire in enumerate(exchange.wires):
                named[wire] = held[index].at[:, here, :]
        body(named)
        if exchange:
            moves = exchange.moves(held)

            @pl.when(step % CHUNK_STEPS == CHUNK_STEPS - 1)
            def _():
                @pl.when(step == CHUNK_STEPS - 1)
                def _():
                    ring.meet()

                ring.start(moves, step // CHUNK_STEPS)

            @pl.when(step == steps - 1)
            def _():
                lax.fori_loop(0, steps // CHUNK_STEPS, lambda chunk, _: ring.wait(moves, chunk), None)
                exchange.finish(ring, named, held)

    results = pl.pallas_call(
        kernel,
        grid=(steps,),
        in_specs=[block_spec(inputs[key][0].shape, inputs[key][1]) for key in in_names],
        out_specs=[block_spec(outputs[key][0], outputs[key][2]) for key in out_names],
        out_shape=[jax.ShapeDtypeStruct(outputs[key][0], outputs[key][1]) for key in out_names],
        scratch_shapes=scratch,
        compiler_params=pltpu.CompilerParams(
            dimension_semantics=("arbitrary",),
            vmem_limit_bytes=VMEM_BYTES,
            has_side_effects=exchange is not None,
            collective_id=exchange.collective_id if exchange else None,
        ),
        name=name,
    )(*[inputs[key][0] for key in in_names])
    return dict(zip(out_names, results))


def flip(value, step, count):
    result, bit = 0, 1
    while bit < count:
        result = result + lax.rem(lax.div(value, bit) + (step // bit) % 2, 2) * bit
        bit *= 2
    return result


def position(row, head, half, heads):
    inner = half // 2 * heads
    return (row % 2) * inner + (row // 2) * heads + head


def place_of(position, half, heads):
    inner = half // 2 * heads
    rest = lax.rem(position, inner)
    return (lax.div(rest, heads) * 2 + lax.div(position, inner), lax.rem(rest, heads))


class Exchange:
    def __init__(self, count, half):
        row, head = lax.axis_index("row"), lax.axis_index("head")
        place = lax.rem(row, half)
        inner = count // 2
        self.count = count
        self.half = half
        self.base = row - place
        self.me = lax.rem(place, 2) * inner + lax.div(place, 2) * (count // half) + head
        self.order = []
        for step in range(1, count):
            for other in (step, step ^ (inner - 1)):
                if other and other not in self.order:
                    self.order.append(other)

    def peer(self, step):
        return flip(self.me, step, self.count)

    def device(self, peer):
        place, head = place_of(peer, self.half, self.count // self.half)
        return (self.base + place, head)

    def greet(self):
        barrier = pltpu.get_barrier_semaphore()
        for step in self.order:
            pl.semaphore_signal(
                barrier, inc=1, device_id=self.device(self.peer(step)), device_id_type=MESH
            )

    def meet(self):
        pl.semaphore_wait(pltpu.get_barrier_semaphore(), self.count - 1)

    def copies(self, moves, chunk, steps):
        found = []
        for step in steps:
            peer = self.peer(step)
            for source, target, send_sems, recv_sems in moves:
                size = source.shape[1] // send_sems.shape[0]
                rows = pl.ds(pl.multiple_of(chunk * size, 16), size)
                if step == 0:
                    copy = pltpu.make_async_copy(
                        source.at[self.me, rows, :],
                        target.at[self.me, rows, :],
                        send_sems.at[chunk, 0],
                    )
                else:
                    copy = pltpu.make_async_remote_copy(
                        src_ref=source.at[peer, rows, :],
                        dst_ref=target.at[self.me, rows, :],
                        send_sem=send_sems.at[chunk, step],
                        recv_sem=recv_sems.at[chunk, step],
                        device_id=self.device(peer),
                        device_id_type=MESH,
                    )
                found.append(copy)
        return found

    def start(self, moves, chunk):
        for copy in self.copies(moves, chunk, self.order + [0]):
            copy.start()

    def wait(self, moves, chunk):
        for copy in self.copies(moves, chunk, self.order + [0]):
            copy.wait()


def widen(wide, low):
    peers, rows, cols = low.shape

    def step(peer, carry):
        value = low[peer].astype(F32)
        start = pl.multiple_of(peer * rows, SUBLANES)
        for lane in range(cols // LANES):
            wide[lane, pl.ds(start, rows), :] = value[:, lane * LANES : (lane + 1) * LANES]
        return carry

    lax.fori_loop(0, peers, step, 0)


def narrow(low, wide, first, last):
    _, rows, cols = low.shape

    def step(peer, carry):
        start = pl.multiple_of(peer * rows, SUBLANES)
        low[peer] = jnp.concatenate(
            [wide[lane, pl.ds(start, rows), :] for lane in range(cols // LANES)], axis=1
        ).astype(low.dtype)
        return carry

    lax.fori_loop(first, last, step, 0)


def take_channel(wide, channel):
    lanes, rows, _ = wide.shape
    count = rows // SUBLANES
    return jnp.concatenate(
        [wide[lane, pl.ds(channel, count, stride=SUBLANES), :] for lane in range(lanes)], axis=1
    ).astype(BF16)


def put_channel(wide, channel, value, first=0):
    for lane in range(wide.shape[0]):
        wide[lane, pl.ds(first * SUBLANES + channel, value.shape[0], stride=SUBLANES), :] = value[
            :, lane * LANES : (lane + 1) * LANES
        ]


def product_of(left, right, left_axis, right_axis):
    return lax.dot_general(
        left, right, (((left_axis,), (right_axis,)), ((), ())), preferred_element_type=F32
    )


class Forward:
    def __init__(self, peers, half, rows, tokens, name, incoming, collective_id):
        self.peers, self.half, self.incoming = peers, half, incoming
        self.rows, self.tokens, self.name = rows * SUBLANES, tokens, name
        self.chunks = rows // ROW_BLOCK // CHUNK_STEPS
        self.wires = [name + "a", name + "b"]
        self.collective_id = collective_id

    def outs(self):
        block = ((SUBLANES, self.tokens, self.tokens), BF16, "whole")
        tri = ((self.peers, self.rows, self.tokens), BF16, "anywhere")
        return {self.name + "left": block, self.name + "right": block, self.name + "tri": tri}

    def scratch(self):
        low = pltpu.VMEM((self.peers, self.rows, self.tokens), BF16)
        wide = pltpu.VMEM((self.tokens // LANES, self.peers * self.rows, LANES), F32)
        many = pltpu.SemaphoreType.DMA((self.chunks, self.peers))
        once = pltpu.SemaphoreType.DMA((1, self.peers))
        return [low] * 5 + [wide] * 3 + [many] * 4 + [once] * 2

    def moves(self, held):
        return [(held[0], held[2], held[8], held[9]), (held[1], held[3], held[10], held[11])]

    def finish(self, ring, named, held):
        _, _, a_got, b_got, low, wide_a, wide_b, wide_tri = held[:8]
        left_out, right_out = named[self.name + "left"], named[self.name + "right"]
        widen(wide_a, a_got)
        widen(wide_b, b_got)
        axis = 0 if self.incoming else 1
        middle = self.tokens * 2 // 3 // LANES * LANES
        reach = self.peers // 2
        tri = [(low, named[self.name + "tri"], held[12], held[13])]

        def first(channel, carry):
            left, right = take_channel(wide_a, channel), take_channel(wide_b, channel)
            left_out[channel] = left
            right_out[channel] = right
            part = left[:, :middle] if self.incoming else left[:middle]
            put_channel(wide_tri, channel, product_of(part, right, axis, axis))
            return carry

        def second(channel, carry):
            left, right = left_out[channel], right_out[channel]
            part = left[:, middle:] if self.incoming else left[middle:]
            put_channel(wide_tri, channel, product_of(part, right, axis, axis), middle)
            return carry

        lax.fori_loop(0, SUBLANES, first, 0)
        narrow(low, wide_tri, 0, reach)
        self.send_to(ring, tri, 0)
        lax.fori_loop(0, SUBLANES, second, 0)
        narrow(low, wide_tri, reach, self.peers)
        self.send_to(ring, tri, 1)
        ring.wait(tri, 0)

    def send_to(self, ring, tri, part):
        inner = self.peers // 2
        mine = lax.div(ring.me, inner)

        @pl.when(mine == part)
        def _():
            for copy in ring.copies(tri, 0, [step for step in ring.order if step < inner] + [0]):
                copy.start()

        @pl.when(mine != part)
        def _():
            for copy in ring.copies(tri, 0, [step for step in ring.order if step >= inner]):
                copy.start()


class Backward:
    def __init__(self, peers, half, rows, tokens, name, incoming, collective_id):
        self.peers, self.half, self.incoming = peers, half, incoming
        self.rows, self.tokens, self.name = rows * SUBLANES, tokens, name
        self.chunks = rows // ROW_BLOCK // CHUNK_STEPS
        self.wires = [name + "dtri"]
        self.collective_id = collective_id

    def outs(self):
        grad = ((self.peers, self.rows, self.tokens), BF16, "anywhere")
        return {self.name + "da": grad, self.name + "db": grad}

    def scratch(self):
        low = pltpu.VMEM((self.peers, self.rows, self.tokens), BF16)
        wide = pltpu.VMEM((self.tokens // LANES, self.peers * self.rows, LANES), F32)
        many = pltpu.SemaphoreType.DMA((self.chunks, self.peers))
        once = pltpu.SemaphoreType.DMA((1, self.peers))
        return [low] * 4 + [wide] * 2 + [many] * 2 + [once] * 4

    def moves(self, held):
        return [(held[0], held[1], held[6], held[7])]

    def finish(self, ring, named, held):
        _, got, low_a, low_b, wide, wide_grad = held[:6]
        left_in, right_in = named[self.name + "left"], named[self.name + "right"]
        widen(wide, got)

        def left_step(channel, carry):
            grad, right = take_channel(wide, channel), right_in[channel]
            put_channel(
                wide_grad,
                channel,
                product_of(right, grad, 1, 1) if self.incoming else product_of(grad, right, 1, 0),
            )
            return carry

        def right_step(channel, carry):
            grad, left = take_channel(wide, channel), left_in[channel]
            put_channel(
                wide_grad,
                channel,
                product_of(left, grad, 1, 0) if self.incoming else product_of(grad, left, 0, 0),
            )
            return carry

        lax.fori_loop(0, SUBLANES, left_step, 0)
        narrow(low_a, wide_grad, 0, self.peers)
        left_moves = [(low_a, named[self.name + "da"], held[8], held[9])]
        right_moves = [(low_b, named[self.name + "db"], held[10], held[11])]
        ring.start(left_moves, 0)
        lax.fori_loop(0, SUBLANES, right_step, 0)
        narrow(low_b, wide_grad, 0, self.peers)
        ring.start(right_moves, 0)
        ring.wait(left_moves, 0)
        ring.wait(right_moves, 0)


def by_crop(value, rows_axis, head_axis):
    count, heads = rows_axis, head_axis
    half = count // 2
    same, other = [], []
    for row in range(count):
        for head in range(heads):
            source = row * heads + head
            inner = half // 2 * heads
            place = row % inner // heads * 2 + row // inner
            for crop, pairs in ((head, same), (1 - head, other)):
                pairs.append((source, (crop * half + place) * heads + row % heads))
    head = lax.axis_index("head")
    crop = lax.axis_index("row") // half
    mine = lax.dynamic_index_in_dim(value, head, 0, keepdims=False)
    rest = lax.dynamic_index_in_dim(value, 1 - head, 0, keepdims=False)
    mine = lax.ppermute(mine, ("row", "head"), same)
    rest = lax.ppermute(rest, ("row", "head"), other)
    low = jnp.where(crop == 0, mine, rest)
    high = jnp.where(crop == 0, rest, mine)
    return jnp.concatenate([low, high], axis=-1)


def gradients_by_crop(
    row_count,
    head_count,
    single,
    residue_index,
    chain_index,
    token_mask,
    pair_valid,
    target_bins,
    relative_table,
    single_weight,
    triangle_input,
    triangle_output,
    expand_weight,
    reduce_weight,
    distogram_weight,
    norm_gains,
):
    crops, tokens = token_mask.shape
    width = relative_table.shape[1]
    layers = triangle_input.shape[0]
    half = row_count // crops
    peers = half * head_count
    rows = tokens // peers
    row_index = lax.axis_index("row")
    crop = row_index // half
    start = position(row_index % half, lax.axis_index("head"), half, head_count) * rows

    placed = by_crop(jnp.stack([pair_valid, target_bins], axis=1), row_count, head_count)
    valid, target = placed[0], placed[1]

    def of_crop(array):
        return lax.dynamic_index_in_dim(array, crop, 0, keepdims=False)

    def of_rows(array):
        return lax.dynamic_slice_in_dim(array, start, rows, 0)

    residues, chains = of_crop(residue_index), of_crop(chain_index)
    reach = (relative_table.shape[0] - 2) // 2
    bins = jnp.where(
        of_rows(chains)[:, None] == chains[None, :],
        jnp.clip(of_rows(residues)[:, None] - residues[None, :], -reach, reach) + reach,
        2 * reach + 1,
    )
    present = of_crop(token_mask).astype(F32)
    pair_mask = of_rows(present)[:, None] * present[None, :]
    loss_weight = pair_mask * valid.astype(F32)
    table_rows = -(-relative_table.shape[0] // 16) * 16
    table_t = jnp.pad(relative_table, ((0, table_rows - relative_table.shape[0]), (0, 0))).T
    tokens_single = of_crop(single)
    proj = project(tokens_single, single_weight.astype(BF16))
    proj_rows = of_rows(proj[:, :width])[:, :, None]
    proj_cols = proj[:, width:].T
    bins, pair_mask = bins[:, None, :], pair_mask[:, None, :]

    low_input = triangle_input.astype(BF16)
    low_output = triangle_output.astype(BF16)
    low_expand = expand_weight.astype(BF16)
    low_reduce = reduce_weight.astype(BF16)
    low_logits = distogram_weight.astype(BF16)

    def gain(index):
        return (norm_gains[index][:, None], "whole")

    def triangle_weights(layer, kind, *names):
        weight_in, weight_out = low_input[layer, kind], low_output[layer, kind]
        found = {
            "gain0": gain(5 * layer + 2 * kind),
            "gain1": gain(5 * layer + 2 * kind + 1),
            "mix_t": (weight_in[:, : 4 * width].T, "whole"),
            "gate_t": (weight_in[:, 4 * width :].T, "whole"),
            "in": (weight_in, "whole"),
            "out": (weight_out, "whole"),
            "out_t": (weight_out.T, "whole"),
        }
        return {f"t{layer}{kind}{name}": found[name] for name in " ".join(names).split()}

    def transition_weights(layer, *names):
        found = {
            "gain": gain(5 * layer + 4),
            "up": (low_expand[layer], "whole"),
            "up_t": (low_expand[layer].T, "whole"),
            "down": (low_reduce[layer], "whole"),
            "down_t": (low_reduce[layer].T, "whole"),
        }
        return {f"f{layer}{name}": found[name] for name in " ".join(names).split()}

    state_shape = (rows, width, tokens)
    hidden = low_expand.shape[2]
    state_out = (state_shape, F32, "rows")
    gate_out = (state_shape, BF16, "rows")
    gain_out = ((width, LANES), F32, "sum")
    mask_in = {"mask": (pair_mask, "rows")}

    def forward(name, incoming, collective_id):
        return Forward(peers, half, rows, tokens, name, incoming, collective_id)

    def backward(name, incoming, collective_id):
        return Backward(peers, half, rows, tokens, name, incoming, collective_id)

    def owned(name):
        return {name + "left": (got_of[name]["left"], "whole"), name + "right": (got_of[name]["right"], "whole")}

    def keep(name, got):
        got_of[name] = {part: got[name + part] for part in ("left", "right", "tri")}

    def back_start_outs(name):
        return {
            name + "dgate": gate_out,
            name + "d_out": ((width, width), F32, "sum"),
            name + "d_gain1": gain_out,
        }

    def back_finish_outs(name):
        return {name + "d_in": ((width, 5 * width), F32, "sum"), name + "d_gain0": gain_out}

    def transition_outs(name):
        return {
            name + "d_up": ((width, hidden), F32, "sum"),
            name + "d_down": ((hidden // 2, width), F32, "sum"),
            name + "d_gain": gain_out,
        }

    states, middles, got_of = {}, {}, {}
    sums = {}

    def body(r):
        hot = bins_hot(r)
        state = dot(r["table_t"][...], hot)
        cols = r["proj_cols"][...]
        state = state + jnp.concatenate(
            [cols + r["proj_rows"][row] for row in range(ROW_BLOCK)], axis=1
        )
        write_rows(r["state"], state)
        triangle_start(r, "t00", state)

    exchange = forward("t00", False, 0)
    got = run_stage(
        body,
        "first_state",
        rows,
        {
            "bins": (bins, "rows"),
            "proj_rows": (proj_rows, "rows"),
            "proj_cols": (proj_cols, "whole"),
            "table_t": (table_t.astype(BF16), "whole"),
            **mask_in,
            **triangle_weights(0, 0, "gain0 mix_t"),
        },
        {"state": state_out, **exchange.outs()},
        {"table_rows": table_rows},
        exchange,
    )
    states["t00"] = got["state"]
    keep("t00", got)

    for layer in range(layers):
        for kind in range(2):
            name = f"t{layer}{kind}"
            inputs = {
                "state": (states[name], "rows"),
                name + "tri": (got_of[name]["tri"], "wire"),
                **triangle_weights(layer, kind, "gain0 gain1 gate_t out_t"),
            }
            if kind == 0:
                following = f"t{layer}1"

                def body(r, name=name, following=following):
                    state, _ = triangle_finish(r, name, read_rows(r["state"]))
                    write_rows(r["next"], state)
                    triangle_start(r, following, state)

                exchange = forward(following, True, 1)
                got = run_stage(
                    body,
                    "between_updates",
                    rows,
                    {**inputs, **mask_in, **triangle_weights(layer, 1, "gain0 mix_t")},
                    {"next": state_out, **exchange.outs()},
                    exchange=exchange,
                )
                states[following] = got["next"]
                keep(following, got)
            elif layer + 1 < layers:
                following = f"t{layer + 1}0"
                lift = f"f{layer}"

                def body(r, name=name, following=following, lift=lift):
                    state, _ = triangle_finish(r, name, read_rows(r["state"]))
                    write_rows(r["middle"], state)
                    state = transition_finish(r, lift, state, transition(r, lift, state))
                    write_rows(r["next"], state)
                    triangle_start(r, following, state)

                exchange = forward(following, False, 2)
                got = run_stage(
                    body,
                    "layer_end",
                    rows,
                    {
                        **inputs,
                        **mask_in,
                        **transition_weights(layer, "gain up_t down_t"),
                        **triangle_weights(layer + 1, 0, "gain0 mix_t"),
                    },
                    {"middle": state_out, "next": state_out, **exchange.outs()},
                    exchange=exchange,
                )
                middles[layer] = got["middle"]
                states[following] = got["next"]
                keep(following, got)

    lift = f"f{layers - 1}"

    def body(r, name=name):
        state, kept = triangle_finish(r, name, read_rows(r["state"]))
        lifted = transition(r, lift, state)
        grad = head_back(r, transition_finish(r, lift, state, lifted))
        grad = transition_back(r, lift, grad, lifted)
        write_rows(r["grad"], grad)
        triangle_back_start(r, name, grad, kept)

    exchange = backward(name, True, 3)
    got = run_stage(
        body,
        "loss",
        rows,
        {
            **inputs,
            **owned(name),
            **triangle_weights(layers - 1, 1, "out"),
            **transition_weights(layers - 1, "gain up_t down_t", "up down"),
            "head_gain": gain(5 * layers),
            "logits": (low_logits, "whole"),
            "logits_t": (low_logits.T, "whole"),
            "target": (target[:, None, :], "rows"),
            "weight": (loss_weight[:, None, :], "rows"),
        },
        {
            "grad": state_out,
            "loss": ((1, LANES), F32, "sum"),
            "d_logits": (distogram_weight.shape, F32, "sum"),
            "d_head_gain": gain_out,
            **transition_outs(lift),
            **back_start_outs(name),
            **exchange.outs(),
        },
        exchange=exchange,
    )
    sums.update(got)

    for layer in reversed(range(layers)):
        for kind in (1, 0):
            name = f"t{layer}{kind}"
            inputs = {
                "grad_in": (got["grad"], "rows"),
                "state": (states[name], "rows"),
                name + "da": (got[name + "da"], "wire"),
                name + "db": (got[name + "db"], "wire"),
                name + "dgate_in": (got[name + "dgate"], "rows"),
                **mask_in,
                **triangle_weights(layer, kind, "gain0 mix_t in"),
            }
            if kind == 1:
                before = f"t{layer}0"

                def body(r, name=name, before=before):
                    grad = triangle_back_finish(
                        r, name, read_rows(r["grad_in"]), read_rows(r["state"])
                    )
                    write_rows(r["grad"], grad)
                    _, kept = triangle_finish(r, before, read_rows(r["before"]))
                    triangle_back_start(r, before, grad, kept)

                exchange = backward(before, False, 4)
                got = run_stage(
                    body,
                    "between_updates_back",
                    rows,
                    {
                        **inputs,
                        **owned(before),
                        "before": (states[before], "rows"),
                        before + "tri": (got_of[before]["tri"], "wire"),
                        **triangle_weights(layer, 0, "gain0 gain1 gate_t out_t", "out"),
                    },
                    {
                        "grad": state_out,
                        **back_finish_outs(name),
                        **back_start_outs(before),
                        **exchange.outs(),
                    },
                    exchange=exchange,
                )
            elif layer > 0:
                before = f"t{layer - 1}1"
                lift = f"f{layer - 1}"

                def body(r, name=name, before=before, lift=lift):
                    grad = triangle_back_finish(
                        r, name, read_rows(r["grad_in"]), read_rows(r["state"])
                    )
                    grad = transition_back(r, lift, grad, transition(r, lift, read_rows(r["middle"])))
                    write_rows(r["grad"], grad)
                    _, kept = triangle_finish(r, before, read_rows(r["before"]))
                    triangle_back_start(r, before, grad, kept)

                exchange = backward(before, True, 5)
                got = run_stage(
                    body,
                    "layer_end_back",
                    rows,
                    {
                        **inputs,
                        **owned(before),
                        "middle": (middles[layer - 1], "rows"),
                        "before": (states[before], "rows"),
                        before + "tri": (got_of[before]["tri"], "wire"),
                        **transition_weights(layer - 1, "gain up_t up down"),
                        **triangle_weights(layer - 1, 1, "gain0 gain1 gate_t out_t", "out"),
                    },
                    {
                        "grad": state_out,
                        **back_finish_outs(name),
                        **transition_outs(lift),
                        **back_start_outs(before),
                        **exchange.outs(),
                    },
                    exchange=exchange,
                )
            else:

                def body(r, name=name):
                    grad = triangle_back_finish(
                        r, name, read_rows(r["grad_in"]), read_rows(r["state"])
                    )
                    hot = bins_hot(r)
                    high = grad.astype(BF16)
                    low = (grad - high.astype(F32)).astype(BF16)
                    r["d_table"][...] += dot_pairs(high, hot) + dot_pairs(low, hot)
                    cols = r["d_cols"].shape[1]
                    for row in range(ROW_BLOCK):
                        part = grad[:, row * cols : (row + 1) * cols]
                        r["d_rows"][row] = fold(part)
                        r["d_cols"][...] += part

                got = run_stage(
                    body,
                    "first_state_back",
                    rows,
                    {**inputs, "bins": (bins, "rows")},
                    {
                        **back_finish_outs(name),
                        "d_table": ((width, table_rows), F32, "sum"),
                        "d_rows": ((rows, width, LANES), F32, "rows"),
                        "d_cols": ((width, tokens), F32, "sum"),
                    },
                    {"table_rows": table_rows},
                )
            sums.update(got)

    wide_single = tokens_single.astype(F32)
    row_part = jnp.einsum(
        "is,ic->sc",
        of_rows(wide_single),
        jnp.sum(sums["d_rows"], axis=2),
        precision=lax.Precision.HIGHEST,
    )
    col_part = jnp.einsum(
        "js,cj->sc", wide_single, sums["d_cols"], precision=lax.Precision.HIGHEST
    )
    gains = []
    for layer in range(layers):
        for part in (f"t{layer}0d_gain0", f"t{layer}0d_gain1", f"t{layer}1d_gain0", f"t{layer}1d_gain1", f"f{layer}d_gain"):
            gains.append(jnp.sum(sums[part], axis=1))
    gains.append(jnp.sum(sums["d_head_gain"], axis=1))

    def stacked(part):
        return jnp.stack(
            [jnp.stack([sums[f"t{layer}{kind}{part}"] for kind in range(2)]) for layer in range(layers)]
        )

    return (
        jnp.sum(sums["loss"]),
        jnp.sum(loss_weight),
        sums["d_table"][:, : relative_table.shape[0]].T,
        jnp.concatenate([row_part, col_part], axis=1),
        stacked("d_in"),
        stacked("d_out"),
        jnp.stack([sums[f"f{layer}d_up"] for layer in range(layers)]),
        jnp.stack([sums[f"f{layer}d_down"] for layer in range(layers)]),
        sums["d_logits"],
        jnp.stack(gains),
    )


def per_device(
    row_count,
    head_count,
    single,
    residue_index,
    chain_index,
    token_mask,
    pair_valid,
    target_bins,
    relative_table,
    single_weight,
    triangle_input,
    triangle_output,
    expand_weight,
    reduce_weight,
    distogram_weight,
    norm_gains,
    first_table,
    second_table,
    first_single,
    second_single,
    first_input,
    second_input,
    first_output,
    second_output,
    first_expand,
    second_expand,
    first_reduce,
    second_reduce,
    first_logits,
    second_logits,
    first_gains,
    second_gains,
):
    crops, tokens = token_mask.shape
    width = relative_table.shape[1]
    peers = row_count * head_count // crops
    given = (
        single,
        residue_index,
        chain_index,
        token_mask,
        pair_valid,
        target_bins,
        relative_table,
        single_weight,
        triangle_input,
        triangle_output,
        expand_weight,
        reduce_weight,
        distogram_weight,
        norm_gains,
    )
    if (
        crops == 2
        and head_count == 2
        and width == SUBLANES * peers
        and tokens % (peers * ROW_BLOCK * CHUNK_STEPS) == 0
        and tokens % LANES == 0
    ):
        local = gradients_by_crop(row_count, head_count, *given)
    else:
        local = gradients_by_block(*given)
    summed = lax.psum(local, ("row", "head"))
    loss_sum, valid_count = summed[0], summed[1]
    grads = [grad / valid_count for grad in summed[2:]]
    squares = jnp.zeros((), jnp.float32)
    for g in grads:
        squares = squares + jnp.sum(g * g)
    gradient_norm = jnp.sqrt(squares)
    factor = jnp.minimum(1.0, CLIP_NORM / (gradient_norm + 1e-06))
    weights = (
        relative_table,
        single_weight,
        triangle_input,
        triangle_output,
        expand_weight,
        reduce_weight,
        distogram_weight,
        norm_gains,
    )
    firsts = (
        first_table,
        first_single,
        first_input,
        first_output,
        first_expand,
        first_reduce,
        first_logits,
        first_gains,
    )
    seconds = (
        second_table,
        second_single,
        second_input,
        second_output,
        second_expand,
        second_reduce,
        second_logits,
        second_gains,
    )
    result = []
    for index in range(8):
        rate = GAIN_RATE if index == 7 else WEIGHT_RATE
        decay = 0.0 if index == 7 else WEIGHT_DECAY
        result.extend(
            adamw(weights[index], grads[index] * factor, firsts[index], seconds[index], rate, decay)
        )
    return (
        loss_sum,
        valid_count,
        gradient_norm,
        result[0],
        result[1],
        result[2],
        result[3],
        result[4],
        result[5],
        result[6],
        result[7],
        result[8],
        result[9],
        result[10],
        result[11],
        result[12],
        result[13],
        result[14],
        result[15],
        result[16],
        result[17],
        result[18],
        result[19],
        result[20],
        result[21],
        result[22],
        result[23],
    )


def solution(mesh):
    placed = (
        P(),
        P(),
        P(),
        P(),
        P(None, "row", "head"),
        P(None, "row", "head"),
        P(),
        P(),
        P(),
        P(),
        P(),
        P(),
        P(),
        P(),
        P(),
        P(),
        P(),
        P(),
        P(),
        P(),
        P(),
        P(),
        P(),
        P(),
        P(),
        P(),
        P(),
        P(),
        P(),
        P(),
    )
    return jax.shard_map(
        functools.partial(per_device, mesh.shape["row"], mesh.shape["head"]),
        mesh=mesh,
        in_specs=placed,
        out_specs=(
            P(),
            P(),
            P(),
            P(),
            P(),
            P(),
            P(),
            P(),
            P(),
            P(),
            P(),
            P(),
            P(),
            P(),
            P(),
            P(),
            P(),
            P(),
            P(),
            P(),
            P(),
            P(),
            P(),
            P(),
            P(),
            P(),
            P(),
        ),
        check_vma=False,
    )
```

```python
import functools

import jax
import jax.numpy as jnp
from jax import lax
from jax.experimental import pallas as pl
from jax.experimental.pallas import tpu as pltpu
from jax.sharding import PartitionSpec as P

STEP = 10


EPS = 1e-05
BETA_ONE = 0.9
BETA_TWO = 0.999
ADAM_EPS = 1e-08
WEIGHT_RATE = 0.1
GAIN_RATE = 0.5
WEIGHT_DECAY = 0.01
CLIP_NORM = 0.002


def normalize(value):
    mean = jnp.mean(value, axis=-1, keepdims=True)
    centred = value - mean
    scale = lax.rsqrt(jnp.mean(centred * centred, axis=-1, keepdims=True) + EPS)
    return (centred * scale, scale)


def norm_back(grad_out, unit, scale, gain):
    scaled = grad_out * gain
    first_mean = jnp.mean(scaled, axis=-1, keepdims=True)
    second_mean = jnp.mean(scaled * unit, axis=-1, keepdims=True)
    grad_in = scale * (scaled - first_mean - unit * second_mean)
    grad_gain = jnp.sum(grad_out * unit, axis=tuple(range(grad_out.ndim - 1)))
    return (grad_in, grad_gain)


def project(value, weight):
    return jnp.einsum("...c,cd->...d", value, weight, preferred_element_type=jnp.float32)


def project_back(grad, weight):
    return jnp.einsum("...d,cd->...c", grad, weight, preferred_element_type=jnp.float32)


def weight_grad(value, grad):
    return jnp.einsum("bijc,bijd->cd", value, grad, preferred_element_type=jnp.float32)


def triangle_forward(state, weight_in, weight_out, gains, pair_mask, incoming):
    hidden = weight_out.shape[0]
    pair_unit, pair_scale = normalize(state)
    normed = (pair_unit * gains[0]).astype(jnp.bfloat16)
    mixed = project(normed, weight_in)
    mask = pair_mask[..., None]
    left = (mask * jax.nn.sigmoid(mixed[..., :hidden]) * mixed[..., hidden : 2 * hidden]).astype(
        jnp.bfloat16
    )
    right = (
        mask
        * jax.nn.sigmoid(mixed[..., 2 * hidden : 3 * hidden])
        * mixed[..., 3 * hidden : 4 * hidden]
    ).astype(jnp.bfloat16)
    left_cols, right_cols = (
        lax.all_to_all(left, "head", split_axis=3, concat_axis=2, tiled=True),
        lax.all_to_all(right, "head", split_axis=3, concat_axis=2, tiled=True),
    )
    if incoming:
        left_cols, right_cols = (
            lax.all_to_all(left_cols, "row", split_axis=2, concat_axis=1, tiled=True),
            lax.all_to_all(right_cols, "row", split_axis=2, concat_axis=1, tiled=True),
        )
        left_cols = jnp.swapaxes(left_cols, 1, 2)
        right_cols = jnp.swapaxes(right_cols, 1, 2)
    right_all = lax.all_gather(right_cols, "row", axis=1, tiled=True)
    triangle = jnp.einsum(
        "bikc,bjkc->bijc", left_cols, right_all, preferred_element_type=jnp.float32
    )
    triangle = lax.all_to_all(
        triangle.astype(jnp.bfloat16), "head", split_axis=2, concat_axis=3, tiled=True
    )
    tri_unit, tri_scale = normalize(triangle.astype(jnp.float32))
    shaped = (tri_unit * gains[1]).astype(jnp.bfloat16)
    branch = project(shaped, weight_out)
    gate = jax.nn.sigmoid(mixed[..., 4 * hidden :])
    kept = (
        pair_unit,
        pair_scale,
        normed,
        mixed,
        left_cols,
        right_all,
        tri_unit,
        tri_scale,
        shaped,
        branch,
        gate,
    )
    return (state + gate * branch, kept)


def triangle_backward(grad_state, kept, weight_in, weight_out, gains, pair_mask, incoming):
    hidden = weight_out.shape[0]
    (
        pair_unit,
        pair_scale,
        normed,
        mixed,
        left_cols,
        right_all,
        tri_unit,
        tri_scale,
        shaped,
        branch,
        gate,
    ) = kept
    grad_branch = (grad_state * gate).astype(jnp.bfloat16)
    grad_gate = grad_state * branch * gate * (1.0 - gate)
    grad_out = weight_grad(shaped, grad_branch)
    grad_shaped = project_back(grad_branch, weight_out)
    grad_tri, gain_two = norm_back(grad_shaped, tri_unit, tri_scale, gains[1])
    tri_cols = lax.all_to_all(
        grad_tri.astype(jnp.bfloat16), "head", split_axis=3, concat_axis=2, tiled=True
    )
    grad_left = jnp.einsum(
        "bijc,bjkc->bikc", tri_cols, right_all, preferred_element_type=jnp.float32
    )
    grad_left = grad_left.astype(jnp.bfloat16)
    summed = lax.psum_scatter(
        jnp.einsum(
            "bijc,bikc->jbkc", tri_cols, left_cols, preferred_element_type=jnp.float32
        ).astype(jnp.bfloat16),
        "row",
        scatter_dimension=0,
        tiled=True,
    ).astype(jnp.float32)
    grad_right = jnp.transpose(summed, (1, 0, 2, 3)).astype(jnp.bfloat16)
    if incoming:
        grad_left, grad_right = (
            lax.all_to_all(
                jnp.swapaxes(grad_left, 1, 2), "row", split_axis=1, concat_axis=2, tiled=True
            ),
            lax.all_to_all(
                jnp.swapaxes(grad_right, 1, 2), "row", split_axis=1, concat_axis=2, tiled=True
            ),
        )
    back_left, back_right = (
        lax.all_to_all(grad_left, "head", split_axis=2, concat_axis=3, tiled=True),
        lax.all_to_all(grad_right, "head", split_axis=2, concat_axis=3, tiled=True),
    )
    mask = pair_mask[..., None]
    back_left = back_left.astype(jnp.float32) * mask
    back_right = back_right.astype(jnp.float32) * mask
    left_sig = jax.nn.sigmoid(mixed[..., :hidden])
    left_value = mixed[..., hidden : 2 * hidden]
    right_sig = jax.nn.sigmoid(mixed[..., 2 * hidden : 3 * hidden])
    right_value = mixed[..., 3 * hidden : 4 * hidden]
    grad_mixed = jnp.concatenate(
        [
            back_left * left_value * left_sig * (1.0 - left_sig),
            back_left * left_sig,
            back_right * right_value * right_sig * (1.0 - right_sig),
            back_right * right_sig,
            grad_gate,
        ],
        axis=-1,
    ).astype(jnp.bfloat16)
    grad_in = weight_grad(normed, grad_mixed)
    grad_normed = project_back(grad_mixed, weight_in)
    grad_first, gain_one = norm_back(grad_normed, pair_unit, pair_scale, gains[0])
    return (grad_state + grad_first, (grad_in, grad_out, gain_one, gain_two))


def transition_forward(state, weight_up, weight_down, gain):
    expand = weight_down.shape[0]
    unit, scale = normalize(state)
    lifted = (unit * gain).astype(jnp.bfloat16)
    inner = project(lifted, weight_up)
    product = (jax.nn.silu(inner[..., :expand]) * inner[..., expand:]).astype(jnp.bfloat16)
    return (state + project(product, weight_down), (unit, scale, lifted, inner, product))


def transition_backward(grad_state, kept, weight_up, weight_down, gain):
    expand = weight_down.shape[0]
    unit, scale, lifted, inner, product = kept
    grad_low = grad_state.astype(jnp.bfloat16)
    grad_down = weight_grad(product, grad_low)
    grad_product = project_back(grad_low, weight_down)
    gate_part = inner[..., :expand]
    up_part = inner[..., expand:]
    gate_sig = jax.nn.sigmoid(gate_part)
    silu_value = gate_part * gate_sig
    silu_slope = gate_sig * (1.0 + gate_part * (1.0 - gate_sig))
    grad_inner = jnp.concatenate(
        [grad_product * up_part * silu_slope, grad_product * silu_value], axis=-1
    )
    grad_inner = grad_inner.astype(jnp.bfloat16)
    grad_up = weight_grad(lifted, grad_inner)
    grad_lifted = project_back(grad_inner, weight_up)
    grad_middle, gain_grad = norm_back(grad_lifted, unit, scale, gain)
    return (grad_middle + grad_state, (grad_up, grad_down, gain_grad))


def block_forward(state, weight_in, weight_out, weight_up, weight_down, gains, pair_mask):
    first, kept_one = triangle_forward(
        state, weight_in[0], weight_out[0], gains[0:2], pair_mask, False
    )
    second, kept_two = triangle_forward(
        first, weight_in[1], weight_out[1], gains[2:4], pair_mask, True
    )
    output, kept_three = transition_forward(second, weight_up, weight_down, gains[4])
    return (output, (kept_one, kept_two, kept_three))


def block_backward(
    grad_state, state, weight_in, weight_out, weight_up, weight_down, gains, pair_mask
):
    skipped, kept = block_forward(
        state, weight_in, weight_out, weight_up, weight_down, gains, pair_mask
    )
    kept_one, kept_two, kept_three = kept
    grad_state, (grad_up, grad_down, gain_five) = transition_backward(
        grad_state, kept_three, weight_up, weight_down, gains[4]
    )
    grad_state, (in_two, out_two, gain_three, gain_four) = triangle_backward(
        grad_state, kept_two, weight_in[1], weight_out[1], gains[2:4], pair_mask, True
    )
    grad_state, (in_one, out_one, gain_one, gain_two) = triangle_backward(
        grad_state, kept_one, weight_in[0], weight_out[0], gains[0:2], pair_mask, False
    )
    return (
        grad_state,
        (
            jnp.stack([in_one, in_two]),
            jnp.stack([out_one, out_two]),
            grad_up,
            grad_down,
            jnp.stack([gain_one, gain_two, gain_three, gain_four, gain_five]),
        ),
    )


def adamw(weight, grad, first, second, rate, decay):
    first_new = BETA_ONE * first + (1.0 - BETA_ONE) * grad
    second_new = BETA_TWO * second + (1.0 - BETA_TWO) * grad * grad
    moved = (
        first_new
        / (1.0 - BETA_ONE**STEP)
        / (jnp.sqrt(second_new / (1.0 - BETA_TWO**STEP)) + ADAM_EPS)
    )
    return (first_new, second_new, weight - rate * (moved + decay * weight))


def gradients_by_block(
    single,
    residue_index,
    chain_index,
    token_mask,
    pair_valid,
    target_bins,
    relative_table,
    single_weight,
    triangle_input,
    triangle_output,
    expand_weight,
    reduce_weight,
    distogram_weight,
    norm_gains,
):
    crops, rows, cols = pair_valid.shape
    width = relative_table.shape[1]
    layers = triangle_input.shape[0]
    row_start = lax.axis_index("row") * rows
    col_start = lax.axis_index("head") * cols

    def take(array, start, count):
        return lax.dynamic_slice_in_dim(array, start, count, 1)

    offset = (
        take(residue_index, row_start, rows)[:, :, None]
        - take(residue_index, col_start, cols)[:, None, :]
    )
    same = (
        take(chain_index, row_start, rows)[:, :, None]
        == take(chain_index, col_start, cols)[:, None, :]
    )
    reach = (relative_table.shape[0] - 2) // 2
    bins = jnp.where(same, jnp.clip(offset, -reach, reach) + reach, 2 * reach + 1)
    relative_hot = (
        bins[..., None] == jnp.arange(relative_table.shape[0])[None, None, None, :]
    ).astype(jnp.float32)
    token_rows = take(token_mask, row_start, rows).astype(jnp.float32)
    token_cols = take(token_mask, col_start, cols).astype(jnp.float32)
    pair_mask = token_rows[:, :, None] * token_cols[:, None, :]
    loss_weight = pair_mask * pair_valid.astype(jnp.float32)
    low_input = triangle_input.astype(jnp.bfloat16)
    low_output = triangle_output.astype(jnp.bfloat16)
    low_expand = expand_weight.astype(jnp.bfloat16)
    low_reduce = reduce_weight.astype(jnp.bfloat16)
    low_logits = distogram_weight.astype(jnp.bfloat16)
    proj = project(single, single_weight.astype(jnp.bfloat16))
    state = project(relative_hot.astype(jnp.bfloat16), relative_table.astype(jnp.bfloat16))
    state = (
        state
        + take(proj, row_start, rows)[:, :, None, :width]
        + take(proj, col_start, cols)[:, None, :, width:]
    )
    inputs = []
    for layer in range(layers):
        inputs.append(state)
        state, unused = block_forward(
            state,
            low_input[layer],
            low_output[layer],
            low_expand[layer],
            low_reduce[layer],
            norm_gains[5 * layer : 5 * layer + 5],
            pair_mask,
        )
    head_unit, head_scale = normalize(state)
    shown = (head_unit * norm_gains[5 * layers]).astype(jnp.bfloat16)
    logits = project(shown, low_logits)
    largest = jnp.max(logits, axis=-1, keepdims=True)
    log_total = largest + jnp.log(jnp.sum(jnp.exp(logits - largest), axis=-1, keepdims=True))
    target_hot = (
        target_bins[..., None] == jnp.arange(logits.shape[-1])[None, None, None, :]
    ).astype(jnp.float32)
    picked = jnp.sum(logits * target_hot, axis=-1)
    loss_local = jnp.sum(loss_weight * (log_total[..., 0] - picked))
    grad_scores = (loss_weight[..., None] * (jnp.exp(logits - log_total) - target_hot)).astype(
        jnp.bfloat16
    )
    grad_logits = weight_grad(shown, grad_scores)
    grad_shown = project_back(grad_scores, low_logits)
    grad_state, gain_last = norm_back(grad_shown, head_unit, head_scale, norm_gains[5 * layers])
    collected = []
    for layer in reversed(range(layers)):
        grad_state, layer_grads = block_backward(
            grad_state,
            inputs[layer],
            low_input[layer],
            low_output[layer],
            low_expand[layer],
            low_reduce[layer],
            norm_gains[5 * layer : 5 * layer + 5],
            pair_mask,
        )
        collected.insert(0, layer_grads)
    grad_input = jnp.stack([entry[0] for entry in collected])
    grad_output = jnp.stack([entry[1] for entry in collected])
    grad_expand = jnp.stack([entry[2] for entry in collected])
    grad_reduce = jnp.stack([entry[3] for entry in collected])
    grad_gains = jnp.concatenate(
        [jnp.concatenate([entry[4] for entry in collected], axis=0), gain_last[None]], axis=0
    )
    grad_table = jnp.einsum(
        "bijr,bijc->rc", relative_hot, grad_state, precision=lax.Precision.HIGHEST
    )
    single_wide = single.astype(jnp.float32)
    row_part = jnp.einsum(
        "bis,bic->sc",
        take(single_wide, row_start, rows),
        jnp.sum(grad_state, axis=2),
        precision=lax.Precision.HIGHEST,
    )
    col_part = jnp.einsum(
        "bjs,bjc->sc",
        take(single_wide, col_start, cols),
        jnp.sum(grad_state, axis=1),
        precision=lax.Precision.HIGHEST,
    )
    grad_single = jnp.concatenate([row_part, col_part], axis=1)
    return (
        loss_local,
        jnp.sum(loss_weight),
        grad_table,
        grad_single,
        grad_input,
        grad_output,
        grad_expand,
        grad_reduce,
        grad_logits,
        grad_gains,
    )


F32 = jnp.float32
BF16 = jnp.bfloat16
LANES = 128
SUBLANES = 8
PACKED = 16
ROW_BLOCK = 2
PHASES = SUBLANES // ROW_BLOCK
CHUNK_ROWS = SUBLANES * SUBLANES
VMEM_BYTES = 58 * 2**20
MESH = pl.DeviceIdType.MESH
ROWS, WIRE, WHOLE, SUM, ANYWHERE = range(5)


class Bag:
    def __init__(self, **entries):
        self.__dict__.update(entries)


class Arg:
    def __init__(self, array, kind, index=None, block=None, column=None):
        self.array, self.kind, self.index, self.block = array, kind, index, block
        self.column = column

    def spec(self):
        if self.index is None:
            return block_spec(self.array.shape, self.kind)
        index = self.index
        return pl.BlockSpec(self.block, lambda step: index)


class Column:
    def __init__(self, ref, column):
        self.ref, self.column = ref, column

    def __getitem__(self, _):
        return self.ref[:, self.column : self.column + 1]


class Out:
    def __init__(self, shape, dtype, kind):
        self.shape, self.dtype, self.kind = shape, dtype, kind

    def spec(self):
        return block_spec(self.shape, self.kind)


def block_spec(shape, kind):
    if kind == ANYWHERE:
        return pl.BlockSpec(memory_space=pl.ANY)
    if kind == WIRE:
        return pl.BlockSpec((shape[0], CHUNK_ROWS, shape[2]), lambda step: (0, step // PHASES, 0))
    if kind == ROWS:
        return pl.BlockSpec((ROW_BLOCK,) + shape[1:], lambda step: (step,) + (0,) * (len(shape) - 1))
    return pl.BlockSpec(shape, lambda step: (0,) * len(shape))


def is_leaf(value):
    return isinstance(value, (Arg, Out))


def bag_of(tree, leaves):
    return Bag(
        **{
            key: next(leaves) if is_leaf(value) else bag_of(value, leaves)
            for key, value in tree.items()
        }
    )


def leaves_of(tree):
    found = []
    for value in tree.values():
        found.extend([value] if is_leaf(value) else leaves_of(value))
    return found


def dot(left, right):
    return lax.dot_general(left, right, (((1,), (0,)), ((), ())), preferred_element_type=F32)


def dot_pairs(left, right):
    return lax.dot_general(left, right, (((1,), (1,)), ((), ())), preferred_element_type=F32)


def product_of(left, right, left_axis, right_axis):
    return lax.dot_general(
        left, right, (((left_axis,), (right_axis,)), ((), ())), preferred_element_type=F32
    )


def sigmoid(value):
    return 0.5 * jnp.tanh(0.5 * value) + 0.5


def unit_of(value):
    centred = value - jnp.mean(value, axis=0, keepdims=True)
    scale = lax.rsqrt(jnp.mean(centred * centred, axis=0, keepdims=True) + EPS)
    return (centred * scale, scale)


def unit_back(grad, unit, scale, gain):
    scaled = grad * gain
    first = jnp.mean(scaled, axis=0, keepdims=True)
    second = jnp.mean(scaled * unit, axis=0, keepdims=True)
    return scale * (scaled - first - unit * second)


def fold(value):
    total = value[:, :LANES]
    for start in range(LANES, value.shape[1], LANES):
        total = total + value[:, start : start + LANES]
    return total


def read_rows(ref):
    return jnp.concatenate([ref[row] for row in range(ref.shape[0])], axis=1)


def write_rows(ref, value):
    cols = ref.shape[2]
    for row in range(ref.shape[0]):
        ref[row] = value[:, row * cols : (row + 1) * cols].astype(ref.dtype)


class Wire:
    def __init__(self, wide, phase):
        self.wide, self.phase = wide, phase

    def tokens(self, row):
        width = self.wide.shape[1] // SUBLANES
        return pl.ds(self.phase * ROW_BLOCK + row, width, stride=SUBLANES)

    def read(self):
        lanes = self.wide.shape[0]
        return jnp.concatenate(
            [
                self.wide[lane, self.tokens(row), :]
                for row in range(ROW_BLOCK)
                for lane in range(lanes)
            ],
            axis=1,
        )

    def write(self, value):
        lanes = self.wide.shape[0]
        for row in range(ROW_BLOCK):
            for lane in range(lanes):
                start = (row * lanes + lane) * LANES
                self.wide[lane, self.tokens(row), :] = value[:, start : start + LANES]


def widen(wide, block):
    def step(peer, carry):
        value = block[peer].astype(F32)
        start = pl.multiple_of(peer * CHUNK_ROWS, CHUNK_ROWS)
        for lane in range(wide.shape[0]):
            wide[lane, pl.ds(start, CHUNK_ROWS), :] = value[:, lane * LANES : (lane + 1) * LANES]
        return carry

    lax.fori_loop(0, block.shape[0], step, 0)


def narrow(low, wide, chunk):
    rows = pl.ds(pl.multiple_of(chunk * CHUNK_ROWS, CHUNK_ROWS), CHUNK_ROWS)

    def step(peer, carry):
        start = pl.multiple_of(peer * CHUNK_ROWS, CHUNK_ROWS)
        low[peer, rows, :] = jnp.concatenate(
            [wide[lane, pl.ds(start, CHUNK_ROWS), :] for lane in range(wide.shape[0])], axis=1
        ).astype(low.dtype)
        return carry

    lax.fori_loop(0, low.shape[0], step, 0)


def triangle_start(weights, mask, left_wire, right_wire, state):
    width = state.shape[0]
    unit, _ = unit_of(state)
    normed = (unit * weights.gain0[...]).astype(BF16)
    mixed = dot(weights.mix_t[...], normed)
    for wire, base in ((left_wire, 0), (right_wire, 2 * width)):
        gate = sigmoid(mixed[base : base + width])
        wire.write(mask * gate * mixed[base + width : base + 2 * width])


def triangle_finish(weights, wire, state):
    unit, _ = unit_of(state)
    normed = (unit * weights.gain0[...]).astype(BF16)
    gate = sigmoid(dot(weights.gate_t[...], normed))
    tri_unit, tri_scale = unit_of(wire.read())
    shaped = (tri_unit * weights.gain1[...]).astype(BF16)
    branch = dot(weights.out_t[...], shaped)
    return (state + gate * branch, (gate, tri_unit, tri_scale, shaped, branch))


def triangle_back_start(weights, o, wire, grad, kept):
    gate, tri_unit, tri_scale, shaped, branch = kept
    grad_branch = (grad * gate).astype(BF16)
    write_rows(o.grad_gate, grad * branch * gate * (1.0 - gate))
    o.out[...] += dot_pairs(shaped, grad_branch)
    grad_shaped = dot(weights.out[...], grad_branch)
    o.gain1[...] += fold(grad_shaped * tri_unit)
    wire.write(unit_back(grad_shaped, tri_unit, tri_scale, weights.gain1[...]))


def triangle_back_finish(weights, i, o, mask, grad, state):
    width = state.shape[0]
    unit, scale = unit_of(state)
    gain = weights.gain0[...]
    normed = (unit * gain).astype(BF16)
    mixed = dot(weights.mix_t[...], normed)
    parts = []
    for wire, base in ((i.grad_left, 0), (i.grad_right, 2 * width)):
        back = wire.read() * mask
        gate = sigmoid(mixed[base : base + width])
        back_gate = back * gate
        parts.append((back_gate * mixed[base + width : base + 2 * width] * (1.0 - gate)).astype(BF16))
        parts.append(back_gate.astype(BF16))
    parts.append(read_rows(i.grad_gate))
    grad_mixed = jnp.concatenate(parts, axis=0)
    o.mix[...] += dot_pairs(normed, grad_mixed)
    grad_normed = dot(weights.mix[...], grad_mixed)
    o.gain0[...] += fold(grad_normed * unit)
    return grad + unit_back(grad_normed, unit, scale, gain)


def transition(weights, state):
    unit, scale = unit_of(state)
    lifted = (unit * weights.gain[...]).astype(BF16)
    inner = dot(weights.up_t[...], lifted)
    half = inner.shape[0] // 2
    gate = inner[:half]
    slope = sigmoid(gate)
    product = (gate * slope * inner[half:]).astype(BF16)
    return (unit, scale, lifted, inner, slope, product)


def transition_finish(weights, state, kept):
    return state + dot(weights.down_t[...], kept[5])


def transition_back(weights, o, grad, kept):
    unit, scale, lifted, inner, slope, product = kept
    half = inner.shape[0] // 2
    gate, up = inner[:half], inner[half:]
    grad_low = grad.astype(BF16)
    o.down[...] += dot_pairs(product, grad_low)
    grad_product = dot(weights.down[...], grad_low)
    scaled = grad_product * slope
    grad_inner = jnp.concatenate(
        [
            (scaled * up * (1.0 + gate * (1.0 - slope))).astype(BF16),
            (scaled * gate).astype(BF16),
        ],
        axis=0,
    )
    o.up[...] += dot_pairs(lifted, grad_inner)
    grad_lifted = dot(weights.up[...], grad_inner)
    o.gain[...] += fold(grad_lifted * unit)
    return grad + unit_back(grad_lifted, unit, scale, weights.gain[...])


def head_back(i, o, state):
    unit, scale = unit_of(state)
    gain = i.gain[...]
    shown = (unit * gain).astype(BF16)
    logits = dot(i.logits_t[...], shown)
    largest = jnp.max(logits, axis=0, keepdims=True)
    raised = jnp.exp(logits - largest)
    total = jnp.sum(raised, axis=0, keepdims=True)
    log_total = largest + jnp.log(total)
    target = read_rows(i.target)
    weight = read_rows(i.weight)
    hot = lax.broadcasted_iota(jnp.int32, logits.shape, 0) == target
    picked = jnp.sum(jnp.where(hot, logits, 0.0), axis=0, keepdims=True)
    o.loss[...] += fold(weight * (log_total - picked))
    o.count[...] += fold(weight)
    share = raised * (1.0 / total)
    grad_scores = (weight * (share - jnp.where(hot, 1.0, 0.0))).astype(BF16)
    o.logits[...] += dot_pairs(grad_scores, shown)
    grad_shown = dot(i.logits[...], grad_scores)
    o.gain[...] += fold(grad_shown * unit)
    return unit_back(grad_shown, unit, scale, gain)


def bins_hot(bins, table_rows):
    bins = read_rows(bins)
    shape = (table_rows, bins.shape[1])
    return jnp.where(lax.broadcasted_iota(jnp.int32, shape, 0) == bins, 1.0, 0.0).astype(BF16)


def run_stage(body, name, rows, inputs, outputs, exchange=None):
    args, outs = leaves_of(inputs), leaves_of(outputs)
    steps = rows // ROW_BLOCK
    chunks = rows // SUBLANES
    wire_args = [index for index, arg in enumerate(args) if arg.kind == WIRE]
    wires = exchange.wires if exchange else 0
    chunk_scratch = []
    if wire_args:
        peers, _, tokens = args[wire_args[0]].array.shape
    if exchange:
        peers, tokens = exchange.peers, exchange.tokens
    for _ in range(len(wire_args) + wires):
        chunk_scratch.append(pltpu.VMEM((tokens // LANES, peers * CHUNK_ROWS, LANES), F32))
    scratch = exchange.scratch() if exchange else []

    def kernel(*refs):
        step = pl.program_id(0)
        phase, chunk = lax.rem(step, PHASES), lax.div(step, PHASES)
        in_refs = [
            ref if arg.column is None else Column(ref, arg.column) for arg, ref in zip(args, refs)
        ]
        out_refs = list(refs[len(args) : len(args) + len(outs)])
        wide = list(refs[len(args) + len(outs) :][: len(chunk_scratch)])
        held = refs[len(args) + len(outs) + len(chunk_scratch) :]
        ring = Exchange(exchange.peers, exchange.half) if exchange else None

        @pl.when(step == 0)
        def _():
            if exchange:
                ring.greet()
            for out, ref in zip(outs, out_refs):
                if out.kind == SUM:
                    ref[...] = jnp.zeros(out.shape, out.dtype)

        @pl.when(phase == 0)
        def _():
            for index, target in zip(wire_args, wide):
                widen(target, in_refs[index])

        body_in = list(in_refs)
        for index, source in zip(wire_args, wide):
            body_in[index] = Wire(source, phase)
        sent = wide[len(wire_args) :]
        i, o = bag_of(inputs, iter(body_in)), bag_of(outputs, iter(out_refs))
        body(i, o, *[Wire(target, phase) for target in sent])
        if exchange:
            moves = exchange.moves(held)

            @pl.when(phase == PHASES - 1)
            def _():
                for source, move in zip(sent, moves):
                    narrow(move[0], source, chunk)

                @pl.when(chunk == 0)
                def _():
                    ring.meet()

                ring.start(moves, chunk)

            @pl.when(step == steps - 1)
            def _():
                def wait(index, carry):
                    ring.wait(moves, index)
                    return carry

                lax.fori_loop(0, chunks, wait, 0)
                exchange.finish(ring, bag_of(inputs, iter(in_refs)), o, held)

    results = pl.pallas_call(
        kernel,
        grid=(steps,),
        in_specs=[arg.spec() for arg in args],
        out_specs=[out.spec() for out in outs],
        out_shape=[jax.ShapeDtypeStruct(out.shape, out.dtype) for out in outs],
        scratch_shapes=chunk_scratch + scratch,
        compiler_params=pltpu.CompilerParams(
            dimension_semantics=(pltpu.ARBITRARY,),
            vmem_limit_bytes=VMEM_BYTES,
            has_side_effects=exchange is not None,
            collective_id=exchange.collective_id if exchange else None,
        ),
        cost_estimate=pl.CostEstimate(flops=10**11, bytes_accessed=10**6, transcendentals=0),
        name=name,
    )(*[arg.array for arg in args])
    return bag_of(outputs, iter(results))


def flip(value, step, count):
    result, bit = 0, 1
    while bit < count:
        result = result + lax.rem(lax.div(value, bit) + (step // bit) % 2, 2) * bit
        bit *= 2
    return result


def position(row, head, half, heads):
    inner = half // 2 * heads
    return (row % 2) * inner + (row // 2) * heads + head


def place_of(position, half, heads):
    inner = half // 2 * heads
    rest = lax.rem(position, inner)
    return (lax.div(rest, heads) * 2 + lax.div(position, inner), lax.rem(rest, heads))


class Exchange:
    def __init__(self, count, half):
        row, head = lax.axis_index("row"), lax.axis_index("head")
        place = lax.rem(row, half)
        inner = count // 2
        self.count = count
        self.half = half
        self.base = row - place
        self.me = lax.rem(place, 2) * inner + lax.div(place, 2) * (count // half) + head
        self.twin = (lax.rem(row + half, 2 * half), head)
        self.order = []
        for step in range(1, count):
            for other in (step, step ^ (inner - 1)):
                if other and other not in self.order:
                    self.order.append(other)

    def peer(self, step):
        return flip(self.me, step, self.count)

    def device(self, peer):
        place, head = place_of(peer, self.half, self.count // self.half)
        return (self.base + place, head)

    def greet(self):
        barrier = pltpu.get_barrier_semaphore()
        for step in self.order:
            pl.semaphore_signal(
                barrier, inc=1, device_id=self.device(self.peer(step)), device_id_type=MESH
            )

    def meet(self):
        pl.semaphore_wait(pltpu.get_barrier_semaphore(), self.count - 1)

    def copies(self, moves, chunk, steps):
        found = []
        for step in steps:
            peer = self.peer(step)
            for source, target, send_sems, recv_sems in moves:
                size = source.shape[1] // send_sems.shape[0]
                rows = pl.ds(pl.multiple_of(chunk * size, PACKED), size)
                if step == 0:
                    copy = pltpu.make_async_copy(
                        source.at[self.me, rows, :],
                        target.at[self.me, rows, :],
                        send_sems.at[chunk, 0],
                    )
                else:
                    copy = pltpu.make_async_remote_copy(
                        src_ref=source.at[peer, rows, :],
                        dst_ref=target.at[self.me, rows, :],
                        send_sem=send_sems.at[chunk, step],
                        recv_sem=recv_sems.at[chunk, step],
                        device_id=self.device(peer),
                        device_id_type=MESH,
                    )
                found.append(copy)
        return found

    def start(self, moves, chunk):
        for copy in self.copies(moves, chunk, self.order + [0]):
            copy.start()

    def wait(self, moves, chunk):
        for copy in self.copies(moves, chunk, self.order + [0]):
            copy.wait()


def join_channels(got, pair):
    peers, rows, _ = got.shape
    even, odd = [], []
    for peer in range(peers):
        for start in range(0, rows, CHUNK_ROWS):
            piece = got[peer, pl.ds(pl.multiple_of(start + pair * PACKED, PACKED), PACKED), :]
            piece = piece.astype(F32)
            even.append(piece[:SUBLANES])
            odd.append(piece[SUBLANES:])
    return [jnp.concatenate(pieces, axis=0).astype(BF16) for pieces in (even, odd)]


def split_channels(low, pair, even, odd, first=0):
    chunks = low.shape[1] // CHUNK_ROWS
    for start in range(0, even.shape[0], SUBLANES):
        block = (first + start) // SUBLANES
        row = block % chunks * CHUNK_ROWS + pair * PACKED
        low[block // chunks, pl.ds(pl.multiple_of(row, PACKED), PACKED), :] = jnp.concatenate(
            [even[start : start + SUBLANES], odd[start : start + SUBLANES]], axis=0
        ).astype(low.dtype)


def each_pair(body):
    def step(pair, carry):
        body(pair)
        return carry

    lax.fori_loop(0, SUBLANES // 2, step, 0)


class Forward:
    wires = 2

    def __init__(self, peers, half, rows, tokens, incoming, collective_id):
        self.peers, self.half, self.incoming = peers, half, incoming
        self.rows, self.tokens = rows * SUBLANES, tokens
        self.chunks = rows // SUBLANES
        self.collective_id = collective_id

    def outs(self):
        block = (SUBLANES, self.tokens, self.tokens)
        return dict(
            left=Out(block, BF16, WHOLE),
            right=Out(block, BF16, WHOLE),
            tri=Out((self.peers, self.rows, self.tokens), BF16, ANYWHERE),
        )

    def scratch(self):
        low = pltpu.VMEM((self.peers, self.rows, self.tokens), BF16)
        many = pltpu.SemaphoreType.DMA((self.chunks, self.peers))
        once = pltpu.SemaphoreType.DMA((1, self.peers))
        return [low] * 5 + [many] * 4 + [once] * 2

    def moves(self, held):
        return [(held[0], held[2], held[5], held[6]), (held[1], held[3], held[7], held[8])]

    def finish(self, ring, i, o, held):
        _, _, left_got, right_got, low = held[:5]
        axis = 0 if self.incoming else 1
        middle = self.tokens * 2 // 3 // LANES * LANES
        tri = [(low, o.tri, held[9], held[10])]

        def multiply(pair, first, last):
            found = []
            for channel in (2 * pair, 2 * pair + 1):
                left, right = o.left[channel], o.right[channel]
                part = left[:, first:last] if self.incoming else left[first:last]
                found.append(product_of(part, right, axis, axis))
            split_channels(low, pair, *found, first)

        def join(pair):
            for got, out in ((left_got, o.left), (right_got, o.right)):
                for index, value in enumerate(join_channels(got, pair)):
                    out[2 * pair + index] = value
            multiply(pair, 0, middle)

        each_pair(join)
        self.send_to(ring, tri, 0)
        each_pair(lambda pair: multiply(pair, middle, self.tokens))
        self.send_to(ring, tri, 1)
        ring.wait(tri, 0)

    def send_to(self, ring, tri, part):
        inner = self.peers // 2
        mine = lax.div(ring.me, inner)

        @pl.when(mine == part)
        def _():
            for copy in ring.copies(tri, 0, [step for step in ring.order if step < inner] + [0]):
                copy.start()

        @pl.when(mine != part)
        def _():
            for copy in ring.copies(tri, 0, [step for step in ring.order if step >= inner]):
                copy.start()


class Backward:
    wires = 1

    def __init__(self, peers, half, rows, tokens, incoming, collective_id):
        self.peers, self.half, self.incoming = peers, half, incoming
        self.rows, self.tokens = rows * SUBLANES, tokens
        self.chunks = rows // SUBLANES
        self.collective_id = collective_id

    def outs(self):
        wire = (self.peers, self.rows, self.tokens)
        return dict(grad_left=Out(wire, BF16, ANYWHERE), grad_right=Out(wire, BF16, ANYWHERE))

    def scratch(self):
        low = pltpu.VMEM((self.peers, self.rows, self.tokens), BF16)
        block = pltpu.VMEM((SUBLANES, self.tokens, self.tokens), BF16)
        many = pltpu.SemaphoreType.DMA((self.chunks, self.peers))
        once = pltpu.SemaphoreType.DMA((1, self.peers))
        return [low] * 4 + [block] + [many] * 2 + [once] * 4

    def moves(self, held):
        return [(held[0], held[1], held[5], held[6])]

    def finish(self, ring, i, o, held):
        _, got, left_low, right_low, grads = held[:5]

        def left_step(pair):
            found = []
            for index, grad in enumerate(join_channels(got, pair)):
                channel = 2 * pair + index
                grads[channel] = grad
                right = i.owned.right[channel]
                found.append(
                    product_of(right, grad, 1, 1) if self.incoming else product_of(grad, right, 1, 0)
                )
            split_channels(left_low, pair, *found)

        def right_step(pair):
            found = []
            for channel in (2 * pair, 2 * pair + 1):
                grad, left = grads[channel], i.owned.left[channel]
                found.append(
                    product_of(left, grad, 1, 0) if self.incoming else product_of(grad, left, 0, 0)
                )
            split_channels(right_low, pair, *found)

        left_moves = [(left_low, o.grad_left, held[7], held[8])]
        right_moves = [(right_low, o.grad_right, held[9], held[10])]
        each_pair(left_step)
        ring.start(left_moves, 0)
        each_pair(right_step)
        ring.start(right_moves, 0)
        ring.wait(left_moves, 0)
        ring.wait(right_moves, 0)


def prepare(triangle_input, triangle_output, expand_weight, reduce_weight, distogram_weight, norm_gains):
    merged = [
        triangle_input.reshape((-1,) + triangle_input.shape[2:]),
        triangle_output.reshape((-1,) + triangle_output.shape[2:]),
        expand_weight,
        reduce_weight,
        distogram_weight[None],
    ]
    count = len(merged)

    def kernel(*refs):
        for source, plain, turned in zip(refs[:count], refs[count + 1 :: 2], refs[count + 2 :: 2]):
            for index in range(source.shape[0]):
                value = source[index]
                plain[index] = value.astype(BF16)
                turned[index] = value.T.astype(BF16)
        gains = refs[count][...]
        refs[-1][...] = gains.T

    shapes = []
    for array in merged:
        depth, rows, cols = array.shape
        shapes.append(jax.ShapeDtypeStruct((depth, rows, cols), BF16))
        shapes.append(jax.ShapeDtypeStruct((depth, cols, rows), BF16))
    shapes.append(jax.ShapeDtypeStruct(norm_gains.shape[::-1], F32))
    return pl.pallas_call(
        kernel,
        out_shape=shapes,
        compiler_params=pltpu.CompilerParams(vmem_limit_bytes=VMEM_BYTES),
        name="prepare",
    )(*merged, norm_gains)


def by_crop(value, rows_axis, head_axis):
    count, heads = rows_axis, head_axis
    half = count // 2
    inner = half // 2 * heads
    same, other = [], []
    for row in range(count):
        place = row % inner // heads * 2 + row // inner
        for head in range(heads):
            source = row * heads + head
            for crop, pairs in ((head, same), (1 - head, other)):
                pairs.append((source, (crop * half + place) * heads + row % heads))
    head = lax.axis_index("head")
    crop = lax.axis_index("row") // half
    mine = lax.dynamic_index_in_dim(value, head, 0, keepdims=False)
    rest = lax.dynamic_index_in_dim(value, 1 - head, 0, keepdims=False)
    mine = lax.ppermute(mine, ("row", "head"), same)
    rest = lax.ppermute(rest, ("row", "head"), other)
    low = jnp.where(crop == 0, mine, rest)
    high = jnp.where(crop == 0, rest, mine)
    return jnp.concatenate([low, high], axis=-1)


def reduce_rest(half, peers, collective_id, grids, gains, rows):
    sizes = [grid.shape[0] * grid.shape[1] // LANES for grid in grids]
    used = sum(sizes) + len(gains) + SUBLANES * len(rows)
    part = -(-used // (peers * SUBLANES)) * SUBLANES
    total = part * peers
    starts, spot = [], 0
    for size in sizes:
        starts.append(spot)
        spot += size
    row_starts = []
    for _ in rows:
        row_starts.append(spot)
        spot += SUBLANES
    gain_start = spot
    count = len(grids) + len(gains) + len(rows)

    def kernel(*refs):
        out, local, got, mine, other, sends, recvs, back_sends, back_recvs, twin_sems = refs[count:]
        ring = Exchange(peers, half)
        ring.greet()
        barrier = pltpu.get_barrier_semaphore()
        pl.semaphore_signal(barrier, inc=1, device_id=ring.twin, device_id_type=MESH)
        for grid, start in zip(refs[: len(grids)], starts):
            height, width = grid.shape
            for column in range(width // LANES):
                local[pl.ds(start + column * height, height), :] = grid[
                    :, column * LANES : (column + 1) * LANES
                ]
        ones = jnp.ones((SUBLANES, LANES), F32)
        for index, gain in enumerate(refs[len(grids) : len(grids) + len(gains)]):
            folded = lax.dot_general(
                ones,
                gain[...],
                (((1,), (1,)), ((), ())),
                precision=lax.Precision.HIGHEST,
                preferred_element_type=F32,
            )
            local[pl.ds(gain_start + index, 1), :] = folded[:1]
        for row, start in zip(refs[len(grids) + len(gains) : count], row_starts):
            local[pl.ds(start, 1), :] = row[...]
            local[pl.ds(start + 1, SUBLANES - 1), :] = jnp.zeros((SUBLANES - 1, LANES), F32)
        tail = gain_start + len(gains)
        if total > tail:
            local[pl.ds(tail, total - tail), :] = jnp.zeros((total - tail, LANES), F32)
        pl.semaphore_wait(barrier, peers)

        def block(peer):
            return pl.ds(pl.multiple_of(peer * part, SUBLANES), part)

        here = block(ring.me)

        def gather(step):
            peer = ring.peer(step)
            return pltpu.make_async_remote_copy(
                src_ref=local.at[block(peer), :],
                dst_ref=got.at[here, :],
                send_sem=sends.at[step],
                recv_sem=recvs.at[step],
                device_id=ring.device(peer),
                device_id_type=MESH,
            )

        def spread(step):
            return pltpu.make_async_remote_copy(
                src_ref=out.at[here, :],
                dst_ref=out.at[here, :],
                send_sem=back_sends.at[step],
                recv_sem=back_recvs.at[step],
                device_id=ring.device(ring.peer(step)),
                device_id_type=MESH,
            )

        for step in ring.order:
            gather(step).start()
        got[here, :] = local[here, :]
        for step in ring.order:
            gather(step).wait()
        value = got[pl.ds(0, part), :]
        for peer in range(1, peers):
            value = value + got[pl.ds(peer * part, part), :]
        mine[...] = value
        copy = pltpu.make_async_remote_copy(
            src_ref=mine,
            dst_ref=other,
            send_sem=twin_sems.at[0],
            recv_sem=twin_sems.at[1],
            device_id=ring.twin,
            device_id_type=MESH,
        )
        copy.start()
        copy.wait()
        out[here, :] = mine[...] + other[...]
        for step in ring.order:
            spread(step).start()
        for step in ring.order:
            spread(step).wait()

    inside = pl.BlockSpec(memory_space=pltpu.VMEM)
    whole = pl.pallas_call(
        kernel,
        in_specs=[inside] * count,
        out_specs=inside,
        out_shape=jax.ShapeDtypeStruct((total, LANES), F32),
        scratch_shapes=[pltpu.VMEM((total, LANES), F32)] * 2
        + [pltpu.VMEM((part, LANES), F32)] * 2
        + [pltpu.SemaphoreType.DMA((peers,))] * 4
        + [pltpu.SemaphoreType.DMA((2,))],
        compiler_params=pltpu.CompilerParams(
            collective_id=collective_id, has_side_effects=True, vmem_limit_bytes=VMEM_BYTES
        ),
        cost_estimate=pl.CostEstimate(flops=10**10, bytes_accessed=10**6, transcendentals=0),
        name="reduce_rest",
    )(*grids, *gains, *rows)
    return whole, starts, row_starts, gain_start


def update(rest, starts, row_starts, gain_start, early, weights, firsts, seconds):
    layers, kinds, width, mixed = weights[2].shape
    hidden = weights[4].shape[2]
    early_in, early_up, early_rows = early
    given = [rest, *early_in, *early_up, early_rows]
    count = len(given)

    def kernel(*refs):
        whole = refs[0]
        in_refs = refs[1 : 1 + len(early_in)]
        up_refs = refs[1 + len(early_in) : count - 1]
        rows_ref = refs[count - 1]
        states = [refs[count + 8 * kind : count + 8 * (kind + 1)] for kind in range(3)]
        scalars = refs[count + 24 : count + 27]
        results = refs[count + 27 :]

        def taken(start, size):
            return whole[pl.ds(start, size), :]

        def wide(start, height, columns):
            return jnp.concatenate(
                [taken(start + column * height, height) for column in range(columns)], axis=1
            )

        loss = jnp.sum(taken(row_starts[0], 1), axis=1, keepdims=True)
        valid = jnp.sum(taken(row_starts[1], 1), axis=1, keepdims=True)
        table_rows, single_rows = weights[0].shape[0], weights[1].shape[0]
        outs, downs = layers * kinds - 1, hidden // 2
        grads = {}
        grads[0, ()] = taken(starts[4], table_rows)
        grads[1, ()] = jnp.concatenate(
            [taken(starts[5], single_rows), taken(starts[6], single_rows)], axis=1
        )
        spot = 0
        for layer in range(layers):
            for kind in range(kinds):
                if layer == 0:
                    grads[2, (layer, kind)] = wide(starts[kind], width, mixed // LANES)
                else:
                    grads[2, (layer, kind)] = in_refs[(layer - 1) * kinds + kind][...]
                if layer == 0 and kind == 0:
                    grads[3, (layer, kind)] = taken(starts[2], width)
                else:
                    grads[3, (layer, kind)] = rows_ref[pl.ds(spot, width), :]
                    spot += width
        for layer in range(layers):
            grads[4, (layer,)] = up_refs[layer][...]
            grads[5, (layer,)] = rows_ref[pl.ds(spot, downs), :]
            spot += downs
        grads[6, ()] = taken(starts[3], weights[6].shape[1]).T
        grads[7, ()] = taken(gain_start, weights[7].shape[0])
        squares = jnp.zeros((1, 1), F32)
        for key in grads:
            grads[key] = grads[key] / valid
            squares = squares + jnp.sum(grads[key] * grads[key], axis=(0, 1), keepdims=True)
        norm = jnp.sqrt(squares)
        factor = jnp.minimum(1.0, CLIP_NORM / (norm + 1e-06))
        for ref, value in zip(scalars, (loss, valid, norm)):
            ref[...] = value
        for (index, spot), grad in grads.items():
            rate = GAIN_RATE if index == 7 else WEIGHT_RATE
            decay = 0.0 if index == 7 else WEIGHT_DECAY
            new = adamw(
                states[0][index][spot],
                grad * factor,
                states[1][index][spot],
                states[2][index][spot],
                rate,
                decay,
            )
            for ref, value in zip(results[3 * index : 3 * index + 3], new):
                ref[spot] = value

    one = jax.ShapeDtypeStruct((1, 1), F32)
    shapes = [one] * 3
    for weight in weights:
        shapes += [jax.ShapeDtypeStruct(weight.shape, F32)] * 3
    found = pl.pallas_call(
        kernel,
        out_shape=shapes,
        compiler_params=pltpu.CompilerParams(vmem_limit_bytes=VMEM_BYTES),
        name="update",
    )(*given, *weights, *firsts, *seconds)
    return tuple(value[0, 0] for value in found[:3]) + tuple(found[3:])


def step_by_crop(row_count, head_count, given, weights, firsts, seconds):
    single, residue_index, chain_index, token_mask, pair_valid, target_bins = given
    relative_table, single_weight, triangle_input, triangle_output = weights[:4]
    expand_weight, reduce_weight, distogram_weight, norm_gains = weights[4:]
    crops, tokens = token_mask.shape
    width = relative_table.shape[1]
    layers = triangle_input.shape[0]
    half = row_count // crops
    peers = half * head_count
    rows = tokens // peers
    row_index = lax.axis_index("row")
    crop = row_index // half
    start = position(row_index % half, lax.axis_index("head"), half, head_count) * rows

    placed = by_crop(jnp.stack([pair_valid, target_bins], axis=1), row_count, head_count)
    valid, target = placed[0], placed[1]

    def of_crop(array):
        return lax.dynamic_index_in_dim(array, crop, 0, keepdims=False)

    def of_rows(array):
        return lax.dynamic_slice_in_dim(array, start, rows, 0)

    residues, chains = of_crop(residue_index), of_crop(chain_index)
    reach = (relative_table.shape[0] - 2) // 2
    bins = jnp.where(
        of_rows(chains)[:, None] == chains[None, :],
        jnp.clip(of_rows(residues)[:, None] - residues[None, :], -reach, reach) + reach,
        2 * reach + 1,
    )
    present = of_crop(token_mask).astype(F32)
    pair_mask = of_rows(present)[:, None] * present[None, :]
    loss_weight = pair_mask * valid.astype(F32)
    table_rows = -(-relative_table.shape[0] // PACKED) * PACKED
    table_t = jnp.pad(relative_table, ((0, table_rows - relative_table.shape[0]), (0, 0))).T
    tokens_single = of_crop(single)
    proj = project(tokens_single, single_weight.astype(BF16))
    proj_rows = of_rows(proj[:, :width])[:, :, None]
    proj_cols = proj[:, width:].T
    bins, pair_mask = Arg(bins[:, None, :], ROWS), Arg(pair_mask[:, None, :], ROWS)

    prepared = prepare(
        triangle_input, triangle_output, expand_weight, reduce_weight, distogram_weight, norm_gains
    )
    mix, mix_t, out, out_t, up, up_t, down, down_t, logits, logits_t, gains = prepared
    hidden = up.shape[2]

    def gain(index):
        return Arg(gains, WHOLE, column=index)

    def layer_of(array, index, *block):
        shape = block or array.shape[1:]
        return Arg(array, WHOLE, (index, 0, 0), (None,) + tuple(shape))

    def triangle_weights(layer, kind, starts=False, finishes=False, back=False):
        index = 2 * layer + kind
        found = dict(gain0=gain(5 * layer + 2 * kind))
        if starts:
            found.update(mix_t=layer_of(mix_t, index, 4 * width, width))
        if starts and back:
            found.update(mix=layer_of(mix, index))
        if finishes:
            found.update(
                gain1=gain(5 * layer + 2 * kind + 1),
                gate_t=Arg(mix_t, WHOLE, (index, 4, 0), (None, width, width)),
                out_t=layer_of(out_t, index),
            )
        if finishes and back:
            found.update(out=layer_of(out, index))
        return found

    def transition_weights(layer, forth=True, back=False):
        found = dict(gain=gain(5 * layer + 4), up_t=layer_of(up_t, layer))
        if forth:
            found.update(down_t=layer_of(down_t, layer))
        if back:
            found.update(up=layer_of(up, layer), down=layer_of(down, layer))
        return found

    def state_out():
        return Out((rows, width, tokens), F32, ROWS)

    def sum_out(*shape):
        return Out(shape, F32, SUM)

    def gain_out():
        return sum_out(width, LANES)

    def back_start_outs():
        return dict(
            grad_gate=Out((rows, width, tokens), BF16, ROWS),
            out=sum_out(width, width),
            gain1=gain_out(),
        )

    def back_finish_outs():
        return dict(mix=sum_out(width, 5 * width), gain0=gain_out())

    def transition_outs():
        return dict(up=sum_out(width, hidden), down=sum_out(hidden // 2, width), gain=gain_out())

    identities = iter(range(4 * layers))

    def forward(incoming):
        return Forward(peers, half, rows, tokens, incoming, next(identities))

    def backward(incoming):
        return Backward(peers, half, rows, tokens, incoming, next(identities))

    def owned(kept):
        return dict(left=Arg(kept.left, WHOLE), right=Arg(kept.right, WHOLE))

    kept, states, middles, sums = {}, {}, {}, {}

    def first_body(i, o, left, right):
        state = dot(i.table_t[...], bins_hot(i.bins, table_rows))
        cols = i.proj_cols[...]
        state = state + jnp.concatenate(
            [cols + i.proj_rows[row] for row in range(ROW_BLOCK)], axis=1
        )
        write_rows(o.state, state)
        triangle_start(i.start, read_rows(i.mask), left, right, state)

    exchange = forward(False)
    got = run_stage(
        first_body,
        "first_state",
        rows,
        dict(
            bins=bins,
            proj_rows=Arg(proj_rows, ROWS),
            proj_cols=Arg(proj_cols, WHOLE),
            table_t=Arg(table_t.astype(BF16), WHOLE),
            mask=pair_mask,
            start=triangle_weights(0, 0, starts=True),
        ),
        dict(state=state_out(), **exchange.outs()),
        exchange,
    )
    kept[0, 0], states[0, 0] = got, got.state

    def between_body(i, o, left, right):
        state, _ = triangle_finish(i.end, i.tri, read_rows(i.state))
        write_rows(o.state, state)
        triangle_start(i.start, read_rows(i.mask), left, right, state)

    def layer_end_body(i, o, left, right):
        state, _ = triangle_finish(i.end, i.tri, read_rows(i.state))
        write_rows(o.middle, state)
        state = transition_finish(i.lift, state, transition(i.lift, state))
        write_rows(o.state, state)
        triangle_start(i.start, read_rows(i.mask), left, right, state)

    for layer in range(layers):
        exchange = forward(True)
        got = run_stage(
            between_body,
            "between_updates",
            rows,
            dict(
                state=Arg(states[layer, 0], ROWS),
                tri=Arg(kept[layer, 0].tri, WIRE),
                mask=pair_mask,
                end=triangle_weights(layer, 0, finishes=True),
                start=triangle_weights(layer, 1, starts=True),
            ),
            dict(state=state_out(), **exchange.outs()),
            exchange,
        )
        kept[layer, 1], states[layer, 1] = got, got.state
        if layer + 1 == layers:
            break
        exchange = forward(False)
        got = run_stage(
            layer_end_body,
            "layer_end",
            rows,
            dict(
                state=Arg(states[layer, 1], ROWS),
                tri=Arg(kept[layer, 1].tri, WIRE),
                mask=pair_mask,
                end=triangle_weights(layer, 1, finishes=True),
                lift=transition_weights(layer),
                start=triangle_weights(layer + 1, 0, starts=True),
            ),
            dict(middle=state_out(), state=state_out(), **exchange.outs()),
            exchange,
        )
        kept[layer + 1, 0], states[layer + 1, 0] = got, got.state
        middles[layer] = got.middle

    def loss_body(i, o, wire):
        state, kept_triangle = triangle_finish(i.end, i.tri, read_rows(i.state))
        lifted = transition(i.lift, state)
        grad = head_back(i.head, o.head, transition_finish(i.lift, state, lifted))
        grad = transition_back(i.lift, o.lift, grad, lifted)
        write_rows(o.grad, grad)
        triangle_back_start(i.end, o.end, wire, grad, kept_triangle)

    top = layers - 1
    exchange = backward(True)
    got = run_stage(
        loss_body,
        "loss",
        rows,
        dict(
            state=Arg(states[top, 1], ROWS),
            tri=Arg(kept[top, 1].tri, WIRE),
            end=triangle_weights(top, 1, finishes=True, back=True),
            lift=transition_weights(top, back=True),
            head=dict(
                gain=gain(5 * layers),
                logits=layer_of(logits, 0),
                logits_t=layer_of(logits_t, 0),
                target=Arg(target[:, None, :], ROWS),
                weight=Arg(loss_weight[:, None, :], ROWS),
            ),
            owned=owned(kept[top, 1]),
        ),
        dict(
            grad=state_out(),
            head=dict(
                loss=sum_out(1, LANES),
                count=sum_out(1, LANES),
                logits=sum_out(distogram_weight.shape[1], width),
                gain=gain_out(),
            ),
            lift=transition_outs(),
            end=back_start_outs(),
            **exchange.outs(),
        ),
        exchange,
    )
    head, lifts, ends, begins = got.head, {top: got.lift}, {(top, 1): got.end}, {}

    def between_back_body(i, o, wire):
        grad = triangle_back_finish(
            i.start, i.back, o.start, read_rows(i.mask), read_rows(i.grad), read_rows(i.state)
        )
        write_rows(o.grad, grad)
        _, kept_triangle = triangle_finish(i.end, i.tri, read_rows(i.before))
        triangle_back_start(i.end, o.end, wire, grad, kept_triangle)

    def layer_end_back_body(i, o, wire):
        grad = triangle_back_finish(
            i.start, i.back, o.start, read_rows(i.mask), read_rows(i.grad), read_rows(i.state)
        )
        grad = transition_back(i.lift, o.lift, grad, transition(i.lift, read_rows(i.middle)))
        write_rows(o.grad, grad)
        _, kept_triangle = triangle_finish(i.end, i.tri, read_rows(i.before))
        triangle_back_start(i.end, o.end, wire, grad, kept_triangle)

    def first_back_body(i, o):
        grad = triangle_back_finish(
            i.start, i.back, o.start, read_rows(i.mask), read_rows(i.grad), read_rows(i.state)
        )
        hot = bins_hot(i.bins, table_rows)
        high = grad.astype(BF16)
        low = (grad - high.astype(F32)).astype(BF16)
        o.table[...] += dot_pairs(hot, high) + dot_pairs(hot, low)
        for row in range(ROW_BLOCK):
            part = grad[:, row * tokens : (row + 1) * tokens]
            o.rows[row] = fold(part)
            o.cols[...] += part

    for layer in reversed(range(layers)):
        for kind in (1, 0):
            inputs = dict(
                grad=Arg(got.grad, ROWS),
                state=Arg(states[layer, kind], ROWS),
                mask=pair_mask,
                start=triangle_weights(layer, kind, starts=True, back=True),
                back=dict(
                    grad_left=Arg(got.grad_left, WIRE),
                    grad_right=Arg(got.grad_right, WIRE),
                    grad_gate=Arg(got.end.grad_gate, ROWS),
                ),
            )
            outputs = dict(start=back_finish_outs())
            if layer == 0 and kind == 0:
                got = run_stage(
                    first_back_body,
                    "first_state_back",
                    rows,
                    dict(bins=bins, **inputs),
                    dict(
                        table=sum_out(table_rows, width),
                        rows=Out((rows, width, LANES), F32, ROWS),
                        cols=sum_out(width, tokens),
                        **outputs,
                    ),
                )
                begins[layer, kind] = got.start
                break
            before = (layer, 0) if kind == 1 else (layer - 1, 1)
            inputs.update(
                before=Arg(states[before], ROWS),
                tri=Arg(kept[before].tri, WIRE),
                end=triangle_weights(*before, finishes=True, back=True),
                owned=owned(kept[before]),
            )
            outputs.update(grad=state_out(), end=back_start_outs())
            if kind == 1:
                exchange = backward(False)
                body, name = between_back_body, "between_updates_back"
            else:
                exchange = backward(True)
                body, name = layer_end_back_body, "layer_end_back"
                inputs.update(
                    middle=Arg(middles[layer - 1], ROWS),
                    lift=transition_weights(layer - 1, forth=False, back=True),
                )
                outputs.update(lift=transition_outs())
            got = run_stage(body, name, rows, inputs, dict(**outputs, **exchange.outs()), exchange)
            begins[layer, kind], ends[before] = got.start, got.end
            if kind == 0:
                lifts[layer - 1] = got.lift

    early = (
        [begins[layer, kind].mix for layer in range(1, layers) for kind in range(2)],
        [lifts[layer].up for layer in range(layers)],
        jnp.concatenate(
            [
                ends[layer, kind].out
                for layer in range(layers)
                for kind in range(2)
                if (layer, kind) != (0, 0)
            ]
            + [lifts[layer].down for layer in range(layers)],
            axis=0,
        ),
    )
    early = lax.psum(early, ("row", "head"))

    wide_single = tokens_single.astype(F32)
    row_part = jnp.einsum(
        "is,ic->sc",
        of_rows(wide_single),
        jnp.sum(got.rows, axis=2),
        precision=lax.Precision.HIGHEST,
    )
    col_part = jnp.einsum("js,cj->sc", wide_single, got.cols, precision=lax.Precision.HIGHEST)
    partial_gains = []
    for layer in range(layers):
        for kind in range(2):
            partial_gains += [begins[layer, kind].gain0, ends[layer, kind].gain1]
        partial_gains.append(lifts[layer].gain)
    partial_gains.append(head.gain)
    grids = [
        begins[0, 0].mix,
        begins[0, 1].mix,
        ends[0, 0].out,
        head.logits,
        got.table,
        row_part,
        col_part,
    ]
    rest, *starts = reduce_rest(
        half, peers, 4 * layers, grids, partial_gains, [head.loss, head.count]
    )
    return update(rest, *starts, early, weights, firsts, seconds)


def per_device(
    row_count,
    head_count,
    single,
    residue_index,
    chain_index,
    token_mask,
    pair_valid,
    target_bins,
    relative_table,
    single_weight,
    triangle_input,
    triangle_output,
    expand_weight,
    reduce_weight,
    distogram_weight,
    norm_gains,
    first_table,
    second_table,
    first_single,
    second_single,
    first_input,
    second_input,
    first_output,
    second_output,
    first_expand,
    second_expand,
    first_reduce,
    second_reduce,
    first_logits,
    second_logits,
    first_gains,
    second_gains,
):
    crops, tokens = token_mask.shape
    width = relative_table.shape[1]
    peers = row_count * head_count // crops
    given = (
        single,
        residue_index,
        chain_index,
        token_mask,
        pair_valid,
        target_bins,
        relative_table,
        single_weight,
        triangle_input,
        triangle_output,
        expand_weight,
        reduce_weight,
        distogram_weight,
        norm_gains,
    )
    weights = (
        relative_table,
        single_weight,
        triangle_input,
        triangle_output,
        expand_weight,
        reduce_weight,
        distogram_weight,
        norm_gains,
    )
    firsts = (
        first_table,
        first_single,
        first_input,
        first_output,
        first_expand,
        first_reduce,
        first_logits,
        first_gains,
    )
    seconds = (
        second_table,
        second_single,
        second_input,
        second_output,
        second_expand,
        second_reduce,
        second_logits,
        second_gains,
    )
    if (
        crops == 2
        and head_count == 2
        and width == LANES
        and width == SUBLANES * peers
        and tokens % (peers * SUBLANES) == 0
        and tokens % (3 * LANES) == 0
    ):
        return step_by_crop(row_count, head_count, given[:6], weights, firsts, seconds)
    local = gradients_by_block(*given)
    summed = lax.psum(local, ("row", "head"))
    loss_sum, valid_count = summed[0], summed[1]
    grads = [grad / valid_count for grad in summed[2:]]
    squares = jnp.zeros((), jnp.float32)
    for g in grads:
        squares = squares + jnp.sum(g * g)
    gradient_norm = jnp.sqrt(squares)
    factor = jnp.minimum(1.0, CLIP_NORM / (gradient_norm + 1e-06))
    result = []
    for index in range(8):
        rate = GAIN_RATE if index == 7 else WEIGHT_RATE
        decay = 0.0 if index == 7 else WEIGHT_DECAY
        result.extend(
            adamw(weights[index], grads[index] * factor, firsts[index], seconds[index], rate, decay)
        )
    return (
        loss_sum,
        valid_count,
        gradient_norm,
        result[0],
        result[1],
        result[2],
        result[3],
        result[4],
        result[5],
        result[6],
        result[7],
        result[8],
        result[9],
        result[10],
        result[11],
        result[12],
        result[13],
        result[14],
        result[15],
        result[16],
        result[17],
        result[18],
        result[19],
        result[20],
        result[21],
        result[22],
        result[23],
    )


def solution(mesh):
    placed = (
        P(),
        P(),
        P(),
        P(),
        P(None, "row", "head"),
        P(None, "row", "head"),
        P(),
        P(),
        P(),
        P(),
        P(),
        P(),
        P(),
        P(),
        P(),
        P(),
        P(),
        P(),
        P(),
        P(),
        P(),
        P(),
        P(),
        P(),
        P(),
        P(),
        P(),
        P(),
        P(),
        P(),
    )
    return jax.shard_map(
        functools.partial(per_device, mesh.shape["row"], mesh.shape["head"]),
        mesh=mesh,
        in_specs=placed,
        out_specs=(
            P(),
            P(),
            P(),
            P(),
            P(),
            P(),
            P(),
            P(),
            P(),
            P(),
            P(),
            P(),
            P(),
            P(),
            P(),
            P(),
            P(),
            P(),
            P(),
            P(),
            P(),
            P(),
            P(),
            P(),
            P(),
            P(),
            P(),
        ),
        check_vma=False,
    )
```

```python
import functools

import jax
import jax.numpy as jnp
from jax import lax
from jax.experimental import pallas as pl
from jax.experimental.pallas import tpu as pltpu
from jax.sharding import PartitionSpec as P

STEP = 10


EPS = 1e-05
BETA_ONE = 0.9
BETA_TWO = 0.999
ADAM_EPS = 1e-08
WEIGHT_RATE = 0.1
GAIN_RATE = 0.5
WEIGHT_DECAY = 0.01
CLIP_NORM = 0.002


def normalize(value):
    mean = jnp.mean(value, axis=-1, keepdims=True)
    centred = value - mean
    scale = lax.rsqrt(jnp.mean(centred * centred, axis=-1, keepdims=True) + EPS)
    return (centred * scale, scale)


def norm_back(grad_out, unit, scale, gain):
    scaled = grad_out * gain
    first_mean = jnp.mean(scaled, axis=-1, keepdims=True)
    second_mean = jnp.mean(scaled * unit, axis=-1, keepdims=True)
    grad_in = scale * (scaled - first_mean - unit * second_mean)
    grad_gain = jnp.sum(grad_out * unit, axis=tuple(range(grad_out.ndim - 1)))
    return (grad_in, grad_gain)


def project(value, weight):
    return jnp.einsum("...c,cd->...d", value, weight, preferred_element_type=jnp.float32)


def project_back(grad, weight):
    return jnp.einsum("...d,cd->...c", grad, weight, preferred_element_type=jnp.float32)


def weight_grad(value, grad):
    return jnp.einsum("bijc,bijd->cd", value, grad, preferred_element_type=jnp.float32)


def triangle_forward(state, weight_in, weight_out, gains, pair_mask, incoming):
    hidden = weight_out.shape[0]
    pair_unit, pair_scale = normalize(state)
    normed = (pair_unit * gains[0]).astype(jnp.bfloat16)
    mixed = project(normed, weight_in)
    mask = pair_mask[..., None]
    left = (mask * jax.nn.sigmoid(mixed[..., :hidden]) * mixed[..., hidden : 2 * hidden]).astype(
        jnp.bfloat16
    )
    right = (
        mask
        * jax.nn.sigmoid(mixed[..., 2 * hidden : 3 * hidden])
        * mixed[..., 3 * hidden : 4 * hidden]
    ).astype(jnp.bfloat16)
    left_cols, right_cols = (
        lax.all_to_all(left, "head", split_axis=3, concat_axis=2, tiled=True),
        lax.all_to_all(right, "head", split_axis=3, concat_axis=2, tiled=True),
    )
    if incoming:
        left_cols, right_cols = (
            lax.all_to_all(left_cols, "row", split_axis=2, concat_axis=1, tiled=True),
            lax.all_to_all(right_cols, "row", split_axis=2, concat_axis=1, tiled=True),
        )
        left_cols = jnp.swapaxes(left_cols, 1, 2)
        right_cols = jnp.swapaxes(right_cols, 1, 2)
    right_all = lax.all_gather(right_cols, "row", axis=1, tiled=True)
    triangle = jnp.einsum(
        "bikc,bjkc->bijc", left_cols, right_all, preferred_element_type=jnp.float32
    )
    triangle = lax.all_to_all(
        triangle.astype(jnp.bfloat16), "head", split_axis=2, concat_axis=3, tiled=True
    )
    tri_unit, tri_scale = normalize(triangle.astype(jnp.float32))
    shaped = (tri_unit * gains[1]).astype(jnp.bfloat16)
    branch = project(shaped, weight_out)
    gate = jax.nn.sigmoid(mixed[..., 4 * hidden :])
    kept = (
        pair_unit,
        pair_scale,
        normed,
        mixed,
        left_cols,
        right_all,
        tri_unit,
        tri_scale,
        shaped,
        branch,
        gate,
    )
    return (state + gate * branch, kept)


def triangle_backward(grad_state, kept, weight_in, weight_out, gains, pair_mask, incoming):
    hidden = weight_out.shape[0]
    (
        pair_unit,
        pair_scale,
        normed,
        mixed,
        left_cols,
        right_all,
        tri_unit,
        tri_scale,
        shaped,
        branch,
        gate,
    ) = kept
    grad_branch = (grad_state * gate).astype(jnp.bfloat16)
    grad_gate = grad_state * branch * gate * (1.0 - gate)
    grad_out = weight_grad(shaped, grad_branch)
    grad_shaped = project_back(grad_branch, weight_out)
    grad_tri, gain_two = norm_back(grad_shaped, tri_unit, tri_scale, gains[1])
    tri_cols = lax.all_to_all(
        grad_tri.astype(jnp.bfloat16), "head", split_axis=3, concat_axis=2, tiled=True
    )
    grad_left = jnp.einsum(
        "bijc,bjkc->bikc", tri_cols, right_all, preferred_element_type=jnp.float32
    )
    grad_left = grad_left.astype(jnp.bfloat16)
    summed = lax.psum_scatter(
        jnp.einsum(
            "bijc,bikc->jbkc", tri_cols, left_cols, preferred_element_type=jnp.float32
        ).astype(jnp.bfloat16),
        "row",
        scatter_dimension=0,
        tiled=True,
    ).astype(jnp.float32)
    grad_right = jnp.transpose(summed, (1, 0, 2, 3)).astype(jnp.bfloat16)
    if incoming:
        grad_left, grad_right = (
            lax.all_to_all(
                jnp.swapaxes(grad_left, 1, 2), "row", split_axis=1, concat_axis=2, tiled=True
            ),
            lax.all_to_all(
                jnp.swapaxes(grad_right, 1, 2), "row", split_axis=1, concat_axis=2, tiled=True
            ),
        )
    back_left, back_right = (
        lax.all_to_all(grad_left, "head", split_axis=2, concat_axis=3, tiled=True),
        lax.all_to_all(grad_right, "head", split_axis=2, concat_axis=3, tiled=True),
    )
    mask = pair_mask[..., None]
    back_left = back_left.astype(jnp.float32) * mask
    back_right = back_right.astype(jnp.float32) * mask
    left_sig = jax.nn.sigmoid(mixed[..., :hidden])
    left_value = mixed[..., hidden : 2 * hidden]
    right_sig = jax.nn.sigmoid(mixed[..., 2 * hidden : 3 * hidden])
    right_value = mixed[..., 3 * hidden : 4 * hidden]
    grad_mixed = jnp.concatenate(
        [
            back_left * left_value * left_sig * (1.0 - left_sig),
            back_left * left_sig,
            back_right * right_value * right_sig * (1.0 - right_sig),
            back_right * right_sig,
            grad_gate,
        ],
        axis=-1,
    ).astype(jnp.bfloat16)
    grad_in = weight_grad(normed, grad_mixed)
    grad_normed = project_back(grad_mixed, weight_in)
    grad_first, gain_one = norm_back(grad_normed, pair_unit, pair_scale, gains[0])
    return (grad_state + grad_first, (grad_in, grad_out, gain_one, gain_two))


def transition_forward(state, weight_up, weight_down, gain):
    expand = weight_down.shape[0]
    unit, scale = normalize(state)
    lifted = (unit * gain).astype(jnp.bfloat16)
    inner = project(lifted, weight_up)
    product = (jax.nn.silu(inner[..., :expand]) * inner[..., expand:]).astype(jnp.bfloat16)
    return (state + project(product, weight_down), (unit, scale, lifted, inner, product))


def transition_backward(grad_state, kept, weight_up, weight_down, gain):
    expand = weight_down.shape[0]
    unit, scale, lifted, inner, product = kept
    grad_low = grad_state.astype(jnp.bfloat16)
    grad_down = weight_grad(product, grad_low)
    grad_product = project_back(grad_low, weight_down)
    gate_part = inner[..., :expand]
    up_part = inner[..., expand:]
    gate_sig = jax.nn.sigmoid(gate_part)
    silu_value = gate_part * gate_sig
    silu_slope = gate_sig * (1.0 + gate_part * (1.0 - gate_sig))
    grad_inner = jnp.concatenate(
        [grad_product * up_part * silu_slope, grad_product * silu_value], axis=-1
    )
    grad_inner = grad_inner.astype(jnp.bfloat16)
    grad_up = weight_grad(lifted, grad_inner)
    grad_lifted = project_back(grad_inner, weight_up)
    grad_middle, gain_grad = norm_back(grad_lifted, unit, scale, gain)
    return (grad_middle + grad_state, (grad_up, grad_down, gain_grad))


def block_forward(state, weight_in, weight_out, weight_up, weight_down, gains, pair_mask):
    first, kept_one = triangle_forward(
        state, weight_in[0], weight_out[0], gains[0:2], pair_mask, False
    )
    second, kept_two = triangle_forward(
        first, weight_in[1], weight_out[1], gains[2:4], pair_mask, True
    )
    output, kept_three = transition_forward(second, weight_up, weight_down, gains[4])
    return (output, (kept_one, kept_two, kept_three))


def block_backward(
    grad_state, state, weight_in, weight_out, weight_up, weight_down, gains, pair_mask
):
    skipped, kept = block_forward(
        state, weight_in, weight_out, weight_up, weight_down, gains, pair_mask
    )
    kept_one, kept_two, kept_three = kept
    grad_state, (grad_up, grad_down, gain_five) = transition_backward(
        grad_state, kept_three, weight_up, weight_down, gains[4]
    )
    grad_state, (in_two, out_two, gain_three, gain_four) = triangle_backward(
        grad_state, kept_two, weight_in[1], weight_out[1], gains[2:4], pair_mask, True
    )
    grad_state, (in_one, out_one, gain_one, gain_two) = triangle_backward(
        grad_state, kept_one, weight_in[0], weight_out[0], gains[0:2], pair_mask, False
    )
    return (
        grad_state,
        (
            jnp.stack([in_one, in_two]),
            jnp.stack([out_one, out_two]),
            grad_up,
            grad_down,
            jnp.stack([gain_one, gain_two, gain_three, gain_four, gain_five]),
        ),
    )


def adamw(weight, grad, first, second, rate, decay):
    first_new = BETA_ONE * first + (1.0 - BETA_ONE) * grad
    second_new = BETA_TWO * second + (1.0 - BETA_TWO) * grad * grad
    moved = (
        first_new
        / (1.0 - BETA_ONE**STEP)
        / (jnp.sqrt(second_new / (1.0 - BETA_TWO**STEP)) + ADAM_EPS)
    )
    return (first_new, second_new, weight - rate * (moved + decay * weight))


def gradients_by_block(
    single,
    residue_index,
    chain_index,
    token_mask,
    pair_valid,
    target_bins,
    relative_table,
    single_weight,
    triangle_input,
    triangle_output,
    expand_weight,
    reduce_weight,
    distogram_weight,
    norm_gains,
):
    crops, rows, cols = pair_valid.shape
    width = relative_table.shape[1]
    layers = triangle_input.shape[0]
    row_start = lax.axis_index("row") * rows
    col_start = lax.axis_index("head") * cols

    def take(array, start, count):
        return lax.dynamic_slice_in_dim(array, start, count, 1)

    offset = (
        take(residue_index, row_start, rows)[:, :, None]
        - take(residue_index, col_start, cols)[:, None, :]
    )
    same = (
        take(chain_index, row_start, rows)[:, :, None]
        == take(chain_index, col_start, cols)[:, None, :]
    )
    reach = (relative_table.shape[0] - 2) // 2
    bins = jnp.where(same, jnp.clip(offset, -reach, reach) + reach, 2 * reach + 1)
    relative_hot = (
        bins[..., None] == jnp.arange(relative_table.shape[0])[None, None, None, :]
    ).astype(jnp.float32)
    token_rows = take(token_mask, row_start, rows).astype(jnp.float32)
    token_cols = take(token_mask, col_start, cols).astype(jnp.float32)
    pair_mask = token_rows[:, :, None] * token_cols[:, None, :]
    loss_weight = pair_mask * pair_valid.astype(jnp.float32)
    low_input = triangle_input.astype(jnp.bfloat16)
    low_output = triangle_output.astype(jnp.bfloat16)
    low_expand = expand_weight.astype(jnp.bfloat16)
    low_reduce = reduce_weight.astype(jnp.bfloat16)
    low_logits = distogram_weight.astype(jnp.bfloat16)
    proj = project(single, single_weight.astype(jnp.bfloat16))
    state = project(relative_hot.astype(jnp.bfloat16), relative_table.astype(jnp.bfloat16))
    state = (
        state
        + take(proj, row_start, rows)[:, :, None, :width]
        + take(proj, col_start, cols)[:, None, :, width:]
    )
    inputs = []
    for layer in range(layers):
        inputs.append(state)
        state, unused = block_forward(
            state,
            low_input[layer],
            low_output[layer],
            low_expand[layer],
            low_reduce[layer],
            norm_gains[5 * layer : 5 * layer + 5],
            pair_mask,
        )
    head_unit, head_scale = normalize(state)
    shown = (head_unit * norm_gains[5 * layers]).astype(jnp.bfloat16)
    logits = project(shown, low_logits)
    largest = jnp.max(logits, axis=-1, keepdims=True)
    log_total = largest + jnp.log(jnp.sum(jnp.exp(logits - largest), axis=-1, keepdims=True))
    target_hot = (
        target_bins[..., None] == jnp.arange(logits.shape[-1])[None, None, None, :]
    ).astype(jnp.float32)
    picked = jnp.sum(logits * target_hot, axis=-1)
    loss_local = jnp.sum(loss_weight * (log_total[..., 0] - picked))
    grad_scores = (loss_weight[..., None] * (jnp.exp(logits - log_total) - target_hot)).astype(
        jnp.bfloat16
    )
    grad_logits = weight_grad(shown, grad_scores)
    grad_shown = project_back(grad_scores, low_logits)
    grad_state, gain_last = norm_back(grad_shown, head_unit, head_scale, norm_gains[5 * layers])
    collected = []
    for layer in reversed(range(layers)):
        grad_state, layer_grads = block_backward(
            grad_state,
            inputs[layer],
            low_input[layer],
            low_output[layer],
            low_expand[layer],
            low_reduce[layer],
            norm_gains[5 * layer : 5 * layer + 5],
            pair_mask,
        )
        collected.insert(0, layer_grads)
    grad_input = jnp.stack([entry[0] for entry in collected])
    grad_output = jnp.stack([entry[1] for entry in collected])
    grad_expand = jnp.stack([entry[2] for entry in collected])
    grad_reduce = jnp.stack([entry[3] for entry in collected])
    grad_gains = jnp.concatenate(
        [jnp.concatenate([entry[4] for entry in collected], axis=0), gain_last[None]], axis=0
    )
    grad_table = jnp.einsum(
        "bijr,bijc->rc", relative_hot, grad_state, precision=lax.Precision.HIGHEST
    )
    single_wide = single.astype(jnp.float32)
    row_part = jnp.einsum(
        "bis,bic->sc",
        take(single_wide, row_start, rows),
        jnp.sum(grad_state, axis=2),
        precision=lax.Precision.HIGHEST,
    )
    col_part = jnp.einsum(
        "bjs,bjc->sc",
        take(single_wide, col_start, cols),
        jnp.sum(grad_state, axis=1),
        precision=lax.Precision.HIGHEST,
    )
    grad_single = jnp.concatenate([row_part, col_part], axis=1)
    return (
        loss_local,
        jnp.sum(loss_weight),
        grad_table,
        grad_single,
        grad_input,
        grad_output,
        grad_expand,
        grad_reduce,
        grad_logits,
        grad_gains,
    )


F32 = jnp.float32
BF16 = jnp.bfloat16
LANES = 128
SUBLANES = 8
PACKED = 16
ROW_BLOCK = 2
PHASES = SUBLANES // ROW_BLOCK
CHUNK_ROWS = SUBLANES * SUBLANES
VMEM_BYTES = 58 * 2**20
MESH = pl.DeviceIdType.MESH
ROWS, WIRE, LANDED, WHOLE, SUM, ANYWHERE = range(6)


class Bag:
    def __init__(self, **entries):
        self.__dict__.update(entries)


class Arg:
    def __init__(self, array, kind, index=None, block=None, column=None, half=None):
        self.array, self.kind, self.index, self.block = array, kind, index, block
        self.column, self.half = column, half

    def spec(self):
        if self.index is None:
            return block_spec(self.array.shape, self.kind)
        index = self.index
        return pl.BlockSpec(self.block, lambda step: index)


class Column:
    def __init__(self, ref, column):
        self.ref, self.column = ref, column

    def __getitem__(self, _):
        return self.ref[:, self.column : self.column + 1]


class Out:
    def __init__(self, shape, dtype, kind):
        self.shape, self.dtype, self.kind = shape, dtype, kind

    def spec(self):
        return block_spec(self.shape, ANYWHERE if self.kind == LANDED else self.kind)


def block_spec(shape, kind):
    if kind in (WIRE, ANYWHERE):
        return pl.BlockSpec(memory_space=pl.ANY)
    if kind == LANDED:
        return pl.BlockSpec((shape[0], CHUNK_ROWS, shape[2]), lambda step: (0, step // PHASES, 0))
    if kind == ROWS:
        return pl.BlockSpec((ROW_BLOCK,) + shape[1:], lambda step: (step,) + (0,) * (len(shape) - 1))
    return pl.BlockSpec(shape, lambda step: (0,) * len(shape))


def is_leaf(value):
    return isinstance(value, (Arg, Out))


def bag_of(tree, leaves):
    return Bag(
        **{
            key: next(leaves) if is_leaf(value) else bag_of(value, leaves)
            for key, value in tree.items()
        }
    )


def leaves_of(tree):
    found = []
    for value in tree.values():
        found.extend([value] if is_leaf(value) else leaves_of(value))
    return found


def dot(left, right):
    return lax.dot_general(left, right, (((1,), (0,)), ((), ())), preferred_element_type=F32)


def dot_pairs(left, right):
    return lax.dot_general(left, right, (((1,), (1,)), ((), ())), preferred_element_type=F32)


def product_of(left, right, left_axis, right_axis):
    return lax.dot_general(
        left, right, (((left_axis,), (right_axis,)), ((), ())), preferred_element_type=F32
    )


def sigmoid(value):
    return 0.5 * jnp.tanh(0.5 * value) + 0.5


def unit_of(value):
    centred = value - jnp.mean(value, axis=0, keepdims=True)
    scale = lax.rsqrt(jnp.mean(centred * centred, axis=0, keepdims=True) + EPS)
    return (centred * scale, scale)


def unit_back(grad, unit, scale, gain):
    scaled = grad * gain
    first = jnp.mean(scaled, axis=0, keepdims=True)
    second = jnp.mean(scaled * unit, axis=0, keepdims=True)
    return scale * (scaled - first - unit * second)


def fold(value):
    total = value[:, :LANES]
    for start in range(LANES, value.shape[1], LANES):
        total = total + value[:, start : start + LANES]
    return total


def read_rows(ref):
    return jnp.concatenate([ref[row] for row in range(ref.shape[0])], axis=1)


def write_rows(ref, value):
    cols = ref.shape[2]
    for row in range(ref.shape[0]):
        ref[row] = value[:, row * cols : (row + 1) * cols].astype(ref.dtype)


class Wire:
    def __init__(self, wide, phase):
        self.wide, self.phase = wide, phase

    def tokens(self, row):
        width = self.wide.shape[1] // SUBLANES
        return pl.ds(self.phase * ROW_BLOCK + row, width, stride=SUBLANES)

    def read(self):
        lanes = self.wide.shape[0]
        return jnp.concatenate(
            [
                self.wide[lane, self.tokens(row), :]
                for row in range(ROW_BLOCK)
                for lane in range(lanes)
            ],
            axis=1,
        )

    def write(self, value):
        lanes = self.wide.shape[0]
        for row in range(ROW_BLOCK):
            for lane in range(lanes):
                start = (row * lanes + lane) * LANES
                self.wide[lane, self.tokens(row), :] = value[:, start : start + LANES]


def widen(wide, low, chunk):
    rows = pl.ds(pl.multiple_of(chunk * CHUNK_ROWS, CHUNK_ROWS), CHUNK_ROWS)

    def step(peer, carry):
        value = low[peer, rows, :].astype(F32)
        start = pl.multiple_of(peer * CHUNK_ROWS, CHUNK_ROWS)
        for lane in range(wide.shape[0]):
            wide[lane, pl.ds(start, CHUNK_ROWS), :] = value[:, lane * LANES : (lane + 1) * LANES]
        return carry

    lax.fori_loop(0, low.shape[0], step, 0)


def narrow(low, wide, chunk):
    rows = pl.ds(pl.multiple_of(chunk * CHUNK_ROWS, CHUNK_ROWS), CHUNK_ROWS)

    def step(peer, carry):
        start = pl.multiple_of(peer * CHUNK_ROWS, CHUNK_ROWS)
        low[peer, rows, :] = jnp.concatenate(
            [wide[lane, pl.ds(start, CHUNK_ROWS), :] for lane in range(wide.shape[0])], axis=1
        ).astype(low.dtype)
        return carry

    lax.fori_loop(0, low.shape[0], step, 0)


def triangle_start(weights, mask, left_wire, right_wire, state):
    width = state.shape[0]
    unit, _ = unit_of(state)
    normed = (unit * weights.gain0[...]).astype(BF16)
    mixed = dot(weights.mix_t[...], normed)
    for wire, base in ((left_wire, 0), (right_wire, 2 * width)):
        gate = sigmoid(mixed[base : base + width])
        wire.write(mask * gate * mixed[base + width : base + 2 * width])


def triangle_finish(weights, wire, state):
    unit, _ = unit_of(state)
    normed = (unit * weights.gain0[...]).astype(BF16)
    gate = sigmoid(dot(weights.gate_t[...], normed))
    tri_unit, tri_scale = unit_of(wire.read())
    shaped = (tri_unit * weights.gain1[...]).astype(BF16)
    branch = dot(weights.out_t[...], shaped)
    return (state + gate * branch, (gate, tri_unit, tri_scale, shaped, branch))


def triangle_back_start(weights, o, wire, grad, kept):
    gate, tri_unit, tri_scale, shaped, branch = kept
    grad_branch = (grad * gate).astype(BF16)
    write_rows(o.grad_gate, grad * branch * gate * (1.0 - gate))
    o.out[...] += dot_pairs(shaped, grad_branch)
    grad_shaped = dot(weights.out[...], grad_branch)
    o.gain1[...] += fold(grad_shaped * tri_unit)
    wire.write(unit_back(grad_shaped, tri_unit, tri_scale, weights.gain1[...]))


def triangle_back_finish(weights, i, o, mask, grad, state):
    width = state.shape[0]
    unit, scale = unit_of(state)
    gain = weights.gain0[...]
    normed = (unit * gain).astype(BF16)
    mixed = dot(weights.mix_t[...], normed)
    parts = []
    for wire, base in ((i.grad_left, 0), (i.grad_right, 2 * width)):
        back = wire.read() * mask
        gate = sigmoid(mixed[base : base + width])
        back_gate = back * gate
        parts.append((back_gate * mixed[base + width : base + 2 * width] * (1.0 - gate)).astype(BF16))
        parts.append(back_gate.astype(BF16))
    parts.append(read_rows(i.grad_gate))
    grad_mixed = jnp.concatenate(parts, axis=0)
    o.mix[...] += dot_pairs(normed, grad_mixed)
    grad_normed = dot(weights.mix[...], grad_mixed)
    o.gain0[...] += fold(grad_normed * unit)
    return grad + unit_back(grad_normed, unit, scale, gain)


def transition(weights, state):
    unit, scale = unit_of(state)
    lifted = (unit * weights.gain[...]).astype(BF16)
    inner = dot(weights.up_t[...], lifted)
    half = inner.shape[0] // 2
    gate = inner[:half]
    slope = sigmoid(gate)
    product = (gate * slope * inner[half:]).astype(BF16)
    return (unit, scale, lifted, inner, slope, product)


def transition_finish(weights, state, kept):
    return state + dot(weights.down_t[...], kept[5])


def transition_back(weights, o, grad, kept):
    unit, scale, lifted, inner, slope, product = kept
    half = inner.shape[0] // 2
    gate, up = inner[:half], inner[half:]
    grad_low = grad.astype(BF16)
    o.down[...] += dot_pairs(product, grad_low)
    grad_product = dot(weights.down[...], grad_low)
    scaled = grad_product * slope
    grad_inner = jnp.concatenate(
        [
            (scaled * up * (1.0 + gate * (1.0 - slope))).astype(BF16),
            (scaled * gate).astype(BF16),
        ],
        axis=0,
    )
    o.up[...] += dot_pairs(lifted, grad_inner)
    grad_lifted = dot(weights.up[...], grad_inner)
    o.gain[...] += fold(grad_lifted * unit)
    return grad + unit_back(grad_lifted, unit, scale, weights.gain[...])


def head_back(i, o, state):
    unit, scale = unit_of(state)
    gain = i.gain[...]
    shown = (unit * gain).astype(BF16)
    logits = dot(i.logits_t[...], shown)
    largest = jnp.max(logits, axis=0, keepdims=True)
    raised = jnp.exp(logits - largest)
    total = jnp.sum(raised, axis=0, keepdims=True)
    log_total = largest + jnp.log(total)
    target = read_rows(i.target)
    weight = read_rows(i.weight)
    hot = lax.broadcasted_iota(jnp.int32, logits.shape, 0) == target
    picked = jnp.sum(jnp.where(hot, logits, 0.0), axis=0, keepdims=True)
    o.loss[...] += fold(weight * (log_total - picked))
    o.count[...] += fold(weight)
    share = raised * (1.0 / total)
    grad_scores = (weight * (share - jnp.where(hot, 1.0, 0.0))).astype(BF16)
    o.logits[...] += dot_pairs(grad_scores, shown)
    grad_shown = dot(i.logits[...], grad_scores)
    o.gain[...] += fold(grad_shown * unit)
    return unit_back(grad_shown, unit, scale, gain)


def bins_hot(bins, table_rows):
    bins = read_rows(bins)
    shape = (table_rows, bins.shape[1])
    return jnp.where(lax.broadcasted_iota(jnp.int32, shape, 0) == bins, 1.0, 0.0).astype(BF16)


def run_stage(body, name, collective_id, rows, inputs, outputs, exchange=None):
    args, outs = leaves_of(inputs), leaves_of(outputs)
    steps = rows // ROW_BLOCK
    chunks = rows // SUBLANES
    wire_args = [index for index, arg in enumerate(args) if arg.kind == WIRE]
    landed_args = [index for index, arg in enumerate(args) if arg.kind == LANDED]
    keeps = [place for place, out in enumerate(outs) if out.kind == LANDED]
    wires = exchange.wires if exchange else 0
    if wire_args:
        peers, half, tokens = args[wire_args[0]].array.shape[0], args[wire_args[0]].half, 0
        tokens = args[wire_args[0]].array.shape[2]
    if exchange:
        peers, half, tokens = exchange.peers, exchange.half, exchange.tokens
    low = pltpu.VMEM((peers, rows * SUBLANES, tokens), BF16)
    many = pltpu.SemaphoreType.DMA((chunks, peers))
    wide = pltpu.VMEM((tokens // LANES, peers * CHUNK_ROWS, LANES), F32)
    groups = [
        [wide] * (len(wire_args) + len(landed_args) + wires),
        [low] * len(wire_args),
        [many] * (2 * len(wire_args)),
        [pltpu.SemaphoreType.DMA((1,))] * len(keeps),
        exchange.scratch() if exchange else [],
    ]

    def kernel(*refs):
        step = pl.program_id(0)
        phase, chunk = lax.rem(step, PHASES), lax.div(step, PHASES)
        in_refs = [
            ref if arg.column is None else Column(ref, arg.column) for arg, ref in zip(args, refs)
        ]
        out_refs = list(refs[len(args) : len(args) + len(outs)])
        rest, parts = list(refs[len(args) + len(outs) :]), []
        for group in groups:
            parts.append(rest[: len(group)])
            rest = rest[len(group) :]
        wides, lands, sems, keep_sems, held = parts
        saves = [
            pltpu.make_async_copy(land, out_refs[place], sem.at[0])
            for land, place, sem in zip(lands, keeps, keep_sems)
        ]
        ring = Exchange(peers, half)
        arrivals = [
            (in_refs[index], land, sems[2 * place], sems[2 * place + 1])
            for place, (index, land) in enumerate(zip(wire_args, lands))
        ]
        i, o = bag_of(inputs, iter(in_refs)), bag_of(outputs, iter(out_refs))

        @pl.when(step == 0)
        def _():
            ring.greet()
            for out, ref in zip(outs, out_refs):
                if out.kind == SUM:
                    ref[...] = jnp.zeros(out.shape, out.dtype)
            if exchange:
                exchange.begin(i, held)
            if arrivals:
                ring.meet()

                def start(index, carry):
                    ring.start(arrivals, index)
                    return carry

                lax.fori_loop(0, chunks, start, 0)

        if arrivals:

            @pl.when(phase == 0)
            def _():
                ring.wait(arrivals, chunk)
                for target, land in zip(wides, lands):
                    widen(target, land, chunk)

        if landed_args:

            @pl.when(phase == 0)
            def _():
                for target, index in zip(wides[len(wire_args) :], landed_args):
                    widen(target, in_refs[index], 0)

        if saves:

            @pl.when(step == steps - PHASES)
            def _():
                for save in saves:
                    save.start()

        body_in = list(in_refs)
        for index, source in zip(wire_args + landed_args, wides):
            body_in[index] = Wire(source, phase)
        sent = wides[len(wire_args) + len(landed_args) :]
        body(bag_of(inputs, iter(body_in)), o, *[Wire(target, phase) for target in sent])
        if exchange:
            moves = exchange.moves(held)

            @pl.when(phase == PHASES - 1)
            def _():
                for source, move in zip(sent, moves):
                    narrow(move[0], source, chunk)
                if not arrivals:

                    @pl.when(chunk == 0)
                    def _():
                        ring.meet()

                ring.start(moves, chunk)

            @pl.when(step == steps - 1)
            def _():
                def wait(index, carry):
                    ring.wait(moves, index)
                    return carry

                lax.fori_loop(0, chunks, wait, 0)
                exchange.finish(i, o, held)
                for save in saves:
                    save.wait()

    results = pl.pallas_call(
        kernel,
        grid=(steps,),
        in_specs=[arg.spec() for arg in args],
        out_specs=[out.spec() for out in outs],
        out_shape=[jax.ShapeDtypeStruct(out.shape, out.dtype) for out in outs],
        scratch_shapes=sum(groups, []),
        compiler_params=pltpu.CompilerParams(
            dimension_semantics=(pltpu.ARBITRARY,),
            vmem_limit_bytes=VMEM_BYTES,
            has_side_effects=True,
            collective_id=collective_id,
        ),
        cost_estimate=pl.CostEstimate(flops=0, bytes_accessed=0, transcendentals=0),
        name=name,
    )(*[arg.array for arg in args])
    return bag_of(outputs, iter(results))


def flip(value, step, count):
    result, bit = 0, 1
    while bit < count:
        result = result + lax.rem(lax.div(value, bit) + (step // bit) % 2, 2) * bit
        bit *= 2
    return result


def position(row, head, half, heads):
    inner = half // 2 * heads
    return (row % 2) * inner + (row // 2) * heads + head


def place_of(position, half, heads):
    inner = half // 2 * heads
    rest = lax.rem(position, inner)
    return (lax.div(rest, heads) * 2 + lax.div(position, inner), lax.rem(rest, heads))


class Exchange:
    def __init__(self, count, half):
        row, head = lax.axis_index("row"), lax.axis_index("head")
        place = lax.rem(row, half)
        inner = count // 2
        self.count = count
        self.half = half
        self.base = row - place
        self.me = lax.rem(place, 2) * inner + lax.div(place, 2) * (count // half) + head
        self.twin = (lax.rem(row + half, 2 * half), head)
        self.order = []
        for step in range(1, count):
            for other in (step, step ^ (inner - 1)):
                if other and other not in self.order:
                    self.order.append(other)

    def peer(self, step):
        return flip(self.me, step, self.count)

    def device(self, peer):
        place, head = place_of(peer, self.half, self.count // self.half)
        return (self.base + place, head)

    def greet(self):
        barrier = pltpu.get_barrier_semaphore()
        for step in self.order:
            pl.semaphore_signal(
                barrier, inc=1, device_id=self.device(self.peer(step)), device_id_type=MESH
            )

    def meet(self):
        pl.semaphore_wait(pltpu.get_barrier_semaphore(), self.count - 1)

    def copies(self, moves, chunk, steps):
        found = []
        for step in steps:
            peer = self.peer(step)
            for source, target, send_sems, recv_sems in moves:
                size = source.shape[1] // send_sems.shape[0]
                rows = pl.ds(pl.multiple_of(chunk * size, PACKED), size)
                if step == 0:
                    copy = pltpu.make_async_copy(
                        source.at[self.me, rows, :],
                        target.at[self.me, rows, :],
                        send_sems.at[chunk, 0],
                    )
                else:
                    copy = pltpu.make_async_remote_copy(
                        src_ref=source.at[peer, rows, :],
                        dst_ref=target.at[self.me, rows, :],
                        send_sem=send_sems.at[chunk, step],
                        recv_sem=recv_sems.at[chunk, step],
                        device_id=self.device(peer),
                        device_id_type=MESH,
                    )
                found.append(copy)
        return found

    def start(self, moves, chunk):
        for copy in self.copies(moves, chunk, self.order + [0]):
            copy.start()

    def wait(self, moves, chunk):
        for copy in self.copies(moves, chunk, self.order + [0]):
            copy.wait()


def join_channels(got, pair):
    peers, rows, _ = got.shape
    even, odd = [], []
    for peer in range(peers):
        for start in range(0, rows, CHUNK_ROWS):
            piece = got[peer, pl.ds(pl.multiple_of(start + pair * PACKED, PACKED), PACKED), :]
            piece = piece.astype(F32)
            even.append(piece[:SUBLANES])
            odd.append(piece[SUBLANES:])
    return [jnp.concatenate(pieces, axis=0).astype(BF16) for pieces in (even, odd)]


def split_channels(low, pair, even, odd, first=0):
    chunks = low.shape[1] // CHUNK_ROWS
    for start in range(0, even.shape[0], SUBLANES):
        block = (first + start) // SUBLANES
        row = block % chunks * CHUNK_ROWS + pair * PACKED
        low[block // chunks, pl.ds(pl.multiple_of(row, PACKED), PACKED), :] = jnp.concatenate(
            [even[start : start + SUBLANES], odd[start : start + SUBLANES]], axis=0
        ).astype(low.dtype)


def each_pair(body):
    def step(pair, carry):
        body(pair)
        return carry

    lax.fori_loop(0, SUBLANES // 2, step, 0)


class Forward:
    wires = 2

    def __init__(self, peers, half, rows, tokens, incoming):
        self.peers, self.half, self.incoming = peers, half, incoming
        self.rows, self.tokens = rows * SUBLANES, tokens
        self.chunks = rows // SUBLANES

    def outs(self):
        block = (SUBLANES, self.tokens, self.tokens)
        return dict(
            left=Out(block, BF16, WHOLE),
            right=Out(block, BF16, WHOLE),
            tri=Out((self.peers, self.rows, self.tokens), BF16, WHOLE),
        )

    def scratch(self):
        low = pltpu.VMEM((self.peers, self.rows, self.tokens), BF16)
        many = pltpu.SemaphoreType.DMA((self.chunks, self.peers))
        return [low] * 4 + [many] * 4

    def moves(self, held):
        return [(held[0], held[2], held[4], held[5]), (held[1], held[3], held[6], held[7])]

    def begin(self, i, held):
        pass

    def finish(self, i, o, held):
        axis = 0 if self.incoming else 1

        def step(pair):
            lefts, rights = join_channels(held[2], pair), join_channels(held[3], pair)
            found = []
            for index in range(2):
                o.left[2 * pair + index] = lefts[index]
                o.right[2 * pair + index] = rights[index]
                found.append(product_of(lefts[index], rights[index], axis, axis))
            split_channels(o.tri, pair, *found)

        each_pair(step)


class Backward:
    wires = 1

    def __init__(self, peers, half, rows, tokens, incoming):
        self.peers, self.half, self.incoming = peers, half, incoming
        self.rows, self.tokens = rows * SUBLANES, tokens
        self.chunks = rows // SUBLANES

    def outs(self):
        wire = (self.peers, self.rows, self.tokens)
        return dict(grad_left=Out(wire, BF16, WHOLE), grad_right=Out(wire, BF16, WHOLE))

    def scratch(self):
        low = pltpu.VMEM((self.peers, self.rows, self.tokens), BF16)
        block = pltpu.VMEM((SUBLANES, self.tokens, self.tokens), BF16)
        many = pltpu.SemaphoreType.DMA((self.chunks, self.peers))
        return [low] * 2 + [block] * 2 + [many] * 2 + [pltpu.SemaphoreType.DMA((2,))]

    def moves(self, held):
        return [(held[0], held[1], held[4], held[5])]

    def owned(self, i, held):
        return [
            pltpu.make_async_copy(i.owned.left, held[2], held[6].at[0]),
            pltpu.make_async_copy(i.owned.right, held[3], held[6].at[1]),
        ]

    def begin(self, i, held):
        for copy in self.owned(i, held):
            copy.start()

    def finish(self, i, o, held):
        for copy in self.owned(i, held):
            copy.wait()

        def step(pair):
            lefts, rights = [], []
            for index, grad in enumerate(join_channels(held[1], pair)):
                left, right = held[2][2 * pair + index], held[3][2 * pair + index]
                if self.incoming:
                    lefts.append(product_of(right, grad, 1, 1))
                    rights.append(product_of(left, grad, 1, 0))
                else:
                    lefts.append(product_of(grad, right, 1, 0))
                    rights.append(product_of(grad, left, 0, 0))
            split_channels(o.grad_left, pair, *lefts)
            split_channels(o.grad_right, pair, *rights)

        each_pair(step)


def prepare(triangle_input, triangle_output, expand_weight, reduce_weight, distogram_weight, norm_gains):
    merged = [
        triangle_input.reshape((-1,) + triangle_input.shape[2:]),
        triangle_output.reshape((-1,) + triangle_output.shape[2:]),
        expand_weight,
        reduce_weight,
        distogram_weight[None],
    ]
    count = len(merged)

    def kernel(*refs):
        for source, plain, turned in zip(refs[:count], refs[count + 1 :: 2], refs[count + 2 :: 2]):
            for index in range(source.shape[0]):
                value = source[index]
                plain[index] = value.astype(BF16)
                turned[index] = value.T.astype(BF16)
        gains = refs[count][...]
        refs[-1][...] = gains.T

    shapes = []
    for array in merged:
        depth, rows, cols = array.shape
        shapes.append(jax.ShapeDtypeStruct((depth, rows, cols), BF16))
        shapes.append(jax.ShapeDtypeStruct((depth, cols, rows), BF16))
    shapes.append(jax.ShapeDtypeStruct(norm_gains.shape[::-1], F32))
    return pl.pallas_call(
        kernel,
        out_shape=shapes,
        compiler_params=pltpu.CompilerParams(vmem_limit_bytes=VMEM_BYTES),
        name="prepare",
    )(*merged, norm_gains)


def by_crop(value, rows_axis, head_axis):
    count, heads = rows_axis, head_axis
    half = count // 2
    inner = half // 2 * heads
    same, other = [], []
    for row in range(count):
        place = row % inner // heads * 2 + row // inner
        for head in range(heads):
            source = row * heads + head
            for crop, pairs in ((head, same), (1 - head, other)):
                pairs.append((source, (crop * half + place) * heads + row % heads))
    head = lax.axis_index("head")
    crop = lax.axis_index("row") // half
    mine = lax.dynamic_index_in_dim(value, head, 0, keepdims=False)
    rest = lax.dynamic_index_in_dim(value, 1 - head, 0, keepdims=False)
    mine = lax.ppermute(mine, ("row", "head"), same)
    rest = lax.ppermute(rest, ("row", "head"), other)
    low = jnp.where(crop == 0, mine, rest)
    high = jnp.where(crop == 0, rest, mine)
    return jnp.concatenate([low, high], axis=-1)


def reduce_rest(half, peers, collective_id, grids, gains, rows):
    sizes = [grid.shape[0] * grid.shape[1] // LANES for grid in grids]
    used = sum(sizes) + len(gains) + SUBLANES * len(rows)
    part = -(-used // (peers * SUBLANES)) * SUBLANES
    total = part * peers
    starts, spot = [], 0
    for size in sizes:
        starts.append(spot)
        spot += size
    row_starts = []
    for _ in rows:
        row_starts.append(spot)
        spot += SUBLANES
    gain_start = spot
    count = len(grids) + len(gains) + len(rows)

    def kernel(*refs):
        out, local, got, mine, other, sends, recvs, back_sends, back_recvs, twin_sems = refs[count:]
        ring = Exchange(peers, half)
        ring.greet()
        barrier = pltpu.get_barrier_semaphore()
        pl.semaphore_signal(barrier, inc=1, device_id=ring.twin, device_id_type=MESH)
        for grid, start in zip(refs[: len(grids)], starts):
            height, width = grid.shape
            for column in range(width // LANES):
                local[pl.ds(start + column * height, height), :] = grid[
                    :, column * LANES : (column + 1) * LANES
                ]
        ones = jnp.ones((SUBLANES, LANES), F32)
        for index, gain in enumerate(refs[len(grids) : len(grids) + len(gains)]):
            folded = lax.dot_general(
                ones,
                gain[...],
                (((1,), (1,)), ((), ())),
                precision=lax.Precision.HIGHEST,
                preferred_element_type=F32,
            )
            local[pl.ds(gain_start + index, 1), :] = folded[:1]
        for row, start in zip(refs[len(grids) + len(gains) : count], row_starts):
            local[pl.ds(start, 1), :] = row[...]
            local[pl.ds(start + 1, SUBLANES - 1), :] = jnp.zeros((SUBLANES - 1, LANES), F32)
        tail = gain_start + len(gains)
        if total > tail:
            local[pl.ds(tail, total - tail), :] = jnp.zeros((total - tail, LANES), F32)
        pl.semaphore_wait(barrier, peers)

        def block(peer):
            return pl.ds(pl.multiple_of(peer * part, SUBLANES), part)

        here = block(ring.me)

        def gather(step):
            peer = ring.peer(step)
            return pltpu.make_async_remote_copy(
                src_ref=local.at[block(peer), :],
                dst_ref=got.at[here, :],
                send_sem=sends.at[step],
                recv_sem=recvs.at[step],
                device_id=ring.device(peer),
                device_id_type=MESH,
            )

        def spread(step):
            return pltpu.make_async_remote_copy(
                src_ref=out.at[here, :],
                dst_ref=out.at[here, :],
                send_sem=back_sends.at[step],
                recv_sem=back_recvs.at[step],
                device_id=ring.device(ring.peer(step)),
                device_id_type=MESH,
            )

        for step in ring.order:
            gather(step).start()
        got[here, :] = local[here, :]
        for step in ring.order:
            gather(step).wait()
        value = got[pl.ds(0, part), :]
        for peer in range(1, peers):
            value = value + got[pl.ds(peer * part, part), :]
        mine[...] = value
        copy = pltpu.make_async_remote_copy(
            src_ref=mine,
            dst_ref=other,
            send_sem=twin_sems.at[0],
            recv_sem=twin_sems.at[1],
            device_id=ring.twin,
            device_id_type=MESH,
        )
        copy.start()
        copy.wait()
        out[here, :] = mine[...] + other[...]
        for step in ring.order:
            spread(step).start()
        for step in ring.order:
            spread(step).wait()

    inside = pl.BlockSpec(memory_space=pltpu.VMEM)
    whole = pl.pallas_call(
        kernel,
        in_specs=[inside] * count,
        out_specs=inside,
        out_shape=jax.ShapeDtypeStruct((total, LANES), F32),
        scratch_shapes=[pltpu.VMEM((total, LANES), F32)] * 2
        + [pltpu.VMEM((part, LANES), F32)] * 2
        + [pltpu.SemaphoreType.DMA((peers,))] * 4
        + [pltpu.SemaphoreType.DMA((2,))],
        compiler_params=pltpu.CompilerParams(
            collective_id=collective_id, has_side_effects=True, vmem_limit_bytes=VMEM_BYTES
        ),
        cost_estimate=pl.CostEstimate(flops=0, bytes_accessed=0, transcendentals=0),
        name="reduce_rest",
    )(*grids, *gains, *rows)
    return whole, starts, row_starts, gain_start


def update(rest, starts, row_starts, gain_start, early, weights, firsts, seconds):
    layers, kinds, width, mixed = weights[2].shape
    hidden = weights[4].shape[2]
    early_in, early_up, early_rows = early
    given = [rest, *early_in, *early_up, early_rows]
    count = len(given)

    def kernel(*refs):
        whole = refs[0]
        in_refs = refs[1 : 1 + len(early_in)]
        up_refs = refs[1 + len(early_in) : count - 1]
        rows_ref = refs[count - 1]
        states = [refs[count + 8 * kind : count + 8 * (kind + 1)] for kind in range(3)]
        scalars = refs[count + 24 : count + 27]
        results = refs[count + 27 :]

        def taken(start, size):
            return whole[pl.ds(start, size), :]

        def wide(start, height, columns):
            return jnp.concatenate(
                [taken(start + column * height, height) for column in range(columns)], axis=1
            )

        loss = jnp.sum(taken(row_starts[0], 1), axis=1, keepdims=True)
        valid = jnp.sum(taken(row_starts[1], 1), axis=1, keepdims=True)
        table_rows, single_rows = weights[0].shape[0], weights[1].shape[0]
        outs, downs = layers * kinds - 1, hidden // 2
        grads = {}
        grads[0, ()] = taken(starts[4], table_rows)
        grads[1, ()] = jnp.concatenate(
            [taken(starts[5], single_rows), taken(starts[6], single_rows)], axis=1
        )
        spot = 0
        for layer in range(layers):
            for kind in range(kinds):
                if layer == 0:
                    grads[2, (layer, kind)] = wide(starts[kind], width, mixed // LANES)
                else:
                    grads[2, (layer, kind)] = in_refs[(layer - 1) * kinds + kind][...]
                if layer == 0 and kind == 0:
                    grads[3, (layer, kind)] = taken(starts[2], width)
                else:
                    grads[3, (layer, kind)] = rows_ref[pl.ds(spot, width), :]
                    spot += width
        for layer in range(layers):
            grads[4, (layer,)] = up_refs[layer][...]
            grads[5, (layer,)] = rows_ref[pl.ds(spot, downs), :]
            spot += downs
        grads[6, ()] = taken(starts[3], weights[6].shape[1]).T
        grads[7, ()] = taken(gain_start, weights[7].shape[0])
        squares = jnp.zeros((1, 1), F32)
        for key in grads:
            grads[key] = grads[key] / valid
            squares = squares + jnp.sum(grads[key] * grads[key], axis=(0, 1), keepdims=True)
        norm = jnp.sqrt(squares)
        factor = jnp.minimum(1.0, CLIP_NORM / (norm + 1e-06))
        for ref, value in zip(scalars, (loss, valid, norm)):
            ref[...] = value
        for (index, spot), grad in grads.items():
            rate = GAIN_RATE if index == 7 else WEIGHT_RATE
            decay = 0.0 if index == 7 else WEIGHT_DECAY
            new = adamw(
                states[0][index][spot],
                grad * factor,
                states[1][index][spot],
                states[2][index][spot],
                rate,
                decay,
            )
            for ref, value in zip(results[3 * index : 3 * index + 3], new):
                ref[spot] = value

    one = jax.ShapeDtypeStruct((1, 1), F32)
    shapes = [one] * 3
    for weight in weights:
        shapes += [jax.ShapeDtypeStruct(weight.shape, F32)] * 3
    found = pl.pallas_call(
        kernel,
        out_shape=shapes,
        compiler_params=pltpu.CompilerParams(vmem_limit_bytes=VMEM_BYTES),
        name="update",
    )(*given, *weights, *firsts, *seconds)
    return tuple(value[0, 0] for value in found[:3]) + tuple(found[3:])


def step_by_crop(row_count, head_count, given, weights, firsts, seconds):
    single, residue_index, chain_index, token_mask, pair_valid, target_bins = given
    relative_table, single_weight, triangle_input, triangle_output = weights[:4]
    expand_weight, reduce_weight, distogram_weight, norm_gains = weights[4:]
    crops, tokens = token_mask.shape
    width = relative_table.shape[1]
    layers = triangle_input.shape[0]
    half = row_count // crops
    peers = half * head_count
    rows = tokens // peers
    row_index = lax.axis_index("row")
    crop = row_index // half
    start = position(row_index % half, lax.axis_index("head"), half, head_count) * rows

    placed = by_crop(jnp.stack([pair_valid, target_bins], axis=1), row_count, head_count)
    valid, target = placed[0], placed[1]

    def of_crop(array):
        return lax.dynamic_index_in_dim(array, crop, 0, keepdims=False)

    def of_rows(array):
        return lax.dynamic_slice_in_dim(array, start, rows, 0)

    residues, chains = of_crop(residue_index), of_crop(chain_index)
    reach = (relative_table.shape[0] - 2) // 2
    bins = jnp.where(
        of_rows(chains)[:, None] == chains[None, :],
        jnp.clip(of_rows(residues)[:, None] - residues[None, :], -reach, reach) + reach,
        2 * reach + 1,
    )
    present = of_crop(token_mask).astype(F32)
    pair_mask = of_rows(present)[:, None] * present[None, :]
    loss_weight = pair_mask * valid.astype(F32)
    table_rows = -(-relative_table.shape[0] // PACKED) * PACKED
    table_t = jnp.pad(relative_table, ((0, table_rows - relative_table.shape[0]), (0, 0))).T
    tokens_single = of_crop(single)
    proj = project(tokens_single, single_weight.astype(BF16))
    proj_rows = of_rows(proj[:, :width])[:, :, None]
    proj_cols = proj[:, width:].T
    bins, pair_mask = Arg(bins[:, None, :], ROWS), Arg(pair_mask[:, None, :], ROWS)

    prepared = prepare(
        triangle_input, triangle_output, expand_weight, reduce_weight, distogram_weight, norm_gains
    )
    mix, mix_t, out, out_t, up, up_t, down, down_t, logits, logits_t, gains = prepared
    hidden = up.shape[2]

    def gain(index):
        return Arg(gains, WHOLE, column=index)

    def layer_of(array, index, *block):
        shape = block or array.shape[1:]
        return Arg(array, WHOLE, (index, 0, 0), (None,) + tuple(shape))

    def triangle_weights(layer, kind, starts=False, finishes=False, back=False):
        index = 2 * layer + kind
        found = dict(gain0=gain(5 * layer + 2 * kind))
        if starts:
            found.update(mix_t=layer_of(mix_t, index, 4 * width, width))
        if starts and back:
            found.update(mix=layer_of(mix, index))
        if finishes:
            found.update(
                gain1=gain(5 * layer + 2 * kind + 1),
                gate_t=Arg(mix_t, WHOLE, (index, 4, 0), (None, width, width)),
                out_t=layer_of(out_t, index),
            )
        if finishes and back:
            found.update(out=layer_of(out, index))
        return found

    def transition_weights(layer, forth=True, back=False):
        found = dict(gain=gain(5 * layer + 4), up_t=layer_of(up_t, layer))
        if forth:
            found.update(down_t=layer_of(down_t, layer))
        if back:
            found.update(up=layer_of(up, layer), down=layer_of(down, layer))
        return found

    def state_out():
        return Out((rows, width, tokens), F32, ROWS)

    def sum_out(*shape):
        return Out(shape, F32, SUM)

    def gain_out():
        return sum_out(width, LANES)

    def back_start_outs():
        return dict(
            grad_gate=Out((rows, width, tokens), BF16, ROWS),
            out=sum_out(width, width),
            gain1=gain_out(),
        )

    def back_finish_outs():
        return dict(mix=sum_out(width, 5 * width), gain0=gain_out())

    def transition_outs():
        return dict(up=sum_out(width, hidden), down=sum_out(hidden // 2, width), gain=gain_out())

    identities = iter(range(4 * layers + 2))

    def forward(incoming):
        return Forward(peers, half, rows, tokens, incoming)

    def backward(incoming):
        return Backward(peers, half, rows, tokens, incoming)

    def wire(array):
        return Arg(array, WIRE, half=half)

    def landed_out():
        return Out((peers, rows * SUBLANES, tokens), BF16, LANDED)

    def owned(kept):
        return dict(left=Arg(kept.left, ANYWHERE), right=Arg(kept.right, ANYWHERE))

    kept, states, middles, tris = {}, {}, {}, {}

    def first_body(i, o, left, right):
        state = dot(i.table_t[...], bins_hot(i.bins, table_rows))
        cols = i.proj_cols[...]
        state = state + jnp.concatenate(
            [cols + i.proj_rows[row] for row in range(ROW_BLOCK)], axis=1
        )
        write_rows(o.state, state)
        triangle_start(i.start, read_rows(i.mask), left, right, state)

    exchange = forward(False)
    got = run_stage(
        first_body,
        "first_state",
        next(identities),
            rows,
        dict(
            bins=bins,
            proj_rows=Arg(proj_rows, ROWS),
            proj_cols=Arg(proj_cols, WHOLE),
            table_t=Arg(table_t.astype(BF16), WHOLE),
            mask=pair_mask,
            start=triangle_weights(0, 0, starts=True),
        ),
        dict(state=state_out(), **exchange.outs()),
        exchange,
    )
    kept[0, 0], states[0, 0] = got, got.state

    def between_body(i, o, left, right):
        state, _ = triangle_finish(i.end, i.tri, read_rows(i.state))
        write_rows(o.state, state)
        triangle_start(i.start, read_rows(i.mask), left, right, state)

    def layer_end_body(i, o, left, right):
        state, _ = triangle_finish(i.end, i.tri, read_rows(i.state))
        write_rows(o.middle, state)
        state = transition_finish(i.lift, state, transition(i.lift, state))
        write_rows(o.state, state)
        triangle_start(i.start, read_rows(i.mask), left, right, state)

    for layer in range(layers):
        exchange = forward(True)
        got = run_stage(
            between_body,
            "between_updates",
            next(identities),
            rows,
            dict(
                state=Arg(states[layer, 0], ROWS),
                tri=wire(kept[layer, 0].tri),
                mask=pair_mask,
                end=triangle_weights(layer, 0, finishes=True),
                start=triangle_weights(layer, 1, starts=True),
            ),
            dict(state=state_out(), landed=landed_out(), **exchange.outs()),
            exchange,
        )
        kept[layer, 1], states[layer, 1], tris[layer, 0] = got, got.state, got.landed
        if layer + 1 == layers:
            break
        exchange = forward(False)
        got = run_stage(
            layer_end_body,
            "layer_end",
            next(identities),
            rows,
            dict(
                state=Arg(states[layer, 1], ROWS),
                tri=wire(kept[layer, 1].tri),
                mask=pair_mask,
                end=triangle_weights(layer, 1, finishes=True),
                lift=transition_weights(layer),
                start=triangle_weights(layer + 1, 0, starts=True),
            ),
            dict(middle=state_out(), state=state_out(), landed=landed_out(), **exchange.outs()),
            exchange,
        )
        tris[layer, 1] = got.landed
        kept[layer + 1, 0], states[layer + 1, 0] = got, got.state
        middles[layer] = got.middle

    def loss_body(i, o, sent):
        state, kept_triangle = triangle_finish(i.end, i.tri, read_rows(i.state))
        lifted = transition(i.lift, state)
        grad = head_back(i.head, o.head, transition_finish(i.lift, state, lifted))
        grad = transition_back(i.lift, o.lift, grad, lifted)
        write_rows(o.grad, grad)
        triangle_back_start(i.end, o.end, sent, grad, kept_triangle)

    top = layers - 1
    exchange = backward(True)
    got = run_stage(
        loss_body,
        "loss",
        next(identities),
            rows,
        dict(
            state=Arg(states[top, 1], ROWS),
            tri=wire(kept[top, 1].tri),
            end=triangle_weights(top, 1, finishes=True, back=True),
            lift=transition_weights(top, back=True),
            head=dict(
                gain=gain(5 * layers),
                logits=layer_of(logits, 0),
                logits_t=layer_of(logits_t, 0),
                target=Arg(target[:, None, :], ROWS),
                weight=Arg(loss_weight[:, None, :], ROWS),
            ),
            owned=owned(kept[top, 1]),
        ),
        dict(
            grad=state_out(),
            head=dict(
                loss=sum_out(1, LANES),
                count=sum_out(1, LANES),
                logits=sum_out(distogram_weight.shape[1], width),
                gain=gain_out(),
            ),
            lift=transition_outs(),
            end=back_start_outs(),
            **exchange.outs(),
        ),
        exchange,
    )
    head, lifts, ends, begins = got.head, {top: got.lift}, {(top, 1): got.end}, {}

    def between_back_body(i, o, sent):
        grad = triangle_back_finish(
            i.start, i.back, o.start, read_rows(i.mask), read_rows(i.grad), read_rows(i.state)
        )
        write_rows(o.grad, grad)
        _, kept_triangle = triangle_finish(i.end, i.tri, read_rows(i.before))
        triangle_back_start(i.end, o.end, sent, grad, kept_triangle)

    def layer_end_back_body(i, o, sent):
        grad = triangle_back_finish(
            i.start, i.back, o.start, read_rows(i.mask), read_rows(i.grad), read_rows(i.state)
        )
        grad = transition_back(i.lift, o.lift, grad, transition(i.lift, read_rows(i.middle)))
        write_rows(o.grad, grad)
        _, kept_triangle = triangle_finish(i.end, i.tri, read_rows(i.before))
        triangle_back_start(i.end, o.end, sent, grad, kept_triangle)

    def first_back_body(i, o):
        grad = triangle_back_finish(
            i.start, i.back, o.start, read_rows(i.mask), read_rows(i.grad), read_rows(i.state)
        )
        hot = bins_hot(i.bins, table_rows)
        high = grad.astype(BF16)
        low = (grad - high.astype(F32)).astype(BF16)
        o.table[...] += dot_pairs(hot, high) + dot_pairs(hot, low)
        for row in range(ROW_BLOCK):
            part = grad[:, row * tokens : (row + 1) * tokens]
            o.rows[row] = fold(part)
            o.cols[...] += part

    for layer in reversed(range(layers)):
        for kind in (1, 0):
            inputs = dict(
                grad=Arg(got.grad, ROWS),
                state=Arg(states[layer, kind], ROWS),
                mask=pair_mask,
                start=triangle_weights(layer, kind, starts=True, back=True),
                back=dict(
                    grad_left=wire(got.grad_left),
                    grad_right=wire(got.grad_right),
                    grad_gate=Arg(got.end.grad_gate, ROWS),
                ),
            )
            outputs = dict(start=back_finish_outs())
            if layer == 0 and kind == 0:
                got = run_stage(
                    first_back_body,
                    "first_state_back",
                    next(identities),
            rows,
                    dict(bins=bins, **inputs),
                    dict(
                        table=sum_out(table_rows, width),
                        rows=Out((rows, width, LANES), F32, ROWS),
                        cols=sum_out(width, tokens),
                        **outputs,
                    ),
                )
                begins[layer, kind] = got.start
                break
            before = (layer, 0) if kind == 1 else (layer - 1, 1)
            inputs.update(
                before=Arg(states[before], ROWS),
                tri=Arg(tris[before], LANDED),
                end=triangle_weights(*before, finishes=True, back=True),
                owned=owned(kept[before]),
            )
            outputs.update(grad=state_out(), end=back_start_outs())
            if kind == 1:
                exchange = backward(False)
                body, name = between_back_body, "between_updates_back"
            else:
                exchange = backward(True)
                body, name = layer_end_back_body, "layer_end_back"
                inputs.update(
                    middle=Arg(middles[layer - 1], ROWS),
                    lift=transition_weights(layer - 1, forth=False, back=True),
                )
                outputs.update(lift=transition_outs())
            got = run_stage(
                body,
                name,
                next(identities),
                rows,
                inputs,
                dict(**outputs, **exchange.outs()),
                exchange,
            )
            begins[layer, kind], ends[before] = got.start, got.end
            if kind == 0:
                lifts[layer - 1] = got.lift

    early = (
        [begins[layer, kind].mix for layer in range(1, layers) for kind in range(2)],
        [lifts[layer].up for layer in range(layers)],
        jnp.concatenate(
            [
                ends[layer, kind].out
                for layer in range(layers)
                for kind in range(2)
                if (layer, kind) != (0, 0)
            ]
            + [lifts[layer].down for layer in range(layers)],
            axis=0,
        ),
    )
    early = lax.psum(early, ("row", "head"))

    wide_single = tokens_single.astype(F32)
    row_part = jnp.einsum(
        "is,ic->sc",
        of_rows(wide_single),
        jnp.sum(got.rows, axis=2),
        precision=lax.Precision.HIGHEST,
    )
    col_part = jnp.einsum("js,cj->sc", wide_single, got.cols, precision=lax.Precision.HIGHEST)
    partial_gains = []
    for layer in range(layers):
        for kind in range(2):
            partial_gains += [begins[layer, kind].gain0, ends[layer, kind].gain1]
        partial_gains.append(lifts[layer].gain)
    partial_gains.append(head.gain)
    grids = [
        begins[0, 0].mix,
        begins[0, 1].mix,
        ends[0, 0].out,
        head.logits,
        got.table,
        row_part,
        col_part,
    ]
    rest, *starts = reduce_rest(
        half, peers, next(identities), grids, partial_gains, [head.loss, head.count]
    )
    return update(rest, *starts, early, weights, firsts, seconds)


def per_device(
    row_count,
    head_count,
    single,
    residue_index,
    chain_index,
    token_mask,
    pair_valid,
    target_bins,
    relative_table,
    single_weight,
    triangle_input,
    triangle_output,
    expand_weight,
    reduce_weight,
    distogram_weight,
    norm_gains,
    first_table,
    second_table,
    first_single,
    second_single,
    first_input,
    second_input,
    first_output,
    second_output,
    first_expand,
    second_expand,
    first_reduce,
    second_reduce,
    first_logits,
    second_logits,
    first_gains,
    second_gains,
):
    crops, tokens = token_mask.shape
    width = relative_table.shape[1]
    peers = row_count * head_count // crops
    given = (
        single,
        residue_index,
        chain_index,
        token_mask,
        pair_valid,
        target_bins,
        relative_table,
        single_weight,
        triangle_input,
        triangle_output,
        expand_weight,
        reduce_weight,
        distogram_weight,
        norm_gains,
    )
    weights = (
        relative_table,
        single_weight,
        triangle_input,
        triangle_output,
        expand_weight,
        reduce_weight,
        distogram_weight,
        norm_gains,
    )
    firsts = (
        first_table,
        first_single,
        first_input,
        first_output,
        first_expand,
        first_reduce,
        first_logits,
        first_gains,
    )
    seconds = (
        second_table,
        second_single,
        second_input,
        second_output,
        second_expand,
        second_reduce,
        second_logits,
        second_gains,
    )
    if (
        crops == 2
        and head_count == 2
        and width == LANES
        and width == SUBLANES * peers
        and tokens % (peers * SUBLANES) == 0
        and tokens % (3 * LANES) == 0
    ):
        return step_by_crop(row_count, head_count, given[:6], weights, firsts, seconds)
    local = gradients_by_block(*given)
    summed = lax.psum(local, ("row", "head"))
    loss_sum, valid_count = summed[0], summed[1]
    grads = [grad / valid_count for grad in summed[2:]]
    squares = jnp.zeros((), jnp.float32)
    for g in grads:
        squares = squares + jnp.sum(g * g)
    gradient_norm = jnp.sqrt(squares)
    factor = jnp.minimum(1.0, CLIP_NORM / (gradient_norm + 1e-06))
    result = []
    for index in range(8):
        rate = GAIN_RATE if index == 7 else WEIGHT_RATE
        decay = 0.0 if index == 7 else WEIGHT_DECAY
        result.extend(
            adamw(weights[index], grads[index] * factor, firsts[index], seconds[index], rate, decay)
        )
    return (
        loss_sum,
        valid_count,
        gradient_norm,
        result[0],
        result[1],
        result[2],
        result[3],
        result[4],
        result[5],
        result[6],
        result[7],
        result[8],
        result[9],
        result[10],
        result[11],
        result[12],
        result[13],
        result[14],
        result[15],
        result[16],
        result[17],
        result[18],
        result[19],
        result[20],
        result[21],
        result[22],
        result[23],
    )


def solution(mesh):
    placed = (
        P(),
        P(),
        P(),
        P(),
        P(None, "row", "head"),
        P(None, "row", "head"),
        P(),
        P(),
        P(),
        P(),
        P(),
        P(),
        P(),
        P(),
        P(),
        P(),
        P(),
        P(),
        P(),
        P(),
        P(),
        P(),
        P(),
        P(),
        P(),
        P(),
        P(),
        P(),
        P(),
        P(),
    )
    return jax.shard_map(
        functools.partial(per_device, mesh.shape["row"], mesh.shape["head"]),
        mesh=mesh,
        in_specs=placed,
        out_specs=(
            P(),
            P(),
            P(),
            P(),
            P(),
            P(),
            P(),
            P(),
            P(),
            P(),
            P(),
            P(),
            P(),
            P(),
            P(),
            P(),
            P(),
            P(),
            P(),
            P(),
            P(),
            P(),
            P(),
            P(),
            P(),
            P(),
            P(),
        ),
        check_vma=False,
    )
```

```python
import functools

import jax
import jax.numpy as jnp
from jax import lax
from jax.experimental import pallas as pl
from jax.experimental.pallas import tpu as pltpu
from jax.sharding import PartitionSpec as P

STEP = 10


EPS = 1e-05
BETA_ONE = 0.9
BETA_TWO = 0.999
ADAM_EPS = 1e-08
WEIGHT_RATE = 0.1
GAIN_RATE = 0.5
WEIGHT_DECAY = 0.01
CLIP_NORM = 0.002


def normalize(value):
    mean = jnp.mean(value, axis=-1, keepdims=True)
    centred = value - mean
    scale = lax.rsqrt(jnp.mean(centred * centred, axis=-1, keepdims=True) + EPS)
    return (centred * scale, scale)


def norm_back(grad_out, unit, scale, gain):
    scaled = grad_out * gain
    first_mean = jnp.mean(scaled, axis=-1, keepdims=True)
    second_mean = jnp.mean(scaled * unit, axis=-1, keepdims=True)
    grad_in = scale * (scaled - first_mean - unit * second_mean)
    grad_gain = jnp.sum(grad_out * unit, axis=tuple(range(grad_out.ndim - 1)))
    return (grad_in, grad_gain)


def project(value, weight):
    return jnp.einsum("...c,cd->...d", value, weight, preferred_element_type=jnp.float32)


def project_back(grad, weight):
    return jnp.einsum("...d,cd->...c", grad, weight, preferred_element_type=jnp.float32)


def weight_grad(value, grad):
    return jnp.einsum("bijc,bijd->cd", value, grad, preferred_element_type=jnp.float32)


def triangle_forward(state, weight_in, weight_out, gains, pair_mask, incoming):
    hidden = weight_out.shape[0]
    pair_unit, pair_scale = normalize(state)
    normed = (pair_unit * gains[0]).astype(jnp.bfloat16)
    mixed = project(normed, weight_in)
    mask = pair_mask[..., None]
    left = (mask * jax.nn.sigmoid(mixed[..., :hidden]) * mixed[..., hidden : 2 * hidden]).astype(
        jnp.bfloat16
    )
    right = (
        mask
        * jax.nn.sigmoid(mixed[..., 2 * hidden : 3 * hidden])
        * mixed[..., 3 * hidden : 4 * hidden]
    ).astype(jnp.bfloat16)
    left_cols, right_cols = (
        lax.all_to_all(left, "head", split_axis=3, concat_axis=2, tiled=True),
        lax.all_to_all(right, "head", split_axis=3, concat_axis=2, tiled=True),
    )
    if incoming:
        left_cols, right_cols = (
            lax.all_to_all(left_cols, "row", split_axis=2, concat_axis=1, tiled=True),
            lax.all_to_all(right_cols, "row", split_axis=2, concat_axis=1, tiled=True),
        )
        left_cols = jnp.swapaxes(left_cols, 1, 2)
        right_cols = jnp.swapaxes(right_cols, 1, 2)
    right_all = lax.all_gather(right_cols, "row", axis=1, tiled=True)
    triangle = jnp.einsum(
        "bikc,bjkc->bijc", left_cols, right_all, preferred_element_type=jnp.float32
    )
    triangle = lax.all_to_all(
        triangle.astype(jnp.bfloat16), "head", split_axis=2, concat_axis=3, tiled=True
    )
    tri_unit, tri_scale = normalize(triangle.astype(jnp.float32))
    shaped = (tri_unit * gains[1]).astype(jnp.bfloat16)
    branch = project(shaped, weight_out)
    gate = jax.nn.sigmoid(mixed[..., 4 * hidden :])
    kept = (
        pair_unit,
        pair_scale,
        normed,
        mixed,
        left_cols,
        right_all,
        tri_unit,
        tri_scale,
        shaped,
        branch,
        gate,
    )
    return (state + gate * branch, kept)


def triangle_backward(grad_state, kept, weight_in, weight_out, gains, pair_mask, incoming):
    hidden = weight_out.shape[0]
    (
        pair_unit,
        pair_scale,
        normed,
        mixed,
        left_cols,
        right_all,
        tri_unit,
        tri_scale,
        shaped,
        branch,
        gate,
    ) = kept
    grad_branch = (grad_state * gate).astype(jnp.bfloat16)
    grad_gate = grad_state * branch * gate * (1.0 - gate)
    grad_out = weight_grad(shaped, grad_branch)
    grad_shaped = project_back(grad_branch, weight_out)
    grad_tri, gain_two = norm_back(grad_shaped, tri_unit, tri_scale, gains[1])
    tri_cols = lax.all_to_all(
        grad_tri.astype(jnp.bfloat16), "head", split_axis=3, concat_axis=2, tiled=True
    )
    grad_left = jnp.einsum(
        "bijc,bjkc->bikc", tri_cols, right_all, preferred_element_type=jnp.float32
    )
    grad_left = grad_left.astype(jnp.bfloat16)
    summed = lax.psum_scatter(
        jnp.einsum(
            "bijc,bikc->jbkc", tri_cols, left_cols, preferred_element_type=jnp.float32
        ).astype(jnp.bfloat16),
        "row",
        scatter_dimension=0,
        tiled=True,
    ).astype(jnp.float32)
    grad_right = jnp.transpose(summed, (1, 0, 2, 3)).astype(jnp.bfloat16)
    if incoming:
        grad_left, grad_right = (
            lax.all_to_all(
                jnp.swapaxes(grad_left, 1, 2), "row", split_axis=1, concat_axis=2, tiled=True
            ),
            lax.all_to_all(
                jnp.swapaxes(grad_right, 1, 2), "row", split_axis=1, concat_axis=2, tiled=True
            ),
        )
    back_left, back_right = (
        lax.all_to_all(grad_left, "head", split_axis=2, concat_axis=3, tiled=True),
        lax.all_to_all(grad_right, "head", split_axis=2, concat_axis=3, tiled=True),
    )
    mask = pair_mask[..., None]
    back_left = back_left.astype(jnp.float32) * mask
    back_right = back_right.astype(jnp.float32) * mask
    left_sig = jax.nn.sigmoid(mixed[..., :hidden])
    left_value = mixed[..., hidden : 2 * hidden]
    right_sig = jax.nn.sigmoid(mixed[..., 2 * hidden : 3 * hidden])
    right_value = mixed[..., 3 * hidden : 4 * hidden]
    grad_mixed = jnp.concatenate(
        [
            back_left * left_value * left_sig * (1.0 - left_sig),
            back_left * left_sig,
            back_right * right_value * right_sig * (1.0 - right_sig),
            back_right * right_sig,
            grad_gate,
        ],
        axis=-1,
    ).astype(jnp.bfloat16)
    grad_in = weight_grad(normed, grad_mixed)
    grad_normed = project_back(grad_mixed, weight_in)
    grad_first, gain_one = norm_back(grad_normed, pair_unit, pair_scale, gains[0])
    return (grad_state + grad_first, (grad_in, grad_out, gain_one, gain_two))


def transition_forward(state, weight_up, weight_down, gain):
    expand = weight_down.shape[0]
    unit, scale = normalize(state)
    lifted = (unit * gain).astype(jnp.bfloat16)
    inner = project(lifted, weight_up)
    product = (jax.nn.silu(inner[..., :expand]) * inner[..., expand:]).astype(jnp.bfloat16)
    return (state + project(product, weight_down), (unit, scale, lifted, inner, product))


def transition_backward(grad_state, kept, weight_up, weight_down, gain):
    expand = weight_down.shape[0]
    unit, scale, lifted, inner, product = kept
    grad_low = grad_state.astype(jnp.bfloat16)
    grad_down = weight_grad(product, grad_low)
    grad_product = project_back(grad_low, weight_down)
    gate_part = inner[..., :expand]
    up_part = inner[..., expand:]
    gate_sig = jax.nn.sigmoid(gate_part)
    silu_value = gate_part * gate_sig
    silu_slope = gate_sig * (1.0 + gate_part * (1.0 - gate_sig))
    grad_inner = jnp.concatenate(
        [grad_product * up_part * silu_slope, grad_product * silu_value], axis=-1
    )
    grad_inner = grad_inner.astype(jnp.bfloat16)
    grad_up = weight_grad(lifted, grad_inner)
    grad_lifted = project_back(grad_inner, weight_up)
    grad_middle, gain_grad = norm_back(grad_lifted, unit, scale, gain)
    return (grad_middle + grad_state, (grad_up, grad_down, gain_grad))


def block_forward(state, weight_in, weight_out, weight_up, weight_down, gains, pair_mask):
    first, kept_one = triangle_forward(
        state, weight_in[0], weight_out[0], gains[0:2], pair_mask, False
    )
    second, kept_two = triangle_forward(
        first, weight_in[1], weight_out[1], gains[2:4], pair_mask, True
    )
    output, kept_three = transition_forward(second, weight_up, weight_down, gains[4])
    return (output, (kept_one, kept_two, kept_three))


def block_backward(
    grad_state, state, weight_in, weight_out, weight_up, weight_down, gains, pair_mask
):
    skipped, kept = block_forward(
        state, weight_in, weight_out, weight_up, weight_down, gains, pair_mask
    )
    kept_one, kept_two, kept_three = kept
    grad_state, (grad_up, grad_down, gain_five) = transition_backward(
        grad_state, kept_three, weight_up, weight_down, gains[4]
    )
    grad_state, (in_two, out_two, gain_three, gain_four) = triangle_backward(
        grad_state, kept_two, weight_in[1], weight_out[1], gains[2:4], pair_mask, True
    )
    grad_state, (in_one, out_one, gain_one, gain_two) = triangle_backward(
        grad_state, kept_one, weight_in[0], weight_out[0], gains[0:2], pair_mask, False
    )
    return (
        grad_state,
        (
            jnp.stack([in_one, in_two]),
            jnp.stack([out_one, out_two]),
            grad_up,
            grad_down,
            jnp.stack([gain_one, gain_two, gain_three, gain_four, gain_five]),
        ),
    )


def adamw(weight, grad, first, second, rate, decay):
    first_new = BETA_ONE * first + (1.0 - BETA_ONE) * grad
    second_new = BETA_TWO * second + (1.0 - BETA_TWO) * grad * grad
    moved = (
        first_new
        / (1.0 - BETA_ONE**STEP)
        / (jnp.sqrt(second_new / (1.0 - BETA_TWO**STEP)) + ADAM_EPS)
    )
    return (first_new, second_new, weight - rate * (moved + decay * weight))


def gradients_by_block(
    single,
    residue_index,
    chain_index,
    token_mask,
    pair_valid,
    target_bins,
    relative_table,
    single_weight,
    triangle_input,
    triangle_output,
    expand_weight,
    reduce_weight,
    distogram_weight,
    norm_gains,
):
    crops, rows, cols = pair_valid.shape
    width = relative_table.shape[1]
    layers = triangle_input.shape[0]
    row_start = lax.axis_index("row") * rows
    col_start = lax.axis_index("head") * cols

    def take(array, start, count):
        return lax.dynamic_slice_in_dim(array, start, count, 1)

    offset = (
        take(residue_index, row_start, rows)[:, :, None]
        - take(residue_index, col_start, cols)[:, None, :]
    )
    same = (
        take(chain_index, row_start, rows)[:, :, None]
        == take(chain_index, col_start, cols)[:, None, :]
    )
    reach = (relative_table.shape[0] - 2) // 2
    bins = jnp.where(same, jnp.clip(offset, -reach, reach) + reach, 2 * reach + 1)
    relative_hot = (
        bins[..., None] == jnp.arange(relative_table.shape[0])[None, None, None, :]
    ).astype(jnp.float32)
    token_rows = take(token_mask, row_start, rows).astype(jnp.float32)
    token_cols = take(token_mask, col_start, cols).astype(jnp.float32)
    pair_mask = token_rows[:, :, None] * token_cols[:, None, :]
    loss_weight = pair_mask * pair_valid.astype(jnp.float32)
    low_input = triangle_input.astype(jnp.bfloat16)
    low_output = triangle_output.astype(jnp.bfloat16)
    low_expand = expand_weight.astype(jnp.bfloat16)
    low_reduce = reduce_weight.astype(jnp.bfloat16)
    low_logits = distogram_weight.astype(jnp.bfloat16)
    proj = project(single, single_weight.astype(jnp.bfloat16))
    state = project(relative_hot.astype(jnp.bfloat16), relative_table.astype(jnp.bfloat16))
    state = (
        state
        + take(proj, row_start, rows)[:, :, None, :width]
        + take(proj, col_start, cols)[:, None, :, width:]
    )
    inputs = []
    for layer in range(layers):
        inputs.append(state)
        state, unused = block_forward(
            state,
            low_input[layer],
            low_output[layer],
            low_expand[layer],
            low_reduce[layer],
            norm_gains[5 * layer : 5 * layer + 5],
            pair_mask,
        )
    head_unit, head_scale = normalize(state)
    shown = (head_unit * norm_gains[5 * layers]).astype(jnp.bfloat16)
    logits = project(shown, low_logits)
    largest = jnp.max(logits, axis=-1, keepdims=True)
    log_total = largest + jnp.log(jnp.sum(jnp.exp(logits - largest), axis=-1, keepdims=True))
    target_hot = (
        target_bins[..., None] == jnp.arange(logits.shape[-1])[None, None, None, :]
    ).astype(jnp.float32)
    picked = jnp.sum(logits * target_hot, axis=-1)
    loss_local = jnp.sum(loss_weight * (log_total[..., 0] - picked))
    grad_scores = (loss_weight[..., None] * (jnp.exp(logits - log_total) - target_hot)).astype(
        jnp.bfloat16
    )
    grad_logits = weight_grad(shown, grad_scores)
    grad_shown = project_back(grad_scores, low_logits)
    grad_state, gain_last = norm_back(grad_shown, head_unit, head_scale, norm_gains[5 * layers])
    collected = []
    for layer in reversed(range(layers)):
        grad_state, layer_grads = block_backward(
            grad_state,
            inputs[layer],
            low_input[layer],
            low_output[layer],
            low_expand[layer],
            low_reduce[layer],
            norm_gains[5 * layer : 5 * layer + 5],
            pair_mask,
        )
        collected.insert(0, layer_grads)
    grad_input = jnp.stack([entry[0] for entry in collected])
    grad_output = jnp.stack([entry[1] for entry in collected])
    grad_expand = jnp.stack([entry[2] for entry in collected])
    grad_reduce = jnp.stack([entry[3] for entry in collected])
    grad_gains = jnp.concatenate(
        [jnp.concatenate([entry[4] for entry in collected], axis=0), gain_last[None]], axis=0
    )
    grad_table = jnp.einsum(
        "bijr,bijc->rc", relative_hot, grad_state, precision=lax.Precision.HIGHEST
    )
    single_wide = single.astype(jnp.float32)
    row_part = jnp.einsum(
        "bis,bic->sc",
        take(single_wide, row_start, rows),
        jnp.sum(grad_state, axis=2),
        precision=lax.Precision.HIGHEST,
    )
    col_part = jnp.einsum(
        "bjs,bjc->sc",
        take(single_wide, col_start, cols),
        jnp.sum(grad_state, axis=1),
        precision=lax.Precision.HIGHEST,
    )
    grad_single = jnp.concatenate([row_part, col_part], axis=1)
    return (
        loss_local,
        jnp.sum(loss_weight),
        grad_table,
        grad_single,
        grad_input,
        grad_output,
        grad_expand,
        grad_reduce,
        grad_logits,
        grad_gains,
    )


F32 = jnp.float32
BF16 = jnp.bfloat16
LANES = 128
SUBLANES = 8
PACKED = 16
ROW_BLOCK = 4
STREAM_ROWS = 2
PHASES = SUBLANES // ROW_BLOCK
CHUNK_ROWS = SUBLANES * SUBLANES
VMEM_BYTES = 58 * 2**20
MESH = pl.DeviceIdType.MESH
ROWS, WIRE, LANDED, WHOLE, SUM, ANYWHERE = range(6)


class Bag:
    def __init__(self, **entries):
        self.__dict__.update(entries)


class Arg:
    def __init__(self, array, kind, index=None, block=None, column=None, half=None):
        self.array, self.kind, self.index, self.block = array, kind, index, block
        self.column, self.half = column, half

    def spec(self):
        if self.index is None:
            return block_spec(self.array.shape, self.kind)
        index = self.index
        return pl.BlockSpec(self.block, lambda step: index)


class Column:
    def __init__(self, ref, column):
        self.ref, self.column = ref, column

    def __getitem__(self, _):
        return self.ref[:, self.column : self.column + 1]


class Out:
    def __init__(self, shape, dtype, kind):
        self.shape, self.dtype, self.kind = shape, dtype, kind

    def spec(self):
        return block_spec(self.shape, ANYWHERE if self.kind == LANDED else self.kind)


def block_spec(shape, kind):
    if kind in (WIRE, ANYWHERE):
        return pl.BlockSpec(memory_space=pl.ANY)
    if kind == LANDED:
        return pl.BlockSpec((shape[0], CHUNK_ROWS, shape[2]), lambda step: (0, step // PHASES, 0))
    if kind == ROWS:
        return pl.BlockSpec((ROW_BLOCK,) + shape[1:], lambda step: (step,) + (0,) * (len(shape) - 1))
    return pl.BlockSpec(shape, lambda step: (0,) * len(shape))


def is_leaf(value):
    return isinstance(value, (Arg, Out))


def bag_of(tree, leaves):
    return Bag(
        **{
            key: next(leaves) if is_leaf(value) else bag_of(value, leaves)
            for key, value in tree.items()
        }
    )


def leaves_of(tree):
    found = []
    for value in tree.values():
        found.extend([value] if is_leaf(value) else leaves_of(value))
    return found


def dot(left, right):
    return lax.dot_general(left, right, (((1,), (0,)), ((), ())), preferred_element_type=F32)


def dot_pairs(left, right):
    return lax.dot_general(left, right, (((1,), (1,)), ((), ())), preferred_element_type=F32)


def product_of(left, right, left_axis, right_axis):
    return lax.dot_general(
        left, right, (((left_axis,), (right_axis,)), ((), ())), preferred_element_type=F32
    )


def sigmoid(value):
    return 0.5 * jnp.tanh(0.5 * value) + 0.5


def unit_of(value):
    centred = value - jnp.mean(value, axis=0, keepdims=True)
    scale = lax.rsqrt(jnp.mean(centred * centred, axis=0, keepdims=True) + EPS)
    return (centred * scale, scale)


def unit_back(grad, unit, scale, gain):
    scaled = grad * gain
    first = jnp.mean(scaled, axis=0, keepdims=True)
    second = jnp.mean(scaled * unit, axis=0, keepdims=True)
    return scale * (scaled - first - unit * second)


def fold(value):
    total = value[:, :LANES]
    for start in range(LANES, value.shape[1], LANES):
        total = total + value[:, start : start + LANES]
    return total


def read_rows(ref, rows):
    return jnp.concatenate([ref[row] for row in rows], axis=1)


def write_rows(ref, rows, value):
    cols = ref.shape[2]
    for place, row in enumerate(rows):
        ref[row] = value[:, place * cols : (place + 1) * cols].astype(ref.dtype)


def alternate(streams):
    while streams:
        going = []
        for stream in streams:
            try:
                next(stream)
                going.append(stream)
            except StopIteration:
                pass
        streams = going


class Wire:
    def __init__(self, wide, phase):
        self.wide, self.phase = wide, phase

    def tokens(self, row):
        width = self.wide.shape[1] // SUBLANES
        return pl.ds(self.phase * ROW_BLOCK + row, width, stride=SUBLANES)

    def read(self, rows):
        lanes = self.wide.shape[0]
        return jnp.concatenate(
            [self.wide[lane, self.tokens(row), :] for row in rows for lane in range(lanes)], axis=1
        )

    def write(self, rows, value):
        lanes = self.wide.shape[0]
        for place, row in enumerate(rows):
            for lane in range(lanes):
                start = (place * lanes + lane) * LANES
                self.wide[lane, self.tokens(row), :] = value[:, start : start + LANES]


def widen(wide, low, chunk):
    rows = pl.ds(pl.multiple_of(chunk * CHUNK_ROWS, CHUNK_ROWS), CHUNK_ROWS)

    def step(peer, carry):
        value = low[peer, rows, :].astype(F32)
        start = pl.multiple_of(peer * CHUNK_ROWS, CHUNK_ROWS)
        for lane in range(wide.shape[0]):
            wide[lane, pl.ds(start, CHUNK_ROWS), :] = value[:, lane * LANES : (lane + 1) * LANES]
        return carry

    lax.fori_loop(0, low.shape[0], step, 0)


def narrow(low, wide, chunk):
    rows = pl.ds(pl.multiple_of(chunk * CHUNK_ROWS, CHUNK_ROWS), CHUNK_ROWS)

    def step(peer, carry):
        start = pl.multiple_of(peer * CHUNK_ROWS, CHUNK_ROWS)
        low[peer, rows, :] = jnp.concatenate(
            [wide[lane, pl.ds(start, CHUNK_ROWS), :] for lane in range(wide.shape[0])], axis=1
        ).astype(low.dtype)
        return carry

    lax.fori_loop(0, low.shape[0], step, 0)


def triangle_start(weights, i, rows, wires, state):
    width = state.shape[0]
    unit, _ = unit_of(state)
    normed = (unit * weights.gain0[...]).astype(BF16)
    mixed = dot(weights.mix_t[...], normed)
    yield
    mask = read_rows(i.mask, rows)
    for wire, base in zip(wires, (0, 2 * width)):
        gate = sigmoid(mixed[base : base + width])
        wire.write(rows, mask * gate * mixed[base + width : base + 2 * width])


def triangle_finish(weights, rows, wire, state):
    unit, _ = unit_of(state)
    normed = (unit * weights.gain0[...]).astype(BF16)
    opened = dot(weights.gate_t[...], normed)
    yield
    tri_unit, tri_scale = unit_of(wire.read(rows))
    shaped = (tri_unit * weights.gain1[...]).astype(BF16)
    branch = dot(weights.out_t[...], shaped)
    yield
    gate = sigmoid(opened)
    return (state + gate * branch, (gate, tri_unit, tri_scale, shaped, branch))


def triangle_back_start(weights, o, rows, wire, grad, kept):
    gate, tri_unit, tri_scale, shaped, branch = kept
    grad_branch = (grad * gate).astype(BF16)
    grad_shaped = dot(weights.out[...], grad_branch)
    yield
    o.out[...] += dot_pairs(shaped, grad_branch)
    write_rows(o.grad_gate, rows, grad * branch * gate * (1.0 - gate))
    yield
    o.gain1[...] += fold(grad_shaped * tri_unit)
    wire.write(rows, unit_back(grad_shaped, tri_unit, tri_scale, weights.gain1[...]))


def triangle_back_finish(weights, i, o, rows):
    grad, state = read_rows(i.grad, rows), read_rows(i.state, rows)
    width = state.shape[0]
    unit, scale = unit_of(state)
    gain = weights.gain0[...]
    normed = (unit * gain).astype(BF16)
    mixed = dot(weights.mix_t[...], normed)
    yield
    mask = read_rows(i.mask, rows)
    parts = []
    for wire, base in ((i.back.grad_left, 0), (i.back.grad_right, 2 * width)):
        back = wire.read(rows) * mask
        gate = sigmoid(mixed[base : base + width])
        back_gate = back * gate
        parts.append((back_gate * mixed[base + width : base + 2 * width] * (1.0 - gate)).astype(BF16))
        parts.append(back_gate.astype(BF16))
    parts.append(read_rows(i.back.grad_gate, rows))
    grad_mixed = jnp.concatenate(parts, axis=0)
    yield
    grad_normed = dot(weights.mix[...], grad_mixed)
    o.mix[...] += dot_pairs(normed, grad_mixed)
    yield
    o.gain0[...] += fold(grad_normed * unit)
    return grad + unit_back(grad_normed, unit, scale, gain)


def transition(weights, state):
    unit, scale = unit_of(state)
    lifted = (unit * weights.gain[...]).astype(BF16)
    inner = dot(weights.up_t[...], lifted)
    yield
    half = inner.shape[0] // 2
    gate = inner[:half]
    slope = sigmoid(gate)
    product = (gate * slope * inner[half:]).astype(BF16)
    return (unit, scale, lifted, inner, slope, product)


def transition_back(weights, o, grad, kept):
    unit, scale, lifted, inner, slope, product = kept
    half = inner.shape[0] // 2
    gate, up = inner[:half], inner[half:]
    grad_low = grad.astype(BF16)
    grad_product = dot(weights.down[...], grad_low)
    o.down[...] += dot_pairs(product, grad_low)
    yield
    scaled = grad_product * slope
    grad_inner = jnp.concatenate(
        [
            (scaled * up * (1.0 + gate * (1.0 - slope))).astype(BF16),
            (scaled * gate).astype(BF16),
        ],
        axis=0,
    )
    yield
    grad_lifted = dot(weights.up[...], grad_inner)
    o.up[...] += dot_pairs(lifted, grad_inner)
    yield
    o.gain[...] += fold(grad_lifted * unit)
    return grad + unit_back(grad_lifted, unit, scale, weights.gain[...])


def head_back(i, o, rows, state):
    unit, scale = unit_of(state)
    gain = i.gain[...]
    shown = (unit * gain).astype(BF16)
    logits = dot(i.logits_t[...], shown)
    yield
    largest = jnp.max(logits, axis=0, keepdims=True)
    raised = jnp.exp(logits - largest)
    total = jnp.sum(raised, axis=0, keepdims=True)
    log_total = largest + jnp.log(total)
    target = read_rows(i.target, rows)
    weight = read_rows(i.weight, rows)
    hot = lax.broadcasted_iota(jnp.int32, logits.shape, 0) == target
    picked = jnp.sum(jnp.where(hot, logits, 0.0), axis=0, keepdims=True)
    o.loss[...] += fold(weight * (log_total - picked))
    o.count[...] += fold(weight)
    share = raised * (1.0 / total)
    grad_scores = (weight * (share - jnp.where(hot, 1.0, 0.0))).astype(BF16)
    grad_shown = dot(i.logits[...], grad_scores)
    o.logits[...] += dot_pairs(grad_scores, shown)
    yield
    o.gain[...] += fold(grad_shown * unit)
    return unit_back(grad_shown, unit, scale, gain)


def bins_hot(bins, rows, table_rows):
    bins = read_rows(bins, rows)
    shape = (table_rows, bins.shape[1])
    return jnp.where(lax.broadcasted_iota(jnp.int32, shape, 0) == bins, 1.0, 0.0).astype(BF16)


def run_stage(body, name, collective_id, rows, inputs, outputs, exchange=None):
    args, outs = leaves_of(inputs), leaves_of(outputs)
    steps = rows // ROW_BLOCK
    chunks = rows // SUBLANES
    wire_args = [index for index, arg in enumerate(args) if arg.kind == WIRE]
    landed_args = [index for index, arg in enumerate(args) if arg.kind == LANDED]
    keeps = [place for place, out in enumerate(outs) if out.kind == LANDED]
    wires = exchange.wires if exchange else 0
    if wire_args:
        peers, half, tokens = args[wire_args[0]].array.shape[0], args[wire_args[0]].half, 0
        tokens = args[wire_args[0]].array.shape[2]
    if exchange:
        peers, half, tokens = exchange.peers, exchange.half, exchange.tokens
    low = pltpu.VMEM((peers, rows * SUBLANES, tokens), BF16)
    many = pltpu.SemaphoreType.DMA((chunks, peers))
    wide = pltpu.VMEM((tokens // LANES, peers * CHUNK_ROWS, LANES), F32)
    groups = [
        [wide] * (len(wire_args) + len(landed_args) + wires),
        [low] * len(wire_args),
        [many] * (2 * len(wire_args)),
        [pltpu.SemaphoreType.DMA((1,))] * len(keeps),
        exchange.scratch() if exchange else [],
    ]

    def kernel(*refs):
        step = pl.program_id(0)
        phase, chunk = lax.rem(step, PHASES), lax.div(step, PHASES)
        in_refs = [
            ref if arg.column is None else Column(ref, arg.column) for arg, ref in zip(args, refs)
        ]
        out_refs = list(refs[len(args) : len(args) + len(outs)])
        rest, parts = list(refs[len(args) + len(outs) :]), []
        for group in groups:
            parts.append(rest[: len(group)])
            rest = rest[len(group) :]
        wides, lands, sems, keep_sems, held = parts
        saves = [
            pltpu.make_async_copy(land, out_refs[place], sem.at[0])
            for land, place, sem in zip(lands, keeps, keep_sems)
        ]
        ring = Exchange(peers, half)
        arrivals = [
            (in_refs[index], land, sems[2 * place], sems[2 * place + 1])
            for place, (index, land) in enumerate(zip(wire_args, lands))
        ]
        i, o = bag_of(inputs, iter(in_refs)), bag_of(outputs, iter(out_refs))

        @pl.when(step == 0)
        def _():
            ring.greet()
            for out, ref in zip(outs, out_refs):
                if out.kind == SUM:
                    ref[...] = jnp.zeros(out.shape, out.dtype)
            if exchange:
                exchange.begin(i, held)
            if arrivals:
                ring.meet()

                def start(index, carry):
                    ring.start(arrivals, index)
                    return carry

                lax.fori_loop(0, chunks, start, 0)

        if arrivals:

            @pl.when(phase == 0)
            def _():
                ring.wait(arrivals, chunk)
                for target, land in zip(wides, lands):
                    widen(target, land, chunk)

        if landed_args:

            @pl.when(phase == 0)
            def _():
                for target, index in zip(wides[len(wire_args) :], landed_args):
                    widen(target, in_refs[index], 0)

        if saves:

            @pl.when(step == steps - PHASES)
            def _():
                for save in saves:
                    save.start()

        body_in = list(in_refs)
        for index, source in zip(wire_args + landed_args, wides):
            body_in[index] = Wire(source, phase)
        sent = wides[len(wire_args) + len(landed_args) :]
        given = bag_of(inputs, iter(body_in))
        out_wires = [Wire(target, phase) for target in sent]
        alternate(
            [
                body(given, o, range(first, first + STREAM_ROWS), *out_wires)
                for first in range(0, ROW_BLOCK, STREAM_ROWS)
            ]
        )
        if exchange:
            moves = exchange.moves(held)

            @pl.when(phase == PHASES - 1)
            def _():
                for source, move in zip(sent, moves):
                    narrow(move[0], source, chunk)
                if not arrivals:

                    @pl.when(chunk == 0)
                    def _():
                        ring.meet()

                ring.start(moves, chunk)

            @pl.when(step == steps - 1)
            def _():
                def wait(index, carry):
                    ring.wait(moves, index)
                    return carry

                lax.fori_loop(0, chunks, wait, 0)
                exchange.finish(i, o, held)
                for save in saves:
                    save.wait()

    results = pl.pallas_call(
        kernel,
        grid=(steps,),
        in_specs=[arg.spec() for arg in args],
        out_specs=[out.spec() for out in outs],
        out_shape=[jax.ShapeDtypeStruct(out.shape, out.dtype) for out in outs],
        scratch_shapes=sum(groups, []),
        compiler_params=pltpu.CompilerParams(
            dimension_semantics=(pltpu.ARBITRARY,),
            vmem_limit_bytes=VMEM_BYTES,
            has_side_effects=True,
            collective_id=collective_id,
        ),
        cost_estimate=pl.CostEstimate(flops=0, bytes_accessed=0, transcendentals=0),
        name=name,
    )(*[arg.array for arg in args])
    return bag_of(outputs, iter(results))


def flip(value, step, count):
    result, bit = 0, 1
    while bit < count:
        result = result + lax.rem(lax.div(value, bit) + (step // bit) % 2, 2) * bit
        bit *= 2
    return result


def position(row, head, half, heads):
    inner = half // 2 * heads
    return (row % 2) * inner + (row // 2) * heads + head


def place_of(position, half, heads):
    inner = half // 2 * heads
    rest = lax.rem(position, inner)
    return (lax.div(rest, heads) * 2 + lax.div(position, inner), lax.rem(rest, heads))


class Exchange:
    def __init__(self, count, half):
        row, head = lax.axis_index("row"), lax.axis_index("head")
        place = lax.rem(row, half)
        inner = count // 2
        self.count = count
        self.half = half
        self.base = row - place
        self.me = lax.rem(place, 2) * inner + lax.div(place, 2) * (count // half) + head
        self.twin = (lax.rem(row + half, 2 * half), head)
        self.order = []
        for step in range(1, count):
            for other in (step, step ^ (inner - 1)):
                if other and other not in self.order:
                    self.order.append(other)

    def peer(self, step):
        return flip(self.me, step, self.count)

    def device(self, peer):
        place, head = place_of(peer, self.half, self.count // self.half)
        return (self.base + place, head)

    def greet(self):
        barrier = pltpu.get_barrier_semaphore()
        for step in self.order:
            pl.semaphore_signal(
                barrier, inc=1, device_id=self.device(self.peer(step)), device_id_type=MESH
            )

    def meet(self):
        pl.semaphore_wait(pltpu.get_barrier_semaphore(), self.count - 1)

    def copies(self, moves, chunk, steps):
        found = []
        for step in steps:
            peer = self.peer(step)
            for source, target, send_sems, recv_sems in moves:
                size = source.shape[1] // send_sems.shape[0]
                rows = pl.ds(pl.multiple_of(chunk * size, PACKED), size)
                if step == 0:
                    copy = pltpu.make_async_copy(
                        source.at[self.me, rows, :],
                        target.at[self.me, rows, :],
                        send_sems.at[chunk, 0],
                    )
                else:
                    copy = pltpu.make_async_remote_copy(
                        src_ref=source.at[peer, rows, :],
                        dst_ref=target.at[self.me, rows, :],
                        send_sem=send_sems.at[chunk, step],
                        recv_sem=recv_sems.at[chunk, step],
                        device_id=self.device(peer),
                        device_id_type=MESH,
                    )
                found.append(copy)
        return found

    def start(self, moves, chunk):
        for copy in self.copies(moves, chunk, self.order + [0]):
            copy.start()

    def wait(self, moves, chunk):
        for copy in self.copies(moves, chunk, self.order + [0]):
            copy.wait()


def join_channels(got, pair):
    peers, rows, _ = got.shape
    even, odd = [], []
    for peer in range(peers):
        for start in range(0, rows, CHUNK_ROWS):
            piece = got[peer, pl.ds(pl.multiple_of(start + pair * PACKED, PACKED), PACKED), :]
            piece = piece.astype(F32)
            even.append(piece[:SUBLANES])
            odd.append(piece[SUBLANES:])
    return [jnp.concatenate(pieces, axis=0).astype(BF16) for pieces in (even, odd)]


def split_channels(low, pair, even, odd, first=0):
    chunks = low.shape[1] // CHUNK_ROWS
    for start in range(0, even.shape[0], SUBLANES):
        block = (first + start) // SUBLANES
        row = block % chunks * CHUNK_ROWS + pair * PACKED
        low[block // chunks, pl.ds(pl.multiple_of(row, PACKED), PACKED), :] = jnp.concatenate(
            [even[start : start + SUBLANES], odd[start : start + SUBLANES]], axis=0
        ).astype(low.dtype)


def each_pair(body):
    for pair in range(SUBLANES // 2):
        body(pair)


class Forward:
    wires = 2

    def __init__(self, peers, half, rows, tokens, incoming):
        self.peers, self.half, self.incoming = peers, half, incoming
        self.rows, self.tokens = rows * SUBLANES, tokens
        self.chunks = rows // SUBLANES

    def outs(self):
        block = (SUBLANES, self.tokens, self.tokens)
        return dict(
            left=Out(block, BF16, WHOLE),
            right=Out(block, BF16, WHOLE),
            tri=Out((self.peers, self.rows, self.tokens), BF16, WHOLE),
        )

    def scratch(self):
        low = pltpu.VMEM((self.peers, self.rows, self.tokens), BF16)
        many = pltpu.SemaphoreType.DMA((self.chunks, self.peers))
        return [low] * 4 + [many] * 4

    def moves(self, held):
        return [(held[0], held[2], held[4], held[5]), (held[1], held[3], held[6], held[7])]

    def begin(self, i, held):
        pass

    def finish(self, i, o, held):
        axis = 0 if self.incoming else 1

        def step(pair):
            lefts, rights = join_channels(held[2], pair), join_channels(held[3], pair)
            found = []
            for index in range(2):
                o.left[2 * pair + index] = lefts[index]
                o.right[2 * pair + index] = rights[index]
                found.append(product_of(lefts[index], rights[index], axis, axis))
            split_channels(o.tri, pair, *found)

        each_pair(step)


class Backward:
    wires = 1

    def __init__(self, peers, half, rows, tokens, incoming):
        self.peers, self.half, self.incoming = peers, half, incoming
        self.rows, self.tokens = rows * SUBLANES, tokens
        self.chunks = rows // SUBLANES

    def outs(self):
        wire = (self.peers, self.rows, self.tokens)
        return dict(grad_left=Out(wire, BF16, WHOLE), grad_right=Out(wire, BF16, WHOLE))

    def scratch(self):
        low = pltpu.VMEM((self.peers, self.rows, self.tokens), BF16)
        block = pltpu.VMEM((SUBLANES, self.tokens, self.tokens), BF16)
        many = pltpu.SemaphoreType.DMA((self.chunks, self.peers))
        return [low] * 2 + [block] * 2 + [many] * 2 + [pltpu.SemaphoreType.DMA((2,))]

    def moves(self, held):
        return [(held[0], held[1], held[4], held[5])]

    def owned(self, i, held):
        return [
            pltpu.make_async_copy(i.owned.left, held[2], held[6].at[0]),
            pltpu.make_async_copy(i.owned.right, held[3], held[6].at[1]),
        ]

    def begin(self, i, held):
        for copy in self.owned(i, held):
            copy.start()

    def finish(self, i, o, held):
        for copy in self.owned(i, held):
            copy.wait()

        def step(pair):
            lefts, rights = [], []
            for index, grad in enumerate(join_channels(held[1], pair)):
                left, right = held[2][2 * pair + index], held[3][2 * pair + index]
                if self.incoming:
                    lefts.append(product_of(right, grad, 1, 1))
                    rights.append(product_of(left, grad, 1, 0))
                else:
                    lefts.append(product_of(grad, right, 1, 0))
                    rights.append(product_of(grad, left, 0, 0))
            split_channels(o.grad_left, pair, *lefts)
            split_channels(o.grad_right, pair, *rights)

        each_pair(step)


def prepare(triangle_input, triangle_output, expand_weight, reduce_weight, distogram_weight, norm_gains):
    merged = [
        triangle_input.reshape((-1,) + triangle_input.shape[2:]),
        triangle_output.reshape((-1,) + triangle_output.shape[2:]),
        expand_weight,
        reduce_weight,
        distogram_weight.T[None],
    ]
    count = len(merged)

    def kernel(*refs):
        for source, plain, turned in zip(refs[:count], refs[count + 1 :: 2], refs[count + 2 :: 2]):
            for index in range(source.shape[0]):
                value = source[index]
                plain[index] = value.astype(BF16)
                turned[index] = value.T.astype(BF16)
        gains = refs[count][...]
        refs[-1][...] = gains.T

    shapes = []
    for array in merged:
        depth, rows, cols = array.shape
        shapes.append(jax.ShapeDtypeStruct((depth, rows, cols), BF16))
        shapes.append(jax.ShapeDtypeStruct((depth, cols, rows), BF16))
    shapes.append(jax.ShapeDtypeStruct(norm_gains.shape[::-1], F32))
    return pl.pallas_call(
        kernel,
        out_shape=shapes,
        compiler_params=pltpu.CompilerParams(vmem_limit_bytes=VMEM_BYTES),
        name="prepare",
    )(*merged, norm_gains)


def by_crop(value, rows_axis, head_axis):
    count, heads = rows_axis, head_axis
    half = count // 2
    inner = half // 2 * heads
    same, other = [], []
    for row in range(count):
        place = row % inner // heads * 2 + row // inner
        for head in range(heads):
            source = row * heads + head
            for crop, pairs in ((head, same), (1 - head, other)):
                pairs.append((source, (crop * half + place) * heads + row % heads))
    head = lax.axis_index("head")
    crop = lax.axis_index("row") // half
    mine = lax.dynamic_index_in_dim(value, head, 0, keepdims=False)
    rest = lax.dynamic_index_in_dim(value, 1 - head, 0, keepdims=False)
    mine = lax.ppermute(mine, ("row", "head"), same)
    rest = lax.ppermute(rest, ("row", "head"), other)
    low = jnp.where(crop == 0, mine, rest)
    high = jnp.where(crop == 0, rest, mine)
    return jnp.concatenate([low, high], axis=-1)


def reduce_rest(half, peers, collective_id, grids, gains, rows):
    sizes = [grid.shape[0] * grid.shape[1] // LANES for grid in grids]
    used = sum(sizes) + len(gains) + SUBLANES * len(rows)
    part = -(-used // (peers * SUBLANES)) * SUBLANES
    total = part * peers
    starts, spot = [], 0
    for size in sizes:
        starts.append(spot)
        spot += size
    row_starts = []
    for _ in rows:
        row_starts.append(spot)
        spot += SUBLANES
    gain_start = spot
    count = len(grids) + len(gains) + len(rows)

    def kernel(*refs):
        out, local, got, mine, other, sends, recvs, back_sends, back_recvs, twin_sems = refs[count:]
        ring = Exchange(peers, half)
        ring.greet()
        barrier = pltpu.get_barrier_semaphore()
        pl.semaphore_signal(barrier, inc=1, device_id=ring.twin, device_id_type=MESH)
        for grid, start in zip(refs[: len(grids)], starts):
            height, width = grid.shape
            for column in range(width // LANES):
                local[pl.ds(start + column * height, height), :] = grid[
                    :, column * LANES : (column + 1) * LANES
                ]
        ones = jnp.ones((SUBLANES, LANES), F32)
        for index, gain in enumerate(refs[len(grids) : len(grids) + len(gains)]):
            folded = lax.dot_general(
                ones,
                gain[...],
                (((1,), (1,)), ((), ())),
                precision=lax.Precision.HIGHEST,
                preferred_element_type=F32,
            )
            local[pl.ds(gain_start + index, 1), :] = folded[:1]
        for row, start in zip(refs[len(grids) + len(gains) : count], row_starts):
            local[pl.ds(start, 1), :] = row[...]
            local[pl.ds(start + 1, SUBLANES - 1), :] = jnp.zeros((SUBLANES - 1, LANES), F32)
        tail = gain_start + len(gains)
        if total > tail:
            local[pl.ds(tail, total - tail), :] = jnp.zeros((total - tail, LANES), F32)
        pl.semaphore_wait(barrier, peers)

        def block(peer):
            return pl.ds(pl.multiple_of(peer * part, SUBLANES), part)

        here = block(ring.me)

        def gather(step):
            peer = ring.peer(step)
            return pltpu.make_async_remote_copy(
                src_ref=local.at[block(peer), :],
                dst_ref=got.at[here, :],
                send_sem=sends.at[step],
                recv_sem=recvs.at[step],
                device_id=ring.device(peer),
                device_id_type=MESH,
            )

        def spread(step):
            return pltpu.make_async_remote_copy(
                src_ref=out.at[here, :],
                dst_ref=out.at[here, :],
                send_sem=back_sends.at[step],
                recv_sem=back_recvs.at[step],
                device_id=ring.device(ring.peer(step)),
                device_id_type=MESH,
            )

        for step in ring.order:
            gather(step).start()
        got[here, :] = local[here, :]
        for step in ring.order:
            gather(step).wait()
        value = got[pl.ds(0, part), :]
        for peer in range(1, peers):
            value = value + got[pl.ds(peer * part, part), :]
        mine[...] = value
        copy = pltpu.make_async_remote_copy(
            src_ref=mine,
            dst_ref=other,
            send_sem=twin_sems.at[0],
            recv_sem=twin_sems.at[1],
            device_id=ring.twin,
            device_id_type=MESH,
        )
        copy.start()
        copy.wait()
        out[here, :] = mine[...] + other[...]
        for step in ring.order:
            spread(step).start()
        for step in ring.order:
            spread(step).wait()

    inside = pl.BlockSpec(memory_space=pltpu.VMEM)
    whole = pl.pallas_call(
        kernel,
        in_specs=[inside] * count,
        out_specs=inside,
        out_shape=jax.ShapeDtypeStruct((total, LANES), F32),
        scratch_shapes=[pltpu.VMEM((total, LANES), F32)] * 2
        + [pltpu.VMEM((part, LANES), F32)] * 2
        + [pltpu.SemaphoreType.DMA((peers,))] * 4
        + [pltpu.SemaphoreType.DMA((2,))],
        compiler_params=pltpu.CompilerParams(
            collective_id=collective_id, has_side_effects=True, vmem_limit_bytes=VMEM_BYTES
        ),
        cost_estimate=pl.CostEstimate(flops=0, bytes_accessed=0, transcendentals=0),
        name="reduce_rest",
    )(*grids, *gains, *rows)
    return whole, starts, row_starts, gain_start


def update(rest, starts, row_starts, gain_start, early, weights, firsts, seconds):
    layers, kinds, width, mixed = weights[2].shape
    hidden = weights[4].shape[2]
    early_in, early_up, early_rows = early
    given = [rest, *early_in, *early_up, *early_rows]
    count = len(given)

    def kernel(*refs):
        whole = refs[0]
        in_refs = refs[1 : 1 + len(early_in)]
        up_refs = refs[1 + len(early_in) : count - layers]
        row_refs = refs[count - layers : count]
        states = [refs[count + 8 * kind : count + 8 * (kind + 1)] for kind in range(3)]
        scalars = refs[count + 24 : count + 27]
        results = refs[count + 27 :]

        def taken(start, size):
            return whole[pl.ds(start, size), :]

        def wide(start, height, columns):
            return jnp.concatenate(
                [taken(start + column * height, height) for column in range(columns)], axis=1
            )

        loss = jnp.sum(taken(row_starts[0], 1), axis=1, keepdims=True)
        valid = jnp.sum(taken(row_starts[1], 1), axis=1, keepdims=True)
        table_rows, single_rows = weights[0].shape[0], weights[1].shape[0]
        downs = hidden // 2
        grads = {}
        grads[0, ()] = taken(starts[4], table_rows)
        grads[1, ()] = jnp.concatenate(
            [taken(starts[5], single_rows), taken(starts[6], single_rows)], axis=1
        )
        for layer in range(layers):
            spot = 0
            for kind in range(kinds):
                if layer == 0:
                    grads[2, (layer, kind)] = wide(starts[kind], width, mixed // LANES)
                else:
                    grads[2, (layer, kind)] = in_refs[(layer - 1) * kinds + kind][...]
                if layer == 0 and kind == 0:
                    grads[3, (layer, kind)] = taken(starts[2], width)
                else:
                    grads[3, (layer, kind)] = row_refs[layer][pl.ds(spot, width), :]
                    spot += width
            grads[4, (layer,)] = up_refs[layer][...]
            grads[5, (layer,)] = row_refs[layer][pl.ds(spot, downs), :]
        grads[6, ()] = taken(starts[3], weights[6].shape[0])
        grads[7, ()] = taken(gain_start, weights[7].shape[0])
        squares = jnp.zeros((1, 1), F32)
        for key in grads:
            grads[key] = grads[key] / valid
            squares = squares + jnp.sum(grads[key] * grads[key], axis=(0, 1), keepdims=True)
        norm = jnp.sqrt(squares)
        factor = jnp.minimum(1.0, CLIP_NORM / (norm + 1e-06))
        for ref, value in zip(scalars, (loss, valid, norm)):
            ref[...] = value
        for (index, spot), grad in grads.items():
            rate = GAIN_RATE if index == 7 else WEIGHT_RATE
            decay = 0.0 if index == 7 else WEIGHT_DECAY
            new = adamw(
                states[0][index][spot],
                grad * factor,
                states[1][index][spot],
                states[2][index][spot],
                rate,
                decay,
            )
            for ref, value in zip(results[3 * index : 3 * index + 3], new):
                ref[spot] = value

    one = jax.ShapeDtypeStruct((1, 1), F32)
    shapes = [one] * 3
    for weight in weights:
        shapes += [jax.ShapeDtypeStruct(weight.shape, F32)] * 3
    found = pl.pallas_call(
        kernel,
        out_shape=shapes,
        compiler_params=pltpu.CompilerParams(vmem_limit_bytes=VMEM_BYTES),
        name="update",
    )(*given, *weights, *firsts, *seconds)
    return tuple(value[0, 0] for value in found[:3]) + tuple(found[3:])


def step_by_crop(row_count, head_count, given, weights, firsts, seconds):
    single, residue_index, chain_index, token_mask, pair_valid, target_bins = given
    relative_table, single_weight, triangle_input, triangle_output = weights[:4]
    expand_weight, reduce_weight, distogram_weight, norm_gains = weights[4:]
    crops, tokens = token_mask.shape
    width = relative_table.shape[1]
    layers = triangle_input.shape[0]
    half = row_count // crops
    peers = half * head_count
    rows = tokens // peers
    row_index = lax.axis_index("row")
    crop = row_index // half
    start = position(row_index % half, lax.axis_index("head"), half, head_count) * rows

    placed = by_crop(jnp.stack([pair_valid, target_bins], axis=1), row_count, head_count)
    valid, target = placed[0], placed[1]

    def of_crop(array):
        return lax.dynamic_index_in_dim(array, crop, 0, keepdims=False)

    def of_rows(array):
        return lax.dynamic_slice_in_dim(array, start, rows, 0)

    residues, chains = of_crop(residue_index), of_crop(chain_index)
    reach = (relative_table.shape[0] - 2) // 2
    bins = jnp.where(
        of_rows(chains)[:, None] == chains[None, :],
        jnp.clip(of_rows(residues)[:, None] - residues[None, :], -reach, reach) + reach,
        2 * reach + 1,
    )
    present = of_crop(token_mask).astype(F32)
    pair_mask = of_rows(present)[:, None] * present[None, :]
    loss_weight = pair_mask * valid.astype(F32)
    table_rows = -(-relative_table.shape[0] // PACKED) * PACKED
    table_t = jnp.pad(relative_table, ((0, table_rows - relative_table.shape[0]), (0, 0))).T
    tokens_single = of_crop(single)
    proj = project(tokens_single, single_weight.astype(BF16))
    proj_rows = of_rows(proj[:, :width])[:, :, None]
    proj_cols = proj[:, width:].T
    bins, pair_mask = Arg(bins[:, None, :], ROWS), Arg(pair_mask[:, None, :], ROWS)

    prepared = prepare(
        triangle_input, triangle_output, expand_weight, reduce_weight, distogram_weight, norm_gains
    )
    mix, mix_t, out, out_t, up, up_t, down, down_t, logits_t, logits, gains = prepared
    hidden = up.shape[2]

    def gain(index):
        return Arg(gains, WHOLE, column=index)

    def layer_of(array, index, *block):
        shape = block or array.shape[1:]
        return Arg(array, WHOLE, (index, 0, 0), (None,) + tuple(shape))

    def triangle_weights(layer, kind, starts=False, finishes=False, back=False):
        index = 2 * layer + kind
        found = dict(gain0=gain(5 * layer + 2 * kind))
        if starts:
            found.update(mix_t=layer_of(mix_t, index, 4 * width, width))
        if starts and back:
            found.update(mix=layer_of(mix, index))
        if finishes:
            found.update(
                gain1=gain(5 * layer + 2 * kind + 1),
                gate_t=Arg(mix_t, WHOLE, (index, 4, 0), (None, width, width)),
                out_t=layer_of(out_t, index),
            )
        if finishes and back:
            found.update(out=layer_of(out, index))
        return found

    def transition_weights(layer, forth=True, back=False):
        found = dict(gain=gain(5 * layer + 4), up_t=layer_of(up_t, layer))
        if forth:
            found.update(down_t=layer_of(down_t, layer))
        if back:
            found.update(up=layer_of(up, layer), down=layer_of(down, layer))
        return found

    def state_out():
        return Out((rows, width, tokens), F32, ROWS)

    def sum_out(*shape):
        return Out(shape, F32, SUM)

    def gain_out():
        return sum_out(width, LANES)

    def back_start_outs():
        return dict(
            grad_gate=Out((rows, width, tokens), BF16, ROWS),
            out=sum_out(width, width),
            gain1=gain_out(),
        )

    def back_finish_outs():
        return dict(mix=sum_out(width, 5 * width), gain0=gain_out())

    def transition_outs():
        return dict(up=sum_out(width, hidden), down=sum_out(hidden // 2, width), gain=gain_out())

    identities = iter(range(4 * layers + 2))

    def forward(incoming):
        return Forward(peers, half, rows, tokens, incoming)

    def backward(incoming):
        return Backward(peers, half, rows, tokens, incoming)

    def wire(array):
        return Arg(array, WIRE, half=half)

    def landed_out():
        return Out((peers, rows * SUBLANES, tokens), BF16, LANDED)

    def owned(kept):
        return dict(left=Arg(kept.left, ANYWHERE), right=Arg(kept.right, ANYWHERE))

    kept, states, middles, tris = {}, {}, {}, {}

    def first_body(i, o, rows, *wires):
        state = dot(i.table_t[...], bins_hot(i.bins, rows, table_rows))
        yield
        cols = i.proj_cols[...]
        state = state + jnp.concatenate([cols + i.proj_rows[row] for row in rows], axis=1)
        write_rows(o.state, rows, state)
        yield from triangle_start(i.start, i, rows, wires, state)

    exchange = forward(False)
    got = run_stage(
        first_body,
        "first_state",
        next(identities),
            rows,
        dict(
            bins=bins,
            proj_rows=Arg(proj_rows, ROWS),
            proj_cols=Arg(proj_cols, WHOLE),
            table_t=Arg(table_t.astype(BF16), WHOLE),
            mask=pair_mask,
            start=triangle_weights(0, 0, starts=True),
        ),
        dict(state=state_out(), **exchange.outs()),
        exchange,
    )
    kept[0, 0], states[0, 0] = got, got.state

    def between_body(i, o, rows, *wires):
        state, _ = yield from triangle_finish(i.end, rows, i.tri, read_rows(i.state, rows))
        write_rows(o.state, rows, state)
        yield from triangle_start(i.start, i, rows, wires, state)

    def layer_end_body(i, o, rows, *wires):
        state, _ = yield from triangle_finish(i.end, rows, i.tri, read_rows(i.state, rows))
        write_rows(o.middle, rows, state)
        lifted = yield from transition(i.lift, state)
        state = state + dot(i.lift.down_t[...], lifted[5])
        yield
        write_rows(o.state, rows, state)
        yield from triangle_start(i.start, i, rows, wires, state)

    for layer in range(layers):
        exchange = forward(True)
        got = run_stage(
            between_body,
            "between_updates",
            next(identities),
            rows,
            dict(
                state=Arg(states[layer, 0], ROWS),
                tri=wire(kept[layer, 0].tri),
                mask=pair_mask,
                end=triangle_weights(layer, 0, finishes=True),
                start=triangle_weights(layer, 1, starts=True),
            ),
            dict(state=state_out(), landed=landed_out(), **exchange.outs()),
            exchange,
        )
        kept[layer, 1], states[layer, 1], tris[layer, 0] = got, got.state, got.landed
        if layer + 1 == layers:
            break
        exchange = forward(False)
        got = run_stage(
            layer_end_body,
            "layer_end",
            next(identities),
            rows,
            dict(
                state=Arg(states[layer, 1], ROWS),
                tri=wire(kept[layer, 1].tri),
                mask=pair_mask,
                end=triangle_weights(layer, 1, finishes=True),
                lift=transition_weights(layer),
                start=triangle_weights(layer + 1, 0, starts=True),
            ),
            dict(middle=state_out(), state=state_out(), landed=landed_out(), **exchange.outs()),
            exchange,
        )
        tris[layer, 1] = got.landed
        kept[layer + 1, 0], states[layer + 1, 0] = got, got.state
        middles[layer] = got.middle

    def loss_body(i, o, rows, sent):
        state, kept_triangle = yield from triangle_finish(
            i.end, rows, i.tri, read_rows(i.state, rows)
        )
        lifted = yield from transition(i.lift, state)
        state = state + dot(i.lift.down_t[...], lifted[5])
        yield
        grad = yield from head_back(i.head, o.head, rows, state)
        grad = yield from transition_back(i.lift, o.lift, grad, lifted)
        write_rows(o.grad, rows, grad)
        yield from triangle_back_start(i.end, o.end, rows, sent, grad, kept_triangle)

    top = layers - 1
    exchange = backward(True)
    got = run_stage(
        loss_body,
        "loss",
        next(identities),
            rows,
        dict(
            state=Arg(states[top, 1], ROWS),
            tri=wire(kept[top, 1].tri),
            end=triangle_weights(top, 1, finishes=True, back=True),
            lift=transition_weights(top, back=True),
            head=dict(
                gain=gain(5 * layers),
                logits=layer_of(logits, 0),
                logits_t=layer_of(logits_t, 0),
                target=Arg(target[:, None, :], ROWS),
                weight=Arg(loss_weight[:, None, :], ROWS),
            ),
            owned=owned(kept[top, 1]),
        ),
        dict(
            grad=state_out(),
            head=dict(
                loss=sum_out(1, LANES),
                count=sum_out(1, LANES),
                logits=sum_out(distogram_weight.shape[1], width),
                gain=gain_out(),
            ),
            lift=transition_outs(),
            end=back_start_outs(),
            **exchange.outs(),
        ),
        exchange,
    )
    head, lifts, ends, begins = got.head, {top: got.lift}, {(top, 1): got.end}, {}

    def between_back_body(i, o, rows, sent):
        grad = yield from triangle_back_finish(i.start, i, o.start, rows)
        write_rows(o.grad, rows, grad)
        _, kept_triangle = yield from triangle_finish(
            i.end, rows, i.tri, read_rows(i.before, rows)
        )
        yield from triangle_back_start(i.end, o.end, rows, sent, grad, kept_triangle)

    def layer_end_back_body(i, o, rows, sent):
        grad = yield from triangle_back_finish(i.start, i, o.start, rows)
        lifted = yield from transition(i.lift, read_rows(i.middle, rows))
        grad = yield from transition_back(i.lift, o.lift, grad, lifted)
        write_rows(o.grad, rows, grad)
        _, kept_triangle = yield from triangle_finish(
            i.end, rows, i.tri, read_rows(i.before, rows)
        )
        yield from triangle_back_start(i.end, o.end, rows, sent, grad, kept_triangle)

    def first_back_body(i, o, rows):
        grad = yield from triangle_back_finish(i.start, i, o.start, rows)
        hot = bins_hot(i.bins, rows, table_rows)
        high = grad.astype(BF16)
        low = (grad - high.astype(F32)).astype(BF16)
        o.table[...] += dot_pairs(hot, high) + dot_pairs(hot, low)
        yield
        for place, row in enumerate(rows):
            part = grad[:, place * tokens : (place + 1) * tokens]
            o.rows[row] = fold(part)
            o.cols[...] += part

    def layer_sums(layer):
        kinds = (0, 1) if layer else (1,)
        mixes = [begins[layer, 1].mix] if layer else []
        if layer + 1 < layers:
            mixes.append(begins[layer + 1, 0].mix)
        outs = [ends[layer, kind].out for kind in kinds]
        return (mixes, lifts[layer].up, jnp.concatenate(outs + [lifts[layer].down], axis=0))

    early = {}
    for layer in reversed(range(layers)):
        for kind in (1, 0):
            if (layer, kind) == (0, 0):
                early, got.grad = lax.optimization_barrier((early, got.grad))
            inputs = dict(
                grad=Arg(got.grad, ROWS),
                state=Arg(states[layer, kind], ROWS),
                mask=pair_mask,
                start=triangle_weights(layer, kind, starts=True, back=True),
                back=dict(
                    grad_left=wire(got.grad_left),
                    grad_right=wire(got.grad_right),
                    grad_gate=Arg(got.end.grad_gate, ROWS),
                ),
            )
            outputs = dict(start=back_finish_outs())
            if layer == 0 and kind == 0:
                got = run_stage(
                    first_back_body,
                    "first_state_back",
                    next(identities),
            rows,
                    dict(bins=bins, **inputs),
                    dict(
                        table=sum_out(table_rows, width),
                        rows=Out((rows, width, LANES), F32, ROWS),
                        cols=sum_out(width, tokens),
                        **outputs,
                    ),
                )
                begins[layer, kind] = got.start
                break
            before = (layer, 0) if kind == 1 else (layer - 1, 1)
            inputs.update(
                before=Arg(states[before], ROWS),
                tri=Arg(tris[before], LANDED),
                end=triangle_weights(*before, finishes=True, back=True),
                owned=owned(kept[before]),
            )
            outputs.update(grad=state_out(), end=back_start_outs())
            if kind == 1:
                exchange = backward(False)
                body, name = between_back_body, "between_updates_back"
            else:
                exchange = backward(True)
                body, name = layer_end_back_body, "layer_end_back"
                inputs.update(
                    middle=Arg(middles[layer - 1], ROWS),
                    lift=transition_weights(layer - 1, forth=False, back=True),
                )
                outputs.update(lift=transition_outs())
            got = run_stage(
                body,
                name,
                next(identities),
                rows,
                inputs,
                dict(**outputs, **exchange.outs()),
                exchange,
            )
            begins[layer, kind], ends[before] = got.start, got.end
            if kind == 0:
                lifts[layer - 1] = got.lift
            ready = layer if kind == 1 else layer - 1
            if ready == 0 and kind == 1 or ready > 0 and kind == 0:
                continue
            group = layer_sums(ready)
            if early:
                group, early, got.grad = lax.optimization_barrier((group, early, got.grad))
            early[ready] = lax.psum(group, ("row", "head"))

    early_mixes = {}
    for layer in range(layers):
        mixes = list(early[layer][0])
        if layer:
            early_mixes[layer, 1] = mixes.pop(0)
        if mixes:
            early_mixes[layer + 1, 0] = mixes.pop(0)
    early = (
        [early_mixes[layer, kind] for layer in range(1, layers) for kind in range(2)],
        [early[layer][1] for layer in range(layers)],
        [early[layer][2] for layer in range(layers)],
    )

    wide_single = tokens_single.astype(F32)
    row_part = jnp.einsum(
        "is,ic->sc",
        of_rows(wide_single),
        jnp.sum(got.rows, axis=2),
        precision=lax.Precision.HIGHEST,
    )
    col_part = jnp.einsum("js,cj->sc", wide_single, got.cols, precision=lax.Precision.HIGHEST)
    partial_gains = []
    for layer in range(layers):
        for kind in range(2):
            partial_gains += [begins[layer, kind].gain0, ends[layer, kind].gain1]
        partial_gains.append(lifts[layer].gain)
    partial_gains.append(head.gain)
    grids = [
        begins[0, 0].mix,
        begins[0, 1].mix,
        ends[0, 0].out,
        head.logits,
        got.table,
        row_part,
        col_part,
    ]
    def turned(arrays):
        return arrays[:6] + (arrays[6].T,) + arrays[7:]

    rest, *starts = reduce_rest(
        half, peers, next(identities), grids, partial_gains, [head.loss, head.count]
    )
    found = update(rest, *starts, early, turned(weights), turned(firsts), turned(seconds))
    return found[:21] + tuple(value.T for value in found[21:24]) + found[24:]


def per_device(
    row_count,
    head_count,
    single,
    residue_index,
    chain_index,
    token_mask,
    pair_valid,
    target_bins,
    relative_table,
    single_weight,
    triangle_input,
    triangle_output,
    expand_weight,
    reduce_weight,
    distogram_weight,
    norm_gains,
    first_table,
    second_table,
    first_single,
    second_single,
    first_input,
    second_input,
    first_output,
    second_output,
    first_expand,
    second_expand,
    first_reduce,
    second_reduce,
    first_logits,
    second_logits,
    first_gains,
    second_gains,
):
    crops, tokens = token_mask.shape
    width = relative_table.shape[1]
    peers = row_count * head_count // crops
    given = (
        single,
        residue_index,
        chain_index,
        token_mask,
        pair_valid,
        target_bins,
        relative_table,
        single_weight,
        triangle_input,
        triangle_output,
        expand_weight,
        reduce_weight,
        distogram_weight,
        norm_gains,
    )
    weights = (
        relative_table,
        single_weight,
        triangle_input,
        triangle_output,
        expand_weight,
        reduce_weight,
        distogram_weight,
        norm_gains,
    )
    firsts = (
        first_table,
        first_single,
        first_input,
        first_output,
        first_expand,
        first_reduce,
        first_logits,
        first_gains,
    )
    seconds = (
        second_table,
        second_single,
        second_input,
        second_output,
        second_expand,
        second_reduce,
        second_logits,
        second_gains,
    )
    if (
        crops == 2
        and head_count == 2
        and width == LANES
        and width == SUBLANES * peers
        and tokens % (peers * SUBLANES) == 0
        and tokens % (3 * LANES) == 0
    ):
        return step_by_crop(row_count, head_count, given[:6], weights, firsts, seconds)
    local = gradients_by_block(*given)
    summed = lax.psum(local, ("row", "head"))
    loss_sum, valid_count = summed[0], summed[1]
    grads = [grad / valid_count for grad in summed[2:]]
    squares = jnp.zeros((), jnp.float32)
    for g in grads:
        squares = squares + jnp.sum(g * g)
    gradient_norm = jnp.sqrt(squares)
    factor = jnp.minimum(1.0, CLIP_NORM / (gradient_norm + 1e-06))
    result = []
    for index in range(8):
        rate = GAIN_RATE if index == 7 else WEIGHT_RATE
        decay = 0.0 if index == 7 else WEIGHT_DECAY
        result.extend(
            adamw(weights[index], grads[index] * factor, firsts[index], seconds[index], rate, decay)
        )
    return (
        loss_sum,
        valid_count,
        gradient_norm,
        result[0],
        result[1],
        result[2],
        result[3],
        result[4],
        result[5],
        result[6],
        result[7],
        result[8],
        result[9],
        result[10],
        result[11],
        result[12],
        result[13],
        result[14],
        result[15],
        result[16],
        result[17],
        result[18],
        result[19],
        result[20],
        result[21],
        result[22],
        result[23],
    )


def solution(mesh):
    placed = (
        P(),
        P(),
        P(),
        P(),
        P(None, "row", "head"),
        P(None, "row", "head"),
        P(),
        P(),
        P(),
        P(),
        P(),
        P(),
        P(),
        P(),
        P(),
        P(),
        P(),
        P(),
        P(),
        P(),
        P(),
        P(),
        P(),
        P(),
        P(),
        P(),
        P(),
        P(),
        P(),
        P(),
    )
    return jax.shard_map(
        functools.partial(per_device, mesh.shape["row"], mesh.shape["head"]),
        mesh=mesh,
        in_specs=placed,
        out_specs=(
            P(),
            P(),
            P(),
            P(),
            P(),
            P(),
            P(),
            P(),
            P(),
            P(),
            P(),
            P(),
            P(),
            P(),
            P(),
            P(),
            P(),
            P(),
            P(),
            P(),
            P(),
            P(),
            P(),
            P(),
            P(),
            P(),
            P(),
        ),
        check_vma=False,
    )
```

```python
import functools

import jax
import jax.numpy as jnp
from jax import lax
from jax.experimental import pallas as pl
from jax.experimental.pallas import tpu as pltpu
from jax.sharding import PartitionSpec as P

STEP = 10


EPS = 1e-05
BETA_ONE = 0.9
BETA_TWO = 0.999
ADAM_EPS = 1e-08
WEIGHT_RATE = 0.1
GAIN_RATE = 0.5
WEIGHT_DECAY = 0.01
CLIP_NORM = 0.002


def normalize(value):
    mean = jnp.mean(value, axis=-1, keepdims=True)
    centred = value - mean
    scale = lax.rsqrt(jnp.mean(centred * centred, axis=-1, keepdims=True) + EPS)
    return (centred * scale, scale)


def norm_back(grad_out, unit, scale, gain):
    scaled = grad_out * gain
    first_mean = jnp.mean(scaled, axis=-1, keepdims=True)
    second_mean = jnp.mean(scaled * unit, axis=-1, keepdims=True)
    grad_in = scale * (scaled - first_mean - unit * second_mean)
    grad_gain = jnp.sum(grad_out * unit, axis=tuple(range(grad_out.ndim - 1)))
    return (grad_in, grad_gain)


def project(value, weight):
    return jnp.einsum("...c,cd->...d", value, weight, preferred_element_type=jnp.float32)


def project_back(grad, weight):
    return jnp.einsum("...d,cd->...c", grad, weight, preferred_element_type=jnp.float32)


def weight_grad(value, grad):
    return jnp.einsum("bijc,bijd->cd", value, grad, preferred_element_type=jnp.float32)


def triangle_forward(state, weight_in, weight_out, gains, pair_mask, incoming):
    hidden = weight_out.shape[0]
    pair_unit, pair_scale = normalize(state)
    normed = (pair_unit * gains[0]).astype(jnp.bfloat16)
    mixed = project(normed, weight_in)
    mask = pair_mask[..., None]
    left = (mask * jax.nn.sigmoid(mixed[..., :hidden]) * mixed[..., hidden : 2 * hidden]).astype(
        jnp.bfloat16
    )
    right = (
        mask
        * jax.nn.sigmoid(mixed[..., 2 * hidden : 3 * hidden])
        * mixed[..., 3 * hidden : 4 * hidden]
    ).astype(jnp.bfloat16)
    left_cols, right_cols = (
        lax.all_to_all(left, "head", split_axis=3, concat_axis=2, tiled=True),
        lax.all_to_all(right, "head", split_axis=3, concat_axis=2, tiled=True),
    )
    if incoming:
        left_cols, right_cols = (
            lax.all_to_all(left_cols, "row", split_axis=2, concat_axis=1, tiled=True),
            lax.all_to_all(right_cols, "row", split_axis=2, concat_axis=1, tiled=True),
        )
        left_cols = jnp.swapaxes(left_cols, 1, 2)
        right_cols = jnp.swapaxes(right_cols, 1, 2)
    right_all = lax.all_gather(right_cols, "row", axis=1, tiled=True)
    triangle = jnp.einsum(
        "bikc,bjkc->bijc", left_cols, right_all, preferred_element_type=jnp.float32
    )
    triangle = lax.all_to_all(
        triangle.astype(jnp.bfloat16), "head", split_axis=2, concat_axis=3, tiled=True
    )
    tri_unit, tri_scale = normalize(triangle.astype(jnp.float32))
    shaped = (tri_unit * gains[1]).astype(jnp.bfloat16)
    branch = project(shaped, weight_out)
    gate = jax.nn.sigmoid(mixed[..., 4 * hidden :])
    kept = (
        pair_unit,
        pair_scale,
        normed,
        mixed,
        left_cols,
        right_all,
        tri_unit,
        tri_scale,
        shaped,
        branch,
        gate,
    )
    return (state + gate * branch, kept)


def triangle_backward(grad_state, kept, weight_in, weight_out, gains, pair_mask, incoming):
    hidden = weight_out.shape[0]
    (
        pair_unit,
        pair_scale,
        normed,
        mixed,
        left_cols,
        right_all,
        tri_unit,
        tri_scale,
        shaped,
        branch,
        gate,
    ) = kept
    grad_branch = (grad_state * gate).astype(jnp.bfloat16)
    grad_gate = grad_state * branch * gate * (1.0 - gate)
    grad_out = weight_grad(shaped, grad_branch)
    grad_shaped = project_back(grad_branch, weight_out)
    grad_tri, gain_two = norm_back(grad_shaped, tri_unit, tri_scale, gains[1])
    tri_cols = lax.all_to_all(
        grad_tri.astype(jnp.bfloat16), "head", split_axis=3, concat_axis=2, tiled=True
    )
    grad_left = jnp.einsum(
        "bijc,bjkc->bikc", tri_cols, right_all, preferred_element_type=jnp.float32
    )
    grad_left = grad_left.astype(jnp.bfloat16)
    summed = lax.psum_scatter(
        jnp.einsum(
            "bijc,bikc->jbkc", tri_cols, left_cols, preferred_element_type=jnp.float32
        ).astype(jnp.bfloat16),
        "row",
        scatter_dimension=0,
        tiled=True,
    ).astype(jnp.float32)
    grad_right = jnp.transpose(summed, (1, 0, 2, 3)).astype(jnp.bfloat16)
    if incoming:
        grad_left, grad_right = (
            lax.all_to_all(
                jnp.swapaxes(grad_left, 1, 2), "row", split_axis=1, concat_axis=2, tiled=True
            ),
            lax.all_to_all(
                jnp.swapaxes(grad_right, 1, 2), "row", split_axis=1, concat_axis=2, tiled=True
            ),
        )
    back_left, back_right = (
        lax.all_to_all(grad_left, "head", split_axis=2, concat_axis=3, tiled=True),
        lax.all_to_all(grad_right, "head", split_axis=2, concat_axis=3, tiled=True),
    )
    mask = pair_mask[..., None]
    back_left = back_left.astype(jnp.float32) * mask
    back_right = back_right.astype(jnp.float32) * mask
    left_sig = jax.nn.sigmoid(mixed[..., :hidden])
    left_value = mixed[..., hidden : 2 * hidden]
    right_sig = jax.nn.sigmoid(mixed[..., 2 * hidden : 3 * hidden])
    right_value = mixed[..., 3 * hidden : 4 * hidden]
    grad_mixed = jnp.concatenate(
        [
            back_left * left_value * left_sig * (1.0 - left_sig),
            back_left * left_sig,
            back_right * right_value * right_sig * (1.0 - right_sig),
            back_right * right_sig,
            grad_gate,
        ],
        axis=-1,
    ).astype(jnp.bfloat16)
    grad_in = weight_grad(normed, grad_mixed)
    grad_normed = project_back(grad_mixed, weight_in)
    grad_first, gain_one = norm_back(grad_normed, pair_unit, pair_scale, gains[0])
    return (grad_state + grad_first, (grad_in, grad_out, gain_one, gain_two))


def transition_forward(state, weight_up, weight_down, gain):
    expand = weight_down.shape[0]
    unit, scale = normalize(state)
    lifted = (unit * gain).astype(jnp.bfloat16)
    inner = project(lifted, weight_up)
    product = (jax.nn.silu(inner[..., :expand]) * inner[..., expand:]).astype(jnp.bfloat16)
    return (state + project(product, weight_down), (unit, scale, lifted, inner, product))


def transition_backward(grad_state, kept, weight_up, weight_down, gain):
    expand = weight_down.shape[0]
    unit, scale, lifted, inner, product = kept
    grad_low = grad_state.astype(jnp.bfloat16)
    grad_down = weight_grad(product, grad_low)
    grad_product = project_back(grad_low, weight_down)
    gate_part = inner[..., :expand]
    up_part = inner[..., expand:]
    gate_sig = jax.nn.sigmoid(gate_part)
    silu_value = gate_part * gate_sig
    silu_slope = gate_sig * (1.0 + gate_part * (1.0 - gate_sig))
    grad_inner = jnp.concatenate(
        [grad_product * up_part * silu_slope, grad_product * silu_value], axis=-1
    )
    grad_inner = grad_inner.astype(jnp.bfloat16)
    grad_up = weight_grad(lifted, grad_inner)
    grad_lifted = project_back(grad_inner, weight_up)
    grad_middle, gain_grad = norm_back(grad_lifted, unit, scale, gain)
    return (grad_middle + grad_state, (grad_up, grad_down, gain_grad))


def block_forward(state, weight_in, weight_out, weight_up, weight_down, gains, pair_mask):
    first, kept_one = triangle_forward(
        state, weight_in[0], weight_out[0], gains[0:2], pair_mask, False
    )
    second, kept_two = triangle_forward(
        first, weight_in[1], weight_out[1], gains[2:4], pair_mask, True
    )
    output, kept_three = transition_forward(second, weight_up, weight_down, gains[4])
    return (output, (kept_one, kept_two, kept_three))


def block_backward(
    grad_state, state, weight_in, weight_out, weight_up, weight_down, gains, pair_mask
):
    skipped, kept = block_forward(
        state, weight_in, weight_out, weight_up, weight_down, gains, pair_mask
    )
    kept_one, kept_two, kept_three = kept
    grad_state, (grad_up, grad_down, gain_five) = transition_backward(
        grad_state, kept_three, weight_up, weight_down, gains[4]
    )
    grad_state, (in_two, out_two, gain_three, gain_four) = triangle_backward(
        grad_state, kept_two, weight_in[1], weight_out[1], gains[2:4], pair_mask, True
    )
    grad_state, (in_one, out_one, gain_one, gain_two) = triangle_backward(
        grad_state, kept_one, weight_in[0], weight_out[0], gains[0:2], pair_mask, False
    )
    return (
        grad_state,
        (
            jnp.stack([in_one, in_two]),
            jnp.stack([out_one, out_two]),
            grad_up,
            grad_down,
            jnp.stack([gain_one, gain_two, gain_three, gain_four, gain_five]),
        ),
    )


def adamw(weight, grad, first, second, rate, decay):
    first_new = BETA_ONE * first + (1.0 - BETA_ONE) * grad
    second_new = BETA_TWO * second + (1.0 - BETA_TWO) * grad * grad
    moved = (
        first_new
        / (1.0 - BETA_ONE**STEP)
        / (jnp.sqrt(second_new / (1.0 - BETA_TWO**STEP)) + ADAM_EPS)
    )
    return (first_new, second_new, weight - rate * (moved + decay * weight))


def gradients_by_block(
    single,
    residue_index,
    chain_index,
    token_mask,
    pair_valid,
    target_bins,
    relative_table,
    single_weight,
    triangle_input,
    triangle_output,
    expand_weight,
    reduce_weight,
    distogram_weight,
    norm_gains,
):
    crops, rows, cols = pair_valid.shape
    width = relative_table.shape[1]
    layers = triangle_input.shape[0]
    row_start = lax.axis_index("row") * rows
    col_start = lax.axis_index("head") * cols

    def take(array, start, count):
        return lax.dynamic_slice_in_dim(array, start, count, 1)

    offset = (
        take(residue_index, row_start, rows)[:, :, None]
        - take(residue_index, col_start, cols)[:, None, :]
    )
    same = (
        take(chain_index, row_start, rows)[:, :, None]
        == take(chain_index, col_start, cols)[:, None, :]
    )
    reach = (relative_table.shape[0] - 2) // 2
    bins = jnp.where(same, jnp.clip(offset, -reach, reach) + reach, 2 * reach + 1)
    relative_hot = (
        bins[..., None] == jnp.arange(relative_table.shape[0])[None, None, None, :]
    ).astype(jnp.float32)
    token_rows = take(token_mask, row_start, rows).astype(jnp.float32)
    token_cols = take(token_mask, col_start, cols).astype(jnp.float32)
    pair_mask = token_rows[:, :, None] * token_cols[:, None, :]
    loss_weight = pair_mask * pair_valid.astype(jnp.float32)
    low_input = triangle_input.astype(jnp.bfloat16)
    low_output = triangle_output.astype(jnp.bfloat16)
    low_expand = expand_weight.astype(jnp.bfloat16)
    low_reduce = reduce_weight.astype(jnp.bfloat16)
    low_logits = distogram_weight.astype(jnp.bfloat16)
    proj = project(single, single_weight.astype(jnp.bfloat16))
    state = project(relative_hot.astype(jnp.bfloat16), relative_table.astype(jnp.bfloat16))
    state = (
        state
        + take(proj, row_start, rows)[:, :, None, :width]
        + take(proj, col_start, cols)[:, None, :, width:]
    )
    inputs = []
    for layer in range(layers):
        inputs.append(state)
        state, unused = block_forward(
            state,
            low_input[layer],
            low_output[layer],
            low_expand[layer],
            low_reduce[layer],
            norm_gains[5 * layer : 5 * layer + 5],
            pair_mask,
        )
    head_unit, head_scale = normalize(state)
    shown = (head_unit * norm_gains[5 * layers]).astype(jnp.bfloat16)
    logits = project(shown, low_logits)
    largest = jnp.max(logits, axis=-1, keepdims=True)
    log_total = largest + jnp.log(jnp.sum(jnp.exp(logits - largest), axis=-1, keepdims=True))
    target_hot = (
        target_bins[..., None] == jnp.arange(logits.shape[-1])[None, None, None, :]
    ).astype(jnp.float32)
    picked = jnp.sum(logits * target_hot, axis=-1)
    loss_local = jnp.sum(loss_weight * (log_total[..., 0] - picked))
    grad_scores = (loss_weight[..., None] * (jnp.exp(logits - log_total) - target_hot)).astype(
        jnp.bfloat16
    )
    grad_logits = weight_grad(shown, grad_scores)
    grad_shown = project_back(grad_scores, low_logits)
    grad_state, gain_last = norm_back(grad_shown, head_unit, head_scale, norm_gains[5 * layers])
    collected = []
    for layer in reversed(range(layers)):
        grad_state, layer_grads = block_backward(
            grad_state,
            inputs[layer],
            low_input[layer],
            low_output[layer],
            low_expand[layer],
            low_reduce[layer],
            norm_gains[5 * layer : 5 * layer + 5],
            pair_mask,
        )
        collected.insert(0, layer_grads)
    grad_input = jnp.stack([entry[0] for entry in collected])
    grad_output = jnp.stack([entry[1] for entry in collected])
    grad_expand = jnp.stack([entry[2] for entry in collected])
    grad_reduce = jnp.stack([entry[3] for entry in collected])
    grad_gains = jnp.concatenate(
        [jnp.concatenate([entry[4] for entry in collected], axis=0), gain_last[None]], axis=0
    )
    grad_table = jnp.einsum(
        "bijr,bijc->rc", relative_hot, grad_state, precision=lax.Precision.HIGHEST
    )
    single_wide = single.astype(jnp.float32)
    row_part = jnp.einsum(
        "bis,bic->sc",
        take(single_wide, row_start, rows),
        jnp.sum(grad_state, axis=2),
        precision=lax.Precision.HIGHEST,
    )
    col_part = jnp.einsum(
        "bjs,bjc->sc",
        take(single_wide, col_start, cols),
        jnp.sum(grad_state, axis=1),
        precision=lax.Precision.HIGHEST,
    )
    grad_single = jnp.concatenate([row_part, col_part], axis=1)
    return (
        loss_local,
        jnp.sum(loss_weight),
        grad_table,
        grad_single,
        grad_input,
        grad_output,
        grad_expand,
        grad_reduce,
        grad_logits,
        grad_gains,
    )


F32 = jnp.float32
BF16 = jnp.bfloat16
LANES = 128
SUBLANES = 8
PACKED = 16
ROW_BLOCK = 4
STREAM_ROWS = 2
PHASES = SUBLANES // ROW_BLOCK
CHUNK_ROWS = SUBLANES * SUBLANES
VMEM_BYTES = 58 * 2**20
MESH = pl.DeviceIdType.MESH
ROWS, WIRE, LANDED, WHOLE, SUM, ANYWHERE = range(6)


class Bag:
    def __init__(self, **entries):
        self.__dict__.update(entries)


class Arg:
    def __init__(self, array, kind, index=None, block=None, column=None, half=None):
        self.array, self.kind, self.index, self.block = array, kind, index, block
        self.column, self.half = column, half

    def spec(self):
        if self.index is None:
            return block_spec(self.array.shape, self.kind)
        index = self.index
        return pl.BlockSpec(self.block, lambda step: index)


class Column:
    def __init__(self, ref, column):
        self.ref, self.column = ref, column

    def __getitem__(self, _):
        return self.ref[:, self.column : self.column + 1]


class Out:
    def __init__(self, shape, dtype, kind):
        self.shape, self.dtype, self.kind = shape, dtype, kind

    def spec(self):
        return block_spec(self.shape, ANYWHERE if self.kind == LANDED else self.kind)


def block_spec(shape, kind):
    if kind in (WIRE, ANYWHERE):
        return pl.BlockSpec(memory_space=pl.ANY)
    if kind == LANDED:
        return pl.BlockSpec((shape[0], CHUNK_ROWS, shape[2]), lambda step: (0, step // PHASES, 0))
    if kind == ROWS:
        return pl.BlockSpec((ROW_BLOCK,) + shape[1:], lambda step: (step,) + (0,) * (len(shape) - 1))
    return pl.BlockSpec(shape, lambda step: (0,) * len(shape))


def is_leaf(value):
    return isinstance(value, (Arg, Out))


def bag_of(tree, leaves):
    return Bag(
        **{
            key: next(leaves) if is_leaf(value) else bag_of(value, leaves)
            for key, value in tree.items()
        }
    )


def leaves_of(tree):
    found = []
    for value in tree.values():
        found.extend([value] if is_leaf(value) else leaves_of(value))
    return found


def dot(left, right):
    return lax.dot_general(left, right, (((1,), (0,)), ((), ())), preferred_element_type=F32)


def dot_pairs(left, right):
    return lax.dot_general(left, right, (((1,), (1,)), ((), ())), preferred_element_type=F32)


def product_of(left, right, left_axis, right_axis):
    return lax.dot_general(
        left, right, (((left_axis,), (right_axis,)), ((), ())), preferred_element_type=F32
    )


def sigmoid(value):
    return 0.5 * jnp.tanh(0.5 * value) + 0.5


def unit_of(value):
    centred = value - jnp.mean(value, axis=0, keepdims=True)
    scale = lax.rsqrt(jnp.mean(centred * centred, axis=0, keepdims=True) + EPS)
    return (centred * scale, scale)


def unit_back(grad, unit, scale, gain):
    scaled = grad * gain
    first = jnp.mean(scaled, axis=0, keepdims=True)
    second = jnp.mean(scaled * unit, axis=0, keepdims=True)
    return scale * (scaled - first - unit * second)


def fold(value):
    total = value[:, :LANES]
    for start in range(LANES, value.shape[1], LANES):
        total = total + value[:, start : start + LANES]
    return total


def read_rows(ref, rows):
    return jnp.concatenate([ref[row] for row in rows], axis=1)


def write_rows(ref, rows, value):
    cols = ref.shape[2]
    for place, row in enumerate(rows):
        ref[row] = value[:, place * cols : (place + 1) * cols].astype(ref.dtype)


def alternate(streams):
    while streams:
        going = []
        for stream in streams:
            try:
                next(stream)
                going.append(stream)
            except StopIteration:
                pass
        streams = going


class Wire:
    def __init__(self, wide, phase):
        self.wide, self.phase = wide, phase

    def tokens(self, row):
        width = self.wide.shape[1] // SUBLANES
        return pl.ds(self.phase * ROW_BLOCK + row, width, stride=SUBLANES)

    def read(self, rows):
        lanes = self.wide.shape[0]
        return jnp.concatenate(
            [self.wide[lane, self.tokens(row), :] for row in rows for lane in range(lanes)], axis=1
        )

    def write(self, rows, value):
        lanes = self.wide.shape[0]
        for place, row in enumerate(rows):
            for lane in range(lanes):
                start = (place * lanes + lane) * LANES
                self.wide[lane, self.tokens(row), :] = value[:, start : start + LANES]


def widen(wide, low, chunk):
    rows = pl.ds(pl.multiple_of(chunk * CHUNK_ROWS, CHUNK_ROWS), CHUNK_ROWS)

    def step(peer, carry):
        value = low[peer, rows, :].astype(F32)
        start = pl.multiple_of(peer * CHUNK_ROWS, CHUNK_ROWS)
        for lane in range(wide.shape[0]):
            wide[lane, pl.ds(start, CHUNK_ROWS), :] = value[:, lane * LANES : (lane + 1) * LANES]
        return carry

    lax.fori_loop(0, low.shape[0], step, 0)


def narrow(low, wide, chunk):
    rows = pl.ds(pl.multiple_of(chunk * CHUNK_ROWS, CHUNK_ROWS), CHUNK_ROWS)

    def step(peer, carry):
        start = pl.multiple_of(peer * CHUNK_ROWS, CHUNK_ROWS)
        low[peer, rows, :] = jnp.concatenate(
            [wide[lane, pl.ds(start, CHUNK_ROWS), :] for lane in range(wide.shape[0])], axis=1
        ).astype(low.dtype)
        return carry

    lax.fori_loop(0, low.shape[0], step, 0)


def triangle_start(weights, i, rows, wires, state):
    width = state.shape[0]
    unit, _ = unit_of(state)
    normed = (unit * weights.gain0[...]).astype(BF16)
    mixed = dot(weights.mix_t[...], normed)
    yield
    mask = read_rows(i.mask, rows)
    for wire, base in zip(wires, (0, 2 * width)):
        gate = sigmoid(mixed[base : base + width])
        wire.write(rows, mask * gate * mixed[base + width : base + 2 * width])


def triangle_finish(weights, rows, wire, state):
    unit, _ = unit_of(state)
    normed = (unit * weights.gain0[...]).astype(BF16)
    opened = dot(weights.gate_t[...], normed)
    yield
    tri_unit, tri_scale = unit_of(wire.read(rows))
    shaped = (tri_unit * weights.gain1[...]).astype(BF16)
    branch = dot(weights.out_t[...], shaped)
    yield
    gate = sigmoid(opened)
    return (state + gate * branch, (gate, tri_unit, tri_scale, shaped, branch))


def triangle_back_start(weights, o, rows, wire, grad, kept):
    gate, tri_unit, tri_scale, shaped, branch = kept
    grad_branch = (grad * gate).astype(BF16)
    grad_shaped = dot(weights.out[...], grad_branch)
    yield
    o.out[...] += dot_pairs(shaped, grad_branch)
    write_rows(o.grad_gate, rows, grad * branch * gate * (1.0 - gate))
    yield
    o.gain1[...] += fold(grad_shaped * tri_unit)
    wire.write(rows, unit_back(grad_shaped, tri_unit, tri_scale, weights.gain1[...]))


def triangle_back_finish(weights, i, o, rows):
    grad, state = read_rows(i.grad, rows), read_rows(i.state, rows)
    width = state.shape[0]
    unit, scale = unit_of(state)
    gain = weights.gain0[...]
    normed = (unit * gain).astype(BF16)
    mixed = dot(weights.mix_t[...], normed)
    yield
    mask = read_rows(i.mask, rows)
    parts = []
    for wire, base in ((i.back.grad_left, 0), (i.back.grad_right, 2 * width)):
        back = wire.read(rows) * mask
        gate = sigmoid(mixed[base : base + width])
        back_gate = back * gate
        parts.append((back_gate * mixed[base + width : base + 2 * width] * (1.0 - gate)).astype(BF16))
        parts.append(back_gate.astype(BF16))
    parts.append(read_rows(i.back.grad_gate, rows))
    grad_mixed = jnp.concatenate(parts, axis=0)
    yield
    grad_normed = dot(weights.mix[...], grad_mixed)
    o.mix[...] += dot_pairs(normed, grad_mixed)
    yield
    o.gain0[...] += fold(grad_normed * unit)
    return grad + unit_back(grad_normed, unit, scale, gain)


def transition(weights, state):
    unit, scale = unit_of(state)
    lifted = (unit * weights.gain[...]).astype(BF16)
    inner = dot(weights.up_t[...], lifted)
    yield
    half = inner.shape[0] // 2
    gate = inner[:half]
    slope = sigmoid(gate)
    product = (gate * slope * inner[half:]).astype(BF16)
    return (unit, scale, lifted, inner, slope, product)


def transition_back(weights, o, grad, kept):
    unit, scale, lifted, inner, slope, product = kept
    half = inner.shape[0] // 2
    gate, up = inner[:half], inner[half:]
    grad_low = grad.astype(BF16)
    grad_product = dot(weights.down[...], grad_low)
    o.down[...] += dot_pairs(product, grad_low)
    yield
    scaled = grad_product * slope
    grad_inner = jnp.concatenate(
        [
            (scaled * up * (1.0 + gate * (1.0 - slope))).astype(BF16),
            (scaled * gate).astype(BF16),
        ],
        axis=0,
    )
    yield
    grad_lifted = dot(weights.up[...], grad_inner)
    o.up[...] += dot_pairs(lifted, grad_inner)
    yield
    o.gain[...] += fold(grad_lifted * unit)
    return grad + unit_back(grad_lifted, unit, scale, weights.gain[...])


def head_back(i, o, rows, state):
    unit, scale = unit_of(state)
    gain = i.gain[...]
    shown = (unit * gain).astype(BF16)
    logits = dot(i.logits_t[...], shown)
    yield
    largest = jnp.max(logits, axis=0, keepdims=True)
    raised = jnp.exp(logits - largest)
    total = jnp.sum(raised, axis=0, keepdims=True)
    log_total = largest + jnp.log(total)
    target = read_rows(i.target, rows)
    weight = read_rows(i.weight, rows)
    hot = lax.broadcasted_iota(jnp.int32, logits.shape, 0) == target
    picked = jnp.sum(jnp.where(hot, logits, 0.0), axis=0, keepdims=True)
    o.loss[...] += fold(weight * (log_total - picked))
    o.count[...] += fold(weight)
    share = raised * (1.0 / total)
    grad_scores = (weight * (share - jnp.where(hot, 1.0, 0.0))).astype(BF16)
    grad_shown = dot(i.logits[...], grad_scores)
    o.logits[...] += dot_pairs(grad_scores, shown)
    yield
    o.gain[...] += fold(grad_shown * unit)
    return unit_back(grad_shown, unit, scale, gain)


def bins_hot(bins, rows, table_rows):
    bins = read_rows(bins, rows)
    shape = (table_rows, bins.shape[1])
    return jnp.where(lax.broadcasted_iota(jnp.int32, shape, 0) == bins, 1.0, 0.0).astype(BF16)


def run_stage(body, name, collective_id, rows, inputs, outputs, exchange=None):
    args, outs = leaves_of(inputs), leaves_of(outputs)
    steps = rows // ROW_BLOCK
    chunks = rows // SUBLANES
    wire_args = [index for index, arg in enumerate(args) if arg.kind == WIRE]
    landed_args = [index for index, arg in enumerate(args) if arg.kind == LANDED]
    keeps = [place for place, out in enumerate(outs) if out.kind == LANDED]
    wires = exchange.wires if exchange else 0
    if wire_args:
        peers, half, tokens = args[wire_args[0]].array.shape[0], args[wire_args[0]].half, 0
        tokens = args[wire_args[0]].array.shape[2]
    if exchange:
        peers, half, tokens = exchange.peers, exchange.half, exchange.tokens
    low = pltpu.VMEM((peers, rows * SUBLANES, tokens), BF16)
    many = pltpu.SemaphoreType.DMA((chunks, peers))
    wide = pltpu.VMEM((tokens // LANES, peers * CHUNK_ROWS, LANES), F32)
    groups = [
        [wide] * (len(wire_args) + len(landed_args) + wires),
        [low] * len(wire_args),
        [many] * (2 * len(wire_args)),
        [pltpu.SemaphoreType.DMA((1,))] * len(keeps),
        exchange.scratch() if exchange else [],
    ]

    def kernel(*refs):
        step = pl.program_id(0)
        phase, chunk = lax.rem(step, PHASES), lax.div(step, PHASES)
        in_refs = [
            ref if arg.column is None else Column(ref, arg.column) for arg, ref in zip(args, refs)
        ]
        out_refs = list(refs[len(args) : len(args) + len(outs)])
        rest, parts = list(refs[len(args) + len(outs) :]), []
        for group in groups:
            parts.append(rest[: len(group)])
            rest = rest[len(group) :]
        wides, lands, sems, keep_sems, held = parts
        saves = [
            pltpu.make_async_copy(land, out_refs[place], sem.at[0])
            for land, place, sem in zip(lands, keeps, keep_sems)
        ]
        ring = Exchange(peers, half)
        arrivals = [
            (in_refs[index], land, sems[2 * place], sems[2 * place + 1])
            for place, (index, land) in enumerate(zip(wire_args, lands))
        ]
        i, o = bag_of(inputs, iter(in_refs)), bag_of(outputs, iter(out_refs))

        @pl.when(step == 0)
        def _():
            ring.greet()
            for out, ref in zip(outs, out_refs):
                if out.kind == SUM:
                    ref[...] = jnp.zeros(out.shape, out.dtype)
            if exchange:
                exchange.begin(i, held)
            if arrivals:
                ring.meet()

                def start(index, carry):
                    ring.start(arrivals, index)
                    return carry

                lax.fori_loop(0, chunks, start, 0)

        if arrivals:

            @pl.when(phase == 0)
            def _():
                ring.wait(arrivals, chunk)
                for target, land in zip(wides, lands):
                    widen(target, land, chunk)

        if landed_args:

            @pl.when(phase == 0)
            def _():
                for target, index in zip(wides[len(wire_args) :], landed_args):
                    widen(target, in_refs[index], 0)

        if saves:

            @pl.when(step == steps - PHASES)
            def _():
                for save in saves:
                    save.start()

        body_in = list(in_refs)
        for index, source in zip(wire_args + landed_args, wides):
            body_in[index] = Wire(source, phase)
        sent = wides[len(wire_args) + len(landed_args) :]
        given = bag_of(inputs, iter(body_in))
        out_wires = [Wire(target, phase) for target in sent]
        alternate(
            [
                body(given, o, range(first, first + STREAM_ROWS), *out_wires)
                for first in range(0, ROW_BLOCK, STREAM_ROWS)
            ]
        )
        if exchange:
            moves = exchange.moves(held)

            @pl.when(phase == PHASES - 1)
            def _():
                for source, move in zip(sent, moves):
                    narrow(move[0], source, chunk)
                if not arrivals:

                    @pl.when(chunk == 0)
                    def _():
                        ring.meet()

                ring.start(moves, chunk)

            @pl.when(step == steps - 1)
            def _():
                def wait(index, carry):
                    ring.wait(moves, index)
                    return carry

                lax.fori_loop(0, chunks, wait, 0)
                exchange.finish(i, o, held)
                for save in saves:
                    save.wait()

    results = pl.pallas_call(
        kernel,
        grid=(steps,),
        in_specs=[arg.spec() for arg in args],
        out_specs=[out.spec() for out in outs],
        out_shape=[jax.ShapeDtypeStruct(out.shape, out.dtype) for out in outs],
        scratch_shapes=sum(groups, []),
        compiler_params=pltpu.CompilerParams(
            dimension_semantics=(pltpu.ARBITRARY,),
            vmem_limit_bytes=VMEM_BYTES,
            has_side_effects=True,
            collective_id=collective_id,
        ),
        cost_estimate=pl.CostEstimate(flops=0, bytes_accessed=0, transcendentals=0),
        name=name,
    )(*[arg.array for arg in args])
    return bag_of(outputs, iter(results))


def flip(value, step, count):
    step = jnp.int32(step)
    result, bit = 0, 1
    while bit < count:
        result = result + lax.rem(lax.div(value, bit) + lax.div(step, bit), 2) * bit
        bit *= 2
    return result


def position(row, head, half, heads):
    inner = half // 2 * heads
    return (row % 2) * inner + (row // 2) * heads + head


def place_of(position, half, heads):
    inner = half // 2 * heads
    rest = lax.rem(position, inner)
    return (lax.div(rest, heads) * 2 + lax.div(position, inner), lax.rem(rest, heads))


class Exchange:
    def __init__(self, count, half):
        row, head = lax.axis_index("row"), lax.axis_index("head")
        place = lax.rem(row, half)
        inner = count // 2
        self.count = count
        self.half = half
        self.base = row - place
        self.me = lax.rem(place, 2) * inner + lax.div(place, 2) * (count // half) + head
        self.twin = (lax.rem(row + half, 2 * half), head)
        core = lax.div(self.me, inner)
        self.order = []
        for low in range(inner // 2):
            for step in (low, low + inner):
                other = step ^ (inner - 1)
                for first, second in ((step, other), (other, step)):
                    if first == 0 or second == 0:
                        if first:
                            self.order.append(first)
                    else:
                        self.order.append(first + core * (second - first))

    def peer(self, step):
        return flip(self.me, step, self.count)

    def device(self, peer):
        place, head = place_of(peer, self.half, self.count // self.half)
        return (self.base + place, head)

    def greet(self):
        barrier = pltpu.get_barrier_semaphore()
        for step in self.order:
            pl.semaphore_signal(
                barrier, inc=1, device_id=self.device(self.peer(step)), device_id_type=MESH
            )

    def meet(self):
        pl.semaphore_wait(pltpu.get_barrier_semaphore(), self.count - 1)

    def copies(self, moves, chunk, steps):
        found = []
        for source, target, send_sems, recv_sems in moves:
            size = source.shape[1] // send_sems.shape[0]
            rows = pl.ds(pl.multiple_of(chunk * size, PACKED), size)
            for step in steps:
                peer = self.me if step is None else self.peer(step)
                if step is None:
                    copy = pltpu.make_async_copy(
                        source.at[self.me, rows, :],
                        target.at[self.me, rows, :],
                        send_sems.at[chunk, 0],
                    )
                else:
                    copy = pltpu.make_async_remote_copy(
                        src_ref=source.at[peer, rows, :],
                        dst_ref=target.at[self.me, rows, :],
                        send_sem=send_sems.at[chunk, step],
                        recv_sem=recv_sems.at[chunk, step],
                        device_id=self.device(peer),
                        device_id_type=MESH,
                    )
                found.append(copy)
        return found

    def start(self, moves, chunk):
        for copy in self.copies(moves, chunk, self.order + [None]):
            copy.start()

    def wait(self, moves, chunk):
        for copy in self.copies(moves, chunk, self.order + [None]):
            copy.wait()


def join_channels(got, pair):
    peers, rows, _ = got.shape
    even, odd = [], []
    for peer in range(peers):
        for start in range(0, rows, CHUNK_ROWS):
            piece = got[peer, pl.ds(pl.multiple_of(start + pair * PACKED, PACKED), PACKED), :]
            piece = piece.astype(F32)
            even.append(piece[:SUBLANES])
            odd.append(piece[SUBLANES:])
    return [jnp.concatenate(pieces, axis=0).astype(BF16) for pieces in (even, odd)]


def split_channels(low, pair, even, odd, first=0):
    chunks = low.shape[1] // CHUNK_ROWS
    for start in range(0, even.shape[0], SUBLANES):
        block = (first + start) // SUBLANES
        row = block % chunks * CHUNK_ROWS + pair * PACKED
        low[block // chunks, pl.ds(pl.multiple_of(row, PACKED), PACKED), :] = jnp.concatenate(
            [even[start : start + SUBLANES], odd[start : start + SUBLANES]], axis=0
        ).astype(low.dtype)


def each_pair(body):
    for pair in range(SUBLANES // 2):
        body(pair)


class Forward:
    wires = 2

    def __init__(self, peers, half, rows, tokens, incoming):
        self.peers, self.half, self.incoming = peers, half, incoming
        self.rows, self.tokens = rows * SUBLANES, tokens
        self.chunks = rows // SUBLANES

    def outs(self):
        block = (SUBLANES, self.tokens, self.tokens)
        return dict(
            left=Out(block, BF16, WHOLE),
            right=Out(block, BF16, WHOLE),
            tri=Out((self.peers, self.rows, self.tokens), BF16, WHOLE),
        )

    def scratch(self):
        low = pltpu.VMEM((self.peers, self.rows, self.tokens), BF16)
        many = pltpu.SemaphoreType.DMA((self.chunks, self.peers))
        return [low] * 4 + [many] * 4

    def moves(self, held):
        return [(held[0], held[2], held[4], held[5]), (held[1], held[3], held[6], held[7])]

    def begin(self, i, held):
        pass

    def finish(self, i, o, held):
        axis = 0 if self.incoming else 1

        def step(pair):
            lefts, rights = join_channels(held[2], pair), join_channels(held[3], pair)
            found = []
            for index in range(2):
                o.left[2 * pair + index] = lefts[index]
                o.right[2 * pair + index] = rights[index]
                found.append(product_of(lefts[index], rights[index], axis, axis))
            split_channels(o.tri, pair, *found)

        each_pair(step)


class Backward:
    wires = 1

    def __init__(self, peers, half, rows, tokens, incoming):
        self.peers, self.half, self.incoming = peers, half, incoming
        self.rows, self.tokens = rows * SUBLANES, tokens
        self.chunks = rows // SUBLANES

    def outs(self):
        wire = (self.peers, self.rows, self.tokens)
        return dict(grad_left=Out(wire, BF16, WHOLE), grad_right=Out(wire, BF16, WHOLE))

    def scratch(self):
        low = pltpu.VMEM((self.peers, self.rows, self.tokens), BF16)
        block = pltpu.VMEM((SUBLANES, self.tokens, self.tokens), BF16)
        many = pltpu.SemaphoreType.DMA((self.chunks, self.peers))
        return [low] * 2 + [block] * 2 + [many] * 2 + [pltpu.SemaphoreType.DMA((2,))]

    def moves(self, held):
        return [(held[0], held[1], held[4], held[5])]

    def owned(self, i, held):
        return [
            pltpu.make_async_copy(i.owned.left, held[2], held[6].at[0]),
            pltpu.make_async_copy(i.owned.right, held[3], held[6].at[1]),
        ]

    def begin(self, i, held):
        for copy in self.owned(i, held):
            copy.start()

    def finish(self, i, o, held):
        for copy in self.owned(i, held):
            copy.wait()

        def step(pair):
            lefts, rights = [], []
            for index, grad in enumerate(join_channels(held[1], pair)):
                left, right = held[2][2 * pair + index], held[3][2 * pair + index]
                if self.incoming:
                    lefts.append(product_of(right, grad, 1, 1))
                    rights.append(product_of(left, grad, 1, 0))
                else:
                    lefts.append(product_of(grad, right, 1, 0))
                    rights.append(product_of(grad, left, 0, 0))
            split_channels(o.grad_left, pair, *lefts)
            split_channels(o.grad_right, pair, *rights)

        each_pair(step)


def prepare(triangle_input, triangle_output, expand_weight, reduce_weight, distogram_weight, norm_gains):
    merged = [
        triangle_input.reshape((-1,) + triangle_input.shape[2:]),
        triangle_output.reshape((-1,) + triangle_output.shape[2:]),
        expand_weight,
        reduce_weight,
        distogram_weight.T[None],
    ]
    count = len(merged)

    def kernel(*refs):
        for source, plain, turned in zip(refs[:count], refs[count + 1 :: 2], refs[count + 2 :: 2]):
            for index in range(source.shape[0]):
                value = source[index]
                plain[index] = value.astype(BF16)
                turned[index] = value.T.astype(BF16)
        gains = refs[count][...]
        refs[-1][...] = gains.T

    shapes = []
    for array in merged:
        depth, rows, cols = array.shape
        shapes.append(jax.ShapeDtypeStruct((depth, rows, cols), BF16))
        shapes.append(jax.ShapeDtypeStruct((depth, cols, rows), BF16))
    shapes.append(jax.ShapeDtypeStruct(norm_gains.shape[::-1], F32))
    return pl.pallas_call(
        kernel,
        out_shape=shapes,
        compiler_params=pltpu.CompilerParams(vmem_limit_bytes=VMEM_BYTES),
        name="prepare",
    )(*merged, norm_gains)


def by_crop(value, rows_axis, head_axis):
    count, heads = rows_axis, head_axis
    half = count // 2
    inner = half // 2 * heads
    same, other = [], []
    for row in range(count):
        place = row % inner // heads * 2 + row // inner
        for head in range(heads):
            source = row * heads + head
            for crop, pairs in ((head, same), (1 - head, other)):
                pairs.append((source, (crop * half + place) * heads + row % heads))
    head = lax.axis_index("head")
    crop = lax.axis_index("row") // half
    mine = lax.dynamic_index_in_dim(value, head, 0, keepdims=False)
    rest = lax.dynamic_index_in_dim(value, 1 - head, 0, keepdims=False)
    mine = lax.ppermute(mine, ("row", "head"), same)
    rest = lax.ppermute(rest, ("row", "head"), other)
    low = jnp.where(crop == 0, mine, rest)
    high = jnp.where(crop == 0, rest, mine)
    return jnp.concatenate([low, high], axis=-1)


def reduce_rest(half, peers, collective_id, grids, gains, rows):
    sizes = [grid.shape[0] * grid.shape[1] // LANES for grid in grids]
    used = sum(sizes) + len(gains) + SUBLANES * len(rows)
    part = -(-used // (peers * SUBLANES)) * SUBLANES
    total = part * peers
    starts, spot = [], 0
    for size in sizes:
        starts.append(spot)
        spot += size
    row_starts = []
    for _ in rows:
        row_starts.append(spot)
        spot += SUBLANES
    gain_start = spot
    count = len(grids) + len(gains) + len(rows)

    def kernel(*refs):
        out, local, got, mine, other, sends, recvs, back_sends, back_recvs, twin_sems = refs[count:]
        ring = Exchange(peers, half)
        ring.greet()
        barrier = pltpu.get_barrier_semaphore()
        pl.semaphore_signal(barrier, inc=1, device_id=ring.twin, device_id_type=MESH)
        for grid, start in zip(refs[: len(grids)], starts):
            height, width = grid.shape
            for column in range(width // LANES):
                local[pl.ds(start + column * height, height), :] = grid[
                    :, column * LANES : (column + 1) * LANES
                ]
        ones = jnp.ones((SUBLANES, LANES), F32)
        for index, gain in enumerate(refs[len(grids) : len(grids) + len(gains)]):
            folded = lax.dot_general(
                ones,
                gain[...],
                (((1,), (1,)), ((), ())),
                precision=lax.Precision.HIGHEST,
                preferred_element_type=F32,
            )
            local[pl.ds(gain_start + index, 1), :] = folded[:1]
        for row, start in zip(refs[len(grids) + len(gains) : count], row_starts):
            local[pl.ds(start, 1), :] = row[...]
            local[pl.ds(start + 1, SUBLANES - 1), :] = jnp.zeros((SUBLANES - 1, LANES), F32)
        tail = gain_start + len(gains)
        if total > tail:
            local[pl.ds(tail, total - tail), :] = jnp.zeros((total - tail, LANES), F32)
        pl.semaphore_wait(barrier, peers)

        def block(peer):
            return pl.ds(pl.multiple_of(peer * part, SUBLANES), part)

        here = block(ring.me)

        def gather(step):
            peer = ring.peer(step)
            return pltpu.make_async_remote_copy(
                src_ref=local.at[block(peer), :],
                dst_ref=got.at[here, :],
                send_sem=sends.at[step],
                recv_sem=recvs.at[step],
                device_id=ring.device(peer),
                device_id_type=MESH,
            )

        def spread(step):
            return pltpu.make_async_remote_copy(
                src_ref=out.at[here, :],
                dst_ref=out.at[here, :],
                send_sem=back_sends.at[step],
                recv_sem=back_recvs.at[step],
                device_id=ring.device(ring.peer(step)),
                device_id_type=MESH,
            )

        for step in ring.order:
            gather(step).start()
        got[here, :] = local[here, :]
        for step in ring.order:
            gather(step).wait()
        value = got[pl.ds(0, part), :]
        for peer in range(1, peers):
            value = value + got[pl.ds(peer * part, part), :]
        mine[...] = value
        copy = pltpu.make_async_remote_copy(
            src_ref=mine,
            dst_ref=other,
            send_sem=twin_sems.at[0],
            recv_sem=twin_sems.at[1],
            device_id=ring.twin,
            device_id_type=MESH,
        )
        copy.start()
        copy.wait()
        out[here, :] = mine[...] + other[...]
        for step in ring.order:
            spread(step).start()
        for step in ring.order:
            spread(step).wait()

    inside = pl.BlockSpec(memory_space=pltpu.VMEM)
    whole = pl.pallas_call(
        kernel,
        in_specs=[inside] * count,
        out_specs=inside,
        out_shape=jax.ShapeDtypeStruct((total, LANES), F32),
        scratch_shapes=[pltpu.VMEM((total, LANES), F32)] * 2
        + [pltpu.VMEM((part, LANES), F32)] * 2
        + [pltpu.SemaphoreType.DMA((peers,))] * 4
        + [pltpu.SemaphoreType.DMA((2,))],
        compiler_params=pltpu.CompilerParams(
            collective_id=collective_id, has_side_effects=True, vmem_limit_bytes=VMEM_BYTES
        ),
        cost_estimate=pl.CostEstimate(flops=0, bytes_accessed=0, transcendentals=0),
        name="reduce_rest",
    )(*grids, *gains, *rows)
    return whole, starts, row_starts, gain_start


def update(rest, starts, row_starts, gain_start, early, weights, firsts, seconds):
    layers, kinds, width, mixed = weights[2].shape
    hidden = weights[4].shape[2]
    early_in, early_up, early_rows = early
    given = [rest, *early_in, *early_up, *early_rows]
    count = len(given)

    def kernel(*refs):
        whole = refs[0]
        in_refs = refs[1 : 1 + len(early_in)]
        up_refs = refs[1 + len(early_in) : count - layers]
        row_refs = refs[count - layers : count]
        states = [refs[count + 8 * kind : count + 8 * (kind + 1)] for kind in range(3)]
        scalars = refs[count + 24 : count + 27]
        results = refs[count + 27 :]

        def taken(start, size):
            return whole[pl.ds(start, size), :]

        def wide(start, height, columns):
            return jnp.concatenate(
                [taken(start + column * height, height) for column in range(columns)], axis=1
            )

        loss = jnp.sum(taken(row_starts[0], 1), axis=1, keepdims=True)
        valid = jnp.sum(taken(row_starts[1], 1), axis=1, keepdims=True)
        table_rows, single_rows = weights[0].shape[0], weights[1].shape[0]
        downs = hidden // 2
        grads = {}
        grads[0, ()] = taken(starts[4], table_rows)
        grads[1, ()] = jnp.concatenate(
            [taken(starts[5], single_rows), taken(starts[6], single_rows)], axis=1
        )
        for layer in range(layers):
            spot = 0
            for kind in range(kinds):
                if layer == 0:
                    grads[2, (layer, kind)] = wide(starts[kind], width, mixed // LANES)
                else:
                    grads[2, (layer, kind)] = in_refs[(layer - 1) * kinds + kind][...]
                if layer == 0 and kind == 0:
                    grads[3, (layer, kind)] = taken(starts[2], width)
                else:
                    grads[3, (layer, kind)] = row_refs[layer][pl.ds(spot, width), :]
                    spot += width
            grads[4, (layer,)] = up_refs[layer][...]
            grads[5, (layer,)] = row_refs[layer][pl.ds(spot, downs), :]
        grads[6, ()] = taken(starts[3], weights[6].shape[0])
        grads[7, ()] = taken(gain_start, weights[7].shape[0])
        squares = jnp.zeros((1, 1), F32)
        for key in grads:
            grads[key] = grads[key] / valid
            squares = squares + jnp.sum(grads[key] * grads[key], axis=(0, 1), keepdims=True)
        norm = jnp.sqrt(squares)
        factor = jnp.minimum(1.0, CLIP_NORM / (norm + 1e-06))
        for ref, value in zip(scalars, (loss, valid, norm)):
            ref[...] = value
        for (index, spot), grad in grads.items():
            rate = GAIN_RATE if index == 7 else WEIGHT_RATE
            decay = 0.0 if index == 7 else WEIGHT_DECAY
            new = adamw(
                states[0][index][spot],
                grad * factor,
                states[1][index][spot],
                states[2][index][spot],
                rate,
                decay,
            )
            for ref, value in zip(results[3 * index : 3 * index + 3], new):
                ref[spot] = value

    one = jax.ShapeDtypeStruct((1, 1), F32)
    shapes = [one] * 3
    for weight in weights:
        shapes += [jax.ShapeDtypeStruct(weight.shape, F32)] * 3
    found = pl.pallas_call(
        kernel,
        out_shape=shapes,
        compiler_params=pltpu.CompilerParams(vmem_limit_bytes=VMEM_BYTES),
        name="update",
    )(*given, *weights, *firsts, *seconds)
    return tuple(value[0, 0] for value in found[:3]) + tuple(found[3:])


def step_by_crop(row_count, head_count, given, weights, firsts, seconds):
    single, residue_index, chain_index, token_mask, pair_valid, target_bins = given
    relative_table, single_weight, triangle_input, triangle_output = weights[:4]
    expand_weight, reduce_weight, distogram_weight, norm_gains = weights[4:]
    crops, tokens = token_mask.shape
    width = relative_table.shape[1]
    layers = triangle_input.shape[0]
    half = row_count // crops
    peers = half * head_count
    rows = tokens // peers
    row_index = lax.axis_index("row")
    crop = row_index // half
    start = position(row_index % half, lax.axis_index("head"), half, head_count) * rows

    placed = by_crop(jnp.stack([pair_valid, target_bins], axis=1), row_count, head_count)
    valid, target = placed[0], placed[1]

    def of_crop(array):
        return lax.dynamic_index_in_dim(array, crop, 0, keepdims=False)

    def of_rows(array):
        return lax.dynamic_slice_in_dim(array, start, rows, 0)

    residues, chains = of_crop(residue_index), of_crop(chain_index)
    reach = (relative_table.shape[0] - 2) // 2
    bins = jnp.where(
        of_rows(chains)[:, None] == chains[None, :],
        jnp.clip(of_rows(residues)[:, None] - residues[None, :], -reach, reach) + reach,
        2 * reach + 1,
    )
    present = of_crop(token_mask).astype(F32)
    pair_mask = of_rows(present)[:, None] * present[None, :]
    loss_weight = pair_mask * valid.astype(F32)
    table_rows = -(-relative_table.shape[0] // PACKED) * PACKED
    table_t = jnp.pad(relative_table, ((0, table_rows - relative_table.shape[0]), (0, 0))).T
    tokens_single = of_crop(single)
    proj = project(tokens_single, single_weight.astype(BF16))
    proj_rows = of_rows(proj[:, :width])[:, :, None]
    proj_cols = proj[:, width:].T
    bins, pair_mask = Arg(bins[:, None, :], ROWS), Arg(pair_mask[:, None, :], ROWS)

    prepared = prepare(
        triangle_input, triangle_output, expand_weight, reduce_weight, distogram_weight, norm_gains
    )
    mix, mix_t, out, out_t, up, up_t, down, down_t, logits_t, logits, gains = prepared
    hidden = up.shape[2]

    def gain(index):
        return Arg(gains, WHOLE, column=index)

    def layer_of(array, index, *block):
        shape = block or array.shape[1:]
        return Arg(array, WHOLE, (index, 0, 0), (None,) + tuple(shape))

    def triangle_weights(layer, kind, starts=False, finishes=False, back=False):
        index = 2 * layer + kind
        found = dict(gain0=gain(5 * layer + 2 * kind))
        if starts:
            found.update(mix_t=layer_of(mix_t, index, 4 * width, width))
        if starts and back:
            found.update(mix=layer_of(mix, index))
        if finishes:
            found.update(
                gain1=gain(5 * layer + 2 * kind + 1),
                gate_t=Arg(mix_t, WHOLE, (index, 4, 0), (None, width, width)),
                out_t=layer_of(out_t, index),
            )
        if finishes and back:
            found.update(out=layer_of(out, index))
        return found

    def transition_weights(layer, forth=True, back=False):
        found = dict(gain=gain(5 * layer + 4), up_t=layer_of(up_t, layer))
        if forth:
            found.update(down_t=layer_of(down_t, layer))
        if back:
            found.update(up=layer_of(up, layer), down=layer_of(down, layer))
        return found

    def state_out():
        return Out((rows, width, tokens), F32, ROWS)

    def sum_out(*shape):
        return Out(shape, F32, SUM)

    def gain_out():
        return sum_out(width, LANES)

    def back_start_outs():
        return dict(
            grad_gate=Out((rows, width, tokens), BF16, ROWS),
            out=sum_out(width, width),
            gain1=gain_out(),
        )

    def back_finish_outs():
        return dict(mix=sum_out(width, 5 * width), gain0=gain_out())

    def transition_outs():
        return dict(up=sum_out(width, hidden), down=sum_out(hidden // 2, width), gain=gain_out())

    identities = iter(range(4 * layers + 2))

    def forward(incoming):
        return Forward(peers, half, rows, tokens, incoming)

    def backward(incoming):
        return Backward(peers, half, rows, tokens, incoming)

    def wire(array):
        return Arg(array, WIRE, half=half)

    def landed_out():
        return Out((peers, rows * SUBLANES, tokens), BF16, LANDED)

    def owned(kept):
        return dict(left=Arg(kept.left, ANYWHERE), right=Arg(kept.right, ANYWHERE))

    kept, states, middles, tris = {}, {}, {}, {}

    def first_body(i, o, rows, *wires):
        state = dot(i.table_t[...], bins_hot(i.bins, rows, table_rows))
        yield
        cols = i.proj_cols[...]
        state = state + jnp.concatenate([cols + i.proj_rows[row] for row in rows], axis=1)
        write_rows(o.state, rows, state)
        yield from triangle_start(i.start, i, rows, wires, state)

    exchange = forward(False)
    got = run_stage(
        first_body,
        "first_state",
        next(identities),
            rows,
        dict(
            bins=bins,
            proj_rows=Arg(proj_rows, ROWS),
            proj_cols=Arg(proj_cols, WHOLE),
            table_t=Arg(table_t.astype(BF16), WHOLE),
            mask=pair_mask,
            start=triangle_weights(0, 0, starts=True),
        ),
        dict(state=state_out(), **exchange.outs()),
        exchange,
    )
    kept[0, 0], states[0, 0] = got, got.state

    def between_body(i, o, rows, *wires):
        state, _ = yield from triangle_finish(i.end, rows, i.tri, read_rows(i.state, rows))
        write_rows(o.state, rows, state)
        yield from triangle_start(i.start, i, rows, wires, state)

    def layer_end_body(i, o, rows, *wires):
        state, _ = yield from triangle_finish(i.end, rows, i.tri, read_rows(i.state, rows))
        write_rows(o.middle, rows, state)
        lifted = yield from transition(i.lift, state)
        state = state + dot(i.lift.down_t[...], lifted[5])
        yield
        write_rows(o.state, rows, state)
        yield from triangle_start(i.start, i, rows, wires, state)

    for layer in range(layers):
        exchange = forward(True)
        got = run_stage(
            between_body,
            "between_updates",
            next(identities),
            rows,
            dict(
                state=Arg(states[layer, 0], ROWS),
                tri=wire(kept[layer, 0].tri),
                mask=pair_mask,
                end=triangle_weights(layer, 0, finishes=True),
                start=triangle_weights(layer, 1, starts=True),
            ),
            dict(state=state_out(), landed=landed_out(), **exchange.outs()),
            exchange,
        )
        kept[layer, 1], states[layer, 1], tris[layer, 0] = got, got.state, got.landed
        if layer + 1 == layers:
            break
        exchange = forward(False)
        got = run_stage(
            layer_end_body,
            "layer_end",
            next(identities),
            rows,
            dict(
                state=Arg(states[layer, 1], ROWS),
                tri=wire(kept[layer, 1].tri),
                mask=pair_mask,
                end=triangle_weights(layer, 1, finishes=True),
                lift=transition_weights(layer),
                start=triangle_weights(layer + 1, 0, starts=True),
            ),
            dict(middle=state_out(), state=state_out(), landed=landed_out(), **exchange.outs()),
            exchange,
        )
        tris[layer, 1] = got.landed
        kept[layer + 1, 0], states[layer + 1, 0] = got, got.state
        middles[layer] = got.middle

    def loss_body(i, o, rows, sent):
        state, kept_triangle = yield from triangle_finish(
            i.end, rows, i.tri, read_rows(i.state, rows)
        )
        lifted = yield from transition(i.lift, state)
        state = state + dot(i.lift.down_t[...], lifted[5])
        yield
        grad = yield from head_back(i.head, o.head, rows, state)
        grad = yield from transition_back(i.lift, o.lift, grad, lifted)
        write_rows(o.grad, rows, grad)
        yield from triangle_back_start(i.end, o.end, rows, sent, grad, kept_triangle)

    top = layers - 1
    exchange = backward(True)
    got = run_stage(
        loss_body,
        "loss",
        next(identities),
            rows,
        dict(
            state=Arg(states[top, 1], ROWS),
            tri=wire(kept[top, 1].tri),
            end=triangle_weights(top, 1, finishes=True, back=True),
            lift=transition_weights(top, back=True),
            head=dict(
                gain=gain(5 * layers),
                logits=layer_of(logits, 0),
                logits_t=layer_of(logits_t, 0),
                target=Arg(target[:, None, :], ROWS),
                weight=Arg(loss_weight[:, None, :], ROWS),
            ),
            owned=owned(kept[top, 1]),
        ),
        dict(
            grad=state_out(),
            head=dict(
                loss=sum_out(1, LANES),
                count=sum_out(1, LANES),
                logits=sum_out(distogram_weight.shape[1], width),
                gain=gain_out(),
            ),
            lift=transition_outs(),
            end=back_start_outs(),
            **exchange.outs(),
        ),
        exchange,
    )
    head, lifts, ends, begins = got.head, {top: got.lift}, {(top, 1): got.end}, {}

    def between_back_body(i, o, rows, sent):
        grad = yield from triangle_back_finish(i.start, i, o.start, rows)
        write_rows(o.grad, rows, grad)
        _, kept_triangle = yield from triangle_finish(
            i.end, rows, i.tri, read_rows(i.before, rows)
        )
        yield from triangle_back_start(i.end, o.end, rows, sent, grad, kept_triangle)

    def layer_end_back_body(i, o, rows, sent):
        grad = yield from triangle_back_finish(i.start, i, o.start, rows)
        lifted = yield from transition(i.lift, read_rows(i.middle, rows))
        grad = yield from transition_back(i.lift, o.lift, grad, lifted)
        write_rows(o.grad, rows, grad)
        _, kept_triangle = yield from triangle_finish(
            i.end, rows, i.tri, read_rows(i.before, rows)
        )
        yield from triangle_back_start(i.end, o.end, rows, sent, grad, kept_triangle)

    def first_back_body(i, o, rows):
        grad = yield from triangle_back_finish(i.start, i, o.start, rows)
        hot = bins_hot(i.bins, rows, table_rows)
        high = grad.astype(BF16)
        low = (grad - high.astype(F32)).astype(BF16)
        o.table[...] += dot_pairs(hot, high) + dot_pairs(hot, low)
        yield
        for place, row in enumerate(rows):
            part = grad[:, place * tokens : (place + 1) * tokens]
            o.rows[row] = fold(part)
            o.cols[...] += part

    def layer_sums(layer):
        kinds = (0, 1) if layer else (1,)
        mixes = [begins[layer, 1].mix] if layer else []
        if layer + 1 < layers:
            mixes.append(begins[layer + 1, 0].mix)
        outs = [ends[layer, kind].out for kind in kinds]
        return (mixes, lifts[layer].up, jnp.concatenate(outs + [lifts[layer].down], axis=0))

    for layer in reversed(range(layers)):
        for kind in (1, 0):
            inputs = dict(
                grad=Arg(got.grad, ROWS),
                state=Arg(states[layer, kind], ROWS),
                mask=pair_mask,
                start=triangle_weights(layer, kind, starts=True, back=True),
                back=dict(
                    grad_left=wire(got.grad_left),
                    grad_right=wire(got.grad_right),
                    grad_gate=Arg(got.end.grad_gate, ROWS),
                ),
            )
            outputs = dict(start=back_finish_outs())
            if layer == 0 and kind == 0:
                got = run_stage(
                    first_back_body,
                    "first_state_back",
                    next(identities),
            rows,
                    dict(bins=bins, **inputs),
                    dict(
                        table=sum_out(table_rows, width),
                        rows=Out((rows, width, LANES), F32, ROWS),
                        cols=sum_out(width, tokens),
                        **outputs,
                    ),
                )
                begins[layer, kind] = got.start
                break
            before = (layer, 0) if kind == 1 else (layer - 1, 1)
            inputs.update(
                before=Arg(states[before], ROWS),
                tri=Arg(tris[before], LANDED),
                end=triangle_weights(*before, finishes=True, back=True),
                owned=owned(kept[before]),
            )
            outputs.update(grad=state_out(), end=back_start_outs())
            if kind == 1:
                exchange = backward(False)
                body, name = between_back_body, "between_updates_back"
            else:
                exchange = backward(True)
                body, name = layer_end_back_body, "layer_end_back"
                inputs.update(
                    middle=Arg(middles[layer - 1], ROWS),
                    lift=transition_weights(layer - 1, forth=False, back=True),
                )
                outputs.update(lift=transition_outs())
            got = run_stage(
                body,
                name,
                next(identities),
                rows,
                inputs,
                dict(**outputs, **exchange.outs()),
                exchange,
            )
            begins[layer, kind], ends[before] = got.start, got.end
            if kind == 0:
                lifts[layer - 1] = got.lift

    early = lax.psum({layer: layer_sums(layer) for layer in range(layers)}, ("row", "head"))
    early_mixes = {}
    for layer in range(layers):
        mixes = list(early[layer][0])
        if layer:
            early_mixes[layer, 1] = mixes.pop(0)
        if mixes:
            early_mixes[layer + 1, 0] = mixes.pop(0)
    early = (
        [early_mixes[layer, kind] for layer in range(1, layers) for kind in range(2)],
        [early[layer][1] for layer in range(layers)],
        [early[layer][2] for layer in range(layers)],
    )

    wide_single = tokens_single.astype(F32)
    row_part = jnp.einsum(
        "is,ic->sc",
        of_rows(wide_single),
        jnp.sum(got.rows, axis=2),
        precision=lax.Precision.HIGHEST,
    )
    col_part = jnp.einsum("js,cj->sc", wide_single, got.cols, precision=lax.Precision.HIGHEST)
    partial_gains = []
    for layer in range(layers):
        for kind in range(2):
            partial_gains += [begins[layer, kind].gain0, ends[layer, kind].gain1]
        partial_gains.append(lifts[layer].gain)
    partial_gains.append(head.gain)
    grids = [
        begins[0, 0].mix,
        begins[0, 1].mix,
        ends[0, 0].out,
        head.logits,
        got.table,
        row_part,
        col_part,
    ]
    def turned(arrays):
        return arrays[:6] + (arrays[6].T,) + arrays[7:]

    rest, *starts = reduce_rest(
        half, peers, next(identities), grids, partial_gains, [head.loss, head.count]
    )
    found = update(rest, *starts, early, turned(weights), turned(firsts), turned(seconds))
    return found[:21] + tuple(value.T for value in found[21:24]) + found[24:]


def per_device(
    row_count,
    head_count,
    single,
    residue_index,
    chain_index,
    token_mask,
    pair_valid,
    target_bins,
    relative_table,
    single_weight,
    triangle_input,
    triangle_output,
    expand_weight,
    reduce_weight,
    distogram_weight,
    norm_gains,
    first_table,
    second_table,
    first_single,
    second_single,
    first_input,
    second_input,
    first_output,
    second_output,
    first_expand,
    second_expand,
    first_reduce,
    second_reduce,
    first_logits,
    second_logits,
    first_gains,
    second_gains,
):
    crops, tokens = token_mask.shape
    width = relative_table.shape[1]
    peers = row_count * head_count // crops
    given = (
        single,
        residue_index,
        chain_index,
        token_mask,
        pair_valid,
        target_bins,
        relative_table,
        single_weight,
        triangle_input,
        triangle_output,
        expand_weight,
        reduce_weight,
        distogram_weight,
        norm_gains,
    )
    weights = (
        relative_table,
        single_weight,
        triangle_input,
        triangle_output,
        expand_weight,
        reduce_weight,
        distogram_weight,
        norm_gains,
    )
    firsts = (
        first_table,
        first_single,
        first_input,
        first_output,
        first_expand,
        first_reduce,
        first_logits,
        first_gains,
    )
    seconds = (
        second_table,
        second_single,
        second_input,
        second_output,
        second_expand,
        second_reduce,
        second_logits,
        second_gains,
    )
    if (
        crops == 2
        and head_count == 2
        and width == LANES
        and width == SUBLANES * peers
        and tokens % (peers * SUBLANES) == 0
        and tokens % (3 * LANES) == 0
    ):
        return step_by_crop(row_count, head_count, given[:6], weights, firsts, seconds)
    local = gradients_by_block(*given)
    summed = lax.psum(local, ("row", "head"))
    loss_sum, valid_count = summed[0], summed[1]
    grads = [grad / valid_count for grad in summed[2:]]
    squares = jnp.zeros((), jnp.float32)
    for g in grads:
        squares = squares + jnp.sum(g * g)
    gradient_norm = jnp.sqrt(squares)
    factor = jnp.minimum(1.0, CLIP_NORM / (gradient_norm + 1e-06))
    result = []
    for index in range(8):
        rate = GAIN_RATE if index == 7 else WEIGHT_RATE
        decay = 0.0 if index == 7 else WEIGHT_DECAY
        result.extend(
            adamw(weights[index], grads[index] * factor, firsts[index], seconds[index], rate, decay)
        )
    return (
        loss_sum,
        valid_count,
        gradient_norm,
        result[0],
        result[1],
        result[2],
        result[3],
        result[4],
        result[5],
        result[6],
        result[7],
        result[8],
        result[9],
        result[10],
        result[11],
        result[12],
        result[13],
        result[14],
        result[15],
        result[16],
        result[17],
        result[18],
        result[19],
        result[20],
        result[21],
        result[22],
        result[23],
    )


def solution(mesh):
    placed = (
        P(),
        P(),
        P(),
        P(),
        P(None, "row", "head"),
        P(None, "row", "head"),
        P(),
        P(),
        P(),
        P(),
        P(),
        P(),
        P(),
        P(),
        P(),
        P(),
        P(),
        P(),
        P(),
        P(),
        P(),
        P(),
        P(),
        P(),
        P(),
        P(),
        P(),
        P(),
        P(),
        P(),
    )
    return jax.shard_map(
        functools.partial(per_device, mesh.shape["row"], mesh.shape["head"]),
        mesh=mesh,
        in_specs=placed,
        out_specs=(
            P(),
            P(),
            P(),
            P(),
            P(),
            P(),
            P(),
            P(),
            P(),
            P(),
            P(),
            P(),
            P(),
            P(),
            P(),
            P(),
            P(),
            P(),
            P(),
            P(),
            P(),
            P(),
            P(),
            P(),
            P(),
            P(),
            P(),
        ),
        check_vma=False,
    )
```

```python
import functools

import jax
import jax.numpy as jnp
from jax import lax
from jax.experimental import pallas as pl
from jax.experimental.pallas import tpu as pltpu
from jax.sharding import PartitionSpec as P

STEP = 10


EPS = 1e-05
BETA_ONE = 0.9
BETA_TWO = 0.999
ADAM_EPS = 1e-08
WEIGHT_RATE = 0.1
GAIN_RATE = 0.5
WEIGHT_DECAY = 0.01
CLIP_NORM = 0.002


def normalize(value):
    mean = jnp.mean(value, axis=-1, keepdims=True)
    centred = value - mean
    scale = lax.rsqrt(jnp.mean(centred * centred, axis=-1, keepdims=True) + EPS)
    return (centred * scale, scale)


def norm_back(grad_out, unit, scale, gain):
    scaled = grad_out * gain
    first_mean = jnp.mean(scaled, axis=-1, keepdims=True)
    second_mean = jnp.mean(scaled * unit, axis=-1, keepdims=True)
    grad_in = scale * (scaled - first_mean - unit * second_mean)
    grad_gain = jnp.sum(grad_out * unit, axis=tuple(range(grad_out.ndim - 1)))
    return (grad_in, grad_gain)


def project(value, weight):
    return jnp.einsum("...c,cd->...d", value, weight, preferred_element_type=jnp.float32)


def project_back(grad, weight):
    return jnp.einsum("...d,cd->...c", grad, weight, preferred_element_type=jnp.float32)


def weight_grad(value, grad):
    return jnp.einsum("bijc,bijd->cd", value, grad, preferred_element_type=jnp.float32)


def triangle_forward(state, weight_in, weight_out, gains, pair_mask, incoming):
    hidden = weight_out.shape[0]
    pair_unit, pair_scale = normalize(state)
    normed = (pair_unit * gains[0]).astype(jnp.bfloat16)
    mixed = project(normed, weight_in)
    mask = pair_mask[..., None]
    left = (mask * jax.nn.sigmoid(mixed[..., :hidden]) * mixed[..., hidden : 2 * hidden]).astype(
        jnp.bfloat16
    )
    right = (
        mask
        * jax.nn.sigmoid(mixed[..., 2 * hidden : 3 * hidden])
        * mixed[..., 3 * hidden : 4 * hidden]
    ).astype(jnp.bfloat16)
    left_cols, right_cols = (
        lax.all_to_all(left, "head", split_axis=3, concat_axis=2, tiled=True),
        lax.all_to_all(right, "head", split_axis=3, concat_axis=2, tiled=True),
    )
    if incoming:
        left_cols, right_cols = (
            lax.all_to_all(left_cols, "row", split_axis=2, concat_axis=1, tiled=True),
            lax.all_to_all(right_cols, "row", split_axis=2, concat_axis=1, tiled=True),
        )
        left_cols = jnp.swapaxes(left_cols, 1, 2)
        right_cols = jnp.swapaxes(right_cols, 1, 2)
    right_all = lax.all_gather(right_cols, "row", axis=1, tiled=True)
    triangle = jnp.einsum(
        "bikc,bjkc->bijc", left_cols, right_all, preferred_element_type=jnp.float32
    )
    triangle = lax.all_to_all(
        triangle.astype(jnp.bfloat16), "head", split_axis=2, concat_axis=3, tiled=True
    )
    tri_unit, tri_scale = normalize(triangle.astype(jnp.float32))
    shaped = (tri_unit * gains[1]).astype(jnp.bfloat16)
    branch = project(shaped, weight_out)
    gate = jax.nn.sigmoid(mixed[..., 4 * hidden :])
    kept = (
        pair_unit,
        pair_scale,
        normed,
        mixed,
        left_cols,
        right_all,
        tri_unit,
        tri_scale,
        shaped,
        branch,
        gate,
    )
    return (state + gate * branch, kept)


def triangle_backward(grad_state, kept, weight_in, weight_out, gains, pair_mask, incoming):
    hidden = weight_out.shape[0]
    (
        pair_unit,
        pair_scale,
        normed,
        mixed,
        left_cols,
        right_all,
        tri_unit,
        tri_scale,
        shaped,
        branch,
        gate,
    ) = kept
    grad_branch = (grad_state * gate).astype(jnp.bfloat16)
    grad_gate = grad_state * branch * gate * (1.0 - gate)
    grad_out = weight_grad(shaped, grad_branch)
    grad_shaped = project_back(grad_branch, weight_out)
    grad_tri, gain_two = norm_back(grad_shaped, tri_unit, tri_scale, gains[1])
    tri_cols = lax.all_to_all(
        grad_tri.astype(jnp.bfloat16), "head", split_axis=3, concat_axis=2, tiled=True
    )
    grad_left = jnp.einsum(
        "bijc,bjkc->bikc", tri_cols, right_all, preferred_element_type=jnp.float32
    )
    grad_left = grad_left.astype(jnp.bfloat16)
    summed = lax.psum_scatter(
        jnp.einsum(
            "bijc,bikc->jbkc", tri_cols, left_cols, preferred_element_type=jnp.float32
        ).astype(jnp.bfloat16),
        "row",
        scatter_dimension=0,
        tiled=True,
    ).astype(jnp.float32)
    grad_right = jnp.transpose(summed, (1, 0, 2, 3)).astype(jnp.bfloat16)
    if incoming:
        grad_left, grad_right = (
            lax.all_to_all(
                jnp.swapaxes(grad_left, 1, 2), "row", split_axis=1, concat_axis=2, tiled=True
            ),
            lax.all_to_all(
                jnp.swapaxes(grad_right, 1, 2), "row", split_axis=1, concat_axis=2, tiled=True
            ),
        )
    back_left, back_right = (
        lax.all_to_all(grad_left, "head", split_axis=2, concat_axis=3, tiled=True),
        lax.all_to_all(grad_right, "head", split_axis=2, concat_axis=3, tiled=True),
    )
    mask = pair_mask[..., None]
    back_left = back_left.astype(jnp.float32) * mask
    back_right = back_right.astype(jnp.float32) * mask
    left_sig = jax.nn.sigmoid(mixed[..., :hidden])
    left_value = mixed[..., hidden : 2 * hidden]
    right_sig = jax.nn.sigmoid(mixed[..., 2 * hidden : 3 * hidden])
    right_value = mixed[..., 3 * hidden : 4 * hidden]
    grad_mixed = jnp.concatenate(
        [
            back_left * left_value * left_sig * (1.0 - left_sig),
            back_left * left_sig,
            back_right * right_value * right_sig * (1.0 - right_sig),
            back_right * right_sig,
            grad_gate,
        ],
        axis=-1,
    ).astype(jnp.bfloat16)
    grad_in = weight_grad(normed, grad_mixed)
    grad_normed = project_back(grad_mixed, weight_in)
    grad_first, gain_one = norm_back(grad_normed, pair_unit, pair_scale, gains[0])
    return (grad_state + grad_first, (grad_in, grad_out, gain_one, gain_two))


def transition_forward(state, weight_up, weight_down, gain):
    expand = weight_down.shape[0]
    unit, scale = normalize(state)
    lifted = (unit * gain).astype(jnp.bfloat16)
    inner = project(lifted, weight_up)
    product = (jax.nn.silu(inner[..., :expand]) * inner[..., expand:]).astype(jnp.bfloat16)
    return (state + project(product, weight_down), (unit, scale, lifted, inner, product))


def transition_backward(grad_state, kept, weight_up, weight_down, gain):
    expand = weight_down.shape[0]
    unit, scale, lifted, inner, product = kept
    grad_low = grad_state.astype(jnp.bfloat16)
    grad_down = weight_grad(product, grad_low)
    grad_product = project_back(grad_low, weight_down)
    gate_part = inner[..., :expand]
    up_part = inner[..., expand:]
    gate_sig = jax.nn.sigmoid(gate_part)
    silu_value = gate_part * gate_sig
    silu_slope = gate_sig * (1.0 + gate_part * (1.0 - gate_sig))
    grad_inner = jnp.concatenate(
        [grad_product * up_part * silu_slope, grad_product * silu_value], axis=-1
    )
    grad_inner = grad_inner.astype(jnp.bfloat16)
    grad_up = weight_grad(lifted, grad_inner)
    grad_lifted = project_back(grad_inner, weight_up)
    grad_middle, gain_grad = norm_back(grad_lifted, unit, scale, gain)
    return (grad_middle + grad_state, (grad_up, grad_down, gain_grad))


def block_forward(state, weight_in, weight_out, weight_up, weight_down, gains, pair_mask):
    first, kept_one = triangle_forward(
        state, weight_in[0], weight_out[0], gains[0:2], pair_mask, False
    )
    second, kept_two = triangle_forward(
        first, weight_in[1], weight_out[1], gains[2:4], pair_mask, True
    )
    output, kept_three = transition_forward(second, weight_up, weight_down, gains[4])
    return (output, (kept_one, kept_two, kept_three))


def block_backward(
    grad_state, state, weight_in, weight_out, weight_up, weight_down, gains, pair_mask
):
    skipped, kept = block_forward(
        state, weight_in, weight_out, weight_up, weight_down, gains, pair_mask
    )
    kept_one, kept_two, kept_three = kept
    grad_state, (grad_up, grad_down, gain_five) = transition_backward(
        grad_state, kept_three, weight_up, weight_down, gains[4]
    )
    grad_state, (in_two, out_two, gain_three, gain_four) = triangle_backward(
        grad_state, kept_two, weight_in[1], weight_out[1], gains[2:4], pair_mask, True
    )
    grad_state, (in_one, out_one, gain_one, gain_two) = triangle_backward(
        grad_state, kept_one, weight_in[0], weight_out[0], gains[0:2], pair_mask, False
    )
    return (
        grad_state,
        (
            jnp.stack([in_one, in_two]),
            jnp.stack([out_one, out_two]),
            grad_up,
            grad_down,
            jnp.stack([gain_one, gain_two, gain_three, gain_four, gain_five]),
        ),
    )


def adamw(weight, grad, first, second, rate, decay):
    first_new = BETA_ONE * first + (1.0 - BETA_ONE) * grad
    second_new = BETA_TWO * second + (1.0 - BETA_TWO) * grad * grad
    moved = (
        first_new
        / (1.0 - BETA_ONE**STEP)
        / (jnp.sqrt(second_new / (1.0 - BETA_TWO**STEP)) + ADAM_EPS)
    )
    return (first_new, second_new, weight - rate * (moved + decay * weight))


def gradients_by_block(
    single,
    residue_index,
    chain_index,
    token_mask,
    pair_valid,
    target_bins,
    relative_table,
    single_weight,
    triangle_input,
    triangle_output,
    expand_weight,
    reduce_weight,
    distogram_weight,
    norm_gains,
):
    crops, rows, cols = pair_valid.shape
    width = relative_table.shape[1]
    layers = triangle_input.shape[0]
    row_start = lax.axis_index("row") * rows
    col_start = lax.axis_index("head") * cols

    def take(array, start, count):
        return lax.dynamic_slice_in_dim(array, start, count, 1)

    offset = (
        take(residue_index, row_start, rows)[:, :, None]
        - take(residue_index, col_start, cols)[:, None, :]
    )
    same = (
        take(chain_index, row_start, rows)[:, :, None]
        == take(chain_index, col_start, cols)[:, None, :]
    )
    reach = (relative_table.shape[0] - 2) // 2
    bins = jnp.where(same, jnp.clip(offset, -reach, reach) + reach, 2 * reach + 1)
    relative_hot = (
        bins[..., None] == jnp.arange(relative_table.shape[0])[None, None, None, :]
    ).astype(jnp.float32)
    token_rows = take(token_mask, row_start, rows).astype(jnp.float32)
    token_cols = take(token_mask, col_start, cols).astype(jnp.float32)
    pair_mask = token_rows[:, :, None] * token_cols[:, None, :]
    loss_weight = pair_mask * pair_valid.astype(jnp.float32)
    low_input = triangle_input.astype(jnp.bfloat16)
    low_output = triangle_output.astype(jnp.bfloat16)
    low_expand = expand_weight.astype(jnp.bfloat16)
    low_reduce = reduce_weight.astype(jnp.bfloat16)
    low_logits = distogram_weight.astype(jnp.bfloat16)
    proj = project(single, single_weight.astype(jnp.bfloat16))
    state = project(relative_hot.astype(jnp.bfloat16), relative_table.astype(jnp.bfloat16))
    state = (
        state
        + take(proj, row_start, rows)[:, :, None, :width]
        + take(proj, col_start, cols)[:, None, :, width:]
    )
    inputs = []
    for layer in range(layers):
        inputs.append(state)
        state, unused = block_forward(
            state,
            low_input[layer],
            low_output[layer],
            low_expand[layer],
            low_reduce[layer],
            norm_gains[5 * layer : 5 * layer + 5],
            pair_mask,
        )
    head_unit, head_scale = normalize(state)
    shown = (head_unit * norm_gains[5 * layers]).astype(jnp.bfloat16)
    logits = project(shown, low_logits)
    largest = jnp.max(logits, axis=-1, keepdims=True)
    log_total = largest + jnp.log(jnp.sum(jnp.exp(logits - largest), axis=-1, keepdims=True))
    target_hot = (
        target_bins[..., None] == jnp.arange(logits.shape[-1])[None, None, None, :]
    ).astype(jnp.float32)
    picked = jnp.sum(logits * target_hot, axis=-1)
    loss_local = jnp.sum(loss_weight * (log_total[..., 0] - picked))
    grad_scores = (loss_weight[..., None] * (jnp.exp(logits - log_total) - target_hot)).astype(
        jnp.bfloat16
    )
    grad_logits = weight_grad(shown, grad_scores)
    grad_shown = project_back(grad_scores, low_logits)
    grad_state, gain_last = norm_back(grad_shown, head_unit, head_scale, norm_gains[5 * layers])
    collected = []
    for layer in reversed(range(layers)):
        grad_state, layer_grads = block_backward(
            grad_state,
            inputs[layer],
            low_input[layer],
            low_output[layer],
            low_expand[layer],
            low_reduce[layer],
            norm_gains[5 * layer : 5 * layer + 5],
            pair_mask,
        )
        collected.insert(0, layer_grads)
    grad_input = jnp.stack([entry[0] for entry in collected])
    grad_output = jnp.stack([entry[1] for entry in collected])
    grad_expand = jnp.stack([entry[2] for entry in collected])
    grad_reduce = jnp.stack([entry[3] for entry in collected])
    grad_gains = jnp.concatenate(
        [jnp.concatenate([entry[4] for entry in collected], axis=0), gain_last[None]], axis=0
    )
    grad_table = jnp.einsum(
        "bijr,bijc->rc", relative_hot, grad_state, precision=lax.Precision.HIGHEST
    )
    single_wide = single.astype(jnp.float32)
    row_part = jnp.einsum(
        "bis,bic->sc",
        take(single_wide, row_start, rows),
        jnp.sum(grad_state, axis=2),
        precision=lax.Precision.HIGHEST,
    )
    col_part = jnp.einsum(
        "bjs,bjc->sc",
        take(single_wide, col_start, cols),
        jnp.sum(grad_state, axis=1),
        precision=lax.Precision.HIGHEST,
    )
    grad_single = jnp.concatenate([row_part, col_part], axis=1)
    return (
        loss_local,
        jnp.sum(loss_weight),
        grad_table,
        grad_single,
        grad_input,
        grad_output,
        grad_expand,
        grad_reduce,
        grad_logits,
        grad_gains,
    )


F32 = jnp.float32
BF16 = jnp.bfloat16
LANES = 128
SUBLANES = 8
PACKED = 16
ROW_BLOCK = 4
STREAM_ROWS = 2
PHASES = SUBLANES // ROW_BLOCK
CHUNK_ROWS = SUBLANES * SUBLANES
VMEM_BYTES = 58 * 2**20
MESH = pl.DeviceIdType.MESH
ROWS, LANDED, WHOLE, SUM, ANYWHERE = range(5)


class Bag:
    def __init__(self, **entries):
        self.__dict__.update(entries)


class Arg:
    def __init__(self, array, kind, index=None, block=None, column=None):
        self.array, self.kind, self.index, self.block = array, kind, index, block
        self.column = column

    def spec(self):
        if self.index is None:
            return block_spec(self.array.shape, self.kind)
        index = self.index
        return pl.BlockSpec(self.block, lambda step: index)


class Column:
    def __init__(self, ref, column):
        self.ref, self.column = ref, column

    def __getitem__(self, _):
        return self.ref[:, self.column : self.column + 1]


class Out:
    def __init__(self, shape, dtype, kind):
        self.shape, self.dtype, self.kind = shape, dtype, kind

    def spec(self):
        return block_spec(self.shape, ANYWHERE if self.kind == LANDED else self.kind)


def block_spec(shape, kind):
    if kind == ANYWHERE:
        return pl.BlockSpec(memory_space=pl.ANY)
    if kind == LANDED:
        return pl.BlockSpec((shape[0], CHUNK_ROWS, shape[2]), lambda step: (0, step // PHASES, 0))
    if kind == ROWS:
        return pl.BlockSpec((ROW_BLOCK,) + shape[1:], lambda step: (step,) + (0,) * (len(shape) - 1))
    return pl.BlockSpec(shape, lambda step: (0,) * len(shape))


def is_leaf(value):
    return isinstance(value, (Arg, Out))


def bag_of(tree, leaves):
    if is_leaf(tree):
        return next(leaves)
    if isinstance(tree, list):
        return [bag_of(value, leaves) for value in tree]
    return Bag(**{key: bag_of(value, leaves) for key, value in tree.items()})


def leaves_of(tree):
    if is_leaf(tree):
        return [tree]
    found = []
    for value in tree if isinstance(tree, list) else tree.values():
        found.extend(leaves_of(value))
    return found


def dot(left, right):
    return lax.dot_general(left, right, (((1,), (0,)), ((), ())), preferred_element_type=F32)


def dot_pairs(left, right):
    return lax.dot_general(left, right, (((1,), (1,)), ((), ())), preferred_element_type=F32)


def product_of(left, right, left_axis, right_axis):
    return lax.dot_general(
        left, right, (((left_axis,), (right_axis,)), ((), ())), preferred_element_type=F32
    )


def sigmoid(value):
    return 0.5 * jnp.tanh(0.5 * value) + 0.5


def unit_of(value):
    centred = value - jnp.mean(value, axis=0, keepdims=True)
    scale = lax.rsqrt(jnp.mean(centred * centred, axis=0, keepdims=True) + EPS)
    return (centred * scale, scale)


def unit_back(grad, unit, scale, gain):
    scaled = grad * gain
    first = jnp.mean(scaled, axis=0, keepdims=True)
    second = jnp.mean(scaled * unit, axis=0, keepdims=True)
    return scale * (scaled - first - unit * second)


def fold(value):
    total = value[:, :LANES]
    for start in range(LANES, value.shape[1], LANES):
        total = total + value[:, start : start + LANES]
    return total


def read_rows(ref, rows):
    return jnp.concatenate([ref[row] for row in rows], axis=1)


def write_rows(ref, rows, value):
    cols = ref.shape[2]
    for place, row in enumerate(rows):
        ref[row] = value[:, place * cols : (place + 1) * cols].astype(ref.dtype)


def alternate(streams):
    while streams:
        going = []
        for stream in streams:
            try:
                next(stream)
                going.append(stream)
            except StopIteration:
                pass
        streams = going


class Wire:
    def __init__(self, wide, phase):
        self.wide, self.phase = wide, phase

    def tokens(self, row):
        width = self.wide.shape[1] // SUBLANES
        return pl.ds(self.phase * ROW_BLOCK + row, width, stride=SUBLANES)

    def read(self, rows):
        lanes = self.wide.shape[0]
        return jnp.concatenate(
            [self.wide[lane, self.tokens(row), :] for row in rows for lane in range(lanes)], axis=1
        )

    def write(self, rows, value):
        lanes = self.wide.shape[0]
        for place, row in enumerate(rows):
            for lane in range(lanes):
                start = (place * lanes + lane) * LANES
                self.wide[lane, self.tokens(row), :] = value[:, start : start + LANES]


def widen(wide, low, chunk):
    rows = pl.ds(pl.multiple_of(chunk * CHUNK_ROWS, CHUNK_ROWS), CHUNK_ROWS)

    def step(peer, carry):
        value = low[peer, rows, :].astype(F32)
        start = pl.multiple_of(peer * CHUNK_ROWS, CHUNK_ROWS)
        for lane in range(wide.shape[0]):
            wide[lane, pl.ds(start, CHUNK_ROWS), :] = value[:, lane * LANES : (lane + 1) * LANES]
        return carry

    lax.fori_loop(0, low.shape[0], step, 0)


def narrow(low, wide, chunk):
    rows = pl.ds(pl.multiple_of(chunk * CHUNK_ROWS, CHUNK_ROWS), CHUNK_ROWS)

    def step(peer, carry):
        start = pl.multiple_of(peer * CHUNK_ROWS, CHUNK_ROWS)
        low[peer, rows, :] = jnp.concatenate(
            [wide[lane, pl.ds(start, CHUNK_ROWS), :] for lane in range(wide.shape[0])], axis=1
        ).astype(low.dtype)
        return carry

    lax.fori_loop(0, low.shape[0], step, 0)


def triangle_start(weights, i, rows, wires, state):
    width = state.shape[0]
    unit, _ = unit_of(state)
    normed = (unit * weights.gain0[...]).astype(BF16)
    mixed = dot(weights.mix_t[...], normed)
    yield
    mask = read_rows(i.mask, rows)
    for wire, base in zip(wires, (0, 2 * width)):
        gate = sigmoid(mixed[base : base + width])
        wire.write(rows, mask * gate * mixed[base + width : base + 2 * width])


def triangle_finish(weights, rows, wire, state):
    unit, _ = unit_of(state)
    normed = (unit * weights.gain0[...]).astype(BF16)
    opened = dot(weights.gate_t[...], normed)
    yield
    tri_unit, tri_scale = unit_of(wire.read(rows))
    shaped = (tri_unit * weights.gain1[...]).astype(BF16)
    branch = dot(weights.out_t[...], shaped)
    yield
    gate = sigmoid(opened)
    return (state + gate * branch, (gate, tri_unit, tri_scale, shaped, branch))


def triangle_back_start(weights, o, rows, wire, grad, kept):
    gate, tri_unit, tri_scale, shaped, branch = kept
    grad_branch = (grad * gate).astype(BF16)
    grad_shaped = dot(weights.out[...], grad_branch)
    yield
    o.out[...] += dot_pairs(shaped, grad_branch)
    write_rows(o.grad_gate, rows, grad * branch * gate * (1.0 - gate))
    yield
    o.gain1[...] += fold(grad_shaped * tri_unit)
    wire.write(rows, unit_back(grad_shaped, tri_unit, tri_scale, weights.gain1[...]))


def triangle_back_finish(weights, i, o, rows, wires):
    grad, state = read_rows(i.grad, rows), read_rows(i.state, rows)
    width = state.shape[0]
    unit, scale = unit_of(state)
    gain = weights.gain0[...]
    normed = (unit * gain).astype(BF16)
    mixed = dot(weights.mix_t[...], normed)
    yield
    mask = read_rows(i.mask, rows)
    parts = []
    for wire, base in zip(wires, (0, 2 * width)):
        back = wire.read(rows) * mask
        gate = sigmoid(mixed[base : base + width])
        back_gate = back * gate
        parts.append((back_gate * mixed[base + width : base + 2 * width] * (1.0 - gate)).astype(BF16))
        parts.append(back_gate.astype(BF16))
    parts.append(read_rows(i.grad_gate, rows))
    grad_mixed = jnp.concatenate(parts, axis=0)
    yield
    grad_normed = dot(weights.mix[...], grad_mixed)
    o.mix[...] += dot_pairs(normed, grad_mixed)
    yield
    o.gain0[...] += fold(grad_normed * unit)
    return grad + unit_back(grad_normed, unit, scale, gain)


def transition(weights, state):
    unit, scale = unit_of(state)
    lifted = (unit * weights.gain[...]).astype(BF16)
    inner = dot(weights.up_t[...], lifted)
    yield
    half = inner.shape[0] // 2
    gate = inner[:half]
    slope = sigmoid(gate)
    product = (gate * slope * inner[half:]).astype(BF16)
    return (unit, scale, lifted, inner, slope, product)


def transition_back(weights, o, grad, kept):
    unit, scale, lifted, inner, slope, product = kept
    half = inner.shape[0] // 2
    gate, up = inner[:half], inner[half:]
    grad_low = grad.astype(BF16)
    grad_product = dot(weights.down[...], grad_low)
    o.down[...] += dot_pairs(product, grad_low)
    yield
    scaled = grad_product * slope
    grad_inner = jnp.concatenate(
        [
            (scaled * up * (1.0 + gate * (1.0 - slope))).astype(BF16),
            (scaled * gate).astype(BF16),
        ],
        axis=0,
    )
    yield
    grad_lifted = dot(weights.up[...], grad_inner)
    o.up[...] += dot_pairs(lifted, grad_inner)
    yield
    o.gain[...] += fold(grad_lifted * unit)
    return grad + unit_back(grad_lifted, unit, scale, weights.gain[...])


def head_back(i, o, rows, state):
    unit, scale = unit_of(state)
    gain = i.gain[...]
    shown = (unit * gain).astype(BF16)
    logits = dot(i.logits_t[...], shown)
    yield
    largest = jnp.max(logits, axis=0, keepdims=True)
    raised = jnp.exp(logits - largest)
    total = jnp.sum(raised, axis=0, keepdims=True)
    log_total = largest + jnp.log(total)
    target = read_rows(i.target, rows)
    weight = read_rows(i.weight, rows)
    hot = lax.broadcasted_iota(jnp.int32, logits.shape, 0) == target
    picked = jnp.sum(jnp.where(hot, logits, 0.0), axis=0, keepdims=True)
    o.loss[...] += fold(weight * (log_total - picked))
    o.count[...] += fold(weight)
    share = raised * (1.0 / total)
    grad_scores = (weight * (share - jnp.where(hot, 1.0, 0.0))).astype(BF16)
    grad_shown = dot(i.logits[...], grad_scores)
    o.logits[...] += dot_pairs(grad_scores, shown)
    yield
    o.gain[...] += fold(grad_shown * unit)
    return unit_back(grad_shown, unit, scale, gain)


def bins_hot(bins, rows, table_rows):
    bins = read_rows(bins, rows)
    shape = (table_rows, bins.shape[1])
    return jnp.where(lax.broadcasted_iota(jnp.int32, shape, 0) == bins, 1.0, 0.0).astype(BF16)


def run_stage(body, name, collective_id, group, inputs, outputs, products=None, wires=0):
    peers, half, rows, tokens = group
    args, outs = leaves_of(inputs), leaves_of(outputs)
    steps = rows // ROW_BLOCK
    chunks = rows // SUBLANES
    arriving = products.results if products else 0
    landed_args = [index for index, arg in enumerate(args) if arg.kind == LANDED]
    keeps = [place for place, out in enumerate(outs) if out.kind == LANDED]
    low = pltpu.VMEM((peers, rows * SUBLANES, tokens), BF16)
    many = pltpu.SemaphoreType.DMA((chunks, peers))
    wide = pltpu.VMEM((tokens // LANES, peers * CHUNK_ROWS, LANES), F32)
    groups = [
        [wide] * (arriving + len(landed_args) + wires),
        [low] * arriving,
        [many] * (2 * arriving),
        [low] * wires,
        [many] * (2 * wires),
        [pltpu.SemaphoreType.DMA((1,))] * len(keeps),
        products.scratch(low) if products else [],
    ]

    def kernel(*refs):
        step = pl.program_id(0)
        phase, chunk = lax.rem(step, PHASES), lax.div(step, PHASES)
        in_refs = [
            ref if arg.column is None else Column(ref, arg.column) for arg, ref in zip(args, refs)
        ]
        out_refs = list(refs[len(args) : len(args) + len(outs)])
        rest, parts = list(refs[len(args) + len(outs) :]), []
        for part in groups:
            parts.append(rest[: len(part)])
            rest = rest[len(part) :]
        wides, lands, land_sems, sends, send_sems, keep_sems, held = parts
        saves = [
            pltpu.make_async_copy(land, out_refs[place], sem.at[0])
            for land, place, sem in zip(lands, keeps, keep_sems)
        ]
        ring = Exchange(peers, half)
        i, o = bag_of(inputs, iter(in_refs)), bag_of(outputs, iter(out_refs))
        arrivals = [
            (result, land, land_sems[2 * place], land_sems[2 * place + 1])
            for place, (result, land) in enumerate(zip(held, lands))
        ]

        @pl.when(step == 0)
        def _():
            ring.greet()
            if products:
                products.load(i, held)
            for out, ref in zip(outs, out_refs):
                if out.kind == SUM:
                    ref[...] = jnp.zeros(out.shape, out.dtype)
            if products:
                products.multiply(i, o, held)
                ring.meet()

                def start(index, carry):
                    ring.start(arrivals, index)
                    return carry

                lax.fori_loop(0, chunks, start, 0)

        if products:

            @pl.when(phase == 0)
            def _():
                ring.wait(arrivals, chunk)
                for target, land in zip(wides, lands):
                    widen(target, land, chunk)

        if landed_args:

            @pl.when(phase == 0)
            def _():
                for target, index in zip(wides[arriving:], landed_args):
                    widen(target, in_refs[index], 0)

        if saves:

            @pl.when(step == steps - PHASES)
            def _():
                for save in saves:
                    save.start()

        body_in = list(in_refs)
        for index, source in zip(landed_args, wides[arriving:]):
            body_in[index] = Wire(source, phase)
        given = bag_of(inputs, iter(body_in))
        arrived = [Wire(source, phase) for source in wides[:arriving]]
        written = wides[arriving + len(landed_args) :]
        sent = [Wire(target, phase) for target in written]
        alternate(
            [
                body(given, o, range(first, first + STREAM_ROWS), arrived, sent)
                for first in range(0, ROW_BLOCK, STREAM_ROWS)
            ]
        )
        moves = [
            (send, land, send_sems[2 * place], send_sems[2 * place + 1])
            for place, (send, land) in enumerate(zip(sends, o.got if wires else []))
        ]
        if wires:

            @pl.when(phase == PHASES - 1)
            def _():
                for source, send in zip(written, sends):
                    narrow(send, source, chunk)
                if not products:

                    @pl.when(chunk == 0)
                    def _():
                        ring.meet()

                ring.start(moves, chunk)

        @pl.when(step == steps - 1)
        def _():
            if wires:

                def wait(index, carry):
                    ring.wait(moves, index)
                    return carry

                lax.fori_loop(0, chunks, wait, 0)
            for save in saves:
                save.wait()
            if products:
                products.end(o, held)

    results = pl.pallas_call(
        kernel,
        grid=(steps,),
        in_specs=[arg.spec() for arg in args],
        out_specs=[out.spec() for out in outs],
        out_shape=[jax.ShapeDtypeStruct(out.shape, out.dtype) for out in outs],
        scratch_shapes=sum(groups, []),
        compiler_params=pltpu.CompilerParams(
            dimension_semantics=(pltpu.ARBITRARY,),
            vmem_limit_bytes=VMEM_BYTES,
            has_side_effects=True,
            collective_id=collective_id,
        ),
        cost_estimate=pl.CostEstimate(flops=0, bytes_accessed=0, transcendentals=0),
        name=name,
    )(*[arg.array for arg in args])
    return bag_of(outputs, iter(results))


def flip(value, step, count):
    step = jnp.int32(step)
    result, bit = 0, 1
    while bit < count:
        result = result + lax.rem(lax.div(value, bit) + lax.div(step, bit), 2) * bit
        bit *= 2
    return result


def position(row, head, half, heads):
    inner = half // 2 * heads
    return (row % 2) * inner + (row // 2) * heads + head


def place_of(position, half, heads):
    inner = half // 2 * heads
    rest = lax.rem(position, inner)
    return (lax.div(rest, heads) * 2 + lax.div(position, inner), lax.rem(rest, heads))


class Exchange:
    def __init__(self, count, half):
        row, head = lax.axis_index("row"), lax.axis_index("head")
        place = lax.rem(row, half)
        inner = count // 2
        self.count = count
        self.half = half
        self.base = row - place
        self.me = lax.rem(place, 2) * inner + lax.div(place, 2) * (count // half) + head
        self.twin = (lax.rem(row + half, 2 * half), head)
        core = lax.div(self.me, inner)
        self.order = []
        for low in range(inner // 2):
            for step in (low, low + inner):
                other = step ^ (inner - 1)
                for first, second in ((step, other), (other, step)):
                    if first == 0 or second == 0:
                        if first:
                            self.order.append(first)
                    else:
                        self.order.append(first + core * (second - first))

    def peer(self, step):
        return flip(self.me, step, self.count)

    def device(self, peer):
        place, head = place_of(peer, self.half, self.count // self.half)
        return (self.base + place, head)

    def greet(self):
        barrier = pltpu.get_barrier_semaphore()
        for step in self.order:
            pl.semaphore_signal(
                barrier, inc=1, device_id=self.device(self.peer(step)), device_id_type=MESH
            )

    def meet(self):
        pl.semaphore_wait(pltpu.get_barrier_semaphore(), self.count - 1)

    def copies(self, moves, chunk, steps):
        found = []
        for source, target, send_sems, recv_sems in moves:
            size = source.shape[1] // send_sems.shape[0]
            rows = pl.ds(pl.multiple_of(chunk * size, PACKED), size)
            for step in steps:
                peer = self.me if step is None else self.peer(step)
                if step is None:
                    copy = pltpu.make_async_copy(
                        source.at[self.me, rows, :],
                        target.at[self.me, rows, :],
                        send_sems.at[chunk, 0],
                    )
                else:
                    copy = pltpu.make_async_remote_copy(
                        src_ref=source.at[peer, rows, :],
                        dst_ref=target.at[self.me, rows, :],
                        send_sem=send_sems.at[chunk, step],
                        recv_sem=recv_sems.at[chunk, step],
                        device_id=self.device(peer),
                        device_id_type=MESH,
                    )
                found.append(copy)
        return found

    def start(self, moves, chunk):
        for copy in self.copies(moves, chunk, self.order + [None]):
            copy.start()

    def wait(self, moves, chunk):
        for copy in self.copies(moves, chunk, self.order + [None]):
            copy.wait()


def join_channels(got, pair):
    peers, rows, _ = got.shape
    even, odd = [], []
    for peer in range(peers):
        for start in range(0, rows, CHUNK_ROWS):
            piece = got[peer, pl.ds(pl.multiple_of(start + pair * PACKED, PACKED), PACKED), :]
            piece = piece.astype(F32)
            even.append(piece[:SUBLANES])
            odd.append(piece[SUBLANES:])
    return [jnp.concatenate(pieces, axis=0).astype(BF16) for pieces in (even, odd)]


def split_channels(low, pair, even, odd, first=0):
    chunks = low.shape[1] // CHUNK_ROWS
    for start in range(0, even.shape[0], SUBLANES):
        block = (first + start) // SUBLANES
        row = block % chunks * CHUNK_ROWS + pair * PACKED
        low[block // chunks, pl.ds(pl.multiple_of(row, PACKED), PACKED), :] = jnp.concatenate(
            [even[start : start + SUBLANES], odd[start : start + SUBLANES]], axis=0
        ).astype(low.dtype)


def each_pair(body):
    for pair in range(SUBLANES // 2):
        body(pair)


class Forward:
    results = 1

    def __init__(self, tokens, incoming):
        self.tokens, self.incoming = tokens, incoming

    def scratch(self, low):
        block = pltpu.VMEM((SUBLANES, self.tokens, self.tokens), BF16)
        return [low] * 3 + [block] * 2 + [pltpu.SemaphoreType.DMA((4,))]

    def loads(self, i, held):
        return [
            pltpu.make_async_copy(i.got[place], held[1 + place], held[5].at[place])
            for place in range(2)
        ]

    def saves(self, o, held):
        return [
            pltpu.make_async_copy(held[3], o.left, held[5].at[2]),
            pltpu.make_async_copy(held[4], o.right, held[5].at[3]),
        ]

    def load(self, i, held):
        for copy in self.loads(i, held):
            copy.start()

    def multiply(self, i, o, held):
        tri, left_got, right_got, left_block, right_block = held[:5]
        for copy in self.loads(i, held):
            copy.wait()
        axis = 0 if self.incoming else 1

        def step(pair):
            lefts, rights = join_channels(left_got, pair), join_channels(right_got, pair)
            found = []
            for index in range(2):
                left_block[2 * pair + index] = lefts[index]
                right_block[2 * pair + index] = rights[index]
                found.append(product_of(lefts[index], rights[index], axis, axis))
            split_channels(tri, pair, *found)

        each_pair(step)
        for copy in self.saves(o, held):
            copy.start()

    def end(self, o, held):
        for copy in self.saves(o, held):
            copy.wait()


class Backward:
    results = 2

    def __init__(self, tokens, incoming):
        self.tokens, self.incoming = tokens, incoming

    def scratch(self, low):
        block = pltpu.VMEM((SUBLANES, self.tokens, self.tokens), BF16)
        return [low] * 3 + [block] * 2 + [pltpu.SemaphoreType.DMA((3,))]

    def loads(self, i, held):
        sources = (i.got[0], i.owned.left, i.owned.right)
        return [
            pltpu.make_async_copy(source, held[2 + place], held[5].at[place])
            for place, source in enumerate(sources)
        ]

    def load(self, i, held):
        for copy in self.loads(i, held):
            copy.start()

    def multiply(self, i, o, held):
        grad_left, grad_right, got, left_block, right_block = held[:5]
        for copy in self.loads(i, held):
            copy.wait()

        def step(pair):
            lefts, rights = [], []
            for index, grad in enumerate(join_channels(got, pair)):
                left, right = left_block[2 * pair + index], right_block[2 * pair + index]
                if self.incoming:
                    lefts.append(product_of(right, grad, 1, 1))
                    rights.append(product_of(left, grad, 1, 0))
                else:
                    lefts.append(product_of(grad, right, 1, 0))
                    rights.append(product_of(grad, left, 0, 0))
            split_channels(grad_left, pair, *lefts)
            split_channels(grad_right, pair, *rights)

        each_pair(step)

    def end(self, o, held):
        pass


def prepare(triangle_input, triangle_output, expand_weight, reduce_weight, distogram_weight, norm_gains):
    merged = [
        triangle_input.reshape((-1,) + triangle_input.shape[2:]),
        triangle_output.reshape((-1,) + triangle_output.shape[2:]),
        expand_weight,
        reduce_weight,
        distogram_weight.T[None],
    ]
    count = len(merged)

    def kernel(*refs):
        for source, plain, turned in zip(refs[:count], refs[count + 1 :: 2], refs[count + 2 :: 2]):
            for index in range(source.shape[0]):
                value = source[index]
                plain[index] = value.astype(BF16)
                turned[index] = value.T.astype(BF16)
        gains = refs[count][...]
        refs[-1][...] = gains.T

    shapes = []
    for array in merged:
        depth, rows, cols = array.shape
        shapes.append(jax.ShapeDtypeStruct((depth, rows, cols), BF16))
        shapes.append(jax.ShapeDtypeStruct((depth, cols, rows), BF16))
    shapes.append(jax.ShapeDtypeStruct(norm_gains.shape[::-1], F32))
    return pl.pallas_call(
        kernel,
        out_shape=shapes,
        compiler_params=pltpu.CompilerParams(vmem_limit_bytes=VMEM_BYTES),
        name="prepare",
    )(*merged, norm_gains)


def by_crop(value, rows_axis, head_axis):
    count, heads = rows_axis, head_axis
    half = count // 2
    inner = half // 2 * heads
    same, other = [], []
    for row in range(count):
        place = row % inner // heads * 2 + row // inner
        for head in range(heads):
            source = row * heads + head
            for crop, pairs in ((head, same), (1 - head, other)):
                pairs.append((source, (crop * half + place) * heads + row % heads))
    head = lax.axis_index("head")
    crop = lax.axis_index("row") // half
    mine = lax.dynamic_index_in_dim(value, head, 0, keepdims=False)
    rest = lax.dynamic_index_in_dim(value, 1 - head, 0, keepdims=False)
    mine = lax.ppermute(mine, ("row", "head"), same)
    rest = lax.ppermute(rest, ("row", "head"), other)
    low = jnp.where(crop == 0, mine, rest)
    high = jnp.where(crop == 0, rest, mine)
    return jnp.concatenate([low, high], axis=-1)


def reduce_rest(half, peers, collective_id, grids, gains, rows):
    sizes = [grid.shape[0] * grid.shape[1] // LANES for grid in grids]
    used = sum(sizes) + len(gains) + SUBLANES * len(rows)
    part = -(-used // (peers * SUBLANES)) * SUBLANES
    total = part * peers
    starts, spot = [], 0
    for size in sizes:
        starts.append(spot)
        spot += size
    row_starts = []
    for _ in rows:
        row_starts.append(spot)
        spot += SUBLANES
    gain_start = spot
    count = len(grids) + len(gains) + len(rows)

    def kernel(*refs):
        out, local, got, mine, other, sends, recvs, back_sends, back_recvs, twin_sems = refs[count:]
        ring = Exchange(peers, half)
        ring.greet()
        barrier = pltpu.get_barrier_semaphore()
        pl.semaphore_signal(barrier, inc=1, device_id=ring.twin, device_id_type=MESH)
        for grid, start in zip(refs[: len(grids)], starts):
            height, width = grid.shape
            for column in range(width // LANES):
                local[pl.ds(start + column * height, height), :] = grid[
                    :, column * LANES : (column + 1) * LANES
                ]
        ones = jnp.ones((SUBLANES, LANES), F32)
        for index, gain in enumerate(refs[len(grids) : len(grids) + len(gains)]):
            folded = lax.dot_general(
                ones,
                gain[...],
                (((1,), (1,)), ((), ())),
                precision=lax.Precision.HIGHEST,
                preferred_element_type=F32,
            )
            local[pl.ds(gain_start + index, 1), :] = folded[:1]
        for row, start in zip(refs[len(grids) + len(gains) : count], row_starts):
            local[pl.ds(start, 1), :] = row[...]
            local[pl.ds(start + 1, SUBLANES - 1), :] = jnp.zeros((SUBLANES - 1, LANES), F32)
        tail = gain_start + len(gains)
        if total > tail:
            local[pl.ds(tail, total - tail), :] = jnp.zeros((total - tail, LANES), F32)
        pl.semaphore_wait(barrier, peers)

        def block(peer):
            return pl.ds(pl.multiple_of(peer * part, SUBLANES), part)

        here = block(ring.me)

        def gather(step):
            peer = ring.peer(step)
            return pltpu.make_async_remote_copy(
                src_ref=local.at[block(peer), :],
                dst_ref=got.at[here, :],
                send_sem=sends.at[step],
                recv_sem=recvs.at[step],
                device_id=ring.device(peer),
                device_id_type=MESH,
            )

        def spread(step):
            return pltpu.make_async_remote_copy(
                src_ref=out.at[here, :],
                dst_ref=out.at[here, :],
                send_sem=back_sends.at[step],
                recv_sem=back_recvs.at[step],
                device_id=ring.device(ring.peer(step)),
                device_id_type=MESH,
            )

        for step in ring.order:
            gather(step).start()
        got[here, :] = local[here, :]
        for step in ring.order:
            gather(step).wait()
        value = got[pl.ds(0, part), :]
        for peer in range(1, peers):
            value = value + got[pl.ds(peer * part, part), :]
        mine[...] = value
        copy = pltpu.make_async_remote_copy(
            src_ref=mine,
            dst_ref=other,
            send_sem=twin_sems.at[0],
            recv_sem=twin_sems.at[1],
            device_id=ring.twin,
            device_id_type=MESH,
        )
        copy.start()
        copy.wait()
        out[here, :] = mine[...] + other[...]
        for step in ring.order:
            spread(step).start()
        for step in ring.order:
            spread(step).wait()

    inside = pl.BlockSpec(memory_space=pltpu.VMEM)
    whole = pl.pallas_call(
        kernel,
        in_specs=[inside] * count,
        out_specs=inside,
        out_shape=jax.ShapeDtypeStruct((total, LANES), F32),
        scratch_shapes=[pltpu.VMEM((total, LANES), F32)] * 2
        + [pltpu.VMEM((part, LANES), F32)] * 2
        + [pltpu.SemaphoreType.DMA((peers,))] * 4
        + [pltpu.SemaphoreType.DMA((2,))],
        compiler_params=pltpu.CompilerParams(
            collective_id=collective_id, has_side_effects=True, vmem_limit_bytes=VMEM_BYTES
        ),
        cost_estimate=pl.CostEstimate(flops=0, bytes_accessed=0, transcendentals=0),
        name="reduce_rest",
    )(*grids, *gains, *rows)
    return whole, starts, row_starts, gain_start


def update(rest, starts, row_starts, gain_start, early, weights, firsts, seconds):
    layers, kinds, width, mixed = weights[2].shape
    hidden = weights[4].shape[2]
    early_in, early_up, early_rows = early
    given = [rest, *early_in, *early_up, *early_rows]
    count = len(given)

    def kernel(*refs):
        whole = refs[0]
        in_refs = refs[1 : 1 + len(early_in)]
        up_refs = refs[1 + len(early_in) : count - layers]
        row_refs = refs[count - layers : count]
        states = [refs[count + 8 * kind : count + 8 * (kind + 1)] for kind in range(3)]
        scalars = refs[count + 24 : count + 27]
        results = refs[count + 27 :]

        def taken(start, size):
            return whole[pl.ds(start, size), :]

        def wide(start, height, columns):
            return jnp.concatenate(
                [taken(start + column * height, height) for column in range(columns)], axis=1
            )

        loss = jnp.sum(taken(row_starts[0], 1), axis=1, keepdims=True)
        valid = jnp.sum(taken(row_starts[1], 1), axis=1, keepdims=True)
        table_rows, single_rows = weights[0].shape[0], weights[1].shape[0]
        downs = hidden // 2
        grads = {}
        grads[0, ()] = taken(starts[4], table_rows)
        grads[1, ()] = jnp.concatenate(
            [taken(starts[5], single_rows), taken(starts[6], single_rows)], axis=1
        )
        for layer in range(layers):
            spot = 0
            for kind in range(kinds):
                if layer == 0:
                    grads[2, (layer, kind)] = wide(starts[kind], width, mixed // LANES)
                else:
                    grads[2, (layer, kind)] = in_refs[(layer - 1) * kinds + kind][...]
                if layer == 0 and kind == 0:
                    grads[3, (layer, kind)] = taken(starts[2], width)
                else:
                    grads[3, (layer, kind)] = row_refs[layer][pl.ds(spot, width), :]
                    spot += width
            grads[4, (layer,)] = up_refs[layer][...]
            grads[5, (layer,)] = row_refs[layer][pl.ds(spot, downs), :]
        grads[6, ()] = taken(starts[3], weights[6].shape[0])
        grads[7, ()] = taken(gain_start, weights[7].shape[0])
        squares = jnp.zeros((1, 1), F32)
        for key in grads:
            grads[key] = grads[key] / valid
            squares = squares + jnp.sum(grads[key] * grads[key], axis=(0, 1), keepdims=True)
        norm = jnp.sqrt(squares)
        factor = jnp.minimum(1.0, CLIP_NORM / (norm + 1e-06))
        for ref, value in zip(scalars, (loss, valid, norm)):
            ref[...] = value
        for (index, spot), grad in grads.items():
            rate = GAIN_RATE if index == 7 else WEIGHT_RATE
            decay = 0.0 if index == 7 else WEIGHT_DECAY
            new = adamw(
                states[0][index][spot],
                grad * factor,
                states[1][index][spot],
                states[2][index][spot],
                rate,
                decay,
            )
            for ref, value in zip(results[3 * index : 3 * index + 3], new):
                ref[spot] = value

    one = jax.ShapeDtypeStruct((1, 1), F32)
    shapes = [one] * 3
    for weight in weights:
        shapes += [jax.ShapeDtypeStruct(weight.shape, F32)] * 3
    found = pl.pallas_call(
        kernel,
        out_shape=shapes,
        compiler_params=pltpu.CompilerParams(vmem_limit_bytes=VMEM_BYTES),
        name="update",
    )(*given, *weights, *firsts, *seconds)
    return tuple(value[0, 0] for value in found[:3]) + tuple(found[3:])


def step_by_crop(row_count, head_count, given, weights, firsts, seconds):
    single, residue_index, chain_index, token_mask, pair_valid, target_bins = given
    relative_table, single_weight, triangle_input, triangle_output = weights[:4]
    expand_weight, reduce_weight, distogram_weight, norm_gains = weights[4:]
    crops, tokens = token_mask.shape
    width = relative_table.shape[1]
    layers = triangle_input.shape[0]
    half = row_count // crops
    peers = half * head_count
    rows = tokens // peers
    row_index = lax.axis_index("row")
    crop = row_index // half
    start = position(row_index % half, lax.axis_index("head"), half, head_count) * rows

    placed = by_crop(jnp.stack([pair_valid, target_bins], axis=1), row_count, head_count)
    valid, target = placed[0], placed[1]

    def of_crop(array):
        return lax.dynamic_index_in_dim(array, crop, 0, keepdims=False)

    def of_rows(array):
        return lax.dynamic_slice_in_dim(array, start, rows, 0)

    residues, chains = of_crop(residue_index), of_crop(chain_index)
    reach = (relative_table.shape[0] - 2) // 2
    bins = jnp.where(
        of_rows(chains)[:, None] == chains[None, :],
        jnp.clip(of_rows(residues)[:, None] - residues[None, :], -reach, reach) + reach,
        2 * reach + 1,
    )
    present = of_crop(token_mask).astype(F32)
    pair_mask = of_rows(present)[:, None] * present[None, :]
    loss_weight = pair_mask * valid.astype(F32)
    table_rows = -(-relative_table.shape[0] // PACKED) * PACKED
    table_t = jnp.pad(relative_table, ((0, table_rows - relative_table.shape[0]), (0, 0))).T
    tokens_single = of_crop(single)
    proj = project(tokens_single, single_weight.astype(BF16))
    proj_rows = of_rows(proj[:, :width])[:, :, None]
    proj_cols = proj[:, width:].T
    bins, pair_mask = Arg(bins[:, None, :], ROWS), Arg(pair_mask[:, None, :], ROWS)

    prepared = prepare(
        triangle_input, triangle_output, expand_weight, reduce_weight, distogram_weight, norm_gains
    )
    mix, mix_t, out, out_t, up, up_t, down, down_t, logits_t, logits, gains = prepared
    hidden = up.shape[2]

    def gain(index):
        return Arg(gains, WHOLE, column=index)

    def layer_of(array, index, *block):
        shape = block or array.shape[1:]
        return Arg(array, WHOLE, (index, 0, 0), (None,) + tuple(shape))

    def triangle_weights(layer, kind, starts=False, finishes=False, back=False):
        index = 2 * layer + kind
        found = dict(gain0=gain(5 * layer + 2 * kind))
        if starts:
            found.update(mix_t=layer_of(mix_t, index, 4 * width, width))
        if starts and back:
            found.update(mix=layer_of(mix, index))
        if finishes:
            found.update(
                gain1=gain(5 * layer + 2 * kind + 1),
                gate_t=Arg(mix_t, WHOLE, (index, 4, 0), (None, width, width)),
                out_t=layer_of(out_t, index),
            )
        if finishes and back:
            found.update(out=layer_of(out, index))
        return found

    def transition_weights(layer, forth=True, back=False):
        found = dict(gain=gain(5 * layer + 4), up_t=layer_of(up_t, layer))
        if forth:
            found.update(down_t=layer_of(down_t, layer))
        if back:
            found.update(up=layer_of(up, layer), down=layer_of(down, layer))
        return found

    def state_out():
        return Out((rows, width, tokens), F32, ROWS)

    def sum_out(*shape):
        return Out(shape, F32, SUM)

    def gain_out():
        return sum_out(width, LANES)

    def back_start_outs():
        return dict(
            grad_gate=Out((rows, width, tokens), BF16, ROWS),
            out=sum_out(width, width),
            gain1=gain_out(),
        )

    def back_finish_outs():
        return dict(mix=sum_out(width, 5 * width), gain0=gain_out())

    def transition_outs():
        return dict(up=sum_out(width, hidden), down=sum_out(hidden // 2, width), gain=gain_out())

    identities = iter(range(4 * layers + 2))

    group = (peers, half, rows, tokens)
    block_out = Out((SUBLANES, tokens, tokens), BF16, ANYWHERE)

    def got_out(count):
        return [Out((peers, rows * SUBLANES, tokens), BF16, ANYWHERE)] * count

    def got_in(stage):
        return [Arg(array, ANYWHERE) for array in stage.got]

    def landed_out():
        return Out((peers, rows * SUBLANES, tokens), BF16, LANDED)

    def owned(kept):
        return dict(left=Arg(kept.left, ANYWHERE), right=Arg(kept.right, ANYWHERE))

    kept, states, middles, tris = {}, {}, {}, {}

    def first_body(i, o, rows, arrived, sent):
        state = dot(i.table_t[...], bins_hot(i.bins, rows, table_rows))
        yield
        cols = i.proj_cols[...]
        state = state + jnp.concatenate([cols + i.proj_rows[row] for row in rows], axis=1)
        write_rows(o.state, rows, state)
        yield from triangle_start(i.start, i, rows, sent, state)

    got = run_stage(
        first_body,
        "first_state",
        next(identities),
        group,
        dict(
            bins=bins,
            proj_rows=Arg(proj_rows, ROWS),
            proj_cols=Arg(proj_cols, WHOLE),
            table_t=Arg(table_t.astype(BF16), WHOLE),
            mask=pair_mask,
            start=triangle_weights(0, 0, starts=True),
        ),
        dict(state=state_out(), got=got_out(2)),
        wires=2,
    )
    states[0, 0] = got.state

    def between_body(i, o, rows, arrived, sent):
        state, _ = yield from triangle_finish(
            i.end, rows, arrived[0], read_rows(i.state, rows)
        )
        write_rows(o.state, rows, state)
        yield from triangle_start(i.start, i, rows, sent, state)

    def layer_end_body(i, o, rows, arrived, sent):
        state, _ = yield from triangle_finish(
            i.end, rows, arrived[0], read_rows(i.state, rows)
        )
        write_rows(o.middle, rows, state)
        lifted = yield from transition(i.lift, state)
        state = state + dot(i.lift.down_t[...], lifted[5])
        yield
        write_rows(o.state, rows, state)
        yield from triangle_start(i.start, i, rows, sent, state)

    for layer in range(layers):
        got = run_stage(
            between_body,
            "between_updates",
            next(identities),
            group,
            dict(
                got=got_in(got),
                state=Arg(states[layer, 0], ROWS),
                mask=pair_mask,
                end=triangle_weights(layer, 0, finishes=True),
                start=triangle_weights(layer, 1, starts=True),
            ),
            dict(
                state=state_out(),
                landed=landed_out(),
                left=block_out,
                right=block_out,
                got=got_out(2),
            ),
            Forward(tokens, False),
            wires=2,
        )
        kept[layer, 0], states[layer, 1], tris[layer, 0] = got, got.state, got.landed
        if layer + 1 == layers:
            break
        got = run_stage(
            layer_end_body,
            "layer_end",
            next(identities),
            group,
            dict(
                got=got_in(got),
                state=Arg(states[layer, 1], ROWS),
                mask=pair_mask,
                end=triangle_weights(layer, 1, finishes=True),
                lift=transition_weights(layer),
                start=triangle_weights(layer + 1, 0, starts=True),
            ),
            dict(
                middle=state_out(),
                state=state_out(),
                landed=landed_out(),
                left=block_out,
                right=block_out,
                got=got_out(2),
            ),
            Forward(tokens, True),
            wires=2,
        )
        kept[layer, 1], states[layer + 1, 0], tris[layer, 1] = got, got.state, got.landed
        middles[layer] = got.middle

    def loss_body(i, o, rows, arrived, sent):
        state, kept_triangle = yield from triangle_finish(
            i.end, rows, arrived[0], read_rows(i.state, rows)
        )
        lifted = yield from transition(i.lift, state)
        state = state + dot(i.lift.down_t[...], lifted[5])
        yield
        grad = yield from head_back(i.head, o.head, rows, state)
        grad = yield from transition_back(i.lift, o.lift, grad, lifted)
        write_rows(o.grad, rows, grad)
        yield from triangle_back_start(i.end, o.end, rows, sent[0], grad, kept_triangle)

    top = layers - 1
    got = run_stage(
        loss_body,
        "loss",
        next(identities),
        group,
        dict(
            got=got_in(got),
            state=Arg(states[top, 1], ROWS),
            end=triangle_weights(top, 1, finishes=True, back=True),
            lift=transition_weights(top, back=True),
            head=dict(
                gain=gain(5 * layers),
                logits=layer_of(logits, 0),
                logits_t=layer_of(logits_t, 0),
                target=Arg(target[:, None, :], ROWS),
                weight=Arg(loss_weight[:, None, :], ROWS),
            ),
        ),
        dict(
            grad=state_out(),
            head=dict(
                loss=sum_out(1, LANES),
                count=sum_out(1, LANES),
                logits=sum_out(distogram_weight.shape[1], width),
                gain=gain_out(),
            ),
            lift=transition_outs(),
            end=back_start_outs(),
            left=block_out,
            right=block_out,
            got=got_out(1),
        ),
        Forward(tokens, True),
        wires=1,
    )
    kept[top, 1] = got
    head, lifts, ends, begins = got.head, {top: got.lift}, {(top, 1): got.end}, {}

    def between_back_body(i, o, rows, arrived, sent):
        grad = yield from triangle_back_finish(i.start, i, o.start, rows, arrived)
        write_rows(o.grad, rows, grad)
        _, kept_triangle = yield from triangle_finish(
            i.end, rows, i.tri, read_rows(i.before, rows)
        )
        yield from triangle_back_start(i.end, o.end, rows, sent[0], grad, kept_triangle)

    def layer_end_back_body(i, o, rows, arrived, sent):
        grad = yield from triangle_back_finish(i.start, i, o.start, rows, arrived)
        lifted = yield from transition(i.lift, read_rows(i.middle, rows))
        grad = yield from transition_back(i.lift, o.lift, grad, lifted)
        write_rows(o.grad, rows, grad)
        _, kept_triangle = yield from triangle_finish(
            i.end, rows, i.tri, read_rows(i.before, rows)
        )
        yield from triangle_back_start(i.end, o.end, rows, sent[0], grad, kept_triangle)

    def first_back_body(i, o, rows, arrived, sent):
        grad = yield from triangle_back_finish(i.start, i, o.start, rows, arrived)
        hot = bins_hot(i.bins, rows, table_rows)
        high = grad.astype(BF16)
        low = (grad - high.astype(F32)).astype(BF16)
        o.table[...] += dot_pairs(hot, high) + dot_pairs(hot, low)
        yield
        for place, row in enumerate(rows):
            part = grad[:, place * tokens : (place + 1) * tokens]
            o.rows[row] = fold(part)
            o.cols[...] += part

    def layer_sums(layer):
        kinds = (0, 1) if layer else (1,)
        mixes = [begins[layer, 1].mix] if layer else []
        if layer + 1 < layers:
            mixes.append(begins[layer + 1, 0].mix)
        outs = [ends[layer, kind].out for kind in kinds]
        return (mixes, lifts[layer].up, jnp.concatenate(outs + [lifts[layer].down], axis=0))

    for layer in reversed(range(layers)):
        for kind in (1, 0):
            inputs = dict(
                got=got_in(got),
                owned=owned(kept[layer, kind]),
                grad=Arg(got.grad, ROWS),
                grad_gate=Arg(got.end.grad_gate, ROWS),
                state=Arg(states[layer, kind], ROWS),
                mask=pair_mask,
                start=triangle_weights(layer, kind, starts=True, back=True),
            )
            outputs = dict(start=back_finish_outs())
            products = Backward(tokens, kind == 1)
            if layer == 0 and kind == 0:
                got = run_stage(
                    first_back_body,
                    "first_state_back",
                    next(identities),
                    group,
                    dict(bins=bins, **inputs),
                    dict(
                        table=sum_out(table_rows, width),
                        rows=Out((rows, width, LANES), F32, ROWS),
                        cols=sum_out(width, tokens),
                        **outputs,
                    ),
                    products,
                )
                begins[layer, kind] = got.start
                break
            before = (layer, 0) if kind == 1 else (layer - 1, 1)
            inputs.update(
                before=Arg(states[before], ROWS),
                tri=Arg(tris[before], LANDED),
                end=triangle_weights(*before, finishes=True, back=True),
            )
            outputs.update(grad=state_out(), end=back_start_outs(), got=got_out(1))
            if kind == 1:
                body, name = between_back_body, "between_updates_back"
            else:
                body, name = layer_end_back_body, "layer_end_back"
                inputs.update(
                    middle=Arg(middles[layer - 1], ROWS),
                    lift=transition_weights(layer - 1, forth=False, back=True),
                )
                outputs.update(lift=transition_outs())
            got = run_stage(
                body, name, next(identities), group, inputs, outputs, products, wires=1
            )
            begins[layer, kind], ends[before] = got.start, got.end
            if kind == 0:
                lifts[layer - 1] = got.lift

    early = lax.psum({layer: layer_sums(layer) for layer in range(layers)}, ("row", "head"))
    early_mixes = {}
    for layer in range(layers):
        mixes = list(early[layer][0])
        if layer:
            early_mixes[layer, 1] = mixes.pop(0)
        if mixes:
            early_mixes[layer + 1, 0] = mixes.pop(0)
    early = (
        [early_mixes[layer, kind] for layer in range(1, layers) for kind in range(2)],
        [early[layer][1] for layer in range(layers)],
        [early[layer][2] for layer in range(layers)],
    )

    wide_single = tokens_single.astype(F32)
    row_part = jnp.einsum(
        "is,ic->sc",
        of_rows(wide_single),
        jnp.sum(got.rows, axis=2),
        precision=lax.Precision.HIGHEST,
    )
    col_part = jnp.einsum("js,cj->sc", wide_single, got.cols, precision=lax.Precision.HIGHEST)
    partial_gains = []
    for layer in range(layers):
        for kind in range(2):
            partial_gains += [begins[layer, kind].gain0, ends[layer, kind].gain1]
        partial_gains.append(lifts[layer].gain)
    partial_gains.append(head.gain)
    grids = [
        begins[0, 0].mix,
        begins[0, 1].mix,
        ends[0, 0].out,
        head.logits,
        got.table,
        row_part,
        col_part,
    ]
    def turned(arrays):
        return arrays[:6] + (arrays[6].T,) + arrays[7:]

    rest, *starts = reduce_rest(
        half, peers, next(identities), grids, partial_gains, [head.loss, head.count]
    )
    found = update(rest, *starts, early, turned(weights), turned(firsts), turned(seconds))
    return found[:21] + tuple(value.T for value in found[21:24]) + found[24:]


def per_device(
    row_count,
    head_count,
    single,
    residue_index,
    chain_index,
    token_mask,
    pair_valid,
    target_bins,
    relative_table,
    single_weight,
    triangle_input,
    triangle_output,
    expand_weight,
    reduce_weight,
    distogram_weight,
    norm_gains,
    first_table,
    second_table,
    first_single,
    second_single,
    first_input,
    second_input,
    first_output,
    second_output,
    first_expand,
    second_expand,
    first_reduce,
    second_reduce,
    first_logits,
    second_logits,
    first_gains,
    second_gains,
):
    crops, tokens = token_mask.shape
    width = relative_table.shape[1]
    peers = row_count * head_count // crops
    given = (
        single,
        residue_index,
        chain_index,
        token_mask,
        pair_valid,
        target_bins,
        relative_table,
        single_weight,
        triangle_input,
        triangle_output,
        expand_weight,
        reduce_weight,
        distogram_weight,
        norm_gains,
    )
    weights = (
        relative_table,
        single_weight,
        triangle_input,
        triangle_output,
        expand_weight,
        reduce_weight,
        distogram_weight,
        norm_gains,
    )
    firsts = (
        first_table,
        first_single,
        first_input,
        first_output,
        first_expand,
        first_reduce,
        first_logits,
        first_gains,
    )
    seconds = (
        second_table,
        second_single,
        second_input,
        second_output,
        second_expand,
        second_reduce,
        second_logits,
        second_gains,
    )
    if (
        crops == 2
        and head_count == 2
        and width == LANES
        and width == SUBLANES * peers
        and tokens % (peers * SUBLANES) == 0
        and tokens % (3 * LANES) == 0
    ):
        return step_by_crop(row_count, head_count, given[:6], weights, firsts, seconds)
    local = gradients_by_block(*given)
    summed = lax.psum(local, ("row", "head"))
    loss_sum, valid_count = summed[0], summed[1]
    grads = [grad / valid_count for grad in summed[2:]]
    squares = jnp.zeros((), jnp.float32)
    for g in grads:
        squares = squares + jnp.sum(g * g)
    gradient_norm = jnp.sqrt(squares)
    factor = jnp.minimum(1.0, CLIP_NORM / (gradient_norm + 1e-06))
    result = []
    for index in range(8):
        rate = GAIN_RATE if index == 7 else WEIGHT_RATE
        decay = 0.0 if index == 7 else WEIGHT_DECAY
        result.extend(
            adamw(weights[index], grads[index] * factor, firsts[index], seconds[index], rate, decay)
        )
    return (
        loss_sum,
        valid_count,
        gradient_norm,
        result[0],
        result[1],
        result[2],
        result[3],
        result[4],
        result[5],
        result[6],
        result[7],
        result[8],
        result[9],
        result[10],
        result[11],
        result[12],
        result[13],
        result[14],
        result[15],
        result[16],
        result[17],
        result[18],
        result[19],
        result[20],
        result[21],
        result[22],
        result[23],
    )


def solution(mesh):
    placed = (
        P(),
        P(),
        P(),
        P(),
        P(None, "row", "head"),
        P(None, "row", "head"),
        P(),
        P(),
        P(),
        P(),
        P(),
        P(),
        P(),
        P(),
        P(),
        P(),
        P(),
        P(),
        P(),
        P(),
        P(),
        P(),
        P(),
        P(),
        P(),
        P(),
        P(),
        P(),
        P(),
        P(),
    )
    return jax.shard_map(
        functools.partial(per_device, mesh.shape["row"], mesh.shape["head"]),
        mesh=mesh,
        in_specs=placed,
        out_specs=(
            P(),
            P(),
            P(),
            P(),
            P(),
            P(),
            P(),
            P(),
            P(),
            P(),
            P(),
            P(),
            P(),
            P(),
            P(),
            P(),
            P(),
            P(),
            P(),
            P(),
            P(),
            P(),
            P(),
            P(),
            P(),
            P(),
            P(),
        ),
        check_vma=False,
    )
```

```python
import functools

import jax
import jax.numpy as jnp
from jax import lax
from jax.experimental import pallas as pl
from jax.experimental.pallas import tpu as pltpu
from jax.sharding import PartitionSpec as P

STEP = 10


EPS = 1e-05
BETA_ONE = 0.9
BETA_TWO = 0.999
ADAM_EPS = 1e-08
WEIGHT_RATE = 0.1
GAIN_RATE = 0.5
WEIGHT_DECAY = 0.01
CLIP_NORM = 0.002


def normalize(value):
    mean = jnp.mean(value, axis=-1, keepdims=True)
    centred = value - mean
    scale = lax.rsqrt(jnp.mean(centred * centred, axis=-1, keepdims=True) + EPS)
    return (centred * scale, scale)


def norm_back(grad_out, unit, scale, gain):
    scaled = grad_out * gain
    first_mean = jnp.mean(scaled, axis=-1, keepdims=True)
    second_mean = jnp.mean(scaled * unit, axis=-1, keepdims=True)
    grad_in = scale * (scaled - first_mean - unit * second_mean)
    grad_gain = jnp.sum(grad_out * unit, axis=tuple(range(grad_out.ndim - 1)))
    return (grad_in, grad_gain)


def project(value, weight):
    return jnp.einsum("...c,cd->...d", value, weight, preferred_element_type=jnp.float32)


def project_back(grad, weight):
    return jnp.einsum("...d,cd->...c", grad, weight, preferred_element_type=jnp.float32)


def weight_grad(value, grad):
    return jnp.einsum("bijc,bijd->cd", value, grad, preferred_element_type=jnp.float32)


def triangle_forward(state, weight_in, weight_out, gains, pair_mask, incoming):
    hidden = weight_out.shape[0]
    pair_unit, pair_scale = normalize(state)
    normed = (pair_unit * gains[0]).astype(jnp.bfloat16)
    mixed = project(normed, weight_in)
    mask = pair_mask[..., None]
    left = (mask * jax.nn.sigmoid(mixed[..., :hidden]) * mixed[..., hidden : 2 * hidden]).astype(
        jnp.bfloat16
    )
    right = (
        mask
        * jax.nn.sigmoid(mixed[..., 2 * hidden : 3 * hidden])
        * mixed[..., 3 * hidden : 4 * hidden]
    ).astype(jnp.bfloat16)
    left_cols, right_cols = (
        lax.all_to_all(left, "head", split_axis=3, concat_axis=2, tiled=True),
        lax.all_to_all(right, "head", split_axis=3, concat_axis=2, tiled=True),
    )
    if incoming:
        left_cols, right_cols = (
            lax.all_to_all(left_cols, "row", split_axis=2, concat_axis=1, tiled=True),
            lax.all_to_all(right_cols, "row", split_axis=2, concat_axis=1, tiled=True),
        )
        left_cols = jnp.swapaxes(left_cols, 1, 2)
        right_cols = jnp.swapaxes(right_cols, 1, 2)
    right_all = lax.all_gather(right_cols, "row", axis=1, tiled=True)
    triangle = jnp.einsum(
        "bikc,bjkc->bijc", left_cols, right_all, preferred_element_type=jnp.float32
    )
    triangle = lax.all_to_all(
        triangle.astype(jnp.bfloat16), "head", split_axis=2, concat_axis=3, tiled=True
    )
    tri_unit, tri_scale = normalize(triangle.astype(jnp.float32))
    shaped = (tri_unit * gains[1]).astype(jnp.bfloat16)
    branch = project(shaped, weight_out)
    gate = jax.nn.sigmoid(mixed[..., 4 * hidden :])
    kept = (
        pair_unit,
        pair_scale,
        normed,
        mixed,
        left_cols,
        right_all,
        tri_unit,
        tri_scale,
        shaped,
        branch,
        gate,
    )
    return (state + gate * branch, kept)


def triangle_backward(grad_state, kept, weight_in, weight_out, gains, pair_mask, incoming):
    hidden = weight_out.shape[0]
    (
        pair_unit,
        pair_scale,
        normed,
        mixed,
        left_cols,
        right_all,
        tri_unit,
        tri_scale,
        shaped,
        branch,
        gate,
    ) = kept
    grad_branch = (grad_state * gate).astype(jnp.bfloat16)
    grad_gate = grad_state * branch * gate * (1.0 - gate)
    grad_out = weight_grad(shaped, grad_branch)
    grad_shaped = project_back(grad_branch, weight_out)
    grad_tri, gain_two = norm_back(grad_shaped, tri_unit, tri_scale, gains[1])
    tri_cols = lax.all_to_all(
        grad_tri.astype(jnp.bfloat16), "head", split_axis=3, concat_axis=2, tiled=True
    )
    grad_left = jnp.einsum(
        "bijc,bjkc->bikc", tri_cols, right_all, preferred_element_type=jnp.float32
    )
    grad_left = grad_left.astype(jnp.bfloat16)
    summed = lax.psum_scatter(
        jnp.einsum(
            "bijc,bikc->jbkc", tri_cols, left_cols, preferred_element_type=jnp.float32
        ).astype(jnp.bfloat16),
        "row",
        scatter_dimension=0,
        tiled=True,
    ).astype(jnp.float32)
    grad_right = jnp.transpose(summed, (1, 0, 2, 3)).astype(jnp.bfloat16)
    if incoming:
        grad_left, grad_right = (
            lax.all_to_all(
                jnp.swapaxes(grad_left, 1, 2), "row", split_axis=1, concat_axis=2, tiled=True
            ),
            lax.all_to_all(
                jnp.swapaxes(grad_right, 1, 2), "row", split_axis=1, concat_axis=2, tiled=True
            ),
        )
    back_left, back_right = (
        lax.all_to_all(grad_left, "head", split_axis=2, concat_axis=3, tiled=True),
        lax.all_to_all(grad_right, "head", split_axis=2, concat_axis=3, tiled=True),
    )
    mask = pair_mask[..., None]
    back_left = back_left.astype(jnp.float32) * mask
    back_right = back_right.astype(jnp.float32) * mask
    left_sig = jax.nn.sigmoid(mixed[..., :hidden])
    left_value = mixed[..., hidden : 2 * hidden]
    right_sig = jax.nn.sigmoid(mixed[..., 2 * hidden : 3 * hidden])
    right_value = mixed[..., 3 * hidden : 4 * hidden]
    grad_mixed = jnp.concatenate(
        [
            back_left * left_value * left_sig * (1.0 - left_sig),
            back_left * left_sig,
            back_right * right_value * right_sig * (1.0 - right_sig),
            back_right * right_sig,
            grad_gate,
        ],
        axis=-1,
    ).astype(jnp.bfloat16)
    grad_in = weight_grad(normed, grad_mixed)
    grad_normed = project_back(grad_mixed, weight_in)
    grad_first, gain_one = norm_back(grad_normed, pair_unit, pair_scale, gains[0])
    return (grad_state + grad_first, (grad_in, grad_out, gain_one, gain_two))


def transition_forward(state, weight_up, weight_down, gain):
    expand = weight_down.shape[0]
    unit, scale = normalize(state)
    lifted = (unit * gain).astype(jnp.bfloat16)
    inner = project(lifted, weight_up)
    product = (jax.nn.silu(inner[..., :expand]) * inner[..., expand:]).astype(jnp.bfloat16)
    return (state + project(product, weight_down), (unit, scale, lifted, inner, product))


def transition_backward(grad_state, kept, weight_up, weight_down, gain):
    expand = weight_down.shape[0]
    unit, scale, lifted, inner, product = kept
    grad_low = grad_state.astype(jnp.bfloat16)
    grad_down = weight_grad(product, grad_low)
    grad_product = project_back(grad_low, weight_down)
    gate_part = inner[..., :expand]
    up_part = inner[..., expand:]
    gate_sig = jax.nn.sigmoid(gate_part)
    silu_value = gate_part * gate_sig
    silu_slope = gate_sig * (1.0 + gate_part * (1.0 - gate_sig))
    grad_inner = jnp.concatenate(
        [grad_product * up_part * silu_slope, grad_product * silu_value], axis=-1
    )
    grad_inner = grad_inner.astype(jnp.bfloat16)
    grad_up = weight_grad(lifted, grad_inner)
    grad_lifted = project_back(grad_inner, weight_up)
    grad_middle, gain_grad = norm_back(grad_lifted, unit, scale, gain)
    return (grad_middle + grad_state, (grad_up, grad_down, gain_grad))


def block_forward(state, weight_in, weight_out, weight_up, weight_down, gains, pair_mask):
    first, kept_one = triangle_forward(
        state, weight_in[0], weight_out[0], gains[0:2], pair_mask, False
    )
    second, kept_two = triangle_forward(
        first, weight_in[1], weight_out[1], gains[2:4], pair_mask, True
    )
    output, kept_three = transition_forward(second, weight_up, weight_down, gains[4])
    return (output, (kept_one, kept_two, kept_three))


def block_backward(
    grad_state, state, weight_in, weight_out, weight_up, weight_down, gains, pair_mask
):
    skipped, kept = block_forward(
        state, weight_in, weight_out, weight_up, weight_down, gains, pair_mask
    )
    kept_one, kept_two, kept_three = kept
    grad_state, (grad_up, grad_down, gain_five) = transition_backward(
        grad_state, kept_three, weight_up, weight_down, gains[4]
    )
    grad_state, (in_two, out_two, gain_three, gain_four) = triangle_backward(
        grad_state, kept_two, weight_in[1], weight_out[1], gains[2:4], pair_mask, True
    )
    grad_state, (in_one, out_one, gain_one, gain_two) = triangle_backward(
        grad_state, kept_one, weight_in[0], weight_out[0], gains[0:2], pair_mask, False
    )
    return (
        grad_state,
        (
            jnp.stack([in_one, in_two]),
            jnp.stack([out_one, out_two]),
            grad_up,
            grad_down,
            jnp.stack([gain_one, gain_two, gain_three, gain_four, gain_five]),
        ),
    )


def adamw(weight, grad, first, second, rate, decay):
    first_new = BETA_ONE * first + (1.0 - BETA_ONE) * grad
    second_new = BETA_TWO * second + (1.0 - BETA_TWO) * grad * grad
    moved = (
        first_new
        / (1.0 - BETA_ONE**STEP)
        / (jnp.sqrt(second_new / (1.0 - BETA_TWO**STEP)) + ADAM_EPS)
    )
    return (first_new, second_new, weight - rate * (moved + decay * weight))


def gradients_by_block(
    single,
    residue_index,
    chain_index,
    token_mask,
    pair_valid,
    target_bins,
    relative_table,
    single_weight,
    triangle_input,
    triangle_output,
    expand_weight,
    reduce_weight,
    distogram_weight,
    norm_gains,
):
    crops, rows, cols = pair_valid.shape
    width = relative_table.shape[1]
    layers = triangle_input.shape[0]
    row_start = lax.axis_index("row") * rows
    col_start = lax.axis_index("head") * cols

    def take(array, start, count):
        return lax.dynamic_slice_in_dim(array, start, count, 1)

    offset = (
        take(residue_index, row_start, rows)[:, :, None]
        - take(residue_index, col_start, cols)[:, None, :]
    )
    same = (
        take(chain_index, row_start, rows)[:, :, None]
        == take(chain_index, col_start, cols)[:, None, :]
    )
    reach = (relative_table.shape[0] - 2) // 2
    bins = jnp.where(same, jnp.clip(offset, -reach, reach) + reach, 2 * reach + 1)
    relative_hot = (
        bins[..., None] == jnp.arange(relative_table.shape[0])[None, None, None, :]
    ).astype(jnp.float32)
    token_rows = take(token_mask, row_start, rows).astype(jnp.float32)
    token_cols = take(token_mask, col_start, cols).astype(jnp.float32)
    pair_mask = token_rows[:, :, None] * token_cols[:, None, :]
    loss_weight = pair_mask * pair_valid.astype(jnp.float32)
    low_input = triangle_input.astype(jnp.bfloat16)
    low_output = triangle_output.astype(jnp.bfloat16)
    low_expand = expand_weight.astype(jnp.bfloat16)
    low_reduce = reduce_weight.astype(jnp.bfloat16)
    low_logits = distogram_weight.astype(jnp.bfloat16)
    proj = project(single, single_weight.astype(jnp.bfloat16))
    state = project(relative_hot.astype(jnp.bfloat16), relative_table.astype(jnp.bfloat16))
    state = (
        state
        + take(proj, row_start, rows)[:, :, None, :width]
        + take(proj, col_start, cols)[:, None, :, width:]
    )
    inputs = []
    for layer in range(layers):
        inputs.append(state)
        state, unused = block_forward(
            state,
            low_input[layer],
            low_output[layer],
            low_expand[layer],
            low_reduce[layer],
            norm_gains[5 * layer : 5 * layer + 5],
            pair_mask,
        )
    head_unit, head_scale = normalize(state)
    shown = (head_unit * norm_gains[5 * layers]).astype(jnp.bfloat16)
    logits = project(shown, low_logits)
    largest = jnp.max(logits, axis=-1, keepdims=True)
    log_total = largest + jnp.log(jnp.sum(jnp.exp(logits - largest), axis=-1, keepdims=True))
    target_hot = (
        target_bins[..., None] == jnp.arange(logits.shape[-1])[None, None, None, :]
    ).astype(jnp.float32)
    picked = jnp.sum(logits * target_hot, axis=-1)
    loss_local = jnp.sum(loss_weight * (log_total[..., 0] - picked))
    grad_scores = (loss_weight[..., None] * (jnp.exp(logits - log_total) - target_hot)).astype(
        jnp.bfloat16
    )
    grad_logits = weight_grad(shown, grad_scores)
    grad_shown = project_back(grad_scores, low_logits)
    grad_state, gain_last = norm_back(grad_shown, head_unit, head_scale, norm_gains[5 * layers])
    collected = []
    for layer in reversed(range(layers)):
        grad_state, layer_grads = block_backward(
            grad_state,
            inputs[layer],
            low_input[layer],
            low_output[layer],
            low_expand[layer],
            low_reduce[layer],
            norm_gains[5 * layer : 5 * layer + 5],
            pair_mask,
        )
        collected.insert(0, layer_grads)
    grad_input = jnp.stack([entry[0] for entry in collected])
    grad_output = jnp.stack([entry[1] for entry in collected])
    grad_expand = jnp.stack([entry[2] for entry in collected])
    grad_reduce = jnp.stack([entry[3] for entry in collected])
    grad_gains = jnp.concatenate(
        [jnp.concatenate([entry[4] for entry in collected], axis=0), gain_last[None]], axis=0
    )
    grad_table = jnp.einsum(
        "bijr,bijc->rc", relative_hot, grad_state, precision=lax.Precision.HIGHEST
    )
    single_wide = single.astype(jnp.float32)
    row_part = jnp.einsum(
        "bis,bic->sc",
        take(single_wide, row_start, rows),
        jnp.sum(grad_state, axis=2),
        precision=lax.Precision.HIGHEST,
    )
    col_part = jnp.einsum(
        "bjs,bjc->sc",
        take(single_wide, col_start, cols),
        jnp.sum(grad_state, axis=1),
        precision=lax.Precision.HIGHEST,
    )
    grad_single = jnp.concatenate([row_part, col_part], axis=1)
    return (
        loss_local,
        jnp.sum(loss_weight),
        grad_table,
        grad_single,
        grad_input,
        grad_output,
        grad_expand,
        grad_reduce,
        grad_logits,
        grad_gains,
    )


F32 = jnp.float32
BF16 = jnp.bfloat16
LANES = 128
SUBLANES = 8
PACKED = 16
ROW_BLOCK = 4
STREAM_ROWS = 2
PHASES = SUBLANES // ROW_BLOCK
CHUNK_ROWS = SUBLANES * SUBLANES
VMEM_BYTES = 58 * 2**20
UPDATE_BYTES = 40 * 2**20
REDUCE_BYTES = 16 * 2**20
MESH = pl.DeviceIdType.MESH
ROWS, LANDED, WHOLE, SUM, ANYWHERE = range(5)


class Bag:
    def __init__(self, **entries):
        self.__dict__.update(entries)


class Arg:
    def __init__(self, array, kind, index=None, block=None, column=None):
        self.array, self.kind, self.index, self.block = array, kind, index, block
        self.column = column

    def spec(self):
        if self.index is None:
            return block_spec(self.array.shape, self.kind)
        index = self.index
        return pl.BlockSpec(self.block, lambda step: index)


class Column:
    def __init__(self, ref, column):
        self.ref, self.column = ref, column

    def __getitem__(self, _):
        return self.ref[:, self.column : self.column + 1]


class Out:
    def __init__(self, shape, dtype, kind):
        self.shape, self.dtype, self.kind = shape, dtype, kind

    def spec(self):
        return block_spec(self.shape, ANYWHERE if self.kind == LANDED else self.kind)


def block_spec(shape, kind):
    if kind == ANYWHERE:
        return pl.BlockSpec(memory_space=pl.ANY)
    if kind == LANDED:
        return pl.BlockSpec((shape[0], CHUNK_ROWS, shape[2]), lambda step: (0, step // PHASES, 0))
    if kind == ROWS:
        return pl.BlockSpec((ROW_BLOCK,) + shape[1:], lambda step: (step,) + (0,) * (len(shape) - 1))
    return pl.BlockSpec(shape, lambda step: (0,) * len(shape))


def is_leaf(value):
    return isinstance(value, (Arg, Out))


def bag_of(tree, leaves):
    if is_leaf(tree):
        return next(leaves)
    if isinstance(tree, list):
        return [bag_of(value, leaves) for value in tree]
    return Bag(**{key: bag_of(value, leaves) for key, value in tree.items()})


def leaves_of(tree):
    if is_leaf(tree):
        return [tree]
    found = []
    for value in tree if isinstance(tree, list) else tree.values():
        found.extend(leaves_of(value))
    return found


def dot(left, right):
    return lax.dot_general(left, right, (((1,), (0,)), ((), ())), preferred_element_type=F32)


def dot_pairs(left, right):
    return lax.dot_general(left, right, (((1,), (1,)), ((), ())), preferred_element_type=F32)


def product_of(left, right, left_axis, right_axis):
    return lax.dot_general(
        left, right, (((left_axis,), (right_axis,)), ((), ())), preferred_element_type=F32
    )


def sigmoid(value):
    return 0.5 * jnp.tanh(0.5 * value) + 0.5


def unit_of(value):
    centred = value - jnp.mean(value, axis=0, keepdims=True)
    scale = lax.rsqrt(jnp.mean(centred * centred, axis=0, keepdims=True) + EPS)
    return (centred * scale, scale)


def unit_back(grad, unit, scale, gain):
    scaled = grad * gain
    first = jnp.mean(scaled, axis=0, keepdims=True)
    second = jnp.mean(scaled * unit, axis=0, keepdims=True)
    return scale * (scaled - first - unit * second)


def fold(value):
    total = value[:, :LANES]
    for start in range(LANES, value.shape[1], LANES):
        total = total + value[:, start : start + LANES]
    return total


def read_rows(ref, rows):
    return jnp.concatenate([ref[row] for row in rows], axis=1)


def write_rows(ref, rows, value):
    cols = ref.shape[2]
    for place, row in enumerate(rows):
        ref[row] = value[:, place * cols : (place + 1) * cols].astype(ref.dtype)


def alternate(streams):
    while streams:
        going = []
        for stream in streams:
            try:
                next(stream)
                going.append(stream)
            except StopIteration:
                pass
        streams = going


class Wire:
    def __init__(self, wide, phase):
        self.wide, self.phase = wide, phase

    def tokens(self, row):
        width = self.wide.shape[1] // SUBLANES
        return pl.ds(self.phase * ROW_BLOCK + row, width, stride=SUBLANES)

    def read(self, rows):
        lanes = self.wide.shape[0]
        return jnp.concatenate(
            [self.wide[lane, self.tokens(row), :] for row in rows for lane in range(lanes)], axis=1
        )

    def write(self, rows, value):
        lanes = self.wide.shape[0]
        for place, row in enumerate(rows):
            for lane in range(lanes):
                start = (place * lanes + lane) * LANES
                self.wide[lane, self.tokens(row), :] = value[:, start : start + LANES]


def widen(wide, low, chunk):
    rows = pl.ds(pl.multiple_of(chunk * CHUNK_ROWS, CHUNK_ROWS), CHUNK_ROWS)

    def step(peer, carry):
        value = low[peer, rows, :].astype(F32)
        start = pl.multiple_of(peer * CHUNK_ROWS, CHUNK_ROWS)
        for lane in range(wide.shape[0]):
            wide[lane, pl.ds(start, CHUNK_ROWS), :] = value[:, lane * LANES : (lane + 1) * LANES]
        return carry

    lax.fori_loop(0, low.shape[0], step, 0)


def narrow(low, wide, chunk):
    rows = pl.ds(pl.multiple_of(chunk * CHUNK_ROWS, CHUNK_ROWS), CHUNK_ROWS)

    def step(peer, carry):
        start = pl.multiple_of(peer * CHUNK_ROWS, CHUNK_ROWS)
        low[peer, rows, :] = jnp.concatenate(
            [wide[lane, pl.ds(start, CHUNK_ROWS), :] for lane in range(wide.shape[0])], axis=1
        ).astype(low.dtype)
        return carry

    lax.fori_loop(0, low.shape[0], step, 0)


def triangle_start(weights, i, rows, wires, state):
    width = state.shape[0]
    unit, _ = unit_of(state)
    normed = (unit * weights.gain0[...]).astype(BF16)
    mixed = dot(weights.mix_t[...], normed)
    yield
    mask = read_rows(i.mask, rows)
    for wire, base in zip(wires, (0, 2 * width)):
        gate = sigmoid(mixed[base : base + width])
        wire.write(rows, mask * gate * mixed[base + width : base + 2 * width])


def triangle_finish(weights, rows, wire, state):
    unit, _ = unit_of(state)
    normed = (unit * weights.gain0[...]).astype(BF16)
    opened = dot(weights.gate_t[...], normed)
    yield
    tri_unit, tri_scale = unit_of(wire.read(rows))
    shaped = (tri_unit * weights.gain1[...]).astype(BF16)
    branch = dot(weights.out_t[...], shaped)
    yield
    gate = sigmoid(opened)
    return (state + gate * branch, (gate, tri_unit, tri_scale, shaped, branch))


def triangle_back_start(weights, o, rows, wire, grad, kept):
    gate, tri_unit, tri_scale, shaped, branch = kept
    grad_branch = (grad * gate).astype(BF16)
    grad_shaped = dot(weights.out[...], grad_branch)
    yield
    o.out[...] += dot_pairs(shaped, grad_branch)
    write_rows(o.grad_gate, rows, grad * branch * gate * (1.0 - gate))
    yield
    o.gain1[...] += fold(grad_shaped * tri_unit)
    wire.write(rows, unit_back(grad_shaped, tri_unit, tri_scale, weights.gain1[...]))


def triangle_back_finish(weights, i, o, rows, wires):
    grad, state = read_rows(i.grad, rows), read_rows(i.state, rows)
    width = state.shape[0]
    unit, scale = unit_of(state)
    gain = weights.gain0[...]
    normed = (unit * gain).astype(BF16)
    mixed = dot(weights.mix_t[...], normed)
    yield
    mask = read_rows(i.mask, rows)
    parts = []
    for wire, base in zip(wires, (0, 2 * width)):
        back = wire.read(rows) * mask
        gate = sigmoid(mixed[base : base + width])
        back_gate = back * gate
        parts.append((back_gate * mixed[base + width : base + 2 * width] * (1.0 - gate)).astype(BF16))
        parts.append(back_gate.astype(BF16))
    parts.append(read_rows(i.grad_gate, rows))
    grad_mixed = jnp.concatenate(parts, axis=0)
    yield
    grad_normed = dot(weights.mix[...], grad_mixed)
    o.mix[...] += dot_pairs(normed, grad_mixed)
    yield
    o.gain0[...] += fold(grad_normed * unit)
    return grad + unit_back(grad_normed, unit, scale, gain)


def transition(weights, state):
    unit, scale = unit_of(state)
    lifted = (unit * weights.gain[...]).astype(BF16)
    inner = dot(weights.up_t[...], lifted)
    yield
    half = inner.shape[0] // 2
    gate = inner[:half]
    slope = sigmoid(gate)
    product = (gate * slope * inner[half:]).astype(BF16)
    return (unit, scale, lifted, inner, slope, product)


def transition_back(weights, o, grad, kept):
    unit, scale, lifted, inner, slope, product = kept
    half = inner.shape[0] // 2
    gate, up = inner[:half], inner[half:]
    grad_low = grad.astype(BF16)
    grad_product = dot(weights.down[...], grad_low)
    o.down[...] += dot_pairs(product, grad_low)
    yield
    scaled = grad_product * slope
    grad_inner = jnp.concatenate(
        [
            (scaled * up * (1.0 + gate * (1.0 - slope))).astype(BF16),
            (scaled * gate).astype(BF16),
        ],
        axis=0,
    )
    yield
    grad_lifted = dot(weights.up[...], grad_inner)
    o.up[...] += dot_pairs(lifted, grad_inner)
    yield
    o.gain[...] += fold(grad_lifted * unit)
    return grad + unit_back(grad_lifted, unit, scale, weights.gain[...])


def head_back(i, o, rows, state):
    unit, scale = unit_of(state)
    gain = i.gain[...]
    shown = (unit * gain).astype(BF16)
    logits = dot(i.logits_t[...], shown)
    yield
    largest = jnp.max(logits, axis=0, keepdims=True)
    raised = jnp.exp(logits - largest)
    total = jnp.sum(raised, axis=0, keepdims=True)
    log_total = largest + jnp.log(total)
    target = read_rows(i.target, rows)
    weight = read_rows(i.weight, rows)
    hot = lax.broadcasted_iota(jnp.int32, logits.shape, 0) == target
    picked = jnp.sum(jnp.where(hot, logits, 0.0), axis=0, keepdims=True)
    o.loss[...] += fold(weight * (log_total - picked))
    o.count[...] += fold(weight)
    share = raised * (1.0 / total)
    grad_scores = (weight * (share - jnp.where(hot, 1.0, 0.0))).astype(BF16)
    grad_shown = dot(i.logits[...], grad_scores)
    o.logits[...] += dot_pairs(grad_scores, shown)
    yield
    o.gain[...] += fold(grad_shown * unit)
    return unit_back(grad_shown, unit, scale, gain)


def bins_hot(bins, rows, table_rows):
    bins = read_rows(bins, rows)
    shape = (table_rows, bins.shape[1])
    return jnp.where(lax.broadcasted_iota(jnp.int32, shape, 0) == bins, 1.0, 0.0).astype(BF16)


def run_stage(body, name, collective_id, group, inputs, outputs, products=None, wires=0):
    peers, half, rows, tokens = group
    args, outs = leaves_of(inputs), leaves_of(outputs)
    steps = rows // ROW_BLOCK
    chunks = rows // SUBLANES
    arriving = products.results if products else 0
    landed_args = [index for index, arg in enumerate(args) if arg.kind == LANDED]
    keeps = [place for place, out in enumerate(outs) if out.kind == LANDED]
    low = pltpu.VMEM((peers, rows * SUBLANES, tokens), BF16)
    many = pltpu.SemaphoreType.DMA((chunks, peers))
    wide = pltpu.VMEM((tokens // LANES, peers * CHUNK_ROWS, LANES), F32)
    groups = [
        [wide] * (arriving + len(landed_args) + wires),
        [low] * arriving,
        [many] * (2 * arriving),
        [low] * wires,
        [many] * (2 * wires),
        [pltpu.SemaphoreType.DMA((1,))] * len(keeps),
        products.scratch(low) if products else [],
    ]

    def kernel(*refs):
        step = pl.program_id(0)
        phase, chunk = lax.rem(step, PHASES), lax.div(step, PHASES)
        in_refs = [
            ref if arg.column is None else Column(ref, arg.column) for arg, ref in zip(args, refs)
        ]
        out_refs = list(refs[len(args) : len(args) + len(outs)])
        rest, parts = list(refs[len(args) + len(outs) :]), []
        for part in groups:
            parts.append(rest[: len(part)])
            rest = rest[len(part) :]
        wides, lands, land_sems, sends, send_sems, keep_sems, held = parts
        saves = [
            pltpu.make_async_copy(land, out_refs[place], sem.at[0])
            for land, place, sem in zip(lands, keeps, keep_sems)
        ]
        ring = Exchange(peers, half)
        i, o = bag_of(inputs, iter(in_refs)), bag_of(outputs, iter(out_refs))
        arrivals = [
            (result, land, land_sems[2 * place], land_sems[2 * place + 1])
            for place, (result, land) in enumerate(zip(held, lands))
        ]

        @pl.when(step == 0)
        def _():
            ring.greet()
            if products:
                products.load(i, held)
            for out, ref in zip(outs, out_refs):
                if out.kind == SUM:
                    ref[...] = jnp.zeros(out.shape, out.dtype)
            if products:
                products.multiply(i, o, held)
                ring.meet()

                def start(index, carry):
                    ring.start(arrivals, index)
                    return carry

                lax.fori_loop(0, chunks, start, 0)

        if products:

            @pl.when(phase == 0)
            def _():
                ring.wait(arrivals, chunk)
                for target, land in zip(wides, lands):
                    widen(target, land, chunk)

        if landed_args:

            @pl.when(phase == 0)
            def _():
                for target, index in zip(wides[arriving:], landed_args):
                    widen(target, in_refs[index], 0)

        if saves:

            @pl.when(step == steps - PHASES)
            def _():
                for save in saves:
                    save.start()

        body_in = list(in_refs)
        for index, source in zip(landed_args, wides[arriving:]):
            body_in[index] = Wire(source, phase)
        given = bag_of(inputs, iter(body_in))
        arrived = [Wire(source, phase) for source in wides[:arriving]]
        written = wides[arriving + len(landed_args) :]
        sent = [Wire(target, phase) for target in written]
        alternate(
            [
                body(given, o, range(first, first + STREAM_ROWS), arrived, sent)
                for first in range(0, ROW_BLOCK, STREAM_ROWS)
            ]
        )
        moves = [
            (send, land, send_sems[2 * place], send_sems[2 * place + 1])
            for place, (send, land) in enumerate(zip(sends, o.got if wires else []))
        ]
        if wires:

            @pl.when(phase == PHASES - 1)
            def _():
                for source, send in zip(written, sends):
                    narrow(send, source, chunk)
                if not products:

                    @pl.when(chunk == 0)
                    def _():
                        ring.meet()

                ring.start(moves, chunk)

        @pl.when(step == steps - 1)
        def _():
            if wires:

                def wait(index, carry):
                    ring.wait(moves, index)
                    return carry

                lax.fori_loop(0, chunks, wait, 0)
            for save in saves:
                save.wait()
            if products:
                products.end(o, held)

    results = pl.pallas_call(
        kernel,
        grid=(steps,),
        in_specs=[arg.spec() for arg in args],
        out_specs=[out.spec() for out in outs],
        out_shape=[jax.ShapeDtypeStruct(out.shape, out.dtype) for out in outs],
        scratch_shapes=sum(groups, []),
        compiler_params=pltpu.CompilerParams(
            dimension_semantics=(pltpu.ARBITRARY,),
            vmem_limit_bytes=VMEM_BYTES,
            has_side_effects=True,
            collective_id=collective_id,
        ),
        cost_estimate=pl.CostEstimate(flops=0, bytes_accessed=0, transcendentals=0),
        name=name,
    )(*[arg.array for arg in args])
    return bag_of(outputs, iter(results))


def flip(value, step, count):
    step = jnp.int32(step)
    result, bit = 0, 1
    while bit < count:
        result = result + lax.rem(lax.div(value, bit) + lax.div(step, bit), 2) * bit
        bit *= 2
    return result


def position(row, head, half, heads):
    inner = half // 2 * heads
    return (row % 2) * inner + (row // 2) * heads + head


def place_of(position, half, heads):
    inner = half // 2 * heads
    rest = lax.rem(position, inner)
    return (lax.div(rest, heads) * 2 + lax.div(position, inner), lax.rem(rest, heads))


class Exchange:
    def __init__(self, count, half):
        row, head = lax.axis_index("row"), lax.axis_index("head")
        place = lax.rem(row, half)
        inner = count // 2
        self.count = count
        self.half = half
        self.base = row - place
        self.me = lax.rem(place, 2) * inner + lax.div(place, 2) * (count // half) + head
        self.twin = (lax.rem(row + half, 2 * half), head)
        core = lax.div(self.me, inner)
        self.order = []
        for low in range(inner // 2):
            for step in (low, low + inner):
                other = step ^ (inner - 1)
                for first, second in ((step, other), (other, step)):
                    if first == 0 or second == 0:
                        if first:
                            self.order.append(first)
                    else:
                        self.order.append(first + core * (second - first))

    def peer(self, step):
        return flip(self.me, step, self.count)

    def device(self, peer):
        place, head = place_of(peer, self.half, self.count // self.half)
        return (self.base + place, head)

    def greet(self):
        barrier = pltpu.get_barrier_semaphore()
        for step in self.order:
            pl.semaphore_signal(
                barrier, inc=1, device_id=self.device(self.peer(step)), device_id_type=MESH
            )

    def meet(self):
        pl.semaphore_wait(pltpu.get_barrier_semaphore(), self.count - 1)

    def copies(self, moves, chunk, steps):
        found = []
        for source, target, send_sems, recv_sems in moves:
            size = source.shape[1] // send_sems.shape[0]
            rows = pl.ds(pl.multiple_of(chunk * size, PACKED), size)
            for step in steps:
                peer = self.me if step is None else self.peer(step)
                if step is None:
                    copy = pltpu.make_async_copy(
                        source.at[self.me, rows, :],
                        target.at[self.me, rows, :],
                        send_sems.at[chunk, 0],
                    )
                else:
                    copy = pltpu.make_async_remote_copy(
                        src_ref=source.at[peer, rows, :],
                        dst_ref=target.at[self.me, rows, :],
                        send_sem=send_sems.at[chunk, step],
                        recv_sem=recv_sems.at[chunk, step],
                        device_id=self.device(peer),
                        device_id_type=MESH,
                    )
                found.append(copy)
        return found

    def start(self, moves, chunk):
        for copy in self.copies(moves, chunk, self.order + [None]):
            copy.start()

    def wait(self, moves, chunk):
        for copy in self.copies(moves, chunk, self.order + [None]):
            copy.wait()


def join_channels(got, pair):
    peers, rows, _ = got.shape
    even, odd = [], []
    for peer in range(peers):
        for start in range(0, rows, CHUNK_ROWS):
            piece = got[peer, pl.ds(pl.multiple_of(start + pair * PACKED, PACKED), PACKED), :]
            piece = piece.astype(F32)
            even.append(piece[:SUBLANES])
            odd.append(piece[SUBLANES:])
    return [jnp.concatenate(pieces, axis=0).astype(BF16) for pieces in (even, odd)]


def split_channels(low, pair, even, odd, first=0):
    chunks = low.shape[1] // CHUNK_ROWS
    for start in range(0, even.shape[0], SUBLANES):
        block = (first + start) // SUBLANES
        row = block % chunks * CHUNK_ROWS + pair * PACKED
        low[block // chunks, pl.ds(pl.multiple_of(row, PACKED), PACKED), :] = jnp.concatenate(
            [even[start : start + SUBLANES], odd[start : start + SUBLANES]], axis=0
        ).astype(low.dtype)


def each_pair(body):
    for pair in range(SUBLANES // 2):
        body(pair)


class Forward:
    results = 1

    def __init__(self, tokens, incoming):
        self.tokens, self.incoming = tokens, incoming

    def scratch(self, low):
        block = pltpu.VMEM((SUBLANES, self.tokens, self.tokens), BF16)
        return [low] * 3 + [block] * 2 + [pltpu.SemaphoreType.DMA((4,))]

    def loads(self, i, held):
        return [
            pltpu.make_async_copy(i.got[place], held[1 + place], held[5].at[place])
            for place in range(2)
        ]

    def saves(self, o, held):
        return [
            pltpu.make_async_copy(held[3], o.left, held[5].at[2]),
            pltpu.make_async_copy(held[4], o.right, held[5].at[3]),
        ]

    def load(self, i, held):
        for copy in self.loads(i, held):
            copy.start()

    def multiply(self, i, o, held):
        tri, left_got, right_got, left_block, right_block = held[:5]
        for copy in self.loads(i, held):
            copy.wait()
        axis = 0 if self.incoming else 1

        def step(pair):
            lefts, rights = join_channels(left_got, pair), join_channels(right_got, pair)
            found = []
            for index in range(2):
                left_block[2 * pair + index] = lefts[index]
                right_block[2 * pair + index] = rights[index]
                found.append(product_of(lefts[index], rights[index], axis, axis))
            split_channels(tri, pair, *found)

        each_pair(step)
        for copy in self.saves(o, held):
            copy.start()

    def end(self, o, held):
        for copy in self.saves(o, held):
            copy.wait()


class Backward:
    results = 2

    def __init__(self, tokens, incoming):
        self.tokens, self.incoming = tokens, incoming

    def scratch(self, low):
        block = pltpu.VMEM((SUBLANES, self.tokens, self.tokens), BF16)
        return [low] * 3 + [block] * 2 + [pltpu.SemaphoreType.DMA((3,))]

    def loads(self, i, held):
        sources = (i.got[0], i.owned.left, i.owned.right)
        return [
            pltpu.make_async_copy(source, held[2 + place], held[5].at[place])
            for place, source in enumerate(sources)
        ]

    def load(self, i, held):
        for copy in self.loads(i, held):
            copy.start()

    def multiply(self, i, o, held):
        grad_left, grad_right, got, left_block, right_block = held[:5]
        for copy in self.loads(i, held):
            copy.wait()

        def step(pair):
            lefts, rights = [], []
            for index, grad in enumerate(join_channels(got, pair)):
                left, right = left_block[2 * pair + index], right_block[2 * pair + index]
                if self.incoming:
                    lefts.append(product_of(right, grad, 1, 1))
                    rights.append(product_of(left, grad, 1, 0))
                else:
                    lefts.append(product_of(grad, right, 1, 0))
                    rights.append(product_of(grad, left, 0, 0))
            split_channels(grad_left, pair, *lefts)
            split_channels(grad_right, pair, *rights)

        each_pair(step)

    def end(self, o, held):
        pass


def prepare(triangle_input, triangle_output, expand_weight, reduce_weight, distogram_weight, norm_gains):
    merged = [
        triangle_input.reshape((-1,) + triangle_input.shape[2:]),
        triangle_output.reshape((-1,) + triangle_output.shape[2:]),
        expand_weight,
        reduce_weight,
        distogram_weight.T[None],
    ]
    count = len(merged)

    def kernel(*refs):
        for source, plain, turned in zip(refs[:count], refs[count + 1 :: 2], refs[count + 2 :: 2]):
            for index in range(source.shape[0]):
                value = source[index]
                plain[index] = value.astype(BF16)
                turned[index] = value.T.astype(BF16)
        gains = refs[count][...]
        refs[-1][...] = gains.T

    shapes = []
    for array in merged:
        depth, rows, cols = array.shape
        shapes.append(jax.ShapeDtypeStruct((depth, rows, cols), BF16))
        shapes.append(jax.ShapeDtypeStruct((depth, cols, rows), BF16))
    shapes.append(jax.ShapeDtypeStruct(norm_gains.shape[::-1], F32))
    return pl.pallas_call(
        kernel,
        out_shape=shapes,
        compiler_params=pltpu.CompilerParams(vmem_limit_bytes=VMEM_BYTES),
        name="prepare",
    )(*merged, norm_gains)


def by_crop(value, rows_axis, head_axis):
    count, heads = rows_axis, head_axis
    half = count // 2
    inner = half // 2 * heads
    same, other = [], []
    for row in range(count):
        place = row % inner // heads * 2 + row // inner
        for head in range(heads):
            source = row * heads + head
            for crop, pairs in ((head, same), (1 - head, other)):
                pairs.append((source, (crop * half + place) * heads + row % heads))
    head = lax.axis_index("head")
    crop = lax.axis_index("row") // half
    mine = lax.dynamic_index_in_dim(value, head, 0, keepdims=False)
    rest = lax.dynamic_index_in_dim(value, 1 - head, 0, keepdims=False)
    mine = lax.ppermute(mine, ("row", "head"), same)
    rest = lax.ppermute(rest, ("row", "head"), other)
    low = jnp.where(crop == 0, mine, rest)
    high = jnp.where(crop == 0, rest, mine)
    return jnp.concatenate([low, high], axis=-1)


def reduce_rest(half, peers, collective_id, grids, gains, rows):
    sizes = [grid.shape[0] * grid.shape[1] // LANES for grid in grids]
    used = sum(sizes) + len(gains) + SUBLANES * len(rows)
    part = -(-used // (peers * SUBLANES)) * SUBLANES
    total = part * peers
    starts, spot = [], 0
    for size in sizes:
        starts.append(spot)
        spot += size
    row_starts = []
    for _ in rows:
        row_starts.append(spot)
        spot += SUBLANES
    gain_start = spot
    count = len(grids) + len(gains) + len(rows)

    def kernel(*refs):
        out, local, got, mine, other, sends, recvs, back_sends, back_recvs, twin_sems = refs[count:]
        ring = Exchange(peers, half)
        ring.greet()
        barrier = pltpu.get_barrier_semaphore()
        pl.semaphore_signal(barrier, inc=1, device_id=ring.twin, device_id_type=MESH)
        for grid, start in zip(refs[: len(grids)], starts):
            height, width = grid.shape
            for column in range(width // LANES):
                local[pl.ds(start + column * height, height), :] = grid[
                    :, column * LANES : (column + 1) * LANES
                ]
        ones = jnp.ones((SUBLANES, LANES), F32)
        for index, gain in enumerate(refs[len(grids) : len(grids) + len(gains)]):
            folded = lax.dot_general(
                ones,
                gain[...],
                (((1,), (1,)), ((), ())),
                precision=lax.Precision.HIGHEST,
                preferred_element_type=F32,
            )
            local[pl.ds(gain_start + index, 1), :] = folded[:1]
        for row, start in zip(refs[len(grids) + len(gains) : count], row_starts):
            local[pl.ds(start, 1), :] = row[...]
            local[pl.ds(start + 1, SUBLANES - 1), :] = jnp.zeros((SUBLANES - 1, LANES), F32)
        tail = gain_start + len(gains)
        if total > tail:
            local[pl.ds(tail, total - tail), :] = jnp.zeros((total - tail, LANES), F32)
        pl.semaphore_wait(barrier, peers)

        def block(peer):
            return pl.ds(pl.multiple_of(peer * part, SUBLANES), part)

        here = block(ring.me)

        def gather(step):
            peer = ring.peer(step)
            return pltpu.make_async_remote_copy(
                src_ref=local.at[block(peer), :],
                dst_ref=got.at[here, :],
                send_sem=sends.at[step],
                recv_sem=recvs.at[step],
                device_id=ring.device(peer),
                device_id_type=MESH,
            )

        def spread(step):
            return pltpu.make_async_remote_copy(
                src_ref=out.at[here, :],
                dst_ref=out.at[here, :],
                send_sem=back_sends.at[step],
                recv_sem=back_recvs.at[step],
                device_id=ring.device(ring.peer(step)),
                device_id_type=MESH,
            )

        for step in ring.order:
            gather(step).start()
        got[here, :] = local[here, :]
        for step in ring.order:
            gather(step).wait()
        value = got[pl.ds(0, part), :]
        for peer in range(1, peers):
            value = value + got[pl.ds(peer * part, part), :]
        mine[...] = value
        copy = pltpu.make_async_remote_copy(
            src_ref=mine,
            dst_ref=other,
            send_sem=twin_sems.at[0],
            recv_sem=twin_sems.at[1],
            device_id=ring.twin,
            device_id_type=MESH,
        )
        copy.start()
        copy.wait()
        out[here, :] = mine[...] + other[...]
        for step in ring.order:
            spread(step).start()
        for step in ring.order:
            spread(step).wait()

    inside = pl.BlockSpec(memory_space=pltpu.VMEM)
    whole = pl.pallas_call(
        kernel,
        in_specs=[inside] * count,
        out_specs=inside,
        out_shape=jax.ShapeDtypeStruct((total, LANES), F32),
        scratch_shapes=[pltpu.VMEM((total, LANES), F32)] * 2
        + [pltpu.VMEM((part, LANES), F32)] * 2
        + [pltpu.SemaphoreType.DMA((peers,))] * 4
        + [pltpu.SemaphoreType.DMA((2,))],
        compiler_params=pltpu.CompilerParams(
            collective_id=collective_id, has_side_effects=True, vmem_limit_bytes=REDUCE_BYTES
        ),
        cost_estimate=pl.CostEstimate(flops=0, bytes_accessed=0, transcendentals=0),
        name="reduce_rest",
    )(*grids, *gains, *rows)
    return whole, starts, row_starts, gain_start


def update(rest, starts, row_starts, gain_start, early, weights, firsts, seconds):
    layers, kinds, width, mixed = weights[2].shape
    hidden = weights[4].shape[2]
    early_in, early_up, early_rows = early
    given = [rest, *early_in, *early_up, *early_rows]
    count = len(given)

    def kernel(*refs):
        whole = refs[0]
        in_refs = refs[1 : 1 + len(early_in)]
        up_refs = refs[1 + len(early_in) : count - layers]
        row_refs = refs[count - layers : count]
        states = [refs[count + 8 * kind : count + 8 * (kind + 1)] for kind in range(3)]
        scalars = refs[count + 24 : count + 27]
        results = refs[count + 27 :]

        def taken(start, size):
            return whole[pl.ds(start, size), :]

        def wide(start, height, columns):
            return jnp.concatenate(
                [taken(start + column * height, height) for column in range(columns)], axis=1
            )

        loss = jnp.sum(taken(row_starts[0], 1), axis=1, keepdims=True)
        valid = jnp.sum(taken(row_starts[1], 1), axis=1, keepdims=True)
        table_rows, single_rows = weights[0].shape[0], weights[1].shape[0]
        downs = hidden // 2
        grads = {}
        grads[0, ()] = taken(starts[4], table_rows)
        grads[1, ()] = jnp.concatenate(
            [taken(starts[5], single_rows), taken(starts[6], single_rows)], axis=1
        )
        for layer in range(layers):
            spot = 0
            for kind in range(kinds):
                if layer == 0:
                    grads[2, (layer, kind)] = wide(starts[kind], width, mixed // LANES)
                else:
                    grads[2, (layer, kind)] = in_refs[(layer - 1) * kinds + kind][...]
                if layer == 0 and kind == 0:
                    grads[3, (layer, kind)] = taken(starts[2], width)
                else:
                    grads[3, (layer, kind)] = row_refs[layer][pl.ds(spot, width), :]
                    spot += width
            grads[4, (layer,)] = up_refs[layer][...]
            grads[5, (layer,)] = row_refs[layer][pl.ds(spot, downs), :]
        grads[6, ()] = taken(starts[3], weights[6].shape[0])
        grads[7, ()] = taken(gain_start, weights[7].shape[0])
        squares = jnp.zeros((1, 1), F32)
        for key in grads:
            grads[key] = grads[key] / valid
            squares = squares + jnp.sum(grads[key] * grads[key], axis=(0, 1), keepdims=True)
        norm = jnp.sqrt(squares)
        factor = jnp.minimum(1.0, CLIP_NORM / (norm + 1e-06))
        for ref, value in zip(scalars, (loss, valid, norm)):
            ref[...] = value
        for (index, spot), grad in grads.items():
            rate = GAIN_RATE if index == 7 else WEIGHT_RATE
            decay = 0.0 if index == 7 else WEIGHT_DECAY
            new = adamw(
                states[0][index][spot],
                grad * factor,
                states[1][index][spot],
                states[2][index][spot],
                rate,
                decay,
            )
            for ref, value in zip(results[3 * index : 3 * index + 3], new):
                ref[spot] = value

    one = jax.ShapeDtypeStruct((1, 1), F32)
    shapes = [one] * 3
    for weight in weights:
        shapes += [jax.ShapeDtypeStruct(weight.shape, F32)] * 3
    found = pl.pallas_call(
        kernel,
        out_shape=shapes,
        compiler_params=pltpu.CompilerParams(vmem_limit_bytes=UPDATE_BYTES),
        name="update",
    )(*given, *weights, *firsts, *seconds)
    return tuple(value[0, 0] for value in found[:3]) + tuple(found[3:])


def step_by_crop(row_count, head_count, given, weights, firsts, seconds):
    single, residue_index, chain_index, token_mask, pair_valid, target_bins = given
    relative_table, single_weight, triangle_input, triangle_output = weights[:4]
    expand_weight, reduce_weight, distogram_weight, norm_gains = weights[4:]
    crops, tokens = token_mask.shape
    width = relative_table.shape[1]
    layers = triangle_input.shape[0]
    half = row_count // crops
    peers = half * head_count
    rows = tokens // peers
    row_index = lax.axis_index("row")
    crop = row_index // half
    start = position(row_index % half, lax.axis_index("head"), half, head_count) * rows

    placed = by_crop(jnp.stack([pair_valid, target_bins], axis=1), row_count, head_count)
    valid, target = placed[0], placed[1]

    def of_crop(array):
        return lax.dynamic_index_in_dim(array, crop, 0, keepdims=False)

    def of_rows(array):
        return lax.dynamic_slice_in_dim(array, start, rows, 0)

    residues, chains = of_crop(residue_index), of_crop(chain_index)
    reach = (relative_table.shape[0] - 2) // 2
    bins = jnp.where(
        of_rows(chains)[:, None] == chains[None, :],
        jnp.clip(of_rows(residues)[:, None] - residues[None, :], -reach, reach) + reach,
        2 * reach + 1,
    )
    present = of_crop(token_mask).astype(F32)
    pair_mask = of_rows(present)[:, None] * present[None, :]
    loss_weight = pair_mask * valid.astype(F32)
    table_rows = -(-relative_table.shape[0] // PACKED) * PACKED
    table_t = jnp.pad(relative_table, ((0, table_rows - relative_table.shape[0]), (0, 0))).T
    tokens_single = of_crop(single)
    proj = project(tokens_single, single_weight.astype(BF16))
    proj_rows = of_rows(proj[:, :width])[:, :, None]
    proj_cols = proj[:, width:].T
    bins, pair_mask = Arg(bins[:, None, :], ROWS), Arg(pair_mask[:, None, :], ROWS)

    prepared = prepare(
        triangle_input, triangle_output, expand_weight, reduce_weight, distogram_weight, norm_gains
    )
    mix, mix_t, out, out_t, up, up_t, down, down_t, logits_t, logits, gains = prepared
    hidden = up.shape[2]

    def gain(index):
        return Arg(gains, WHOLE, column=index)

    def layer_of(array, index, *block):
        shape = block or array.shape[1:]
        return Arg(array, WHOLE, (index, 0, 0), (None,) + tuple(shape))

    def triangle_weights(layer, kind, starts=False, finishes=False, back=False):
        index = 2 * layer + kind
        found = dict(gain0=gain(5 * layer + 2 * kind))
        if starts:
            found.update(mix_t=layer_of(mix_t, index, 4 * width, width))
        if starts and back:
            found.update(mix=layer_of(mix, index))
        if finishes:
            found.update(
                gain1=gain(5 * layer + 2 * kind + 1),
                gate_t=Arg(mix_t, WHOLE, (index, 4, 0), (None, width, width)),
                out_t=layer_of(out_t, index),
            )
        if finishes and back:
            found.update(out=layer_of(out, index))
        return found

    def transition_weights(layer, forth=True, back=False):
        found = dict(gain=gain(5 * layer + 4), up_t=layer_of(up_t, layer))
        if forth:
            found.update(down_t=layer_of(down_t, layer))
        if back:
            found.update(up=layer_of(up, layer), down=layer_of(down, layer))
        return found

    def state_out():
        return Out((rows, width, tokens), F32, ROWS)

    def sum_out(*shape):
        return Out(shape, F32, SUM)

    def gain_out():
        return sum_out(width, LANES)

    def back_start_outs():
        return dict(
            grad_gate=Out((rows, width, tokens), BF16, ROWS),
            out=sum_out(width, width),
            gain1=gain_out(),
        )

    def back_finish_outs():
        return dict(mix=sum_out(width, 5 * width), gain0=gain_out())

    def transition_outs():
        return dict(up=sum_out(width, hidden), down=sum_out(hidden // 2, width), gain=gain_out())

    identities = iter(range(4 * layers + 2))

    group = (peers, half, rows, tokens)
    block_out = Out((SUBLANES, tokens, tokens), BF16, ANYWHERE)

    def got_out(count):
        return [Out((peers, rows * SUBLANES, tokens), BF16, ANYWHERE)] * count

    def got_in(stage):
        return [Arg(array, ANYWHERE) for array in stage.got]

    def landed_out():
        return Out((peers, rows * SUBLANES, tokens), BF16, LANDED)

    def owned(kept):
        return dict(left=Arg(kept.left, ANYWHERE), right=Arg(kept.right, ANYWHERE))

    kept, states, middles, tris = {}, {}, {}, {}

    def first_body(i, o, rows, arrived, sent):
        state = dot(i.table_t[...], bins_hot(i.bins, rows, table_rows))
        yield
        cols = i.proj_cols[...]
        state = state + jnp.concatenate([cols + i.proj_rows[row] for row in rows], axis=1)
        write_rows(o.state, rows, state)
        yield from triangle_start(i.start, i, rows, sent, state)

    got = run_stage(
        first_body,
        "first_state",
        next(identities),
        group,
        dict(
            bins=bins,
            proj_rows=Arg(proj_rows, ROWS),
            proj_cols=Arg(proj_cols, WHOLE),
            table_t=Arg(table_t.astype(BF16), WHOLE),
            mask=pair_mask,
            start=triangle_weights(0, 0, starts=True),
        ),
        dict(state=state_out(), got=got_out(2)),
        wires=2,
    )
    states[0, 0] = got.state

    def between_body(i, o, rows, arrived, sent):
        state, _ = yield from triangle_finish(
            i.end, rows, arrived[0], read_rows(i.state, rows)
        )
        write_rows(o.state, rows, state)
        yield from triangle_start(i.start, i, rows, sent, state)

    def layer_end_body(i, o, rows, arrived, sent):
        state, _ = yield from triangle_finish(
            i.end, rows, arrived[0], read_rows(i.state, rows)
        )
        write_rows(o.middle, rows, state)
        lifted = yield from transition(i.lift, state)
        state = state + dot(i.lift.down_t[...], lifted[5])
        yield
        write_rows(o.state, rows, state)
        yield from triangle_start(i.start, i, rows, sent, state)

    for layer in range(layers):
        got = run_stage(
            between_body,
            "between_updates",
            next(identities),
            group,
            dict(
                got=got_in(got),
                state=Arg(states[layer, 0], ROWS),
                mask=pair_mask,
                end=triangle_weights(layer, 0, finishes=True),
                start=triangle_weights(layer, 1, starts=True),
            ),
            dict(
                state=state_out(),
                landed=landed_out(),
                left=block_out,
                right=block_out,
                got=got_out(2),
            ),
            Forward(tokens, False),
            wires=2,
        )
        kept[layer, 0], states[layer, 1], tris[layer, 0] = got, got.state, got.landed
        if layer + 1 == layers:
            break
        got = run_stage(
            layer_end_body,
            "layer_end",
            next(identities),
            group,
            dict(
                got=got_in(got),
                state=Arg(states[layer, 1], ROWS),
                mask=pair_mask,
                end=triangle_weights(layer, 1, finishes=True),
                lift=transition_weights(layer),
                start=triangle_weights(layer + 1, 0, starts=True),
            ),
            dict(
                middle=state_out(),
                state=state_out(),
                landed=landed_out(),
                left=block_out,
                right=block_out,
                got=got_out(2),
            ),
            Forward(tokens, True),
            wires=2,
        )
        kept[layer, 1], states[layer + 1, 0], tris[layer, 1] = got, got.state, got.landed
        middles[layer] = got.middle

    def loss_body(i, o, rows, arrived, sent):
        state, kept_triangle = yield from triangle_finish(
            i.end, rows, arrived[0], read_rows(i.state, rows)
        )
        lifted = yield from transition(i.lift, state)
        state = state + dot(i.lift.down_t[...], lifted[5])
        yield
        grad = yield from head_back(i.head, o.head, rows, state)
        grad = yield from transition_back(i.lift, o.lift, grad, lifted)
        write_rows(o.grad, rows, grad)
        yield from triangle_back_start(i.end, o.end, rows, sent[0], grad, kept_triangle)

    top = layers - 1
    got = run_stage(
        loss_body,
        "loss",
        next(identities),
        group,
        dict(
            got=got_in(got),
            state=Arg(states[top, 1], ROWS),
            end=triangle_weights(top, 1, finishes=True, back=True),
            lift=transition_weights(top, back=True),
            head=dict(
                gain=gain(5 * layers),
                logits=layer_of(logits, 0),
                logits_t=layer_of(logits_t, 0),
                target=Arg(target[:, None, :], ROWS),
                weight=Arg(loss_weight[:, None, :], ROWS),
            ),
        ),
        dict(
            grad=state_out(),
            head=dict(
                loss=sum_out(1, LANES),
                count=sum_out(1, LANES),
                logits=sum_out(distogram_weight.shape[1], width),
                gain=gain_out(),
            ),
            lift=transition_outs(),
            end=back_start_outs(),
            left=block_out,
            right=block_out,
            got=got_out(1),
        ),
        Forward(tokens, True),
        wires=1,
    )
    kept[top, 1] = got
    head, lifts, ends, begins = got.head, {top: got.lift}, {(top, 1): got.end}, {}

    def between_back_body(i, o, rows, arrived, sent):
        grad = yield from triangle_back_finish(i.start, i, o.start, rows, arrived)
        write_rows(o.grad, rows, grad)
        _, kept_triangle = yield from triangle_finish(
            i.end, rows, i.tri, read_rows(i.before, rows)
        )
        yield from triangle_back_start(i.end, o.end, rows, sent[0], grad, kept_triangle)

    def layer_end_back_body(i, o, rows, arrived, sent):
        grad = yield from triangle_back_finish(i.start, i, o.start, rows, arrived)
        lifted = yield from transition(i.lift, read_rows(i.middle, rows))
        grad = yield from transition_back(i.lift, o.lift, grad, lifted)
        write_rows(o.grad, rows, grad)
        _, kept_triangle = yield from triangle_finish(
            i.end, rows, i.tri, read_rows(i.before, rows)
        )
        yield from triangle_back_start(i.end, o.end, rows, sent[0], grad, kept_triangle)

    def first_back_body(i, o, rows, arrived, sent):
        grad = yield from triangle_back_finish(i.start, i, o.start, rows, arrived)
        hot = bins_hot(i.bins, rows, table_rows)
        high = grad.astype(BF16)
        low = (grad - high.astype(F32)).astype(BF16)
        o.table[...] += dot_pairs(hot, high) + dot_pairs(hot, low)
        yield
        for place, row in enumerate(rows):
            part = grad[:, place * tokens : (place + 1) * tokens]
            o.rows[row] = fold(part)
            o.cols[...] += part

    def layer_sums(layer):
        kinds = (0, 1) if layer else (1,)
        mixes = [begins[layer, 1].mix] if layer else []
        if layer + 1 < layers:
            mixes.append(begins[layer + 1, 0].mix)
        outs = [ends[layer, kind].out for kind in kinds]
        return (mixes, lifts[layer].up, jnp.concatenate(outs + [lifts[layer].down], axis=0))

    for layer in reversed(range(layers)):
        for kind in (1, 0):
            if (layer, kind) == (0, 0):
                first = lax.psum(layer_sums(top), ("row", "head"))
                first, got.grad = lax.optimization_barrier((first, got.grad))
            inputs = dict(
                got=got_in(got),
                owned=owned(kept[layer, kind]),
                grad=Arg(got.grad, ROWS),
                grad_gate=Arg(got.end.grad_gate, ROWS),
                state=Arg(states[layer, kind], ROWS),
                mask=pair_mask,
                start=triangle_weights(layer, kind, starts=True, back=True),
            )
            outputs = dict(start=back_finish_outs())
            products = Backward(tokens, kind == 1)
            if layer == 0 and kind == 0:
                got = run_stage(
                    first_back_body,
                    "first_state_back",
                    next(identities),
                    group,
                    dict(bins=bins, **inputs),
                    dict(
                        table=sum_out(table_rows, width),
                        rows=Out((rows, width, LANES), F32, ROWS),
                        cols=sum_out(width, tokens),
                        **outputs,
                    ),
                    products,
                )
                begins[layer, kind] = got.start
                break
            before = (layer, 0) if kind == 1 else (layer - 1, 1)
            inputs.update(
                before=Arg(states[before], ROWS),
                tri=Arg(tris[before], LANDED),
                end=triangle_weights(*before, finishes=True, back=True),
            )
            outputs.update(grad=state_out(), end=back_start_outs(), got=got_out(1))
            if kind == 1:
                body, name = between_back_body, "between_updates_back"
            else:
                body, name = layer_end_back_body, "layer_end_back"
                inputs.update(
                    middle=Arg(middles[layer - 1], ROWS),
                    lift=transition_weights(layer - 1, forth=False, back=True),
                )
                outputs.update(lift=transition_outs())
            got = run_stage(
                body, name, next(identities), group, inputs, outputs, products, wires=1
            )
            begins[layer, kind], ends[before] = got.start, got.end
            if kind == 0:
                lifts[layer - 1] = got.lift

    early = {layer: layer_sums(layer) for layer in range(top)}
    early = lax.psum(early, ("head", "row"))
    early[top] = first
    early_mixes = {}
    for layer in range(layers):
        mixes = list(early[layer][0])
        if layer:
            early_mixes[layer, 1] = mixes.pop(0)
        if mixes:
            early_mixes[layer + 1, 0] = mixes.pop(0)
    early = (
        [early_mixes[layer, kind] for layer in range(1, layers) for kind in range(2)],
        [early[layer][1] for layer in range(layers)],
        [early[layer][2] for layer in range(layers)],
    )

    wide_single = tokens_single.astype(F32)
    row_part = jnp.einsum(
        "is,ic->sc",
        of_rows(wide_single),
        jnp.sum(got.rows, axis=2),
        precision=lax.Precision.HIGHEST,
    )
    col_part = jnp.einsum("js,cj->sc", wide_single, got.cols, precision=lax.Precision.HIGHEST)
    partial_gains = []
    for layer in range(layers):
        for kind in range(2):
            partial_gains += [begins[layer, kind].gain0, ends[layer, kind].gain1]
        partial_gains.append(lifts[layer].gain)
    partial_gains.append(head.gain)
    grids = [
        begins[0, 0].mix,
        begins[0, 1].mix,
        ends[0, 0].out,
        head.logits,
        got.table,
        row_part,
        col_part,
    ]
    def turned(arrays):
        return arrays[:6] + (arrays[6].T,) + arrays[7:]

    rest, *starts = reduce_rest(
        half, peers, next(identities), grids, partial_gains, [head.loss, head.count]
    )
    found = update(rest, *starts, early, turned(weights), turned(firsts), turned(seconds))
    return found[:21] + tuple(value.T for value in found[21:24]) + found[24:]


def per_device(
    row_count,
    head_count,
    single,
    residue_index,
    chain_index,
    token_mask,
    pair_valid,
    target_bins,
    relative_table,
    single_weight,
    triangle_input,
    triangle_output,
    expand_weight,
    reduce_weight,
    distogram_weight,
    norm_gains,
    first_table,
    second_table,
    first_single,
    second_single,
    first_input,
    second_input,
    first_output,
    second_output,
    first_expand,
    second_expand,
    first_reduce,
    second_reduce,
    first_logits,
    second_logits,
    first_gains,
    second_gains,
):
    crops, tokens = token_mask.shape
    width = relative_table.shape[1]
    peers = row_count * head_count // crops
    given = (
        single,
        residue_index,
        chain_index,
        token_mask,
        pair_valid,
        target_bins,
        relative_table,
        single_weight,
        triangle_input,
        triangle_output,
        expand_weight,
        reduce_weight,
        distogram_weight,
        norm_gains,
    )
    weights = (
        relative_table,
        single_weight,
        triangle_input,
        triangle_output,
        expand_weight,
        reduce_weight,
        distogram_weight,
        norm_gains,
    )
    firsts = (
        first_table,
        first_single,
        first_input,
        first_output,
        first_expand,
        first_reduce,
        first_logits,
        first_gains,
    )
    seconds = (
        second_table,
        second_single,
        second_input,
        second_output,
        second_expand,
        second_reduce,
        second_logits,
        second_gains,
    )
    if (
        crops == 2
        and head_count == 2
        and width == LANES
        and width == SUBLANES * peers
        and tokens % (peers * SUBLANES) == 0
        and tokens % (3 * LANES) == 0
    ):
        return step_by_crop(row_count, head_count, given[:6], weights, firsts, seconds)
    local = gradients_by_block(*given)
    summed = lax.psum(local, ("row", "head"))
    loss_sum, valid_count = summed[0], summed[1]
    grads = [grad / valid_count for grad in summed[2:]]
    squares = jnp.zeros((), jnp.float32)
    for g in grads:
        squares = squares + jnp.sum(g * g)
    gradient_norm = jnp.sqrt(squares)
    factor = jnp.minimum(1.0, CLIP_NORM / (gradient_norm + 1e-06))
    result = []
    for index in range(8):
        rate = GAIN_RATE if index == 7 else WEIGHT_RATE
        decay = 0.0 if index == 7 else WEIGHT_DECAY
        result.extend(
            adamw(weights[index], grads[index] * factor, firsts[index], seconds[index], rate, decay)
        )
    return (
        loss_sum,
        valid_count,
        gradient_norm,
        result[0],
        result[1],
        result[2],
        result[3],
        result[4],
        result[5],
        result[6],
        result[7],
        result[8],
        result[9],
        result[10],
        result[11],
        result[12],
        result[13],
        result[14],
        result[15],
        result[16],
        result[17],
        result[18],
        result[19],
        result[20],
        result[21],
        result[22],
        result[23],
    )


def solution(mesh):
    placed = (
        P(),
        P(),
        P(),
        P(),
        P(None, "row", "head"),
        P(None, "row", "head"),
        P(),
        P(),
        P(),
        P(),
        P(),
        P(),
        P(),
        P(),
        P(),
        P(),
        P(),
        P(),
        P(),
        P(),
        P(),
        P(),
        P(),
        P(),
        P(),
        P(),
        P(),
        P(),
        P(),
        P(),
    )
    return jax.shard_map(
        functools.partial(per_device, mesh.shape["row"], mesh.shape["head"]),
        mesh=mesh,
        in_specs=placed,
        out_specs=(
            P(),
            P(),
            P(),
            P(),
            P(),
            P(),
            P(),
            P(),
            P(),
            P(),
            P(),
            P(),
            P(),
            P(),
            P(),
            P(),
            P(),
            P(),
            P(),
            P(),
            P(),
            P(),
            P(),
            P(),
            P(),
            P(),
            P(),
        ),
        check_vma=False,
    )
```

```python
import functools

import jax
import jax.numpy as jnp
from jax import lax
from jax.experimental import pallas as pl
from jax.experimental.pallas import tpu as pltpu
from jax.sharding import PartitionSpec as P

STEP = 10


EPS = 1e-05
BETA_ONE = 0.9
BETA_TWO = 0.999
ADAM_EPS = 1e-08
WEIGHT_RATE = 0.1
GAIN_RATE = 0.5
WEIGHT_DECAY = 0.01
CLIP_NORM = 0.002


def normalize(value):
    mean = jnp.mean(value, axis=-1, keepdims=True)
    centred = value - mean
    scale = lax.rsqrt(jnp.mean(centred * centred, axis=-1, keepdims=True) + EPS)
    return (centred * scale, scale)


def norm_back(grad_out, unit, scale, gain):
    scaled = grad_out * gain
    first_mean = jnp.mean(scaled, axis=-1, keepdims=True)
    second_mean = jnp.mean(scaled * unit, axis=-1, keepdims=True)
    grad_in = scale * (scaled - first_mean - unit * second_mean)
    grad_gain = jnp.sum(grad_out * unit, axis=tuple(range(grad_out.ndim - 1)))
    return (grad_in, grad_gain)


def project(value, weight):
    return jnp.einsum("...c,cd->...d", value, weight, preferred_element_type=jnp.float32)


def project_back(grad, weight):
    return jnp.einsum("...d,cd->...c", grad, weight, preferred_element_type=jnp.float32)


def weight_grad(value, grad):
    return jnp.einsum("bijc,bijd->cd", value, grad, preferred_element_type=jnp.float32)


def triangle_forward(state, weight_in, weight_out, gains, pair_mask, incoming):
    hidden = weight_out.shape[0]
    pair_unit, pair_scale = normalize(state)
    normed = (pair_unit * gains[0]).astype(jnp.bfloat16)
    mixed = project(normed, weight_in)
    mask = pair_mask[..., None]
    left = (mask * jax.nn.sigmoid(mixed[..., :hidden]) * mixed[..., hidden : 2 * hidden]).astype(
        jnp.bfloat16
    )
    right = (
        mask
        * jax.nn.sigmoid(mixed[..., 2 * hidden : 3 * hidden])
        * mixed[..., 3 * hidden : 4 * hidden]
    ).astype(jnp.bfloat16)
    left_cols, right_cols = (
        lax.all_to_all(left, "head", split_axis=3, concat_axis=2, tiled=True),
        lax.all_to_all(right, "head", split_axis=3, concat_axis=2, tiled=True),
    )
    if incoming:
        left_cols, right_cols = (
            lax.all_to_all(left_cols, "row", split_axis=2, concat_axis=1, tiled=True),
            lax.all_to_all(right_cols, "row", split_axis=2, concat_axis=1, tiled=True),
        )
        left_cols = jnp.swapaxes(left_cols, 1, 2)
        right_cols = jnp.swapaxes(right_cols, 1, 2)
    right_all = lax.all_gather(right_cols, "row", axis=1, tiled=True)
    triangle = jnp.einsum(
        "bikc,bjkc->bijc", left_cols, right_all, preferred_element_type=jnp.float32
    )
    triangle = lax.all_to_all(
        triangle.astype(jnp.bfloat16), "head", split_axis=2, concat_axis=3, tiled=True
    )
    tri_unit, tri_scale = normalize(triangle.astype(jnp.float32))
    shaped = (tri_unit * gains[1]).astype(jnp.bfloat16)
    branch = project(shaped, weight_out)
    gate = jax.nn.sigmoid(mixed[..., 4 * hidden :])
    kept = (
        pair_unit,
        pair_scale,
        normed,
        mixed,
        left_cols,
        right_all,
        tri_unit,
        tri_scale,
        shaped,
        branch,
        gate,
    )
    return (state + gate * branch, kept)


def triangle_backward(grad_state, kept, weight_in, weight_out, gains, pair_mask, incoming):
    hidden = weight_out.shape[0]
    (
        pair_unit,
        pair_scale,
        normed,
        mixed,
        left_cols,
        right_all,
        tri_unit,
        tri_scale,
        shaped,
        branch,
        gate,
    ) = kept
    grad_branch = (grad_state * gate).astype(jnp.bfloat16)
    grad_gate = grad_state * branch * gate * (1.0 - gate)
    grad_out = weight_grad(shaped, grad_branch)
    grad_shaped = project_back(grad_branch, weight_out)
    grad_tri, gain_two = norm_back(grad_shaped, tri_unit, tri_scale, gains[1])
    tri_cols = lax.all_to_all(
        grad_tri.astype(jnp.bfloat16), "head", split_axis=3, concat_axis=2, tiled=True
    )
    grad_left = jnp.einsum(
        "bijc,bjkc->bikc", tri_cols, right_all, preferred_element_type=jnp.float32
    )
    grad_left = grad_left.astype(jnp.bfloat16)
    summed = lax.psum_scatter(
        jnp.einsum(
            "bijc,bikc->jbkc", tri_cols, left_cols, preferred_element_type=jnp.float32
        ).astype(jnp.bfloat16),
        "row",
        scatter_dimension=0,
        tiled=True,
    ).astype(jnp.float32)
    grad_right = jnp.transpose(summed, (1, 0, 2, 3)).astype(jnp.bfloat16)
    if incoming:
        grad_left, grad_right = (
            lax.all_to_all(
                jnp.swapaxes(grad_left, 1, 2), "row", split_axis=1, concat_axis=2, tiled=True
            ),
            lax.all_to_all(
                jnp.swapaxes(grad_right, 1, 2), "row", split_axis=1, concat_axis=2, tiled=True
            ),
        )
    back_left, back_right = (
        lax.all_to_all(grad_left, "head", split_axis=2, concat_axis=3, tiled=True),
        lax.all_to_all(grad_right, "head", split_axis=2, concat_axis=3, tiled=True),
    )
    mask = pair_mask[..., None]
    back_left = back_left.astype(jnp.float32) * mask
    back_right = back_right.astype(jnp.float32) * mask
    left_sig = jax.nn.sigmoid(mixed[..., :hidden])
    left_value = mixed[..., hidden : 2 * hidden]
    right_sig = jax.nn.sigmoid(mixed[..., 2 * hidden : 3 * hidden])
    right_value = mixed[..., 3 * hidden : 4 * hidden]
    grad_mixed = jnp.concatenate(
        [
            back_left * left_value * left_sig * (1.0 - left_sig),
            back_left * left_sig,
            back_right * right_value * right_sig * (1.0 - right_sig),
            back_right * right_sig,
            grad_gate,
        ],
        axis=-1,
    ).astype(jnp.bfloat16)
    grad_in = weight_grad(normed, grad_mixed)
    grad_normed = project_back(grad_mixed, weight_in)
    grad_first, gain_one = norm_back(grad_normed, pair_unit, pair_scale, gains[0])
    return (grad_state + grad_first, (grad_in, grad_out, gain_one, gain_two))


def transition_forward(state, weight_up, weight_down, gain):
    expand = weight_down.shape[0]
    unit, scale = normalize(state)
    lifted = (unit * gain).astype(jnp.bfloat16)
    inner = project(lifted, weight_up)
    product = (jax.nn.silu(inner[..., :expand]) * inner[..., expand:]).astype(jnp.bfloat16)
    return (state + project(product, weight_down), (unit, scale, lifted, inner, product))


def transition_backward(grad_state, kept, weight_up, weight_down, gain):
    expand = weight_down.shape[0]
    unit, scale, lifted, inner, product = kept
    grad_low = grad_state.astype(jnp.bfloat16)
    grad_down = weight_grad(product, grad_low)
    grad_product = project_back(grad_low, weight_down)
    gate_part = inner[..., :expand]
    up_part = inner[..., expand:]
    gate_sig = jax.nn.sigmoid(gate_part)
    silu_value = gate_part * gate_sig
    silu_slope = gate_sig * (1.0 + gate_part * (1.0 - gate_sig))
    grad_inner = jnp.concatenate(
        [grad_product * up_part * silu_slope, grad_product * silu_value], axis=-1
    )
    grad_inner = grad_inner.astype(jnp.bfloat16)
    grad_up = weight_grad(lifted, grad_inner)
    grad_lifted = project_back(grad_inner, weight_up)
    grad_middle, gain_grad = norm_back(grad_lifted, unit, scale, gain)
    return (grad_middle + grad_state, (grad_up, grad_down, gain_grad))


def block_forward(state, weight_in, weight_out, weight_up, weight_down, gains, pair_mask):
    first, kept_one = triangle_forward(
        state, weight_in[0], weight_out[0], gains[0:2], pair_mask, False
    )
    second, kept_two = triangle_forward(
        first, weight_in[1], weight_out[1], gains[2:4], pair_mask, True
    )
    output, kept_three = transition_forward(second, weight_up, weight_down, gains[4])
    return (output, (kept_one, kept_two, kept_three))


def block_backward(
    grad_state, state, weight_in, weight_out, weight_up, weight_down, gains, pair_mask
):
    skipped, kept = block_forward(
        state, weight_in, weight_out, weight_up, weight_down, gains, pair_mask
    )
    kept_one, kept_two, kept_three = kept
    grad_state, (grad_up, grad_down, gain_five) = transition_backward(
        grad_state, kept_three, weight_up, weight_down, gains[4]
    )
    grad_state, (in_two, out_two, gain_three, gain_four) = triangle_backward(
        grad_state, kept_two, weight_in[1], weight_out[1], gains[2:4], pair_mask, True
    )
    grad_state, (in_one, out_one, gain_one, gain_two) = triangle_backward(
        grad_state, kept_one, weight_in[0], weight_out[0], gains[0:2], pair_mask, False
    )
    return (
        grad_state,
        (
            jnp.stack([in_one, in_two]),
            jnp.stack([out_one, out_two]),
            grad_up,
            grad_down,
            jnp.stack([gain_one, gain_two, gain_three, gain_four, gain_five]),
        ),
    )


def adamw(weight, grad, first, second, rate, decay):
    first_new = BETA_ONE * first + (1.0 - BETA_ONE) * grad
    second_new = BETA_TWO * second + (1.0 - BETA_TWO) * grad * grad
    moved = (
        first_new
        / (1.0 - BETA_ONE**STEP)
        / (jnp.sqrt(second_new / (1.0 - BETA_TWO**STEP)) + ADAM_EPS)
    )
    return (first_new, second_new, weight - rate * (moved + decay * weight))


def gradients_by_block(
    single,
    residue_index,
    chain_index,
    token_mask,
    pair_valid,
    target_bins,
    relative_table,
    single_weight,
    triangle_input,
    triangle_output,
    expand_weight,
    reduce_weight,
    distogram_weight,
    norm_gains,
):
    crops, rows, cols = pair_valid.shape
    width = relative_table.shape[1]
    layers = triangle_input.shape[0]
    row_start = lax.axis_index("row") * rows
    col_start = lax.axis_index("head") * cols

    def take(array, start, count):
        return lax.dynamic_slice_in_dim(array, start, count, 1)

    offset = (
        take(residue_index, row_start, rows)[:, :, None]
        - take(residue_index, col_start, cols)[:, None, :]
    )
    same = (
        take(chain_index, row_start, rows)[:, :, None]
        == take(chain_index, col_start, cols)[:, None, :]
    )
    reach = (relative_table.shape[0] - 2) // 2
    bins = jnp.where(same, jnp.clip(offset, -reach, reach) + reach, 2 * reach + 1)
    relative_hot = (
        bins[..., None] == jnp.arange(relative_table.shape[0])[None, None, None, :]
    ).astype(jnp.float32)
    token_rows = take(token_mask, row_start, rows).astype(jnp.float32)
    token_cols = take(token_mask, col_start, cols).astype(jnp.float32)
    pair_mask = token_rows[:, :, None] * token_cols[:, None, :]
    loss_weight = pair_mask * pair_valid.astype(jnp.float32)
    low_input = triangle_input.astype(jnp.bfloat16)
    low_output = triangle_output.astype(jnp.bfloat16)
    low_expand = expand_weight.astype(jnp.bfloat16)
    low_reduce = reduce_weight.astype(jnp.bfloat16)
    low_logits = distogram_weight.astype(jnp.bfloat16)
    proj = project(single, single_weight.astype(jnp.bfloat16))
    state = project(relative_hot.astype(jnp.bfloat16), relative_table.astype(jnp.bfloat16))
    state = (
        state
        + take(proj, row_start, rows)[:, :, None, :width]
        + take(proj, col_start, cols)[:, None, :, width:]
    )
    inputs = []
    for layer in range(layers):
        inputs.append(state)
        state, unused = block_forward(
            state,
            low_input[layer],
            low_output[layer],
            low_expand[layer],
            low_reduce[layer],
            norm_gains[5 * layer : 5 * layer + 5],
            pair_mask,
        )
    head_unit, head_scale = normalize(state)
    shown = (head_unit * norm_gains[5 * layers]).astype(jnp.bfloat16)
    logits = project(shown, low_logits)
    largest = jnp.max(logits, axis=-1, keepdims=True)
    log_total = largest + jnp.log(jnp.sum(jnp.exp(logits - largest), axis=-1, keepdims=True))
    target_hot = (
        target_bins[..., None] == jnp.arange(logits.shape[-1])[None, None, None, :]
    ).astype(jnp.float32)
    picked = jnp.sum(logits * target_hot, axis=-1)
    loss_local = jnp.sum(loss_weight * (log_total[..., 0] - picked))
    grad_scores = (loss_weight[..., None] * (jnp.exp(logits - log_total) - target_hot)).astype(
        jnp.bfloat16
    )
    grad_logits = weight_grad(shown, grad_scores)
    grad_shown = project_back(grad_scores, low_logits)
    grad_state, gain_last = norm_back(grad_shown, head_unit, head_scale, norm_gains[5 * layers])
    collected = []
    for layer in reversed(range(layers)):
        grad_state, layer_grads = block_backward(
            grad_state,
            inputs[layer],
            low_input[layer],
            low_output[layer],
            low_expand[layer],
            low_reduce[layer],
            norm_gains[5 * layer : 5 * layer + 5],
            pair_mask,
        )
        collected.insert(0, layer_grads)
    grad_input = jnp.stack([entry[0] for entry in collected])
    grad_output = jnp.stack([entry[1] for entry in collected])
    grad_expand = jnp.stack([entry[2] for entry in collected])
    grad_reduce = jnp.stack([entry[3] for entry in collected])
    grad_gains = jnp.concatenate(
        [jnp.concatenate([entry[4] for entry in collected], axis=0), gain_last[None]], axis=0
    )
    grad_table = jnp.einsum(
        "bijr,bijc->rc", relative_hot, grad_state, precision=lax.Precision.HIGHEST
    )
    single_wide = single.astype(jnp.float32)
    row_part = jnp.einsum(
        "bis,bic->sc",
        take(single_wide, row_start, rows),
        jnp.sum(grad_state, axis=2),
        precision=lax.Precision.HIGHEST,
    )
    col_part = jnp.einsum(
        "bjs,bjc->sc",
        take(single_wide, col_start, cols),
        jnp.sum(grad_state, axis=1),
        precision=lax.Precision.HIGHEST,
    )
    grad_single = jnp.concatenate([row_part, col_part], axis=1)
    return (
        loss_local,
        jnp.sum(loss_weight),
        grad_table,
        grad_single,
        grad_input,
        grad_output,
        grad_expand,
        grad_reduce,
        grad_logits,
        grad_gains,
    )


F32 = jnp.float32
BF16 = jnp.bfloat16
LANES = 128
SUBLANES = 8
PACKED = 16
ROW_BLOCK = 4
STREAM_ROWS = 2
PHASES = SUBLANES // ROW_BLOCK
CHUNK_ROWS = SUBLANES * SUBLANES
VMEM_BYTES = 58 * 2**20
UPDATE_BYTES = VMEM_BYTES
REDUCE_BYTES = VMEM_BYTES
MESH = pl.DeviceIdType.MESH
ROWS, LANDED, WHOLE, SUM, ANYWHERE = range(5)


class Bag:
    def __init__(self, **entries):
        self.__dict__.update(entries)


class Arg:
    def __init__(self, array, kind, index=None, block=None, column=None):
        self.array, self.kind, self.index, self.block = array, kind, index, block
        self.column = column

    def spec(self):
        if self.index is None:
            return block_spec(self.array.shape, self.kind)
        index = self.index
        return pl.BlockSpec(self.block, lambda step: index)


class Column:
    def __init__(self, ref, column):
        self.ref, self.column = ref, column

    def __getitem__(self, _):
        return self.ref[:, self.column : self.column + 1]


class Out:
    def __init__(self, shape, dtype, kind):
        self.shape, self.dtype, self.kind = shape, dtype, kind

    def spec(self):
        return block_spec(self.shape, ANYWHERE if self.kind == LANDED else self.kind)


def block_spec(shape, kind):
    if kind == ANYWHERE:
        return pl.BlockSpec(memory_space=pl.ANY)
    if kind == LANDED:
        return pl.BlockSpec((shape[0], CHUNK_ROWS, shape[2]), lambda step: (0, step // PHASES, 0))
    if kind == ROWS:
        return pl.BlockSpec((ROW_BLOCK,) + shape[1:], lambda step: (step,) + (0,) * (len(shape) - 1))
    return pl.BlockSpec(shape, lambda step: (0,) * len(shape))


def is_leaf(value):
    return isinstance(value, (Arg, Out))


def bag_of(tree, leaves):
    if is_leaf(tree):
        return next(leaves)
    if isinstance(tree, list):
        return [bag_of(value, leaves) for value in tree]
    return Bag(**{key: bag_of(value, leaves) for key, value in tree.items()})


def leaves_of(tree):
    if is_leaf(tree):
        return [tree]
    found = []
    for value in tree if isinstance(tree, list) else tree.values():
        found.extend(leaves_of(value))
    return found


def dot(left, right):
    return lax.dot_general(left, right, (((1,), (0,)), ((), ())), preferred_element_type=F32)


def dot_pairs(left, right):
    return lax.dot_general(left, right, (((1,), (1,)), ((), ())), preferred_element_type=F32)


def product_of(left, right, left_axis, right_axis):
    return lax.dot_general(
        left, right, (((left_axis,), (right_axis,)), ((), ())), preferred_element_type=F32
    )


def sigmoid(value):
    return 0.5 * jnp.tanh(0.5 * value) + 0.5


def unit_of(value):
    centred = value - jnp.mean(value, axis=0, keepdims=True)
    scale = lax.rsqrt(jnp.mean(centred * centred, axis=0, keepdims=True) + EPS)
    return (centred * scale, scale)


def unit_back(grad, unit, scale, gain):
    scaled = grad * gain
    first = jnp.mean(scaled, axis=0, keepdims=True)
    second = jnp.mean(scaled * unit, axis=0, keepdims=True)
    return scale * (scaled - first - unit * second)


def fold(value):
    total = value[:, :LANES]
    for start in range(LANES, value.shape[1], LANES):
        total = total + value[:, start : start + LANES]
    return total


def read_rows(ref, rows):
    return jnp.concatenate([ref[row] for row in rows], axis=1)


def write_rows(ref, rows, value):
    cols = ref.shape[2]
    for place, row in enumerate(rows):
        ref[row] = value[:, place * cols : (place + 1) * cols].astype(ref.dtype)


def alternate(streams):
    while streams:
        going = []
        for stream in streams:
            try:
                next(stream)
                going.append(stream)
            except StopIteration:
                pass
        streams = going


class Wire:
    def __init__(self, wide, phase):
        self.wide, self.phase = wide, phase

    def tokens(self, row):
        width = self.wide.shape[1] // SUBLANES
        return pl.ds(self.phase * ROW_BLOCK + row, width, stride=SUBLANES)

    def read(self, rows):
        lanes = self.wide.shape[0]
        return jnp.concatenate(
            [self.wide[lane, self.tokens(row), :] for row in rows for lane in range(lanes)], axis=1
        )

    def write(self, rows, value):
        lanes = self.wide.shape[0]
        for place, row in enumerate(rows):
            for lane in range(lanes):
                start = (place * lanes + lane) * LANES
                self.wide[lane, self.tokens(row), :] = value[:, start : start + LANES]


def widen(wide, low, chunk):
    rows = pl.ds(pl.multiple_of(chunk * CHUNK_ROWS, CHUNK_ROWS), CHUNK_ROWS)

    def step(peer, carry):
        value = low[peer, rows, :].astype(F32)
        start = pl.multiple_of(peer * CHUNK_ROWS, CHUNK_ROWS)
        for lane in range(wide.shape[0]):
            wide[lane, pl.ds(start, CHUNK_ROWS), :] = value[:, lane * LANES : (lane + 1) * LANES]
        return carry

    lax.fori_loop(0, low.shape[0], step, 0)


def narrow(low, wide, chunk):
    rows = pl.ds(pl.multiple_of(chunk * CHUNK_ROWS, CHUNK_ROWS), CHUNK_ROWS)

    def step(peer, carry):
        start = pl.multiple_of(peer * CHUNK_ROWS, CHUNK_ROWS)
        low[peer, rows, :] = jnp.concatenate(
            [wide[lane, pl.ds(start, CHUNK_ROWS), :] for lane in range(wide.shape[0])], axis=1
        ).astype(low.dtype)
        return carry

    lax.fori_loop(0, low.shape[0], step, 0)


def triangle_start(weights, i, rows, wires, state):
    width = state.shape[0]
    unit, _ = unit_of(state)
    normed = (unit * weights.gain0[...]).astype(BF16)
    mixed = dot(weights.mix_t[...], normed)
    yield
    mask = read_rows(i.mask, rows)
    for wire, base in zip(wires, (0, 2 * width)):
        gate = sigmoid(mixed[base : base + width])
        wire.write(rows, mask * gate * mixed[base + width : base + 2 * width])


def triangle_finish(weights, rows, wire, state):
    unit, _ = unit_of(state)
    normed = (unit * weights.gain0[...]).astype(BF16)
    opened = dot(weights.gate_t[...], normed)
    yield
    tri_unit, tri_scale = unit_of(wire.read(rows))
    shaped = (tri_unit * weights.gain1[...]).astype(BF16)
    branch = dot(weights.out_t[...], shaped)
    yield
    gate = sigmoid(opened)
    return (state + gate * branch, (gate, tri_unit, tri_scale, shaped, branch))


def triangle_back_start(weights, o, rows, wire, grad, kept):
    gate, tri_unit, tri_scale, shaped, branch = kept
    grad_branch = (grad * gate).astype(BF16)
    grad_shaped = dot(weights.out[...], grad_branch)
    yield
    o.out[...] += dot_pairs(shaped, grad_branch)
    write_rows(o.grad_gate, rows, grad * branch * gate * (1.0 - gate))
    yield
    o.gain1[...] += fold(grad_shaped * tri_unit)
    wire.write(rows, unit_back(grad_shaped, tri_unit, tri_scale, weights.gain1[...]))


def triangle_back_finish(weights, i, o, rows, wires):
    grad, state = read_rows(i.grad, rows), read_rows(i.state, rows)
    width = state.shape[0]
    unit, scale = unit_of(state)
    gain = weights.gain0[...]
    normed = (unit * gain).astype(BF16)
    mixed = dot(weights.mix_t[...], normed)
    yield
    mask = read_rows(i.mask, rows)
    parts = []
    for wire, base in zip(wires, (0, 2 * width)):
        back = wire.read(rows) * mask
        gate = sigmoid(mixed[base : base + width])
        back_gate = back * gate
        parts.append((back_gate * mixed[base + width : base + 2 * width] * (1.0 - gate)).astype(BF16))
        parts.append(back_gate.astype(BF16))
    parts.append(read_rows(i.grad_gate, rows))
    grad_mixed = jnp.concatenate(parts, axis=0)
    yield
    grad_normed = dot(weights.mix[...], grad_mixed)
    o.mix[...] += dot_pairs(normed, grad_mixed)
    yield
    o.gain0[...] += fold(grad_normed * unit)
    return grad + unit_back(grad_normed, unit, scale, gain)


def transition(weights, state):
    unit, scale = unit_of(state)
    lifted = (unit * weights.gain[...]).astype(BF16)
    inner = dot(weights.up_t[...], lifted)
    yield
    half = inner.shape[0] // 2
    gate = inner[:half]
    slope = sigmoid(gate)
    product = (gate * slope * inner[half:]).astype(BF16)
    return (unit, scale, lifted, inner, slope, product)


def transition_back(weights, o, grad, kept):
    unit, scale, lifted, inner, slope, product = kept
    half = inner.shape[0] // 2
    gate, up = inner[:half], inner[half:]
    grad_low = grad.astype(BF16)
    grad_product = dot(weights.down[...], grad_low)
    o.down[...] += dot_pairs(product, grad_low)
    yield
    scaled = grad_product * slope
    grad_inner = jnp.concatenate(
        [
            (scaled * up * (1.0 + gate * (1.0 - slope))).astype(BF16),
            (scaled * gate).astype(BF16),
        ],
        axis=0,
    )
    yield
    grad_lifted = dot(weights.up[...], grad_inner)
    o.up[...] += dot_pairs(lifted, grad_inner)
    yield
    o.gain[...] += fold(grad_lifted * unit)
    return grad + unit_back(grad_lifted, unit, scale, weights.gain[...])


def head_back(i, o, rows, state):
    unit, scale = unit_of(state)
    gain = i.gain[...]
    shown = (unit * gain).astype(BF16)
    logits = dot(i.logits_t[...], shown)
    yield
    largest = jnp.max(logits, axis=0, keepdims=True)
    raised = jnp.exp(logits - largest)
    total = jnp.sum(raised, axis=0, keepdims=True)
    log_total = largest + jnp.log(total)
    target = read_rows(i.target, rows)
    weight = read_rows(i.weight, rows)
    hot = lax.broadcasted_iota(jnp.int32, logits.shape, 0) == target
    picked = jnp.sum(jnp.where(hot, logits, 0.0), axis=0, keepdims=True)
    o.loss[...] += fold(weight * (log_total - picked))
    o.count[...] += fold(weight)
    share = raised * (1.0 / total)
    grad_scores = (weight * (share - jnp.where(hot, 1.0, 0.0))).astype(BF16)
    grad_shown = dot(i.logits[...], grad_scores)
    o.logits[...] += dot_pairs(grad_scores, shown)
    yield
    o.gain[...] += fold(grad_shown * unit)
    return unit_back(grad_shown, unit, scale, gain)


def bins_hot(bins, rows, table_rows):
    bins = read_rows(bins, rows)
    shape = (table_rows, bins.shape[1])
    return jnp.where(lax.broadcasted_iota(jnp.int32, shape, 0) == bins, 1.0, 0.0).astype(BF16)


def run_stage(body, name, collective_id, group, inputs, outputs, products=None, wires=0):
    peers, half, rows, tokens = group
    args, outs = leaves_of(inputs), leaves_of(outputs)
    steps = rows // ROW_BLOCK
    chunks = rows // SUBLANES
    arriving = products.results if products else 0
    landed_args = [index for index, arg in enumerate(args) if arg.kind == LANDED]
    keeps = [place for place, out in enumerate(outs) if out.kind == LANDED]
    low = pltpu.VMEM((peers, rows * SUBLANES, tokens), BF16)
    many = pltpu.SemaphoreType.DMA((chunks, peers))
    wide = pltpu.VMEM((tokens // LANES, peers * CHUNK_ROWS, LANES), F32)
    groups = [
        [wide] * (arriving + len(landed_args) + wires),
        [low] * arriving,
        [many] * (2 * arriving),
        [low] * wires,
        [many] * (2 * wires),
        [pltpu.SemaphoreType.DMA((1,))] * len(keeps),
        products.scratch(low) if products else [],
    ]

    def kernel(*refs):
        step = pl.program_id(0)
        phase, chunk = lax.rem(step, PHASES), lax.div(step, PHASES)
        in_refs = [
            ref if arg.column is None else Column(ref, arg.column) for arg, ref in zip(args, refs)
        ]
        out_refs = list(refs[len(args) : len(args) + len(outs)])
        rest, parts = list(refs[len(args) + len(outs) :]), []
        for part in groups:
            parts.append(rest[: len(part)])
            rest = rest[len(part) :]
        wides, lands, land_sems, sends, send_sems, keep_sems, held = parts
        saves = [
            pltpu.make_async_copy(land, out_refs[place], sem.at[0])
            for land, place, sem in zip(lands, keeps, keep_sems)
        ]
        ring = Exchange(peers, half)
        i, o = bag_of(inputs, iter(in_refs)), bag_of(outputs, iter(out_refs))
        arrivals = [
            (result, land, land_sems[2 * place], land_sems[2 * place + 1])
            for place, (result, land) in enumerate(zip(held, lands))
        ]

        @pl.when(step == 0)
        def _():
            ring.greet()
            if products:
                products.load(i, held)
            for out, ref in zip(outs, out_refs):
                if out.kind == SUM:
                    ref[...] = jnp.zeros(out.shape, out.dtype)
            if products:
                products.multiply(i, o, held)
                ring.meet()

                def start(index, carry):
                    ring.start(arrivals, index)
                    return carry

                lax.fori_loop(0, chunks, start, 0)

        if products:

            @pl.when(phase == 0)
            def _():
                ring.wait(arrivals, chunk)
                for target, land in zip(wides, lands):
                    widen(target, land, chunk)

        if landed_args:

            @pl.when(phase == 0)
            def _():
                for target, index in zip(wides[arriving:], landed_args):
                    widen(target, in_refs[index], 0)

        if saves:

            @pl.when(step == steps - PHASES)
            def _():
                for save in saves:
                    save.start()

        body_in = list(in_refs)
        for index, source in zip(landed_args, wides[arriving:]):
            body_in[index] = Wire(source, phase)
        given = bag_of(inputs, iter(body_in))
        arrived = [Wire(source, phase) for source in wides[:arriving]]
        written = wides[arriving + len(landed_args) :]
        sent = [Wire(target, phase) for target in written]
        alternate(
            [
                body(given, o, range(first, first + STREAM_ROWS), arrived, sent)
                for first in range(0, ROW_BLOCK, STREAM_ROWS)
            ]
        )
        moves = [
            (send, land, send_sems[2 * place], send_sems[2 * place + 1])
            for place, (send, land) in enumerate(zip(sends, o.got if wires else []))
        ]
        if wires:

            @pl.when(phase == PHASES - 1)
            def _():
                for source, send in zip(written, sends):
                    narrow(send, source, chunk)
                if not products:

                    @pl.when(chunk == 0)
                    def _():
                        ring.meet()

                ring.start(moves, chunk)

        @pl.when(step == steps - 1)
        def _():
            if wires:

                def wait(index, carry):
                    ring.wait(moves, index)
                    return carry

                lax.fori_loop(0, chunks, wait, 0)
            for save in saves:
                save.wait()
            if products:
                products.end(o, held)

    results = pl.pallas_call(
        kernel,
        grid=(steps,),
        in_specs=[arg.spec() for arg in args],
        out_specs=[out.spec() for out in outs],
        out_shape=[jax.ShapeDtypeStruct(out.shape, out.dtype) for out in outs],
        scratch_shapes=sum(groups, []),
        compiler_params=pltpu.CompilerParams(
            dimension_semantics=(pltpu.ARBITRARY,),
            vmem_limit_bytes=VMEM_BYTES,
            has_side_effects=True,
            collective_id=collective_id,
        ),
        cost_estimate=pl.CostEstimate(flops=0, bytes_accessed=0, transcendentals=0),
        name=name,
    )(*[arg.array for arg in args])
    return bag_of(outputs, iter(results))


def flip(value, step, count):
    step = jnp.int32(step)
    result, bit = 0, 1
    while bit < count:
        result = result + lax.rem(lax.div(value, bit) + lax.div(step, bit), 2) * bit
        bit *= 2
    return result


def position(row, head, half, heads):
    inner = half // 2 * heads
    return (row % 2) * inner + (row // 2) * heads + head


def place_of(position, half, heads):
    inner = half // 2 * heads
    rest = lax.rem(position, inner)
    return (lax.div(rest, heads) * 2 + lax.div(position, inner), lax.rem(rest, heads))


class Exchange:
    def __init__(self, count, half):
        row, head = lax.axis_index("row"), lax.axis_index("head")
        place = lax.rem(row, half)
        inner = count // 2
        self.count = count
        self.half = half
        self.base = row - place
        self.me = lax.rem(place, 2) * inner + lax.div(place, 2) * (count // half) + head
        self.twin = (lax.rem(row + half, 2 * half), head)
        core = lax.div(self.me, inner)
        self.order = []
        for low in range(inner // 2):
            for step in (low, low + inner):
                other = step ^ (inner - 1)
                for first, second in ((step, other), (other, step)):
                    if first == 0 or second == 0:
                        if first:
                            self.order.append(first)
                    else:
                        self.order.append(first + core * (second - first))

    def peer(self, step):
        return flip(self.me, step, self.count)

    def device(self, peer):
        place, head = place_of(peer, self.half, self.count // self.half)
        return (self.base + place, head)

    def greet(self):
        barrier = pltpu.get_barrier_semaphore()
        for step in self.order:
            pl.semaphore_signal(
                barrier, inc=1, device_id=self.device(self.peer(step)), device_id_type=MESH
            )

    def meet(self):
        pl.semaphore_wait(pltpu.get_barrier_semaphore(), self.count - 1)

    def copies(self, moves, chunk, steps):
        found = []
        for source, target, send_sems, recv_sems in moves:
            size = source.shape[1] // send_sems.shape[0]
            rows = pl.ds(pl.multiple_of(chunk * size, PACKED), size)
            for step in steps:
                peer = self.me if step is None else self.peer(step)
                if step is None:
                    copy = pltpu.make_async_copy(
                        source.at[self.me, rows, :],
                        target.at[self.me, rows, :],
                        send_sems.at[chunk, 0],
                    )
                else:
                    copy = pltpu.make_async_remote_copy(
                        src_ref=source.at[peer, rows, :],
                        dst_ref=target.at[self.me, rows, :],
                        send_sem=send_sems.at[chunk, step],
                        recv_sem=recv_sems.at[chunk, step],
                        device_id=self.device(peer),
                        device_id_type=MESH,
                    )
                found.append(copy)
        return found

    def start(self, moves, chunk):
        for copy in self.copies(moves, chunk, self.order + [None]):
            copy.start()

    def wait(self, moves, chunk):
        for copy in self.copies(moves, chunk, self.order + [None]):
            copy.wait()


def join_channels(got, pair):
    peers, rows, _ = got.shape
    even, odd = [], []
    for peer in range(peers):
        for start in range(0, rows, CHUNK_ROWS):
            piece = got[peer, pl.ds(pl.multiple_of(start + pair * PACKED, PACKED), PACKED), :]
            piece = piece.astype(F32)
            even.append(piece[:SUBLANES])
            odd.append(piece[SUBLANES:])
    return [jnp.concatenate(pieces, axis=0).astype(BF16) for pieces in (even, odd)]


def split_channels(low, pair, even, odd, first=0):
    chunks = low.shape[1] // CHUNK_ROWS
    for start in range(0, even.shape[0], SUBLANES):
        block = (first + start) // SUBLANES
        row = block % chunks * CHUNK_ROWS + pair * PACKED
        low[block // chunks, pl.ds(pl.multiple_of(row, PACKED), PACKED), :] = jnp.concatenate(
            [even[start : start + SUBLANES], odd[start : start + SUBLANES]], axis=0
        ).astype(low.dtype)


def each_pair(body):
    for pair in range(SUBLANES // 2):
        body(pair)


class Forward:
    results = 1

    def __init__(self, tokens, incoming):
        self.tokens, self.incoming = tokens, incoming

    def scratch(self, low):
        block = pltpu.VMEM((SUBLANES, self.tokens, self.tokens), BF16)
        return [low] * 3 + [block] * 2 + [pltpu.SemaphoreType.DMA((4,))]

    def loads(self, i, held):
        return [
            pltpu.make_async_copy(i.got[place], held[1 + place], held[5].at[place])
            for place in range(2)
        ]

    def saves(self, o, held):
        return [
            pltpu.make_async_copy(held[3], o.left, held[5].at[2]),
            pltpu.make_async_copy(held[4], o.right, held[5].at[3]),
        ]

    def load(self, i, held):
        for copy in self.loads(i, held):
            copy.start()

    def multiply(self, i, o, held):
        tri, left_got, right_got, left_block, right_block = held[:5]
        for copy in self.loads(i, held):
            copy.wait()
        axis = 0 if self.incoming else 1

        def step(pair):
            lefts, rights = join_channels(left_got, pair), join_channels(right_got, pair)
            found = []
            for index in range(2):
                left_block[2 * pair + index] = lefts[index]
                right_block[2 * pair + index] = rights[index]
                found.append(product_of(lefts[index], rights[index], axis, axis))
            split_channels(tri, pair, *found)

        each_pair(step)
        for copy in self.saves(o, held):
            copy.start()

    def end(self, o, held):
        for copy in self.saves(o, held):
            copy.wait()


class Backward:
    results = 2

    def __init__(self, tokens, incoming):
        self.tokens, self.incoming = tokens, incoming

    def scratch(self, low):
        block = pltpu.VMEM((SUBLANES, self.tokens, self.tokens), BF16)
        return [low] * 3 + [block] * 2 + [pltpu.SemaphoreType.DMA((3,))]

    def loads(self, i, held):
        sources = (i.got[0], i.owned.left, i.owned.right)
        return [
            pltpu.make_async_copy(source, held[2 + place], held[5].at[place])
            for place, source in enumerate(sources)
        ]

    def load(self, i, held):
        for copy in self.loads(i, held):
            copy.start()

    def multiply(self, i, o, held):
        grad_left, grad_right, got, left_block, right_block = held[:5]
        for copy in self.loads(i, held):
            copy.wait()

        def step(pair):
            lefts, rights = [], []
            for index, grad in enumerate(join_channels(got, pair)):
                left, right = left_block[2 * pair + index], right_block[2 * pair + index]
                if self.incoming:
                    lefts.append(product_of(right, grad, 1, 1))
                    rights.append(product_of(left, grad, 1, 0))
                else:
                    lefts.append(product_of(grad, right, 1, 0))
                    rights.append(product_of(grad, left, 0, 0))
            split_channels(grad_left, pair, *lefts)
            split_channels(grad_right, pair, *rights)

        each_pair(step)

    def end(self, o, held):
        pass


def prepare(triangle_input, triangle_output, expand_weight, reduce_weight, distogram_weight, norm_gains):
    merged = [
        triangle_input.reshape((-1,) + triangle_input.shape[2:]),
        triangle_output.reshape((-1,) + triangle_output.shape[2:]),
        expand_weight,
        reduce_weight,
        distogram_weight.T[None],
    ]
    count = len(merged)

    def kernel(*refs):
        for source, plain, turned in zip(refs[:count], refs[count + 1 :: 2], refs[count + 2 :: 2]):
            for index in range(source.shape[0]):
                value = source[index]
                plain[index] = value.astype(BF16)
                turned[index] = value.T.astype(BF16)
        gains = refs[count][...]
        refs[-1][...] = gains.T

    shapes = []
    for array in merged:
        depth, rows, cols = array.shape
        shapes.append(jax.ShapeDtypeStruct((depth, rows, cols), BF16))
        shapes.append(jax.ShapeDtypeStruct((depth, cols, rows), BF16))
    shapes.append(jax.ShapeDtypeStruct(norm_gains.shape[::-1], F32))
    return pl.pallas_call(
        kernel,
        out_shape=shapes,
        compiler_params=pltpu.CompilerParams(vmem_limit_bytes=VMEM_BYTES),
        name="prepare",
    )(*merged, norm_gains)


def by_crop(value, rows_axis, head_axis):
    count, heads = rows_axis, head_axis
    half = count // 2
    inner = half // 2 * heads
    same, other = [], []
    for row in range(count):
        place = row % inner // heads * 2 + row // inner
        for head in range(heads):
            source = row * heads + head
            for crop, pairs in ((head, same), (1 - head, other)):
                pairs.append((source, (crop * half + place) * heads + row % heads))
    head = lax.axis_index("head")
    crop = lax.axis_index("row") // half
    mine = lax.dynamic_index_in_dim(value, head, 0, keepdims=False)
    rest = lax.dynamic_index_in_dim(value, 1 - head, 0, keepdims=False)
    mine = lax.ppermute(mine, ("row", "head"), same)
    rest = lax.ppermute(rest, ("row", "head"), other)
    low = jnp.where(crop == 0, mine, rest)
    high = jnp.where(crop == 0, rest, mine)
    return jnp.concatenate([low, high], axis=-1)


def reduce_rest(half, peers, collective_id, grids, gains, rows):
    sizes = [grid.shape[0] * grid.shape[1] // LANES for grid in grids]
    used = sum(sizes) + len(gains) + SUBLANES * len(rows)
    part = -(-used // (peers * SUBLANES)) * SUBLANES
    total = part * peers
    starts, spot = [], 0
    for size in sizes:
        starts.append(spot)
        spot += size
    row_starts = []
    for _ in rows:
        row_starts.append(spot)
        spot += SUBLANES
    gain_start = spot
    count = len(grids) + len(gains) + len(rows)

    def kernel(*refs):
        out, local, got, mine, other, sends, recvs, back_sends, back_recvs, twin_sems = refs[count:]
        ring = Exchange(peers, half)
        ring.greet()
        barrier = pltpu.get_barrier_semaphore()
        pl.semaphore_signal(barrier, inc=1, device_id=ring.twin, device_id_type=MESH)
        for grid, start in zip(refs[: len(grids)], starts):
            height, width = grid.shape
            for column in range(width // LANES):
                local[pl.ds(start + column * height, height), :] = grid[
                    :, column * LANES : (column + 1) * LANES
                ]
        ones = jnp.ones((SUBLANES, LANES), F32)
        for index, gain in enumerate(refs[len(grids) : len(grids) + len(gains)]):
            folded = lax.dot_general(
                ones,
                gain[...],
                (((1,), (1,)), ((), ())),
                precision=lax.Precision.HIGHEST,
                preferred_element_type=F32,
            )
            local[pl.ds(gain_start + index, 1), :] = folded[:1]
        for row, start in zip(refs[len(grids) + len(gains) : count], row_starts):
            local[pl.ds(start, 1), :] = row[...]
            local[pl.ds(start + 1, SUBLANES - 1), :] = jnp.zeros((SUBLANES - 1, LANES), F32)
        tail = gain_start + len(gains)
        if total > tail:
            local[pl.ds(tail, total - tail), :] = jnp.zeros((total - tail, LANES), F32)
        pl.semaphore_wait(barrier, peers)

        def block(peer):
            return pl.ds(pl.multiple_of(peer * part, SUBLANES), part)

        here = block(ring.me)

        def gather(step):
            peer = ring.peer(step)
            return pltpu.make_async_remote_copy(
                src_ref=local.at[block(peer), :],
                dst_ref=got.at[here, :],
                send_sem=sends.at[step],
                recv_sem=recvs.at[step],
                device_id=ring.device(peer),
                device_id_type=MESH,
            )

        def spread(step):
            return pltpu.make_async_remote_copy(
                src_ref=out.at[here, :],
                dst_ref=out.at[here, :],
                send_sem=back_sends.at[step],
                recv_sem=back_recvs.at[step],
                device_id=ring.device(ring.peer(step)),
                device_id_type=MESH,
            )

        for step in ring.order:
            gather(step).start()
        got[here, :] = local[here, :]
        for step in ring.order:
            gather(step).wait()
        value = got[pl.ds(0, part), :]
        for peer in range(1, peers):
            value = value + got[pl.ds(peer * part, part), :]
        mine[...] = value
        copy = pltpu.make_async_remote_copy(
            src_ref=mine,
            dst_ref=other,
            send_sem=twin_sems.at[0],
            recv_sem=twin_sems.at[1],
            device_id=ring.twin,
            device_id_type=MESH,
        )
        copy.start()
        copy.wait()
        out[here, :] = mine[...] + other[...]
        for step in ring.order:
            spread(step).start()
        for step in ring.order:
            spread(step).wait()

    inside = pl.BlockSpec(memory_space=pltpu.VMEM)
    whole = pl.pallas_call(
        kernel,
        in_specs=[inside] * count,
        out_specs=inside,
        out_shape=jax.ShapeDtypeStruct((total, LANES), F32),
        scratch_shapes=[pltpu.VMEM((total, LANES), F32)] * 2
        + [pltpu.VMEM((part, LANES), F32)] * 2
        + [pltpu.SemaphoreType.DMA((peers,))] * 4
        + [pltpu.SemaphoreType.DMA((2,))],
        compiler_params=pltpu.CompilerParams(
            collective_id=collective_id, has_side_effects=True, vmem_limit_bytes=REDUCE_BYTES
        ),
        cost_estimate=pl.CostEstimate(flops=0, bytes_accessed=0, transcendentals=0),
        name="reduce_rest",
    )(*grids, *gains, *rows)
    return whole, starts, row_starts, gain_start


def update(rest, starts, row_starts, gain_start, early, weights, firsts, seconds):
    layers, kinds, width, mixed = weights[2].shape
    hidden = weights[4].shape[2]
    early_in, early_up, early_rows = early
    given = [rest, *early_in, *early_up, *early_rows]
    count = len(given)

    def kernel(*refs):
        whole = refs[0]
        in_refs = refs[1 : 1 + len(early_in)]
        up_refs = refs[1 + len(early_in) : count - layers]
        row_refs = refs[count - layers : count]
        states = [refs[count + 8 * kind : count + 8 * (kind + 1)] for kind in range(3)]
        scalars = refs[count + 24 : count + 27]
        results = refs[count + 27 :]

        def taken(start, size):
            return whole[pl.ds(start, size), :]

        def wide(start, height, columns):
            return jnp.concatenate(
                [taken(start + column * height, height) for column in range(columns)], axis=1
            )

        loss = jnp.sum(taken(row_starts[0], 1), axis=1, keepdims=True)
        valid = jnp.sum(taken(row_starts[1], 1), axis=1, keepdims=True)
        table_rows, single_rows = weights[0].shape[0], weights[1].shape[0]
        downs = hidden // 2
        grads = {}
        grads[0, ()] = taken(starts[4], table_rows)
        grads[1, ()] = jnp.concatenate(
            [taken(starts[5], single_rows), taken(starts[6], single_rows)], axis=1
        )
        for layer in range(layers):
            spot = 0
            for kind in range(kinds):
                if layer == 0:
                    grads[2, (layer, kind)] = wide(starts[kind], width, mixed // LANES)
                else:
                    grads[2, (layer, kind)] = in_refs[(layer - 1) * kinds + kind][...]
                if layer == 0 and kind == 0:
                    grads[3, (layer, kind)] = taken(starts[2], width)
                else:
                    grads[3, (layer, kind)] = row_refs[layer][pl.ds(spot, width), :]
                    spot += width
            grads[4, (layer,)] = up_refs[layer][...]
            grads[5, (layer,)] = row_refs[layer][pl.ds(spot, downs), :]
        grads[6, ()] = taken(starts[3], weights[6].shape[0])
        grads[7, ()] = taken(gain_start, weights[7].shape[0])
        squares = jnp.zeros((1, 1), F32)
        for key in grads:
            grads[key] = grads[key] / valid
            squares = squares + jnp.sum(grads[key] * grads[key], axis=(0, 1), keepdims=True)
        norm = jnp.sqrt(squares)
        factor = jnp.minimum(1.0, CLIP_NORM / (norm + 1e-06))
        for ref, value in zip(scalars, (loss, valid, norm)):
            ref[...] = value
        for (index, spot), grad in grads.items():
            rate = GAIN_RATE if index == 7 else WEIGHT_RATE
            decay = 0.0 if index == 7 else WEIGHT_DECAY
            new = adamw(
                states[0][index][spot],
                grad * factor,
                states[1][index][spot],
                states[2][index][spot],
                rate,
                decay,
            )
            for ref, value in zip(results[3 * index : 3 * index + 3], new):
                ref[spot] = value

    one = jax.ShapeDtypeStruct((1, 1), F32)
    shapes = [one] * 3
    for weight in weights:
        shapes += [jax.ShapeDtypeStruct(weight.shape, F32)] * 3
    found = pl.pallas_call(
        kernel,
        out_shape=shapes,
        compiler_params=pltpu.CompilerParams(vmem_limit_bytes=UPDATE_BYTES),
        name="update",
    )(*given, *weights, *firsts, *seconds)
    return tuple(value[0, 0] for value in found[:3]) + tuple(found[3:])


def step_by_crop(row_count, head_count, given, weights, firsts, seconds):
    single, residue_index, chain_index, token_mask, pair_valid, target_bins = given
    relative_table, single_weight, triangle_input, triangle_output = weights[:4]
    expand_weight, reduce_weight, distogram_weight, norm_gains = weights[4:]
    crops, tokens = token_mask.shape
    width = relative_table.shape[1]
    layers = triangle_input.shape[0]
    half = row_count // crops
    peers = half * head_count
    rows = tokens // peers
    row_index = lax.axis_index("row")
    crop = row_index // half
    start = position(row_index % half, lax.axis_index("head"), half, head_count) * rows

    placed = by_crop(jnp.stack([pair_valid, target_bins], axis=1), row_count, head_count)
    valid, target = placed[0], placed[1]

    def of_crop(array):
        return lax.dynamic_index_in_dim(array, crop, 0, keepdims=False)

    def of_rows(array):
        return lax.dynamic_slice_in_dim(array, start, rows, 0)

    residues, chains = of_crop(residue_index), of_crop(chain_index)
    reach = (relative_table.shape[0] - 2) // 2
    bins = jnp.where(
        of_rows(chains)[:, None] == chains[None, :],
        jnp.clip(of_rows(residues)[:, None] - residues[None, :], -reach, reach) + reach,
        2 * reach + 1,
    )
    present = of_crop(token_mask).astype(F32)
    pair_mask = of_rows(present)[:, None] * present[None, :]
    loss_weight = pair_mask * valid.astype(F32)
    table_rows = -(-relative_table.shape[0] // PACKED) * PACKED
    table_t = jnp.pad(relative_table, ((0, table_rows - relative_table.shape[0]), (0, 0))).T
    tokens_single = of_crop(single)
    proj = project(tokens_single, single_weight.astype(BF16))
    proj_rows = of_rows(proj[:, :width])[:, :, None]
    proj_cols = proj[:, width:].T
    bins, pair_mask = Arg(bins[:, None, :], ROWS), Arg(pair_mask[:, None, :], ROWS)

    prepared = prepare(
        triangle_input, triangle_output, expand_weight, reduce_weight, distogram_weight, norm_gains
    )
    mix, mix_t, out, out_t, up, up_t, down, down_t, logits_t, logits, gains = prepared
    hidden = up.shape[2]

    def gain(index):
        return Arg(gains, WHOLE, column=index)

    def layer_of(array, index, *block):
        shape = block or array.shape[1:]
        return Arg(array, WHOLE, (index, 0, 0), (None,) + tuple(shape))

    def triangle_weights(layer, kind, starts=False, finishes=False, back=False):
        index = 2 * layer + kind
        found = dict(gain0=gain(5 * layer + 2 * kind))
        if starts:
            found.update(mix_t=layer_of(mix_t, index, 4 * width, width))
        if starts and back:
            found.update(mix=layer_of(mix, index))
        if finishes:
            found.update(
                gain1=gain(5 * layer + 2 * kind + 1),
                gate_t=Arg(mix_t, WHOLE, (index, 4, 0), (None, width, width)),
                out_t=layer_of(out_t, index),
            )
        if finishes and back:
            found.update(out=layer_of(out, index))
        return found

    def transition_weights(layer, forth=True, back=False):
        found = dict(gain=gain(5 * layer + 4), up_t=layer_of(up_t, layer))
        if forth:
            found.update(down_t=layer_of(down_t, layer))
        if back:
            found.update(up=layer_of(up, layer), down=layer_of(down, layer))
        return found

    def state_out():
        return Out((rows, width, tokens), F32, ROWS)

    def sum_out(*shape):
        return Out(shape, F32, SUM)

    def gain_out():
        return sum_out(width, LANES)

    def back_start_outs():
        return dict(
            grad_gate=Out((rows, width, tokens), BF16, ROWS),
            out=sum_out(width, width),
            gain1=gain_out(),
        )

    def back_finish_outs():
        return dict(mix=sum_out(width, 5 * width), gain0=gain_out())

    def transition_outs():
        return dict(up=sum_out(width, hidden), down=sum_out(hidden // 2, width), gain=gain_out())

    identities = iter(range(4 * layers + 2))

    group = (peers, half, rows, tokens)
    block_out = Out((SUBLANES, tokens, tokens), BF16, ANYWHERE)

    def got_out(count):
        return [Out((peers, rows * SUBLANES, tokens), BF16, ANYWHERE)] * count

    def got_in(stage):
        return [Arg(array, ANYWHERE) for array in stage.got]

    def landed_out():
        return Out((peers, rows * SUBLANES, tokens), BF16, LANDED)

    def owned(kept):
        return dict(left=Arg(kept.left, ANYWHERE), right=Arg(kept.right, ANYWHERE))

    kept, states, middles, tris = {}, {}, {}, {}

    def first_body(i, o, rows, arrived, sent):
        state = dot(i.table_t[...], bins_hot(i.bins, rows, table_rows))
        yield
        cols = i.proj_cols[...]
        state = state + jnp.concatenate([cols + i.proj_rows[row] for row in rows], axis=1)
        write_rows(o.state, rows, state)
        yield from triangle_start(i.start, i, rows, sent, state)

    got = run_stage(
        first_body,
        "first_state",
        next(identities),
        group,
        dict(
            bins=bins,
            proj_rows=Arg(proj_rows, ROWS),
            proj_cols=Arg(proj_cols, WHOLE),
            table_t=Arg(table_t.astype(BF16), WHOLE),
            mask=pair_mask,
            start=triangle_weights(0, 0, starts=True),
        ),
        dict(state=state_out(), got=got_out(2)),
        wires=2,
    )
    states[0, 0] = got.state

    def between_body(i, o, rows, arrived, sent):
        state, _ = yield from triangle_finish(
            i.end, rows, arrived[0], read_rows(i.state, rows)
        )
        write_rows(o.state, rows, state)
        yield from triangle_start(i.start, i, rows, sent, state)

    def layer_end_body(i, o, rows, arrived, sent):
        state, _ = yield from triangle_finish(
            i.end, rows, arrived[0], read_rows(i.state, rows)
        )
        write_rows(o.middle, rows, state)
        lifted = yield from transition(i.lift, state)
        state = state + dot(i.lift.down_t[...], lifted[5])
        yield
        write_rows(o.state, rows, state)
        yield from triangle_start(i.start, i, rows, sent, state)

    for layer in range(layers):
        got = run_stage(
            between_body,
            "between_updates",
            next(identities),
            group,
            dict(
                got=got_in(got),
                state=Arg(states[layer, 0], ROWS),
                mask=pair_mask,
                end=triangle_weights(layer, 0, finishes=True),
                start=triangle_weights(layer, 1, starts=True),
            ),
            dict(
                state=state_out(),
                landed=landed_out(),
                left=block_out,
                right=block_out,
                got=got_out(2),
            ),
            Forward(tokens, False),
            wires=2,
        )
        kept[layer, 0], states[layer, 1], tris[layer, 0] = got, got.state, got.landed
        if layer + 1 == layers:
            break
        got = run_stage(
            layer_end_body,
            "layer_end",
            next(identities),
            group,
            dict(
                got=got_in(got),
                state=Arg(states[layer, 1], ROWS),
                mask=pair_mask,
                end=triangle_weights(layer, 1, finishes=True),
                lift=transition_weights(layer),
                start=triangle_weights(layer + 1, 0, starts=True),
            ),
            dict(
                middle=state_out(),
                state=state_out(),
                landed=landed_out(),
                left=block_out,
                right=block_out,
                got=got_out(2),
            ),
            Forward(tokens, True),
            wires=2,
        )
        kept[layer, 1], states[layer + 1, 0], tris[layer, 1] = got, got.state, got.landed
        middles[layer] = got.middle

    def loss_body(i, o, rows, arrived, sent):
        state, kept_triangle = yield from triangle_finish(
            i.end, rows, arrived[0], read_rows(i.state, rows)
        )
        lifted = yield from transition(i.lift, state)
        state = state + dot(i.lift.down_t[...], lifted[5])
        yield
        grad = yield from head_back(i.head, o.head, rows, state)
        grad = yield from transition_back(i.lift, o.lift, grad, lifted)
        write_rows(o.grad, rows, grad)
        yield from triangle_back_start(i.end, o.end, rows, sent[0], grad, kept_triangle)

    top = layers - 1
    got = run_stage(
        loss_body,
        "loss",
        next(identities),
        group,
        dict(
            got=got_in(got),
            state=Arg(states[top, 1], ROWS),
            end=triangle_weights(top, 1, finishes=True, back=True),
            lift=transition_weights(top, back=True),
            head=dict(
                gain=gain(5 * layers),
                logits=layer_of(logits, 0),
                logits_t=layer_of(logits_t, 0),
                target=Arg(target[:, None, :], ROWS),
                weight=Arg(loss_weight[:, None, :], ROWS),
            ),
        ),
        dict(
            grad=state_out(),
            head=dict(
                loss=sum_out(1, LANES),
                count=sum_out(1, LANES),
                logits=sum_out(distogram_weight.shape[1], width),
                gain=gain_out(),
            ),
            lift=transition_outs(),
            end=back_start_outs(),
            left=block_out,
            right=block_out,
            got=got_out(1),
        ),
        Forward(tokens, True),
        wires=1,
    )
    kept[top, 1] = got
    head, lifts, ends, begins = got.head, {top: got.lift}, {(top, 1): got.end}, {}

    def between_back_body(i, o, rows, arrived, sent):
        grad = yield from triangle_back_finish(i.start, i, o.start, rows, arrived)
        write_rows(o.grad, rows, grad)
        _, kept_triangle = yield from triangle_finish(
            i.end, rows, i.tri, read_rows(i.before, rows)
        )
        yield from triangle_back_start(i.end, o.end, rows, sent[0], grad, kept_triangle)

    def layer_end_back_body(i, o, rows, arrived, sent):
        grad = yield from triangle_back_finish(i.start, i, o.start, rows, arrived)
        lifted = yield from transition(i.lift, read_rows(i.middle, rows))
        grad = yield from transition_back(i.lift, o.lift, grad, lifted)
        write_rows(o.grad, rows, grad)
        _, kept_triangle = yield from triangle_finish(
            i.end, rows, i.tri, read_rows(i.before, rows)
        )
        yield from triangle_back_start(i.end, o.end, rows, sent[0], grad, kept_triangle)

    def first_back_body(i, o, rows, arrived, sent):
        grad = yield from triangle_back_finish(i.start, i, o.start, rows, arrived)
        hot = bins_hot(i.bins, rows, table_rows)
        high = grad.astype(BF16)
        low = (grad - high.astype(F32)).astype(BF16)
        o.table[...] += dot_pairs(hot, high) + dot_pairs(hot, low)
        yield
        for place, row in enumerate(rows):
            part = grad[:, place * tokens : (place + 1) * tokens]
            o.rows[row] = fold(part)
            o.cols[...] += part

    def layer_sums(layer):
        kinds = (0, 1) if layer else (1,)
        mixes = [begins[layer, 1].mix] if layer else []
        if layer + 1 < layers:
            mixes.append(begins[layer + 1, 0].mix)
        outs = [ends[layer, kind].out for kind in kinds]
        return (mixes, lifts[layer].up, jnp.concatenate(outs + [lifts[layer].down], axis=0))

    for layer in reversed(range(layers)):
        for kind in (1, 0):
            if (layer, kind) == (0, 0):
                first = lax.psum(layer_sums(top), ("row", "head"))
                first, got.grad = lax.optimization_barrier((first, got.grad))
            inputs = dict(
                got=got_in(got),
                owned=owned(kept[layer, kind]),
                grad=Arg(got.grad, ROWS),
                grad_gate=Arg(got.end.grad_gate, ROWS),
                state=Arg(states[layer, kind], ROWS),
                mask=pair_mask,
                start=triangle_weights(layer, kind, starts=True, back=True),
            )
            outputs = dict(start=back_finish_outs())
            products = Backward(tokens, kind == 1)
            if layer == 0 and kind == 0:
                got = run_stage(
                    first_back_body,
                    "first_state_back",
                    next(identities),
                    group,
                    dict(bins=bins, **inputs),
                    dict(
                        table=sum_out(table_rows, width),
                        rows=Out((rows, width, LANES), F32, ROWS),
                        cols=sum_out(width, tokens),
                        **outputs,
                    ),
                    products,
                )
                begins[layer, kind] = got.start
                break
            before = (layer, 0) if kind == 1 else (layer - 1, 1)
            inputs.update(
                before=Arg(states[before], ROWS),
                tri=Arg(tris[before], LANDED),
                end=triangle_weights(*before, finishes=True, back=True),
            )
            outputs.update(grad=state_out(), end=back_start_outs(), got=got_out(1))
            if kind == 1:
                body, name = between_back_body, "between_updates_back"
            else:
                body, name = layer_end_back_body, "layer_end_back"
                inputs.update(
                    middle=Arg(middles[layer - 1], ROWS),
                    lift=transition_weights(layer - 1, forth=False, back=True),
                )
                outputs.update(lift=transition_outs())
            got = run_stage(
                body, name, next(identities), group, inputs, outputs, products, wires=1
            )
            begins[layer, kind], ends[before] = got.start, got.end
            if kind == 0:
                lifts[layer - 1] = got.lift

    early = {layer: layer_sums(layer) for layer in range(top)}
    early = lax.psum(early, ("head", "row"))
    early[top] = first
    early_mixes = {}
    for layer in range(layers):
        mixes = list(early[layer][0])
        if layer:
            early_mixes[layer, 1] = mixes.pop(0)
        if mixes:
            early_mixes[layer + 1, 0] = mixes.pop(0)
    early = (
        [early_mixes[layer, kind] for layer in range(1, layers) for kind in range(2)],
        [early[layer][1] for layer in range(layers)],
        [early[layer][2] for layer in range(layers)],
    )

    wide_single = tokens_single.astype(F32)
    row_part = jnp.einsum(
        "is,ic->sc",
        of_rows(wide_single),
        jnp.sum(got.rows, axis=2),
        precision=lax.Precision.HIGHEST,
    )
    col_part = jnp.einsum("js,cj->sc", wide_single, got.cols, precision=lax.Precision.HIGHEST)
    partial_gains = []
    for layer in range(layers):
        for kind in range(2):
            partial_gains += [begins[layer, kind].gain0, ends[layer, kind].gain1]
        partial_gains.append(lifts[layer].gain)
    partial_gains.append(head.gain)
    grids = [
        begins[0, 0].mix,
        begins[0, 1].mix,
        ends[0, 0].out,
        head.logits,
        got.table,
        row_part,
        col_part,
    ]
    def turned(arrays):
        return arrays[:6] + (arrays[6].T,) + arrays[7:]

    rest, *starts = reduce_rest(
        half, peers, next(identities), grids, partial_gains, [head.loss, head.count]
    )
    found = update(rest, *starts, early, turned(weights), turned(firsts), turned(seconds))
    return found[:21] + tuple(value.T for value in found[21:24]) + found[24:]


def per_device(
    row_count,
    head_count,
    single,
    residue_index,
    chain_index,
    token_mask,
    pair_valid,
    target_bins,
    relative_table,
    single_weight,
    triangle_input,
    triangle_output,
    expand_weight,
    reduce_weight,
    distogram_weight,
    norm_gains,
    first_table,
    second_table,
    first_single,
    second_single,
    first_input,
    second_input,
    first_output,
    second_output,
    first_expand,
    second_expand,
    first_reduce,
    second_reduce,
    first_logits,
    second_logits,
    first_gains,
    second_gains,
):
    crops, tokens = token_mask.shape
    width = relative_table.shape[1]
    peers = row_count * head_count // crops
    given = (
        single,
        residue_index,
        chain_index,
        token_mask,
        pair_valid,
        target_bins,
        relative_table,
        single_weight,
        triangle_input,
        triangle_output,
        expand_weight,
        reduce_weight,
        distogram_weight,
        norm_gains,
    )
    weights = (
        relative_table,
        single_weight,
        triangle_input,
        triangle_output,
        expand_weight,
        reduce_weight,
        distogram_weight,
        norm_gains,
    )
    firsts = (
        first_table,
        first_single,
        first_input,
        first_output,
        first_expand,
        first_reduce,
        first_logits,
        first_gains,
    )
    seconds = (
        second_table,
        second_single,
        second_input,
        second_output,
        second_expand,
        second_reduce,
        second_logits,
        second_gains,
    )
    if (
        crops == 2
        and head_count == 2
        and width == LANES
        and width == SUBLANES * peers
        and tokens % (peers * SUBLANES) == 0
        and tokens % (3 * LANES) == 0
    ):
        return step_by_crop(row_count, head_count, given[:6], weights, firsts, seconds)
    local = gradients_by_block(*given)
    summed = lax.psum(local, ("row", "head"))
    loss_sum, valid_count = summed[0], summed[1]
    grads = [grad / valid_count for grad in summed[2:]]
    squares = jnp.zeros((), jnp.float32)
    for g in grads:
        squares = squares + jnp.sum(g * g)
    gradient_norm = jnp.sqrt(squares)
    factor = jnp.minimum(1.0, CLIP_NORM / (gradient_norm + 1e-06))
    result = []
    for index in range(8):
        rate = GAIN_RATE if index == 7 else WEIGHT_RATE
        decay = 0.0 if index == 7 else WEIGHT_DECAY
        result.extend(
            adamw(weights[index], grads[index] * factor, firsts[index], seconds[index], rate, decay)
        )
    return (
        loss_sum,
        valid_count,
        gradient_norm,
        result[0],
        result[1],
        result[2],
        result[3],
        result[4],
        result[5],
        result[6],
        result[7],
        result[8],
        result[9],
        result[10],
        result[11],
        result[12],
        result[13],
        result[14],
        result[15],
        result[16],
        result[17],
        result[18],
        result[19],
        result[20],
        result[21],
        result[22],
        result[23],
    )


def solution(mesh):
    placed = (
        P(),
        P(),
        P(),
        P(),
        P(None, "row", "head"),
        P(None, "row", "head"),
        P(),
        P(),
        P(),
        P(),
        P(),
        P(),
        P(),
        P(),
        P(),
        P(),
        P(),
        P(),
        P(),
        P(),
        P(),
        P(),
        P(),
        P(),
        P(),
        P(),
        P(),
        P(),
        P(),
        P(),
    )
    return jax.shard_map(
        functools.partial(per_device, mesh.shape["row"], mesh.shape["head"]),
        mesh=mesh,
        in_specs=placed,
        out_specs=(
            P(),
            P(),
            P(),
            P(),
            P(),
            P(),
            P(),
            P(),
            P(),
            P(),
            P(),
            P(),
            P(),
            P(),
            P(),
            P(),
            P(),
            P(),
            P(),
            P(),
            P(),
            P(),
            P(),
            P(),
            P(),
            P(),
            P(),
        ),
        check_vma=False,
    )
```
